32 devices in a mesh: seq: 8 (over z, y), dp: 4 (over x, core).
Axes of the slice: x: 2, y: 2, z: 4, core: 2. Of those that a mesh axis runs over, the one named last changes fastest.
Arguments:
- queries: bfloat16 [4, 1024, 2048], P('dp', 'seq'), may hold values from -48 to 48
- keys: bfloat16 [4, 1024, 2048], P('dp', 'seq'), may hold values from -8 to 8
- values: bfloat16 [4, 1024, 2048], P('dp', 'seq'), may hold values from -6 to 6
- shifts: float32 [4, 2048], P('dp'), may hold values from -1.2 to 1.2
- scales: float32 [4, 2048], P('dp'), may hold values from -0.9 to 0.9
- proj_out: bfloat16 [2048, 64], replicated, may hold values from -0.125 to 0.125
- patch_embed: bfloat16 [16, 64, 1280], P(None, 'seq'), may hold values from -0.1875 to 0.1875
- pos_embed: bfloat16 [64, 1280], replicated, may hold values from -1.796875 to 1.796875
- pre_gain: float32 [1280], replicated, may hold values from 0.25 to 1.75
- post_gain: float32 [1280], replicated, may hold values from 0.25 to 1.75
- prompt: float32 [4, 1280], P('dp'), may hold values from -6 to 6
- cotangent: float32 [4], P('dp'), may hold values from 2 to 20
Outputs:
- rewards: float32 [4], P('dp')
- attn_grad: bfloat16 [4, 16, 1024, 128], P('dp', 'seq')
- proj_grad: float32 [2048, 64], replicated
The draws below stay inside these ranges and needn't reach their ends.
All inputs are finite; a program needn't handle non-finite values.
Results may differ from the reference program's by a relative error of at most 0.0065.
Values may be sent and summed in bfloat16 or wider, within the bound.
No kernel may reach another device: no remote copies, remote signals or barrier semaphores. Data moves between devices by JAX's collectives and lax.ppermute only.
A program may use at most 64 MiB of HBM per device.

```python
import math
import jax
import jax.numpy as jnp
from jax import lax

HEADS = 16
HD = 128
CH = 64
GW = 64
VW = 1280
TOK_DEV = 128
IMAGES = 4
LAT = 1024
QSPLIT = 1
NPATCH = 64
N_SEQ = 8


def keys_common(key, spread):
    array_shape = (IMAGES, LAT, HEADS * HD)
    noise_key = jax.random.fold_in(key, 101)
    gauss = jax.random.normal(key, array_shape, jnp.float32)
    shared = spread * gauss
    nearby = jnp.roll(shared, 1, axis=1) + 0.3 * jax.random.normal(noise_key, array_shape, jnp.float32)
    position = jnp.arange(LAT)[None, :, None]
    shared = jnp.where(position % 64 == 1, nearby, shared)
    return jnp.clip(shared, -8.0, 8.0)


def draw_keys(key, part):
    shared = keys_common(key, 2.0)
    return shared.astype(jnp.bfloat16)


def draw_queries(key, part):
    key = jax.random.fold_in(key, 7)
    array_shape = (IMAGES, LAT, HEADS * HD)
    query_key = jax.random.fold_in(key, 0)
    drawn = 2.0 * jax.random.normal(query_key, array_shape, jnp.float32)
    return jnp.clip(drawn, -48.0, 48.0).astype(jnp.bfloat16)


def shard_levels(stream_key, dims, cuts, low, top_value):
    gain, own = 1.0, jax.random.fold_in(stream_key, 6)
    for dim, shards_of in cuts:
        steps = jnp.exp(jax.random.uniform(jax.random.fold_in(own, dim), (shards_of,), jnp.float32, low / len(cuts), top_value / len(cuts)))
        gain = gain * jnp.repeat(steps, dims[dim] // shards_of).reshape([-1 if axis == dim else 1 for axis in range(len(dims))])
    return gain


def noise(stream_key, extent, width, bound, cuts=(), kind=jnp.bfloat16):
    values = width * jax.random.normal(stream_key, extent, jnp.float32)
    if cuts:
        values = values * shard_levels(stream_key, extent, cuts, -0.22, 0.18)
    return jnp.clip(values, -bound, bound).astype(kind)


def setup_inputs(seed: int = 0) -> dict:
    key_of = jax.random.split(jax.random.key(seed), 13)
    return {
        "queries": draw_queries(jax.random.fold_in(key_of[12], 71), 0),
        "keys": draw_keys(jax.random.fold_in(key_of[12], 71), 0),
        "values": noise(key_of[2], (IMAGES, LAT, HEADS * HD), 1.0, 6.0, ((0, 4), (1, 8))),
        "shifts": noise(key_of[3], (IMAGES, HEADS * HD), 0.2, 1.2, ((0, 4),), jnp.float32),
        "scales": noise(key_of[4], (IMAGES, HEADS * HD), 0.3, 0.9, ((0, 4),), jnp.float32),
        "proj_out": noise(key_of[5], (HEADS * HD, CH), (HEADS * HD) ** -0.5, 0.125),
        "patch_embed": noise(key_of[6], (16, CH, VW), (16 * CH) ** -0.5, 0.1875, ((1, 8),)),
        "pos_embed": noise(key_of[7], (NPATCH, VW), 0.3, 1.796875),
        "pre_gain": jnp.clip(1.0 + 0.15 * jax.random.normal(key_of[8], (VW,), jnp.float32), 0.25, 1.75),
        "post_gain": jnp.clip(1.0 + 0.15 * jax.random.normal(key_of[9], (VW,), jnp.float32), 0.25, 1.75),
        "prompt": noise(key_of[10], (IMAGES, VW), 1.0, 6.0, ((0, 4),), jnp.float32),
        "cotangent": jnp.clip(jnp.exp(math.log(20.0) - 2.3025851 * jax.random.uniform(key_of[11], (IMAGES,), jnp.float32) ** shard_levels(key_of[11], (IMAGES,), ((0, 4),), -0.2, 0.2)), 2.0, 20.0),
    }


epsilon = 1e-05

def layer_norm(features):
    center = features - lax.optimization_barrier(jnp.mean(features, axis=-1, keepdims=True))
    variance = lax.optimization_barrier(jnp.mean(center * center, axis=-1, keepdims=True))
    return center * lax.rsqrt(variance + epsilon)

def reward_of(embedded, pre_gain, post_gain, prompt):
    normed = layer_norm(embedded) * pre_gain
    pooled = lax.optimization_barrier(jnp.mean(normed, axis=0))
    final = layer_norm(pooled) * post_gain
    cosine = jnp.sum(final * prompt) / (jnp.sqrt(jnp.sum(final * final)) * jnp.sqrt(jnp.sum(prompt * prompt)))
    return 100.0 * cosine

def image_reward(latent, patch_embed, pos_embed, pre_gain, post_gain, prompt):
    patch_grid = latent.reshape(LAT // GW // 4, 4, GW // 4, 4, CH).transpose(0, 2, 1, 3, 4).reshape(NPATCH, 16 * CH)
    embed_rows = patch_embed.reshape(16 * CH, VW).astype(jnp.float32)
    embedded = jnp.dot(patch_grid, embed_rows, precision=lax.Precision.HIGHEST) + pos_embed.astype(jnp.float32)
    return reward_of(embedded, pre_gain, post_gain, prompt)

def attend_head(inputs):
    query_head, key_head, value_head = inputs
    row_total = query_head.shape[0]
    block_rows = math.gcd(row_total, 512)

    def block_attend(query_block):
        logits = jnp.dot(query_block, key_head.T, preferred_element_type=jnp.float32) * HD ** (-0.5)
        row_max = lax.optimization_barrier(jnp.max(logits, axis=-1, keepdims=True))
        weights = jnp.exp(logits - row_max)
        totals = lax.optimization_barrier(jnp.sum(weights, axis=-1, keepdims=True))
        return jnp.dot(weights.astype(jnp.bfloat16), value_head, preferred_element_type=jnp.float32) / totals
    blocks = lax.map(block_attend, query_head.reshape(row_total // block_rows, block_rows, HD))
    return blocks.reshape(row_total, HD)

def attend(queries, keys, values):

    def split_heads(matrix):
        return matrix.reshape(LAT, HEADS, HD).transpose(1, 0, 2)
    heads_out = lax.map(attend_head, (split_heads(queries), split_heads(keys), split_heads(values)))
    return heads_out.transpose(1, 0, 2).reshape(LAT, HEADS * HD)

def reference(queries, keys, values, shifts, scales, proj_out, patch_embed, pos_embed, pre_gain, post_gain, prompt, cotangent):

    def one_image(inputs):
        query_img, key_img, value_img, shift_img, scale_img, prompt_img, weight_img = inputs
        attended = attend(query_img, key_img, value_img)
        modulated = (attended * (1.0 + scale_img) + shift_img).astype(jnp.bfloat16)
        latent = jnp.dot(modulated, proj_out, preferred_element_type=jnp.float32).astype(jnp.bfloat16)

        def reward_fn(latent_in):
            return image_reward(latent_in, patch_embed, pos_embed, pre_gain, post_gain, prompt_img)
        reward, pullback = jax.vjp(reward_fn, latent.astype(jnp.float32))
        latent_grad = pullback(weight_img)[0].astype(jnp.bfloat16)
        modulated_grad = jnp.dot(latent_grad, proj_out.T, preferred_element_type=jnp.float32)
        attn_grad = (modulated_grad * (1.0 + scale_img)).astype(jnp.bfloat16)
        attn_grad = attn_grad.reshape(N_SEQ, QSPLIT, TOK_DEV // QSPLIT, HEADS, HD).transpose(3, 1, 0, 2, 4)
        attn_grad = attn_grad.reshape(HEADS * QSPLIT, LAT // QSPLIT, HD)
        weight_grad = jnp.dot(modulated.T, latent_grad, preferred_element_type=jnp.float32)
        return (reward, attn_grad, weight_grad)
    rewards, attn_grad, weight_grads = lax.map(one_image, (queries, keys, values, shifts, scales, prompt, cotangent))
    proj_grad = lax.optimization_barrier(jnp.sum(weight_grads, axis=0)) * (1.0 / math.sqrt(IMAGES * LAT))
    return (rewards, attn_grad, proj_grad)
```

```python
import functools
import math

import jax
import jax.numpy as jnp
from jax import lax
from jax.experimental import pallas as pl
from jax.experimental.pallas import tpu as pltpu
from jax.sharding import PartitionSpec as P

HEADS = 16
HD = 128
CH = 64
GW = 64
VW = 1280
EPS = 1e-05
BF16 = jnp.bfloat16
F32 = jnp.float32
VMEM_LIMIT = 48 * 1024 * 1024


def mm(a, b):
    return jnp.dot(a, b, preferred_element_type=F32)


def mm_nt(a, b):
    return lax.dot_general(a, b, (((1,), (1,)), ((), ())), preferred_element_type=F32)


def mm_tn(a, b):
    return lax.dot_general(a, b, (((0,), (0,)), ((), ())), preferred_element_type=F32)


def pack_kernel(seq_count, query_parts, part_rows, tok_rows, width, q_ref, k_ref, v_ref, out_ref, sems):
    copies = []
    for dest in range(seq_count):
        group, part = dest // query_parts, dest % query_parts
        cols = pl.ds(group * width, width)
        copies.append(
            pltpu.make_async_copy(
                q_ref.at[0, pl.ds(part * part_rows, part_rows), cols],
                out_ref.at[dest, pl.ds(0, part_rows)],
                sems.at[0, dest],
            )
        )
        copies.append(
            pltpu.make_async_copy(
                k_ref.at[0, :, cols], out_ref.at[dest, pl.ds(part_rows, tok_rows)], sems.at[1, dest]
            )
        )
        copies.append(
            pltpu.make_async_copy(
                v_ref.at[0, :, cols],
                out_ref.at[dest, pl.ds(part_rows + tok_rows, tok_rows)],
                sems.at[2, dest],
            )
        )
    for copy in copies:
        copy.start()
    for copy in copies:
        copy.wait()


def pack(queries, keys, values, seq_count, query_parts, part_rows, tok_rows, width):
    rows = part_rows + 2 * tok_rows
    return pl.pallas_call(
        functools.partial(pack_kernel, seq_count, query_parts, part_rows, tok_rows, width),
        out_shape=jax.ShapeDtypeStruct((seq_count, rows, width), BF16),
        in_specs=[pl.BlockSpec(memory_space=pl.ANY)] * 3,
        out_specs=pl.BlockSpec(memory_space=pl.ANY),
        scratch_shapes=[pltpu.SemaphoreType.DMA((3, seq_count))],
        cost_estimate=pl.CostEstimate(
            flops=0, bytes_accessed=4 * seq_count * rows * width, transcendentals=0
        ),
    )(queries, keys, values)


def attend_kernel(
    seq_count, part_rows, tok_rows, heads,
    in_ref, scale_ref, shift_ref, proj_ref, mod_ref, lat_ref, key_scr, value_scr,
):
    half = part_rows // 2
    width = heads * HD
    factor = HD ** (-0.5) * math.log2(math.e)
    for src in range(seq_count):
        key_scr[pl.ds(src * tok_rows, tok_rows), :] = in_ref[src, pl.ds(part_rows, tok_rows), :]
        value_scr[pl.ds(src * tok_rows, tok_rows), :] = in_ref[
            src, pl.ds(part_rows + tok_rows, tok_rows), :
        ]
    gain = 1.0 + scale_ref[...]
    shift = shift_ref[...]
    proj = proj_ref[...]
    zero = jnp.zeros_like(proj)
    proj_pair = jnp.concatenate(
        [jnp.concatenate([proj, zero], axis=1), jnp.concatenate([zero, proj], axis=1)], axis=0
    )

    def body(src, carry):
        mixed = []
        for head in range(heads):
            cols = pl.ds(head * HD, HD)
            query = in_ref[src, pl.ds(0, part_rows), cols]
            logits = mm_nt(query, key_scr[:, cols])
            top = jnp.max(logits, axis=-1, keepdims=True)
            weights = jnp.exp2((logits - top) * factor)
            total = jnp.sum(weights, axis=-1, keepdims=True)
            mixed.append(mm(weights.astype(BF16), value_scr[:, cols]) / total)
        attended = jnp.concatenate(mixed, axis=1) if heads > 1 else mixed[0]
        modulated = (attended * gain + shift).astype(BF16)
        mod_ref[src] = modulated
        pair = jnp.concatenate([modulated[:half], modulated[half:]], axis=1)
        lat_ref[src] = mm(pair, proj_pair).astype(BF16)
        return carry

    lax.fori_loop(0, seq_count, body, 0)


def attend(received, scale, shift, proj, seq_count, part_rows, tok_rows, heads):
    width = heads * HD
    lat_rows = seq_count * tok_rows
    query_rows = seq_count * part_rows
    vmem = pl.BlockSpec(memory_space=pltpu.VMEM)
    return pl.pallas_call(
        functools.partial(attend_kernel, seq_count, part_rows, tok_rows, heads),
        out_shape=(
            jax.ShapeDtypeStruct((seq_count, part_rows, width), BF16),
            jax.ShapeDtypeStruct((seq_count, part_rows // 2, 2 * CH), BF16),
        ),
        in_specs=[vmem] * 4,
        out_specs=(vmem, vmem),
        scratch_shapes=[pltpu.VMEM((lat_rows, width), BF16), pltpu.VMEM((lat_rows, width), BF16)],
        compiler_params=pltpu.CompilerParams(vmem_limit_bytes=VMEM_LIMIT),
        cost_estimate=pl.CostEstimate(
            flops=4 * query_rows * lat_rows * width,
            bytes_accessed=2 * (query_rows * 2 + lat_rows * 2) * width,
            transcendentals=query_rows * lat_rows * heads,
        ),
    )(received, scale, shift, proj)


def lane_mean(x, count):
    return jnp.sum(x, axis=-1, keepdims=True) * (1.0 / count)


def head_kernel(
    grid_rows, fused,
    lat_ref, embed_ref, pos_ref, pre_ref, post_ref, prompt_ref, cot_ref, mod_ref,
    reward_ref, grad_ref, weight_ref, lat_scr, grad_scr,
):
    patch_rows = grid_rows // 4
    patch_cols = GW // 4
    patches = patch_rows * patch_cols
    lat_scr[...] = lat_ref[...].astype(F32)

    def embed_block(hi, tx):
        first = 4 * (2 * hi) + tx
        second = 4 * (2 * hi + 1) + tx
        return jnp.concatenate(
            [embed_ref[pl.ds(first * CH, CH), :], embed_ref[pl.ds(second * CH, CH), :]], axis=0
        )

    embedded = pos_ref[...].astype(F32)
    for hi in range(2):
        for tx in range(4):
            rows = [
                lat_scr[pl.ds((2 * pr + hi) * GW + tx, patch_cols, stride=4), :]
                for pr in range(patch_rows)
            ]
            block = jnp.concatenate(rows, axis=0).astype(BF16)
            embedded = embedded + mm(block, embed_block(hi, tx))
    pre = pre_ref[...]
    post = post_ref[...]
    prompt = prompt_ref[...]
    center = embedded - lane_mean(embedded, VW)
    rstd = lax.rsqrt(lane_mean(center * center, VW) + EPS)
    unit = center * rstd
    pooled = jnp.sum(unit, axis=0, keepdims=True) * (1.0 / patches) * pre
    pooled_center = pooled - lane_mean(pooled, VW)
    pooled_rstd = lax.rsqrt(lane_mean(pooled_center * pooled_center, VW) + EPS)
    pooled_unit = pooled_center * pooled_rstd
    final = pooled_unit * post
    dot = jnp.sum(final * prompt, axis=-1, keepdims=True)
    final_sq = jnp.sum(final * final, axis=-1, keepdims=True)
    prompt_sq = jnp.sum(prompt * prompt, axis=-1, keepdims=True)
    final_len = jnp.sqrt(final_sq)
    prompt_len = jnp.sqrt(prompt_sq)
    cosine = dot / (final_len * prompt_len)
    reward_ref[...] = jnp.broadcast_to(100.0 * cosine, reward_ref.shape)
    cot = cot_ref[...]
    final_grad = (100.0 * cot) * (prompt / (final_len * prompt_len) - final * (cosine / final_sq))
    unit_grad = final_grad * post
    pooled_grad = pooled_rstd * (
        unit_grad
        - lane_mean(unit_grad, VW)
        - pooled_unit * lane_mean(unit_grad * pooled_unit, VW)
    )
    flow = pooled_grad * pre * (1.0 / patches)
    embed_grad = rstd * (flow - lane_mean(flow, VW) - unit * lane_mean(flow * unit, VW))
    high = embed_grad.astype(BF16)
    low = (embed_grad - high.astype(F32)).astype(BF16)
    stacked = jnp.concatenate([high, low], axis=0)
    for hi in range(2):
        for tx in range(4):
            both = mm_nt(stacked, embed_block(hi, tx))
            piece = both[:patches] + both[patches:]
            for pr in range(patch_rows):
                grad_scr[pl.ds((2 * pr + hi) * GW + tx, patch_cols, stride=4), :] = piece[
                    pr * patch_cols : (pr + 1) * patch_cols
                ]
    grad = grad_scr[...].astype(BF16)
    grad_ref[...] = grad
    if fused:
        weight_ref[...] = readout_grad(grad, mod_ref)
    else:
        weight_ref[...] = jnp.zeros_like(weight_ref)


def readout_grad(grad, mod_ref):
    count, rows, width = mod_ref.shape
    half = rows // 2
    first = mod_ref[:, :half, :].reshape(count * half, width)
    second = mod_ref[:, half:, :].reshape(count * half, width)
    return mm_tn(grad, first)[:CH] + mm_tn(grad, second)[CH:]


def reward_head(latent, embed, pos, pre, post, prompt, cot, modulated, grid_rows, fused):
    patches = grid_rows * GW // 16
    rows = grid_rows * GW // 2
    width = modulated.shape[2]
    vmem = pl.BlockSpec(memory_space=pltpu.VMEM)
    return pl.pallas_call(
        functools.partial(head_kernel, grid_rows, fused),
        out_shape=(
            jax.ShapeDtypeStruct((1, 128), F32),
            jax.ShapeDtypeStruct((rows, 2 * CH), BF16),
            jax.ShapeDtypeStruct((CH, width), F32),
        ),
        in_specs=[vmem] * 8,
        out_specs=(vmem, vmem, vmem),
        scratch_shapes=[pltpu.VMEM((rows, 2 * CH), F32), pltpu.VMEM((rows, 2 * CH), F32)],
        compiler_params=pltpu.CompilerParams(vmem_limit_bytes=VMEM_LIMIT),
        cost_estimate=pl.CostEstimate(
            flops=6 * patches * 16 * CH * VW,
            bytes_accessed=2 * 16 * CH * VW + 2 * patches * VW,
            transcendentals=0,
        ),
    )(latent, embed, pos, pre, post, prompt, cot, modulated)


def spread_kernel(count, half, heads, grad_ref, scale_ref, proj_ref, out_ref):
    gain = 1.0 + scale_ref[...]
    proj = proj_ref[...]
    zero = jnp.zeros_like(proj)
    sides = (jnp.concatenate([proj, zero], axis=1), jnp.concatenate([zero, proj], axis=1))
    for src in range(count):
        grad = grad_ref[pl.ds(src * half, half), :]
        for side in range(2):
            rows = (mm_nt(grad, sides[side]) * gain).astype(BF16)
            for head in range(heads):
                out_ref[0, head, pl.ds((2 * src + side) * half, half), :] = rows[
                    :, head * HD : (head + 1) * HD
                ]


def spread(grad, scale, proj, count, half, heads):
    vmem = pl.BlockSpec(memory_space=pltpu.VMEM)
    return pl.pallas_call(
        functools.partial(spread_kernel, count, half, heads),
        out_shape=jax.ShapeDtypeStruct((1, heads, 2 * count * half, HD), BF16),
        in_specs=[vmem] * 3,
        out_specs=vmem,
        compiler_params=pltpu.CompilerParams(vmem_limit_bytes=VMEM_LIMIT),
        cost_estimate=pl.CostEstimate(
            flops=8 * count * half * CH * heads * HD,
            bytes_accessed=4 * count * half * heads * HD,
            transcendentals=0,
        ),
    )(grad, scale, proj)


def weight_kernel(grad_ref, mod_ref, out_ref):
    out_ref[...] = readout_grad(grad_ref[...], mod_ref)


def weight_call(grad, modulated):
    vmem = pl.BlockSpec(memory_space=pltpu.VMEM)
    return pl.pallas_call(
        weight_kernel,
        out_shape=jax.ShapeDtypeStruct((CH, modulated.shape[2]), F32),
        in_specs=[vmem] * 2,
        out_specs=vmem,
        compiler_params=pltpu.CompilerParams(vmem_limit_bytes=VMEM_LIMIT),
    )(grad, modulated)


def swap(x, axis, bit):
    count = lax.axis_size(axis)
    return lax.ppermute(x, axis, [(i, i ^ bit) for i in range(count)])


def gather_doubling(x, axis):
    count = lax.axis_size(axis)
    index = lax.axis_index(axis)
    steps = count.bit_length() - 1
    x = x.reshape((1,) * steps + x.shape)
    for step in range(steps):
        bit = count >> (step + 1)
        other = swap(x, axis, bit)
        mine_first = (index & bit) == 0
        x = jnp.concatenate(
            [jnp.where(mine_first, x, other), jnp.where(mine_first, other, x)], axis=step
        )
    return x.reshape((count,) + x.shape[steps:])


def gather_direct(x, axis):
    count = lax.axis_size(axis)
    index = lax.axis_index(axis)
    parts = [x] + [swap(x, axis, k) for k in range(1, count)]
    stacked = jnp.stack(parts)
    order = jnp.arange(count) ^ index
    return stacked[order]


def sum_direct(x, axis):
    count = lax.axis_size(axis)
    parts = [x] + [swap(x, axis, k) for k in range(1, count)]
    parts = [part.astype(F32) for part in parts]
    while len(parts) > 1:
        parts = [parts[i] + parts[i + 1] for i in range(0, len(parts), 2)]
    return parts[0]


def gather_embed(patch_embed):
    seq_count = lax.axis_size("seq")
    data_count = lax.axis_size("dp")
    positions, local, width = patch_embed.shape
    share = positions // data_count if positions % data_count == 0 else 0
    if share:
        mine = lax.dynamic_slice_in_dim(patch_embed, lax.axis_index("dp") * share, share, 0)
    else:
        mine = patch_embed
    gathered = gather_doubling(mine, "seq")
    full = gathered.transpose(1, 0, 2, 3).reshape(mine.shape[0], seq_count * local, width)
    if share:
        full = gather_doubling(full, "dp")
    return full.reshape(positions * seq_count * local, width)


def on_device(
    queries,
    keys,
    values,
    shifts,
    scales,
    proj_out,
    patch_embed,
    pos_embed,
    pre_gain,
    post_gain,
    prompt,
    cotangent,
):
    seq_count = lax.axis_size("seq")
    data_count = lax.axis_size("dp")
    tok_rows = queries.shape[1]
    query_parts = max(1, seq_count // HEADS)
    head_count = max(1, HEADS // seq_count)
    group_count = HEADS // head_count
    width = head_count * HD
    seq_index = lax.axis_index("seq")
    head_group = seq_index // query_parts
    query_part = seq_index % query_parts
    part_rows = tok_rows // query_parts
    half = part_rows // 2
    lat_rows = seq_count * tok_rows
    grid_rows = lat_rows // GW
    canonical = part_rows == 2 * GW

    scale_mine = lax.dynamic_slice_in_dim(scales, head_group * width, width, 1)
    shift_mine = lax.dynamic_slice_in_dim(shifts, head_group * width, width, 1)
    proj_mine = lax.dynamic_slice_in_dim(proj_out, head_group * width, width, 0)

    send = pack(queries, keys, values, seq_count, query_parts, part_rows, tok_rows, width)
    received = lax.all_to_all(send, "seq", split_axis=0, concat_axis=0, tiled=True)
    embed_full = gather_embed(patch_embed)

    modulated, latent_part = attend(
        received, scale_mine, shift_mine, proj_mine, seq_count, part_rows, tok_rows, head_count
    )

    shares = latent_part.reshape(group_count, seq_count // group_count * half, 2 * CH)
    groups = [[g * query_parts + r for g in range(group_count)] for r in range(query_parts)]
    pieces = lax.all_to_all(
        shares, "seq", split_axis=0, concat_axis=0, tiled=True,
        axis_index_groups=groups if query_parts > 1 else None,
    )
    summed = jnp.sum(pieces.astype(F32), axis=0).astype(BF16)
    latent = gather_direct(summed, "seq")
    per_share = seq_count // group_count
    if canonical:
        latent = latent.reshape(lat_rows // 2, 2 * CH)
    else:
        latent = latent.reshape(group_count, query_parts, per_share, half, 2, CH)
        latent = latent.transpose(0, 2, 1, 4, 3, 5).reshape(grid_rows // 2, 2, GW, CH)
        latent = latent.transpose(0, 2, 1, 3).reshape(lat_rows // 2, 2 * CH)

    reward, grad, weight = reward_head(
        latent, embed_full, pos_embed, pre_gain[None], post_gain[None], prompt,
        cotangent[None], modulated, grid_rows, canonical,
    )
    if not canonical:
        tokens = grad.reshape(grid_rows // 2, GW, 2, CH).transpose(0, 2, 1, 3)
        tokens = tokens.reshape(seq_count, query_parts, 2, half, CH)
        tokens = lax.dynamic_index_in_dim(tokens, query_part, 1, keepdims=False)
        grad = tokens.transpose(0, 2, 1, 3).reshape(seq_count * half, 2 * CH)
        weight = weight_call(grad, modulated)

    weight = weight * (1.0 / math.sqrt(data_count * lat_rows))
    total = sum_direct(weight.astype(BF16), "dp")
    attn_grad = spread(grad, scale_mine, proj_mine, seq_count, half, head_count)
    for part in range(1, query_parts):
        total = total + swap(total, "seq", part)
    weight_all = gather_direct(total.astype(BF16), "seq")
    weight_all = weight_all.reshape(group_count, query_parts, CH, width)[:, 0]
    proj_grad = weight_all.transpose(0, 2, 1).reshape(HEADS * HD, CH).astype(F32)
    return (reward[0, :1], attn_grad, proj_grad)


def solution(mesh):
    return jax.shard_map(
        on_device,
        mesh=mesh,
        in_specs=(
            P("dp", "seq", None),
            P("dp", "seq", None),
            P("dp", "seq", None),
            P("dp", None),
            P("dp", None),
            P(),
            P(None, "seq", None),
            P(),
            P(),
            P(),
            P("dp", None),
            P("dp"),
        ),
        out_specs=(P("dp"), P("dp", "seq", None, None), P()),
        check_vma=False,
    )
```

```python
import functools
import math

import jax
import jax.numpy as jnp
from jax import lax
from jax.experimental import pallas as pl
from jax.experimental.pallas import tpu as pltpu
from jax.sharding import PartitionSpec as P

HEADS = 16
HD = 128
CH = 64
GW = 64
VW = 1280
EPS = 1e-05
BF16 = jnp.bfloat16
F32 = jnp.float32
VMEM_LIMIT = 48 * 1024 * 1024


def mm(a, b):
    return jnp.dot(a, b, preferred_element_type=F32)


def mm_nt(a, b):
    return lax.dot_general(a, b, (((1,), (1,)), ((), ())), preferred_element_type=F32)


def mm_tn(a, b):
    return lax.dot_general(a, b, (((0,), (0,)), ((), ())), preferred_element_type=F32)


def pack_kernel(count, query_parts, part_rows, tok_rows, width, place_ref, q_ref, k_ref, v_ref, *out_refs):
    me = place_ref[0]
    for mask in range(count):
        dest = jnp.bitwise_xor(me, mask)
        group, part = dest // query_parts, dest % query_parts
        cols = pl.ds(pl.multiple_of(group * width, HD), width)
        first = pl.multiple_of(part * part_rows, part_rows)
        out = out_refs[mask]
        out[pl.ds(0, part_rows), :] = q_ref[0, pl.ds(first, part_rows), cols]
        out[pl.ds(part_rows, tok_rows), :] = k_ref[0, :, cols]
        out[pl.ds(part_rows + tok_rows, tok_rows), :] = v_ref[0, :, cols]


def pack(place, queries, keys, values, count, query_parts, part_rows, tok_rows, width):
    rows = part_rows + 2 * tok_rows
    vmem = pl.BlockSpec(memory_space=pltpu.VMEM)
    return pl.pallas_call(
        functools.partial(pack_kernel, count, query_parts, part_rows, tok_rows, width),
        out_shape=[jax.ShapeDtypeStruct((rows, width), BF16)] * count,
        in_specs=[pl.BlockSpec(memory_space=pltpu.SMEM)] + [vmem] * 3,
        out_specs=[vmem] * count,
        compiler_params=pltpu.CompilerParams(vmem_limit_bytes=VMEM_LIMIT),
        cost_estimate=pl.CostEstimate(
            flops=0, bytes_accessed=4 * count * rows * width, transcendentals=0
        ),
    )(place, queries, keys, values)


def attend_kernel(count, query_parts, part_rows, tok_rows, heads, *refs):
    in_refs = refs[:count]
    scale_ref, shift_ref, proj_ref, mod_ref, keep_ref, send_ref, key_scr, value_scr = refs[count:]
    half = part_rows // 2
    factor = HD ** (-0.5) * math.log2(math.e)
    ones = jnp.ones((tok_rows, HD), BF16)
    for src in range(count):
        rows = pl.ds(src * tok_rows, tok_rows)
        key_scr[rows, :] = in_refs[src][pl.ds(part_rows, tok_rows), :]
        for head in range(heads):
            value_scr[rows, pl.ds(2 * head * HD, HD)] = in_refs[src][
                pl.ds(part_rows + tok_rows, tok_rows), pl.ds(head * HD, HD)
            ]
            value_scr[rows, pl.ds((2 * head + 1) * HD, HD)] = ones
    gain = 1.0 + scale_ref[...]
    shift = shift_ref[...]
    proj = proj_ref[...]
    zero = jnp.zeros_like(proj)
    proj_pair = jnp.concatenate(
        [jnp.concatenate([proj, zero], axis=1), jnp.concatenate([zero, proj], axis=1)], axis=0
    )
    for src in range(count):
        mixed = []
        for head in range(heads):
            cols = pl.ds(head * HD, HD)
            query = in_refs[src][pl.ds(0, part_rows), cols]
            logits = mm_nt(query, key_scr[:, cols])
            top = jnp.max(logits, axis=-1, keepdims=True)
            weights = jnp.exp2((logits - top) * factor).astype(BF16)
            both = mm(weights, value_scr[:, pl.ds(2 * head * HD, 2 * HD)])
            mixed.append(both[:, :HD] / both[:, HD:])
        attended = jnp.concatenate(mixed, axis=1) if heads > 1 else mixed[0]
        modulated = (attended * gain + shift).astype(BF16)
        mod_ref[src] = modulated
        pair = jnp.concatenate([modulated[:half], modulated[half:]], axis=1)
        group, inner = src // query_parts, src % query_parts
        out_ref = send_ref if group % 2 else keep_ref
        out_ref[(group // 2) * query_parts + inner] = mm(pair, proj_pair).astype(BF16)


def attend(received, scale, shift, proj, query_parts, part_rows, tok_rows, heads):
    count = len(received)
    width = heads * HD
    lat_rows = count * tok_rows
    query_rows = count * part_rows
    vmem = pl.BlockSpec(memory_space=pltpu.VMEM)
    blocks = jax.ShapeDtypeStruct((count // 2, part_rows // 2, 2 * CH), BF16)
    return pl.pallas_call(
        functools.partial(attend_kernel, count, query_parts, part_rows, tok_rows, heads),
        out_shape=(jax.ShapeDtypeStruct((count, part_rows, width), BF16), blocks, blocks),
        in_specs=[vmem] * (count + 3),
        out_specs=(vmem, vmem, vmem),
        scratch_shapes=[
            pltpu.VMEM((lat_rows, width), BF16),
            pltpu.VMEM((lat_rows, 2 * width), BF16),
        ],
        compiler_params=pltpu.CompilerParams(vmem_limit_bytes=VMEM_LIMIT),
        cost_estimate=pl.CostEstimate(
            flops=4 * query_rows * lat_rows * width,
            bytes_accessed=2 * (query_rows * 2 + lat_rows * 2) * width,
            transcendentals=query_rows * lat_rows * heads,
        ),
    )(*received, scale, shift, proj)


def add_split_kernel(ways, keep_ref, got_ref, *out_refs):
    for way in range(ways):
        for slot in range(keep_ref.shape[0] // ways):
            block = slot * ways + way
            total = keep_ref[block].astype(F32) + got_ref[block].astype(F32)
            out_refs[way][slot] = total.astype(BF16)


def add_split(keep, got, ways):
    vmem = pl.BlockSpec(memory_space=pltpu.VMEM)
    shape = (keep.shape[0] // ways,) + keep.shape[1:]
    return pl.pallas_call(
        functools.partial(add_split_kernel, ways),
        out_shape=[jax.ShapeDtypeStruct(shape, BF16)] * ways,
        in_specs=[vmem] * 2,
        out_specs=[vmem] * ways,
    )(keep, got)


def lane_mean(x, count):
    return jnp.sum(x, axis=-1, keepdims=True) * (1.0 / count)


def head_kernel(grid_rows, fused, lat_masks, embed_masks, place_ref, *refs):
    lat_refs, refs = refs[: len(lat_masks)], refs[len(lat_masks) :]
    embed_refs, refs = refs[: len(embed_masks)], refs[len(embed_masks) :]
    pos_ref, pre_ref, post_ref, prompt_ref, cot_ref, mod_ref, *refs = refs
    reward_ref, grad_ref, weight_ref, lat_scr, grad_scr, embed_ref, sems = refs
    patch_rows = grid_rows // 4
    patch_cols = GW // 4
    patches = patch_rows * patch_cols
    me = place_ref[0]
    copies = []
    for slot, mask in enumerate(embed_masks):
        rows = embed_refs[slot].shape[0]
        first = pl.multiple_of(jnp.bitwise_xor(place_ref[1], mask) * rows, rows)
        copies.append(
            pltpu.make_async_copy(embed_refs[slot], embed_ref.at[pl.ds(first, rows)], sems.at[slot])
        )
        copies[-1].start()
    for ref, masks in zip(lat_refs, lat_masks):
        for slot, mask in enumerate(masks):
            first = pl.multiple_of(jnp.bitwise_xor(me, mask) * GW, GW)
            lat_scr[pl.ds(first, GW), :] = ref[slot].astype(F32)
    for copy in copies:
        copy.wait()

    def embed_block(hi, tx):
        first = 4 * (2 * hi) + tx
        second = 4 * (2 * hi + 1) + tx
        return jnp.concatenate(
            [embed_ref[pl.ds(first * CH, CH), :], embed_ref[pl.ds(second * CH, CH), :]], axis=0
        )

    embedded = pos_ref[...].astype(F32)
    for hi in range(2):
        for tx in range(4):
            rows = [
                lat_scr[pl.ds((2 * pr + hi) * GW + tx, patch_cols, stride=4), :]
                for pr in range(patch_rows)
            ]
            block = jnp.concatenate(rows, axis=0).astype(BF16)
            embedded = embedded + mm(block, embed_block(hi, tx))
    pre = pre_ref[...]
    post = post_ref[...]
    prompt = prompt_ref[...]
    center = embedded - lane_mean(embedded, VW)
    rstd = lax.rsqrt(lane_mean(center * center, VW) + EPS)
    unit = center * rstd
    pooled = jnp.sum(unit, axis=0, keepdims=True) * (1.0 / patches) * pre
    pooled_center = pooled - lane_mean(pooled, VW)
    pooled_rstd = lax.rsqrt(lane_mean(pooled_center * pooled_center, VW) + EPS)
    pooled_unit = pooled_center * pooled_rstd
    final = pooled_unit * post
    dot = jnp.sum(final * prompt, axis=-1, keepdims=True)
    final_sq = jnp.sum(final * final, axis=-1, keepdims=True)
    prompt_sq = jnp.sum(prompt * prompt, axis=-1, keepdims=True)
    final_len = jnp.sqrt(final_sq)
    prompt_len = jnp.sqrt(prompt_sq)
    cosine = dot / (final_len * prompt_len)
    reward_ref[...] = jnp.broadcast_to(100.0 * cosine, reward_ref.shape)
    cot = cot_ref[...]
    final_grad = (100.0 * cot) * (prompt / (final_len * prompt_len) - final * (cosine / final_sq))
    unit_grad = final_grad * post
    pooled_grad = pooled_rstd * (
        unit_grad
        - lane_mean(unit_grad, VW)
        - pooled_unit * lane_mean(unit_grad * pooled_unit, VW)
    )
    flow = pooled_grad * pre * (1.0 / patches)
    embed_grad = rstd * (flow - lane_mean(flow, VW) - unit * lane_mean(flow * unit, VW))
    high = embed_grad.astype(BF16)
    low = (embed_grad - high.astype(F32)).astype(BF16)
    stacked = jnp.concatenate([high, low], axis=0)
    for hi in range(2):
        for tx in range(4):
            both = mm_nt(stacked, embed_block(hi, tx))
            piece = both[:patches] + both[patches:]
            for pr in range(patch_rows):
                grad_scr[pl.ds((2 * pr + hi) * GW + tx, patch_cols, stride=4), :] = piece[
                    pr * patch_cols : (pr + 1) * patch_cols
                ]
    grad = grad_scr[...].astype(BF16)
    grad_ref[...] = grad
    if fused:
        blocks = [
            grad_scr[pl.ds(pl.multiple_of(jnp.bitwise_xor(me, mask) * GW, GW), GW), :].astype(BF16)
            for mask in range(grid_rows // 2)
        ]
        weight_ref[...] = readout_grad(jnp.concatenate(blocks, axis=0), mod_ref)
    else:
        weight_ref[...] = jnp.zeros_like(weight_ref)


def readout_grad(grad, mod_ref):
    count, rows, width = mod_ref.shape
    half = rows // 2
    first = mod_ref[:, :half, :].reshape(count * half, width)
    second = mod_ref[:, half:, :].reshape(count * half, width)
    return mm_tn(grad, first)[:CH] + mm_tn(grad, second)[CH:]


def reward_head(place, latent, embed, pos, pre, post, prompt, cot, modulated, grid_rows, fused):
    patches = grid_rows * GW // 16
    rows = grid_rows * GW // 2
    width = modulated.shape[2]
    lat_arrays, lat_masks = [x for x, _ in latent], [masks for _, masks in latent]
    embed_arrays, embed_masks = [x for x, _ in embed], [mask for _, mask in embed]
    vmem = pl.BlockSpec(memory_space=pltpu.VMEM)
    anywhere = pl.BlockSpec(memory_space=pl.ANY)
    return pl.pallas_call(
        functools.partial(head_kernel, grid_rows, fused, lat_masks, embed_masks),
        out_shape=(
            jax.ShapeDtypeStruct((1, 128), F32),
            jax.ShapeDtypeStruct((rows, 2 * CH), BF16),
            jax.ShapeDtypeStruct((CH, width), F32),
        ),
        in_specs=[pl.BlockSpec(memory_space=pltpu.SMEM)]
        + [vmem] * len(lat_arrays)
        + [anywhere] * len(embed_arrays)
        + [vmem] * 6,
        out_specs=(vmem, vmem, vmem),
        scratch_shapes=[
            pltpu.VMEM((rows, 2 * CH), F32),
            pltpu.VMEM((rows, 2 * CH), F32),
            pltpu.VMEM((16 * CH, VW), BF16),
            pltpu.SemaphoreType.DMA((len(embed_arrays),)),
        ],
        compiler_params=pltpu.CompilerParams(vmem_limit_bytes=VMEM_LIMIT),
        cost_estimate=pl.CostEstimate(
            flops=6 * patches * 16 * CH * VW,
            bytes_accessed=2 * 16 * CH * VW + 2 * patches * VW,
            transcendentals=0,
        ),
    )(place, *lat_arrays, *embed_arrays, pos, pre, post, prompt, cot, modulated)


def spread_kernel(count, half, heads, grad_ref, scale_ref, proj_ref, out_ref):
    gain = 1.0 + scale_ref[...]
    proj = proj_ref[...]
    zero = jnp.zeros_like(proj)
    sides = (jnp.concatenate([proj, zero], axis=1), jnp.concatenate([zero, proj], axis=1))
    for src in range(count):
        grad = grad_ref[pl.ds(src * half, half), :]
        for side in range(2):
            rows = (mm_nt(grad, sides[side]) * gain).astype(BF16)
            for head in range(heads):
                out_ref[0, head, pl.ds((2 * src + side) * half, half), :] = rows[
                    :, head * HD : (head + 1) * HD
                ]


def spread(grad, scale, proj, count, half, heads):
    vmem = pl.BlockSpec(memory_space=pltpu.VMEM)
    return pl.pallas_call(
        functools.partial(spread_kernel, count, half, heads),
        out_shape=jax.ShapeDtypeStruct((1, heads, 2 * count * half, HD), BF16),
        in_specs=[vmem] * 3,
        out_specs=vmem,
        compiler_params=pltpu.CompilerParams(vmem_limit_bytes=VMEM_LIMIT),
        cost_estimate=pl.CostEstimate(
            flops=8 * count * half * CH * heads * HD,
            bytes_accessed=4 * count * half * heads * HD,
            transcendentals=0,
        ),
    )(grad, scale, proj)


def weight_kernel(grad_ref, mod_ref, out_ref):
    out_ref[...] = readout_grad(grad_ref[...], mod_ref)


def weight_call(grad, modulated):
    vmem = pl.BlockSpec(memory_space=pltpu.VMEM)
    return pl.pallas_call(
        weight_kernel,
        out_shape=jax.ShapeDtypeStruct((CH, modulated.shape[2]), F32),
        in_specs=[vmem] * 2,
        out_specs=vmem,
        compiler_params=pltpu.CompilerParams(vmem_limit_bytes=VMEM_LIMIT),
    )(grad, modulated)


def finish_kernel(masks, width, place_ref, *refs):
    group = place_ref[2]
    out_ref = refs[-1]
    for ref, some in zip(refs[:-1], masks):
        for slot, mask in enumerate(some):
            first = pl.multiple_of(jnp.bitwise_xor(group, mask) * width, width)
            out_ref[pl.ds(first, width), :] = ref[slot].astype(F32).T


def finish(place, parts, width):
    vmem = pl.BlockSpec(memory_space=pltpu.VMEM)
    return pl.pallas_call(
        functools.partial(finish_kernel, [masks for _, masks in parts], width),
        out_shape=jax.ShapeDtypeStruct((HEADS * HD, CH), F32),
        in_specs=[pl.BlockSpec(memory_space=pltpu.SMEM)] + [vmem] * len(parts),
        out_specs=vmem,
        compiler_params=pltpu.CompilerParams(vmem_limit_bytes=VMEM_LIMIT),
    )(place, *[x for x, _ in parts])


def swap(x, axis, mask):
    count = lax.axis_size(axis)
    return lax.ppermute(x, axis, [(i, i ^ mask) for i in range(count)])


def stages_of(count):
    bits = [1 << b for b in range(1, count.bit_length() - 1)]
    pairs = [bits[i : i + 2] for i in range(0, len(bits), 2)]
    return [[p[0], p[1], p[0] | p[1]] if len(p) == 2 else p for p in pairs]


def gather_relative(x, axis, unit, count):
    held, masks = x[None], [0]
    for stage in stages_of(count):
        held = jnp.concatenate([held] + [swap(held, axis, unit * m) for m in stage], axis=0)
        masks = masks + [m ^ other for m in stage for other in masks]
    return [(held, masks), (swap(held, axis, unit), [m ^ 1 for m in masks])]


def scatter_relative(keep, send, axis, unit, count, inner):
    got = swap(send, axis, unit)
    stages = stages_of(count)
    shape = keep.shape[1:]
    for stage in stages:
        ways = len(stage) + 1
        if inner > 1:
            keep = keep.reshape((-1, inner * shape[0]) + shape[1:])
            got = got.reshape(keep.shape)
        parts = add_split(keep, got, ways)
        got = [swap(parts[way], axis, unit * mask) for way, mask in enumerate(stage, 1)]
        got = sum(part.astype(F32) for part in got)
        keep = parts[0]
        if stage is not stages[-1]:
            got = got.astype(BF16)
    total = (keep.astype(F32) + got.astype(F32)).astype(BF16)
    return total.reshape((inner,) + shape)


def gather_doubling(x, axis):
    count = lax.axis_size(axis)
    held, masks = x[None], [0]
    bit = count >> 1
    while bit:
        held = jnp.concatenate([held, swap(held, axis, bit)], axis=0)
        masks = masks + [m ^ bit for m in masks]
        bit >>= 1
    where = [masks.index(m) for m in range(count)]
    return held[jnp.asarray(where)[jnp.arange(count) ^ lax.axis_index(axis)]]


def sum_direct(x, axis):
    count = lax.axis_size(axis)
    parts = [x] + [swap(x, axis, k) for k in range(1, count)]
    parts = [part.astype(F32) for part in parts]
    while len(parts) > 1:
        parts = [parts[i] + parts[i + 1] for i in range(0, len(parts), 2)]
    return parts[0]


def gather_embed(patch_embed):
    seq_count = lax.axis_size("seq")
    data_count = lax.axis_size("dp")
    positions, local, width = patch_embed.shape
    share = positions // data_count if positions % data_count == 0 else 0
    if share:
        mine = lax.dynamic_slice_in_dim(patch_embed, lax.axis_index("dp") * share, share, 0)
    else:
        mine = patch_embed
    gathered = gather_doubling(mine, "seq")
    full = gathered.transpose(1, 0, 2, 3).reshape(-1, width)
    if not share:
        return [(full, 0)]
    held = [(full, 0)]
    bit = data_count >> 1
    while bit:
        held = held + [(swap(x, "dp", bit), m ^ bit) for x, m in held]
        bit >>= 1
    return held


def on_device(
    queries,
    keys,
    values,
    shifts,
    scales,
    proj_out,
    patch_embed,
    pos_embed,
    pre_gain,
    post_gain,
    prompt,
    cotangent,
):
    seq_count = lax.axis_size("seq")
    data_count = lax.axis_size("dp")
    tok_rows = queries.shape[1]
    query_parts = max(1, seq_count // HEADS)
    head_count = max(1, HEADS // seq_count)
    group_count = HEADS // head_count
    width = head_count * HD
    seq_index = lax.axis_index("seq")
    head_group = seq_index // query_parts
    query_part = seq_index % query_parts
    part_rows = tok_rows // query_parts
    half = part_rows // 2
    lat_rows = seq_count * tok_rows
    grid_rows = lat_rows // GW
    canonical = part_rows == 2 * GW
    place = jnp.stack([seq_index, lax.axis_index("dp"), head_group]).astype(jnp.int32)

    scale_mine = lax.dynamic_slice_in_dim(scales, head_group * width, width, 1)
    shift_mine = lax.dynamic_slice_in_dim(shifts, head_group * width, width, 1)
    proj_mine = lax.dynamic_slice_in_dim(proj_out, head_group * width, width, 0)

    send = pack(place, queries, keys, values, seq_count, query_parts, part_rows, tok_rows, width)
    received = {0: send[0]}
    for mask in reversed(range(1, seq_count)):
        received[mask] = swap(send[mask], "seq", mask)
    received = [received[mask] for mask in range(seq_count)]
    embed = gather_embed(patch_embed)

    modulated, keep, away = attend(
        received, scale_mine, shift_mine, proj_mine, query_parts, part_rows, tok_rows, head_count
    )

    summed = scatter_relative(keep, away, "seq", query_parts, group_count, query_parts)
    if canonical:
        latent = gather_relative(summed[0], "seq", 1, seq_count)
    else:
        blocks = gather_doubling(summed, "seq").reshape(
            group_count, query_parts, query_parts, half, 2, CH
        )
        order = [[inner ^ part for inner in range(query_parts)] for part in range(query_parts)]
        blocks = jnp.stack([blocks[:, part][:, jnp.asarray(order[part])] for part in range(query_parts)], axis=2)
        blocks = blocks.transpose(0, 1, 2, 4, 3, 5).reshape(grid_rows // 2, 2, GW, CH)
        blocks = blocks.transpose(0, 2, 1, 3).reshape(grid_rows // 2, GW, 2 * CH)
        latent = [(blocks, list(range(grid_rows // 2)))]

    reward, grad, weight = reward_head(
        place if canonical else place * jnp.asarray([0, 1, 1], jnp.int32),
        latent, embed, pos_embed, pre_gain[None], post_gain[None], prompt,
        cotangent[None], modulated, grid_rows, canonical,
    )
    if not canonical:
        tokens = grad.reshape(grid_rows // 2, GW, 2, CH).transpose(0, 2, 1, 3)
        tokens = tokens.reshape(seq_count, query_parts, 2, half, CH)
        tokens = lax.dynamic_index_in_dim(tokens, query_part, 1, keepdims=False)
        tokens = tokens.transpose(0, 2, 1, 3)
        grad = tokens.reshape(seq_count * half, 2 * CH)
        relative = tokens[jnp.arange(seq_count) ^ seq_index].reshape(seq_count * half, 2 * CH)
        weight = weight_call(relative, modulated)

    total = sum_direct((weight * (1.0 / math.sqrt(data_count * lat_rows))).astype(BF16), "dp")
    attn_grad = spread(grad, scale_mine, proj_mine, seq_count, half, head_count)
    for part in range(1, query_parts):
        total = total + swap(total, "seq", part)
    parts = gather_relative(total.astype(BF16), "seq", query_parts, group_count)
    proj_grad = finish(place, parts, width)
    return (reward[0, :1], attn_grad, proj_grad)


def solution(mesh):
    return jax.shard_map(
        on_device,
        mesh=mesh,
        in_specs=(
            P("dp", "seq", None),
            P("dp", "seq", None),
            P("dp", "seq", None),
            P("dp", None),
            P("dp", None),
            P(),
            P(None, "seq", None),
            P(),
            P(),
            P(),
            P("dp", None),
            P("dp"),
        ),
        out_specs=(P("dp"), P("dp", "seq", None, None), P()),
        check_vma=False,
    )
```

```python
import functools
import math

import jax
import jax.numpy as jnp
from jax import lax
from jax.experimental import pallas as pl
from jax.experimental.pallas import tpu as pltpu
from jax.sharding import PartitionSpec as P

HEADS = 16
HD = 128
CH = 64
GW = 64
VW = 1280
EPS = 1e-05
BF16 = jnp.bfloat16
F32 = jnp.float32
VMEM_LIMIT = 20 * 1024 * 1024


def mm(a, b):
    return jnp.dot(a, b, preferred_element_type=F32)


def mm_nt(a, b):
    return lax.dot_general(a, b, (((1,), (1,)), ((), ())), preferred_element_type=F32)


def mm_tn(a, b):
    return lax.dot_general(a, b, (((0,), (0,)), ((), ())), preferred_element_type=F32)


def pack_piece(sizes, me, mask, q_ref, k_ref, v_ref, out):
    query_parts, part_rows, tok_rows, width = sizes
    dest = jnp.bitwise_xor(me, mask)
    group, part = dest // query_parts, dest % query_parts
    cols = pl.ds(pl.multiple_of(group * width, HD), width)
    first = pl.multiple_of(part * part_rows, part_rows)
    out[pl.ds(0, part_rows), :] = q_ref[0, pl.ds(first, part_rows), cols]
    out[pl.ds(part_rows, tok_rows), :] = k_ref[0, :, cols]
    out[pl.ds(part_rows + tok_rows, tok_rows), :] = v_ref[0, :, cols]


def pack_kernel(sizes, masks, share, place_ref, q_ref, k_ref, v_ref, embed_ref, share_ref, *out_refs):
    me = place_ref[0]
    share_ref[...] = embed_ref[pl.ds(place_ref[1] * share, share)] if share else embed_ref[...]
    for mask, out in zip(masks, out_refs):
        pack_piece(sizes, me, mask, q_ref, k_ref, v_ref, out)


def pack_call(kernel, sizes, masks, extra_shape, place, arrays):
    _, part_rows, tok_rows, width = sizes
    rows = part_rows + 2 * tok_rows
    vmem = pl.BlockSpec(memory_space=pltpu.VMEM)
    return pl.pallas_call(
        kernel,
        out_shape=[jax.ShapeDtypeStruct(extra_shape, BF16)]
        + [jax.ShapeDtypeStruct((rows, width), BF16)] * len(masks),
        in_specs=[pl.BlockSpec(memory_space=pltpu.SMEM)] + [vmem] * len(arrays),
        out_specs=[vmem] * (len(masks) + 1),
        compiler_params=pltpu.CompilerParams(vmem_limit_bytes=VMEM_LIMIT),
        cost_estimate=pl.CostEstimate(
            flops=0, bytes_accessed=4 * len(masks) * rows * width, transcendentals=0
        ),
    )(place, *arrays)


def attend_kernel(masks, query_parts, part_rows, tok_rows, heads, place_ref, *refs):
    count = len(masks)
    in_refs = refs[:count]
    scale_ref, shift_ref, proj_ref, mod_ref, lat_ref, key_scr, value_scr = refs[count:]
    half = part_rows // 2
    width = heads * HD
    factor = HD ** (-0.5) * math.log2(math.e)
    me = place_ref[0]
    mine = pl.ds(pl.multiple_of(place_ref[2] * width, HD), width)
    ones = jnp.ones((tok_rows, HD), BF16)
    for src in range(count):
        rows = pl.ds(src * tok_rows, tok_rows)
        key_scr[rows, :] = in_refs[src][pl.ds(part_rows, tok_rows), :]
        for head in range(heads):
            value_scr[rows, pl.ds(2 * head * HD, HD)] = in_refs[src][
                pl.ds(part_rows + tok_rows, tok_rows), pl.ds(head * HD, HD)
            ]
            value_scr[rows, pl.ds((2 * head + 1) * HD, HD)] = ones
    gain = 1.0 + scale_ref[:, mine]
    shift = shift_ref[:, mine]
    proj = proj_ref[:, mine]
    zero = jnp.zeros_like(proj)
    proj_pair = jnp.concatenate(
        [jnp.concatenate([proj, zero], axis=1), jnp.concatenate([zero, proj], axis=1)], axis=0
    )
    for src in range(count):
        mixed = []
        for head in range(heads):
            cols = pl.ds(head * HD, HD)
            query = in_refs[src][pl.ds(0, part_rows), cols]
            logits = mm_nt(query, key_scr[:, cols])
            top = jnp.max(logits, axis=-1, keepdims=True)
            weights = jnp.exp2((logits - top) * factor).astype(BF16)
            both = mm(weights, value_scr[:, pl.ds(2 * head * HD, 2 * HD)])
            mixed.append(both[:, :HD] / both[:, HD:])
        attended = jnp.concatenate(mixed, axis=1) if heads > 1 else mixed[0]
        modulated = (attended * gain + shift).astype(BF16)
        place = jnp.bitwise_xor(me, masks[src])
        mod_ref[place] = modulated
        pair = jnp.concatenate([modulated[:half], modulated[half:]], axis=1)
        lat_ref[place] = mm_nt(pair, proj_pair).astype(BF16)


def attend(place, masks, received, scales, shifts, proj, query_parts, part_rows, tok_rows, heads):
    count = len(received)
    width = heads * HD
    lat_rows = count * tok_rows
    query_rows = count * part_rows
    vmem = pl.BlockSpec(memory_space=pltpu.VMEM)
    return pl.pallas_call(
        functools.partial(attend_kernel, masks, query_parts, part_rows, tok_rows, heads),
        out_shape=(
            jax.ShapeDtypeStruct((count, part_rows, width), BF16),
            jax.ShapeDtypeStruct((count, part_rows // 2, 2 * CH), BF16),
        ),
        in_specs=[pl.BlockSpec(memory_space=pltpu.SMEM)] + [vmem] * (count + 3),
        out_specs=(vmem, vmem),
        scratch_shapes=[
            pltpu.VMEM((lat_rows, width), BF16),
            pltpu.VMEM((lat_rows, 2 * width), BF16),
        ],
        compiler_params=pltpu.CompilerParams(vmem_limit_bytes=VMEM_LIMIT),
        cost_estimate=pl.CostEstimate(
            flops=4 * query_rows * lat_rows * width,
            bytes_accessed=2 * (query_rows * 2 + lat_rows * 2) * width,
            transcendentals=query_rows * lat_rows * heads,
        ),
    )(place, *received, scales, shifts, proj)


def total_kernel(copies, *refs):
    out_ref = refs[-1]
    if len(refs) == 2:
        parts = [refs[0][i].astype(F32) for i in range(refs[0].shape[0])]
    else:
        parts = [ref[...].astype(F32) for ref in refs[:-1]]
    while len(parts) > 1:
        parts = [parts[i] + parts[i + 1] for i in range(0, len(parts), 2)]
    for copy in range(copies):
        out_ref[copy] = parts[0].astype(BF16)


def total_copies(arrays, copies):
    vmem = pl.BlockSpec(memory_space=pltpu.VMEM)
    return pl.pallas_call(
        functools.partial(total_kernel, copies),
        out_shape=jax.ShapeDtypeStruct((copies,) + arrays[0].shape[-2:], BF16),
        in_specs=[vmem] * len(arrays),
        out_specs=vmem,
        compiler_params=pltpu.CompilerParams(vmem_limit_bytes=VMEM_LIMIT),
    )(*arrays)


def lane_mean(x, count):
    return jnp.sum(x, axis=-1, keepdims=True) * (1.0 / count)


def head_kernel(grid_rows, fused, embed_masks, out_factor, place_ref, lat_ref, *refs):
    embed_refs, refs = refs[: len(embed_masks)], refs[len(embed_masks) :]
    pos_ref, pre_ref, post_ref, prompt_ref, cot_ref, mod_ref, *refs = refs
    reward_ref, grad_ref, weight_ref, lat_scr, grad_scr, embed_ref, sems = refs
    patch_rows = grid_rows // 4
    patch_cols = GW // 4
    patches = patch_rows * patch_cols
    copies = []
    for slot, mask in enumerate(embed_masks):
        rows = embed_refs[slot].shape[0]
        first = pl.multiple_of(jnp.bitwise_xor(place_ref[1], mask) * rows, rows)
        copies.append(
            pltpu.make_async_copy(embed_refs[slot], embed_ref.at[pl.ds(first, rows)], sems.at[slot])
        )
        copies[-1].start()
    lat_scr[...] = lat_ref[...].astype(F32)
    for copy in copies:
        copy.wait()

    def embed_block(hi, tx):
        first = 4 * (2 * hi) + tx
        second = 4 * (2 * hi + 1) + tx
        return jnp.concatenate(
            [embed_ref[pl.ds(first * CH, CH), :], embed_ref[pl.ds(second * CH, CH), :]], axis=0
        )

    embedded = pos_ref[...].astype(F32)
    for hi in range(2):
        for tx in range(4):
            rows = [
                lat_scr[pl.ds((2 * pr + hi) * GW + tx, patch_cols, stride=4), :]
                for pr in range(patch_rows)
            ]
            block = jnp.concatenate(rows, axis=0).astype(BF16)
            embedded = embedded + mm(block, embed_block(hi, tx))
    pre = pre_ref[...]
    post = post_ref[...]
    prompt = prompt_ref[...]
    center = embedded - lane_mean(embedded, VW)
    rstd = lax.rsqrt(lane_mean(center * center, VW) + EPS)
    unit = center * rstd
    pooled = jnp.sum(unit, axis=0, keepdims=True) * (1.0 / patches) * pre
    pooled_center = pooled - lane_mean(pooled, VW)
    pooled_rstd = lax.rsqrt(lane_mean(pooled_center * pooled_center, VW) + EPS)
    pooled_unit = pooled_center * pooled_rstd
    final = pooled_unit * post
    dot = jnp.sum(final * prompt, axis=-1, keepdims=True)
    final_sq = jnp.sum(final * final, axis=-1, keepdims=True)
    prompt_sq = jnp.sum(prompt * prompt, axis=-1, keepdims=True)
    final_len = jnp.sqrt(final_sq)
    prompt_len = jnp.sqrt(prompt_sq)
    cosine = dot / (final_len * prompt_len)
    reward_ref[...] = jnp.broadcast_to(100.0 * cosine, reward_ref.shape)
    cot = cot_ref[...]
    final_grad = (100.0 * cot) * (prompt / (final_len * prompt_len) - final * (cosine / final_sq))
    unit_grad = final_grad * post
    pooled_grad = pooled_rstd * (
        unit_grad
        - lane_mean(unit_grad, VW)
        - pooled_unit * lane_mean(unit_grad * pooled_unit, VW)
    )
    flow = pooled_grad * pre * (1.0 / patches)
    embed_grad = rstd * (flow - lane_mean(flow, VW) - unit * lane_mean(flow * unit, VW))
    high = embed_grad.astype(BF16)
    low = (embed_grad - high.astype(F32)).astype(BF16)
    stacked = jnp.concatenate([high, low], axis=0)
    for hi in range(2):
        for tx in range(4):
            both = mm_nt(stacked, embed_block(hi, tx))
            piece = both[:patches] + both[patches:]
            for pr in range(patch_rows):
                grad_scr[pl.ds((2 * pr + hi) * GW + tx, patch_cols, stride=4), :] = piece[
                    pr * patch_cols : (pr + 1) * patch_cols
                ]
    grad = grad_scr[...].astype(BF16)
    grad_ref[...] = grad
    if fused:
        weight_ref[...] = (readout_grad(grad, mod_ref) * out_factor).astype(BF16)
    else:
        weight_ref[...] = jnp.zeros_like(weight_ref)


def readout_grad(grad, mod_ref):
    count, rows, width = mod_ref.shape
    half = rows // 2
    first = mod_ref[:, :half, :].reshape(count * half, width)
    second = mod_ref[:, half:, :].reshape(count * half, width)
    return mm_tn(grad, first)[:CH] + mm_tn(grad, second)[CH:]


def reward_head(
    place, latent, embed, pos, pre, post, prompt, cot, modulated, grid_rows, fused, out_factor
):
    patches = grid_rows * GW // 16
    rows = grid_rows * GW // 2
    width = modulated.shape[2]
    embed_arrays, embed_masks = [x for x, _ in embed], [mask for _, mask in embed]
    vmem = pl.BlockSpec(memory_space=pltpu.VMEM)
    anywhere = pl.BlockSpec(memory_space=pl.ANY)
    return pl.pallas_call(
        functools.partial(head_kernel, grid_rows, fused, embed_masks, out_factor),
        out_shape=(
            jax.ShapeDtypeStruct((1, 128), F32),
            jax.ShapeDtypeStruct((rows, 2 * CH), BF16),
            jax.ShapeDtypeStruct((CH, width), BF16),
        ),
        in_specs=[pl.BlockSpec(memory_space=pltpu.SMEM), vmem]
        + [anywhere] * len(embed_arrays)
        + [vmem] * 6,
        out_specs=(vmem, vmem, vmem),
        scratch_shapes=[
            pltpu.VMEM((rows, 2 * CH), F32),
            pltpu.VMEM((rows, 2 * CH), F32),
            pltpu.VMEM((16 * CH, VW), BF16),
            pltpu.SemaphoreType.DMA((len(embed_arrays),)),
        ],
        compiler_params=pltpu.CompilerParams(vmem_limit_bytes=VMEM_LIMIT),
        cost_estimate=pl.CostEstimate(
            flops=6 * patches * 16 * CH * VW,
            bytes_accessed=2 * 16 * CH * VW + 2 * patches * VW,
            transcendentals=0,
        ),
    )(place, latent, *embed_arrays, pos, pre, post, prompt, cot, modulated)


def spread_kernel(count, half, heads, place_ref, grad_ref, scale_ref, proj_ref, out_ref):
    width = heads * HD
    mine = pl.ds(pl.multiple_of(place_ref[2] * width, HD), width)
    gain = 1.0 + scale_ref[:, mine]
    proj = proj_ref[:, mine]
    zero = jnp.zeros_like(proj)
    sides = (jnp.concatenate([proj, zero], axis=0), jnp.concatenate([zero, proj], axis=0))
    for src in range(count):
        grad = grad_ref[pl.ds(src * half, half), :]
        for side in range(2):
            rows = (mm(grad, sides[side]) * gain).astype(BF16)
            for head in range(heads):
                out_ref[0, head, pl.ds((2 * src + side) * half, half), :] = rows[
                    :, head * HD : (head + 1) * HD
                ]


def spread(place, grad, scales, proj, count, half, heads):
    vmem = pl.BlockSpec(memory_space=pltpu.VMEM)
    return pl.pallas_call(
        functools.partial(spread_kernel, count, half, heads),
        out_shape=jax.ShapeDtypeStruct((1, heads, 2 * count * half, HD), BF16),
        in_specs=[pl.BlockSpec(memory_space=pltpu.SMEM)] + [vmem] * 3,
        out_specs=vmem,
        compiler_params=pltpu.CompilerParams(vmem_limit_bytes=VMEM_LIMIT),
        cost_estimate=pl.CostEstimate(
            flops=8 * count * half * CH * heads * HD,
            bytes_accessed=4 * count * half * heads * HD,
            transcendentals=0,
        ),
    )(place, grad, scales, proj)


def weight_kernel(out_factor, grad_ref, mod_ref, out_ref):
    out_ref[...] = (readout_grad(grad_ref[...], mod_ref) * out_factor).astype(BF16)


def weight_call(grad, modulated, out_factor):
    vmem = pl.BlockSpec(memory_space=pltpu.VMEM)
    return pl.pallas_call(
        functools.partial(weight_kernel, out_factor),
        out_shape=jax.ShapeDtypeStruct((CH, modulated.shape[2]), BF16),
        in_specs=[vmem] * 2,
        out_specs=vmem,
        compiler_params=pltpu.CompilerParams(vmem_limit_bytes=VMEM_LIMIT),
    )(grad, modulated)


def finish_kernel(in_ref, out_ref):
    count, _, width = in_ref.shape
    for group in range(count):
        out_ref[:, pl.ds(group * width, width)] = in_ref[group].astype(F32)


def finish(blocks):
    vmem = pl.BlockSpec(memory_space=pltpu.VMEM)
    return pl.pallas_call(
        finish_kernel,
        out_shape=jax.ShapeDtypeStruct((CH, HEADS * HD), F32),
        in_specs=[vmem],
        out_specs=vmem,
        compiler_params=pltpu.CompilerParams(vmem_limit_bytes=VMEM_LIMIT),
    )(blocks)


def swap(x, axis, mask):
    count = lax.axis_size(axis)
    return lax.ppermute(x, axis, [(i, i ^ mask) for i in range(count)])


def all_to_all(x, groups=None):
    return lax.all_to_all(
        x, "seq", split_axis=0, concat_axis=0, tiled=True, axis_index_groups=groups
    )


def ring_gather(block):
    count = lax.axis_size("seq")
    me = lax.axis_index("seq")
    order = list(range(0, count, 2)) + list(range(count - 1, 0, -2))
    ahead = [(order[i], order[(i + 1) % count]) for i in range(count)]
    behind = [(b, a) for a, b in ahead]
    spot = jnp.where(me % 2 == 0, me // 2, count - 1 - me // 2)

    def place_of(at):
        at = (at + count) % count
        return jnp.where(at < count // 2, 2 * at, 2 * (count - 1 - at) + 1)

    def put(held, piece, at):
        return lax.dynamic_update_slice_in_dim(held, piece[:, None], place_of(at), 1)

    def step(t, carry):
        up, down, held = carry
        up = lax.ppermute(up, "seq", ahead)
        down = lax.ppermute(down, "seq", behind)
        held = put(held, up, spot - t - 1)
        held = put(held, down, spot + t + 1)
        return up, down, held

    held = jnp.zeros((block.shape[0], count) + block.shape[1:], block.dtype)
    held = put(held, block, spot)
    held = lax.fori_loop(0, count // 2, step, (block, block, held))[2]
    return held.reshape(-1, block.shape[2])


def after_kernel(*refs):
    del refs


def after(x, others):
    anywhere = pl.BlockSpec(memory_space=pl.ANY)
    return pl.pallas_call(
        after_kernel,
        out_shape=jax.ShapeDtypeStruct(x.shape, x.dtype),
        in_specs=[anywhere] * (1 + len(others)),
        out_specs=anywhere,
        input_output_aliases={0: 0},
    )(x, *others)


def on_device(
    queries,
    keys,
    values,
    shifts,
    scales,
    proj_out,
    patch_embed,
    pos_embed,
    pre_gain,
    post_gain,
    prompt,
    cotangent,
):
    seq_count = lax.axis_size("seq")
    data_count = lax.axis_size("dp")
    tok_rows = queries.shape[1]
    query_parts = max(1, seq_count // HEADS)
    head_count = max(1, HEADS // seq_count)
    group_count = HEADS // head_count
    width = head_count * HD
    seq_index = lax.axis_index("seq")
    head_group = seq_index // query_parts
    query_part = seq_index % query_parts
    part_rows = tok_rows // query_parts
    half = part_rows // 2
    lat_rows = seq_count * tok_rows
    grid_rows = lat_rows // GW
    canonical = part_rows == 2 * GW
    place = jnp.stack([seq_index, lax.axis_index("dp"), head_group]).astype(jnp.int32)
    proj_turned = proj_out.T
    out_factor = 1.0 / math.sqrt(data_count * lat_rows)

    sizes = (query_parts, part_rows, tok_rows, width)
    positions = patch_embed.shape[0]
    share = positions // data_count if positions % data_count == 0 else 0
    share_shape = (share or positions,) + patch_embed.shape[1:]
    masks = list(range(seq_count - 1, -1, -1))
    embed_share, *pieces = pack_call(
        functools.partial(pack_kernel, sizes, masks, share),
        sizes, masks, share_shape, place, (queries, keys, values, patch_embed),
    )
    received = [swap(piece, "seq", mask) if mask else piece for mask, piece in zip(masks, pieces)]
    embed_mine = after(ring_gather(embed_share), received[:-1])
    embed_bits = [1 << b for b in reversed(range(data_count.bit_length() - 1))] if share else []
    embed = [(embed_mine, 0)]
    for bit in embed_bits[:1]:
        embed = embed + [(swap(x, "dp", bit), m ^ bit) for x, m in embed]

    modulated, latent_part = attend(
        place, masks, received, scales, shifts, proj_turned,
        query_parts, part_rows, tok_rows, head_count,
    )

    groups = None
    if query_parts > 1:
        groups = [[g * query_parts + r for g in range(group_count)] for r in range(query_parts)]
    per_share = seq_count // group_count
    pieces = all_to_all(latent_part.reshape(group_count, per_share * half, 2 * CH), groups)
    embed = [embed[0]] + [(after(x, [pieces]), m) for x, m in embed[1:]]
    for bit in embed_bits[1:]:
        embed = embed + [(swap(x, "dp", bit), m ^ bit) for x, m in embed]
    latent = all_to_all(total_copies([pieces], seq_count))
    if canonical:
        latent = latent.reshape(lat_rows // 2, 2 * CH)
    else:
        latent = latent.reshape(group_count, query_parts, per_share, half, 2, CH)
        latent = latent.transpose(0, 2, 1, 4, 3, 5).reshape(grid_rows // 2, 2, GW, CH)
        latent = latent.transpose(0, 2, 1, 3).reshape(lat_rows // 2, 2 * CH)

    reward, grad, weight = reward_head(
        place, latent, embed, pos_embed, pre_gain[None], post_gain[None], prompt,
        cotangent[None], modulated, grid_rows, canonical, out_factor,
    )
    if not canonical:
        tokens = grad.reshape(grid_rows // 2, GW, 2, CH).transpose(0, 2, 1, 3)
        tokens = tokens.reshape(seq_count, query_parts, 2, half, CH)
        tokens = lax.dynamic_index_in_dim(tokens, query_part, 1, keepdims=False)
        grad = tokens.transpose(0, 2, 1, 3).reshape(seq_count * half, 2 * CH)
        weight = weight_call(grad, modulated, out_factor)

    parts = [weight] + [swap(weight, "dp", mask) for mask in range(1, data_count)]
    attn_grad = spread(place, grad, scales, proj_turned, seq_count, half, head_count)
    if query_parts > 1:
        total = total_copies(parts, 1)[0]
        parts = [total] + [swap(total, "seq", mask) for mask in range(1, query_parts)]
    blocks = all_to_all(total_copies(parts, group_count), groups)
    return (reward[0, :1], attn_grad, finish(blocks).T)


def solution(mesh):
    return jax.shard_map(
        on_device,
        mesh=mesh,
        in_specs=(
            P("dp", "seq", None),
            P("dp", "seq", None),
            P("dp", "seq", None),
            P("dp", None),
            P("dp", None),
            P(),
            P(None, "seq", None),
            P(),
            P(),
            P(),
            P("dp", None),
            P("dp"),
        ),
        out_specs=(P("dp"), P("dp", "seq", None, None), P()),
        check_vma=False,
    )
```

```python
import functools
import math

import jax
import jax.numpy as jnp
from jax import lax
from jax.experimental import pallas as pl
from jax.experimental.pallas import tpu as pltpu
from jax.sharding import PartitionSpec as P

HEADS = 16
HD = 128
CH = 64
GW = 64
VW = 1280
EPS = 1e-05
BF16 = jnp.bfloat16
F32 = jnp.float32
VMEM_LIMIT = 20 * 1024 * 1024


def mm(a, b):
    return jnp.dot(a, b, preferred_element_type=F32)


def mm_nt(a, b):
    return lax.dot_general(a, b, (((1,), (1,)), ((), ())), preferred_element_type=F32)


def mm_tn(a, b):
    return lax.dot_general(a, b, (((0,), (0,)), ((), ())), preferred_element_type=F32)


SMEM_SPEC = pl.BlockSpec(memory_space=pltpu.SMEM)
VMEM_SPEC = pl.BlockSpec(memory_space=pltpu.VMEM)
HBM_SPEC = pl.BlockSpec(memory_space=pltpu.HBM)
ANY_SPEC = pl.BlockSpec(memory_space=pl.ANY)


def in_hbm(x):
    return pltpu.with_memory_space_constraint(x, pltpu.HBM)


def limits():
    return pltpu.CompilerParams(vmem_limit_bytes=VMEM_LIMIT)


class Sizes:
    def __init__(self, seq_count, data_count, tok_rows, patch_embed):
        self.count = seq_count
        self.query_parts = max(1, seq_count // HEADS)
        self.heads = max(1, HEADS // seq_count)
        self.width = self.heads * HD
        self.tok_rows = tok_rows
        self.part_rows = tok_rows // self.query_parts
        positions, self.local, _ = patch_embed.shape
        self.share = positions // data_count if positions % data_count == 0 else positions
        self.rows = self.part_rows + 2 * tok_rows
        self.share_rows = self.share * self.local
        self.chunks = VW // self.width
        self.riding = self.local % 8 == 0 and self.share_rows % 16 == 0 and VW % self.width == 0
        self.ride_rows = self.chunks * self.share_rows if self.riding else 0

    def piece_rows(self, mask):
        return self.rows + (self.ride_rows if mask % 2 == 0 else 0)


def pack_kernel(sizes, masks, place_ref, q_ref, k_ref, v_ref, embed_ref, *refs):
    out_refs = refs[: len(masks)]
    q_scr, k_scr, v_scr, embed_scr, share_scr, in_sems, out_sems = refs[len(masks) :]
    me = place_ref[0]
    tok_rows, part_rows, width = sizes.tok_rows, sizes.part_rows, sizes.width
    share = pl.ds(place_ref[1] * sizes.share, sizes.share)
    loads = [
        pltpu.make_async_copy(embed_ref.at[share], embed_scr, in_sems.at[3]),
        pltpu.make_async_copy(q_ref.at[0], q_scr, in_sems.at[0]),
        pltpu.make_async_copy(k_ref.at[0], k_scr, in_sems.at[1]),
        pltpu.make_async_copy(v_ref.at[0], v_scr, in_sems.at[2]),
    ]
    for load in loads:
        load.start()
    loads[0].wait()
    if sizes.riding:
        for chunk in range(sizes.chunks):
            cols = embed_scr[:, :, pl.ds(chunk * width, width)].astype(F32)
            share_scr[pl.ds(chunk * sizes.share_rows, sizes.share_rows), :] = cols.reshape(
                sizes.share_rows, width
            ).astype(BF16)
    for load in loads[1:]:
        load.wait()
    stores = []
    for slot, (mask, out) in enumerate(zip(masks, out_refs)):
        dest = jnp.bitwise_xor(me, mask)
        group, part = dest // sizes.query_parts, dest % sizes.query_parts
        cols = pl.ds(pl.multiple_of(group * width, HD), width)
        first = pl.ds(pl.multiple_of(part * part_rows, part_rows), part_rows)
        stores += [
            pltpu.make_async_copy(
                q_scr.at[first, cols], out.at[pl.ds(0, part_rows)], out_sems.at[0, slot]
            ),
            pltpu.make_async_copy(
                k_scr.at[:, cols], out.at[pl.ds(part_rows, tok_rows)], out_sems.at[1, slot]
            ),
            pltpu.make_async_copy(
                v_scr.at[:, cols], out.at[pl.ds(part_rows + tok_rows, tok_rows)], out_sems.at[2, slot]
            ),
        ]
        if sizes.riding and mask % 2 == 0:
            stores.append(
                pltpu.make_async_copy(
                    share_scr, out.at[pl.ds(sizes.rows, sizes.ride_rows)], out_sems.at[3, slot]
                )
            )
    for store in stores:
        store.start()
    for store in stores:
        store.wait()


def pack(sizes, masks, place, queries, keys, values, patch_embed):
    tok_rows, full = queries.shape[1:]
    return pl.pallas_call(
        functools.partial(pack_kernel, sizes, masks),
        out_shape=[
            jax.ShapeDtypeStruct((sizes.piece_rows(mask), sizes.width), BF16) for mask in masks
        ],
        in_specs=[SMEM_SPEC] + [HBM_SPEC] * 4,
        out_specs=[HBM_SPEC] * len(masks),
        scratch_shapes=[pltpu.VMEM((tok_rows, full), BF16)] * 3
        + [
            pltpu.VMEM((sizes.share,) + patch_embed.shape[1:], BF16),
            pltpu.VMEM((max(16, sizes.ride_rows), sizes.width), BF16),
            pltpu.SemaphoreType.DMA((4,)),
            pltpu.SemaphoreType.DMA((4, len(masks))),
        ],
        compiler_params=limits(),
        cost_estimate=pl.CostEstimate(
            flops=0, bytes_accessed=12 * tok_rows * full, transcendentals=0
        ),
    )(place, queries, keys, values, patch_embed)


def collect_kernel(sizes, count, *refs):
    in_refs, out_ref, sems = refs[:count], refs[-2], refs[-1]
    copies = [
        pltpu.make_async_copy(
            ref.at[pl.ds(sizes.rows, sizes.ride_rows)], out_ref.at[slot], sems.at[slot]
        )
        for slot, ref in enumerate(in_refs)
    ]
    for copy in copies:
        copy.start()
    for copy in copies:
        copy.wait()


def collect(sizes, pieces, others):
    return pl.pallas_call(
        functools.partial(collect_kernel, sizes, len(pieces)),
        out_shape=jax.ShapeDtypeStruct((len(pieces), sizes.ride_rows, sizes.width), BF16),
        in_specs=[HBM_SPEC] * (len(pieces) + len(others)),
        out_specs=VMEM_SPEC,
        scratch_shapes=[pltpu.SemaphoreType.DMA((len(pieces),))],
        compiler_params=limits(),
    )(*pieces, *others)


def arrange_kernel(sizes, masks, place_ref, held_ref, got_ref, wait_ref, out_ref):
    del wait_ref
    me = place_ref[0]
    odd = me % 2 == 1
    local, width = sizes.local, sizes.width
    for slot, mask in enumerate(masks):
        pair = jnp.bitwise_xor(me, mask) // 2
        for chunk in range(sizes.chunks):
            rows = pl.ds(chunk * sizes.share_rows, sizes.share_rows)
            held = held_ref[slot, rows, :].astype(F32)
            got = got_ref[slot, rows, :].astype(F32)
            first = jnp.where(odd, got, held)
            second = jnp.where(odd, held, got)
            for at in range(sizes.share):
                part = slice(at * local, (at + 1) * local)
                both = jnp.concatenate([first[part], second[part]], axis=0).astype(BF16)
                start = pl.multiple_of(at * sizes.count * local + pair * 2 * local, 2 * local)
                out_ref[pl.ds(start, 2 * local), pl.ds(chunk * width, width)] = both


def arrange(sizes, masks, place, held, got, wait):
    rows = sizes.share * sizes.count * sizes.local
    return pl.pallas_call(
        functools.partial(arrange_kernel, sizes, masks),
        out_shape=jax.ShapeDtypeStruct((rows, VW), BF16),
        in_specs=[SMEM_SPEC, VMEM_SPEC, VMEM_SPEC, ANY_SPEC],
        out_specs=VMEM_SPEC,
        compiler_params=limits(),
    )(place, held, got, wait)


def attend_kernel(sizes, masks, place_ref, *refs):
    count, heads, width = sizes.count, sizes.heads, sizes.width
    tok_rows, part_rows = sizes.tok_rows, sizes.part_rows
    in_refs = refs[:count]
    scale_ref, shift_ref, proj_ref, mod_ref, lat_ref, *refs = refs[count:]
    query_scr, key_scr, value_scr, scale_scr, shift_scr, proj_scr, sems, side_sems = refs
    half = part_rows // 2
    factor = HD ** (-0.5) * math.log2(math.e)
    me = place_ref[0]
    mine = pl.ds(pl.multiple_of(place_ref[2] * width, HD), width)
    copies = [
        pltpu.make_async_copy(scale_ref.at[:, mine], scale_scr, side_sems.at[0]),
        pltpu.make_async_copy(shift_ref.at[:, mine], shift_scr, side_sems.at[1]),
        pltpu.make_async_copy(proj_ref.at[:, mine], proj_scr, side_sems.at[2]),
    ]
    for src in range(count):
        ref = in_refs[src]
        rows = pl.ds(src * tok_rows, tok_rows)
        copies += [
            pltpu.make_async_copy(ref.at[pl.ds(0, part_rows)], query_scr.at[src], sems.at[0, src]),
            pltpu.make_async_copy(
                ref.at[pl.ds(part_rows, tok_rows)], key_scr.at[rows], sems.at[1, src]
            ),
        ]
        for head in range(heads):
            copies.append(
                pltpu.make_async_copy(
                    ref.at[pl.ds(part_rows + tok_rows, tok_rows), pl.ds(head * HD, HD)],
                    value_scr.at[rows, pl.ds(2 * head * HD, HD)],
                    sems.at[2 + head, src],
                )
            )
    for copy in copies:
        copy.start()
    ones = jnp.ones((tok_rows, HD), BF16)
    for src in range(count):
        for head in range(heads):
            value_scr[pl.ds(src * tok_rows, tok_rows), pl.ds((2 * head + 1) * HD, HD)] = ones
    for copy in copies:
        copy.wait()
    gain = 1.0 + scale_scr[...]
    shift = shift_scr[...]
    proj = proj_scr[...]
    zero = jnp.zeros_like(proj)
    proj_pair = jnp.concatenate(
        [jnp.concatenate([proj, zero], axis=1), jnp.concatenate([zero, proj], axis=1)], axis=0
    )
    for src in range(count):
        mixed = []
        for head in range(heads):
            cols = pl.ds(head * HD, HD)
            logits = mm_nt(query_scr[src, :, cols], key_scr[:, cols])
            top = jnp.max(logits, axis=-1, keepdims=True)
            weights = jnp.exp2((logits - top) * factor).astype(BF16)
            both = mm(weights, value_scr[:, pl.ds(2 * head * HD, 2 * HD)])
            mixed.append(both[:, :HD] / both[:, HD:])
        attended = jnp.concatenate(mixed, axis=1) if heads > 1 else mixed[0]
        modulated = (attended * gain + shift).astype(BF16)
        place = jnp.bitwise_xor(me, masks[src])
        mod_ref[place] = modulated
        pair = jnp.concatenate([modulated[:half], modulated[half:]], axis=1)
        lat_ref[place] = mm_nt(pair, proj_pair).astype(BF16)


def attend(sizes, masks, place, received, scales, shifts, proj):
    count, width, heads = sizes.count, sizes.width, sizes.heads
    lat_rows = count * sizes.tok_rows
    query_rows = count * sizes.part_rows
    return pl.pallas_call(
        functools.partial(attend_kernel, sizes, masks),
        out_shape=(
            jax.ShapeDtypeStruct((count, sizes.part_rows, width), BF16),
            jax.ShapeDtypeStruct((count, sizes.part_rows // 2, 2 * CH), BF16),
        ),
        in_specs=[SMEM_SPEC] + [HBM_SPEC] * (count + 3),
        out_specs=(VMEM_SPEC, VMEM_SPEC),
        scratch_shapes=[
            pltpu.VMEM((count, sizes.part_rows, width), BF16),
            pltpu.VMEM((lat_rows, width), BF16),
            pltpu.VMEM((lat_rows, 2 * width), BF16),
            pltpu.VMEM((1, width), F32),
            pltpu.VMEM((1, width), F32),
            pltpu.VMEM((CH, width), BF16),
            pltpu.SemaphoreType.DMA((2 + heads, count)),
            pltpu.SemaphoreType.DMA((3,)),
        ],
        compiler_params=limits(),
        cost_estimate=pl.CostEstimate(
            flops=4 * query_rows * lat_rows * width,
            bytes_accessed=2 * (query_rows * 2 + lat_rows * 2) * width,
            transcendentals=query_rows * lat_rows * heads,
        ),
    )(place, *received, scales, shifts, proj)


def total_kernel(copies, *refs):
    out_ref = refs[-1]
    if len(refs) == 2:
        parts = [refs[0][i].astype(F32) for i in range(refs[0].shape[0])]
    else:
        parts = [ref[...].astype(F32) for ref in refs[:-1]]
    while len(parts) > 1:
        parts = [parts[i] + parts[i + 1] for i in range(0, len(parts), 2)]
    for copy in range(copies):
        out_ref[copy] = parts[0].astype(BF16)


def total_copies(arrays, copies):
    return pl.pallas_call(
        functools.partial(total_kernel, copies),
        out_shape=jax.ShapeDtypeStruct((copies,) + arrays[0].shape[-2:], BF16),
        in_specs=[VMEM_SPEC] * len(arrays),
        out_specs=VMEM_SPEC,
        compiler_params=limits(),
    )(*arrays)


def lane_mean(x, count):
    return jnp.sum(x, axis=-1, keepdims=True) * (1.0 / count)


def head_kernel(grid_rows, fused, embed_masks, out_factor, place_ref, lat_ref, *refs):
    embed_refs, refs = refs[: len(embed_masks)], refs[len(embed_masks) :]
    sides, refs = refs[:4], refs[4:]
    cot_ref, mod_ref, reward_ref, grad_ref, weight_ref, lat_scr, grad_scr, embed_ref, *refs = refs
    pos_ref, pre_ref, post_ref, prompt_ref, sems, side_sems = refs
    patch_rows = grid_rows // 4
    patch_cols = GW // 4
    patches = patch_rows * patch_cols
    copies = []
    for slot, mask in enumerate(embed_masks):
        rows = embed_refs[slot].shape[0]
        first = pl.multiple_of(jnp.bitwise_xor(place_ref[1], mask) * rows, rows)
        copies.append(
            pltpu.make_async_copy(embed_refs[slot], embed_ref.at[pl.ds(first, rows)], sems.at[slot])
        )
    for slot, (side, scr) in enumerate(zip(sides, (pos_ref, pre_ref, post_ref, prompt_ref))):
        copies.append(pltpu.make_async_copy(side, scr, side_sems.at[slot]))
    for copy in copies:
        copy.start()
    lat_scr[...] = lat_ref[...].astype(F32)
    for copy in copies:
        copy.wait()

    def embed_block(hi, tx):
        first = 4 * (2 * hi) + tx
        second = 4 * (2 * hi + 1) + tx
        return jnp.concatenate(
            [embed_ref[pl.ds(first * CH, CH), :], embed_ref[pl.ds(second * CH, CH), :]], axis=0
        )

    embedded = pos_ref[...].astype(F32)
    for hi in range(2):
        for tx in range(4):
            rows = [
                lat_scr[pl.ds((2 * pr + hi) * GW + tx, patch_cols, stride=4), :]
                for pr in range(patch_rows)
            ]
            block = jnp.concatenate(rows, axis=0).astype(BF16)
            embedded = embedded + mm(block, embed_block(hi, tx))
    pre = pre_ref[...]
    post = post_ref[...]
    prompt = prompt_ref[...]
    center = embedded - lane_mean(embedded, VW)
    rstd = lax.rsqrt(lane_mean(center * center, VW) + EPS)
    unit = center * rstd
    pooled = jnp.sum(unit, axis=0, keepdims=True) * (1.0 / patches) * pre
    pooled_center = pooled - lane_mean(pooled, VW)
    pooled_rstd = lax.rsqrt(lane_mean(pooled_center * pooled_center, VW) + EPS)
    pooled_unit = pooled_center * pooled_rstd
    final = pooled_unit * post
    dot = jnp.sum(final * prompt, axis=-1, keepdims=True)
    final_sq = jnp.sum(final * final, axis=-1, keepdims=True)
    prompt_sq = jnp.sum(prompt * prompt, axis=-1, keepdims=True)
    final_len = jnp.sqrt(final_sq)
    prompt_len = jnp.sqrt(prompt_sq)
    cosine = dot / (final_len * prompt_len)
    reward_ref[...] = jnp.broadcast_to(100.0 * cosine, reward_ref.shape)
    cot = cot_ref[0]
    final_grad = (100.0 * cot) * (prompt / (final_len * prompt_len) - final * (cosine / final_sq))
    unit_grad = final_grad * post
    pooled_grad = pooled_rstd * (
        unit_grad
        - lane_mean(unit_grad, VW)
        - pooled_unit * lane_mean(unit_grad * pooled_unit, VW)
    )
    flow = pooled_grad * pre * (1.0 / patches)
    embed_grad = rstd * (flow - lane_mean(flow, VW) - unit * lane_mean(flow * unit, VW))
    high = embed_grad.astype(BF16)
    low = (embed_grad - high.astype(F32)).astype(BF16)
    stacked = jnp.concatenate([high, low], axis=0)
    for hi in range(2):
        for tx in range(4):
            both = mm_nt(stacked, embed_block(hi, tx))
            piece = both[:patches] + both[patches:]
            for pr in range(patch_rows):
                grad_scr[pl.ds((2 * pr + hi) * GW + tx, patch_cols, stride=4), :] = piece[
                    pr * patch_cols : (pr + 1) * patch_cols
                ]
    grad = grad_scr[...].astype(BF16)
    grad_ref[...] = grad
    if fused:
        weight_ref[...] = (readout_grad(grad, mod_ref) * out_factor).astype(BF16)
    else:
        weight_ref[...] = jnp.zeros_like(weight_ref)


def readout_grad(grad, mod_ref):
    count, rows, width = mod_ref.shape
    half = rows // 2
    first = mod_ref[:, :half, :].reshape(count * half, width)
    second = mod_ref[:, half:, :].reshape(count * half, width)
    return mm_tn(grad, first)[:CH] + mm_tn(grad, second)[CH:]


def reward_head(
    place, latent, embed, pos, pre, post, prompt, cot, modulated, grid_rows, fused, out_factor
):
    patches = grid_rows * GW // 16
    rows = grid_rows * GW // 2
    width = modulated.shape[2]
    embed_arrays, embed_masks = [x for x, _ in embed], [mask for _, mask in embed]
    return pl.pallas_call(
        functools.partial(head_kernel, grid_rows, fused, embed_masks, out_factor),
        out_shape=(
            jax.ShapeDtypeStruct((1, 128), F32),
            jax.ShapeDtypeStruct((rows, 2 * CH), BF16),
            jax.ShapeDtypeStruct((CH, width), BF16),
        ),
        in_specs=[SMEM_SPEC, VMEM_SPEC]
        + [ANY_SPEC] * len(embed_arrays)
        + [HBM_SPEC] * 4
        + [SMEM_SPEC, VMEM_SPEC],
        out_specs=(VMEM_SPEC, VMEM_SPEC, VMEM_SPEC),
        scratch_shapes=[
            pltpu.VMEM((rows, 2 * CH), F32),
            pltpu.VMEM((rows, 2 * CH), F32),
            pltpu.VMEM((16 * CH, VW), BF16),
            pltpu.VMEM((patches, VW), BF16),
            pltpu.VMEM((1, VW), F32),
            pltpu.VMEM((1, VW), F32),
            pltpu.VMEM((1, VW), F32),
            pltpu.SemaphoreType.DMA((len(embed_arrays),)),
            pltpu.SemaphoreType.DMA((4,)),
        ],
        compiler_params=limits(),
        cost_estimate=pl.CostEstimate(
            flops=6 * patches * 16 * CH * VW,
            bytes_accessed=2 * 16 * CH * VW + 2 * patches * VW,
            transcendentals=0,
        ),
    )(place, latent, *embed_arrays, pos, pre, post, prompt, cot, modulated)


def spread_kernel(count, half, heads, place_ref, grad_ref, scale_ref, proj_ref, out_ref):
    width = heads * HD
    mine = pl.ds(pl.multiple_of(place_ref[2] * width, HD), width)
    gain = 1.0 + scale_ref[:, mine]
    proj = proj_ref[:, mine]
    zero = jnp.zeros_like(proj)
    sides = (jnp.concatenate([proj, zero], axis=0), jnp.concatenate([zero, proj], axis=0))
    for src in range(count):
        grad = grad_ref[pl.ds(src * half, half), :]
        for side in range(2):
            rows = (mm(grad, sides[side]) * gain).astype(BF16)
            for head in range(heads):
                out_ref[0, head, pl.ds((2 * src + side) * half, half), :] = rows[
                    :, head * HD : (head + 1) * HD
                ]


def spread(place, grad, scales, proj, count, half, heads):
    return pl.pallas_call(
        functools.partial(spread_kernel, count, half, heads),
        out_shape=jax.ShapeDtypeStruct((1, heads, 2 * count * half, HD), BF16),
        in_specs=[SMEM_SPEC] + [VMEM_SPEC] * 3,
        out_specs=VMEM_SPEC,
        compiler_params=limits(),
        cost_estimate=pl.CostEstimate(
            flops=8 * count * half * CH * heads * HD,
            bytes_accessed=4 * count * half * heads * HD,
            transcendentals=0,
        ),
    )(place, grad, scales, proj)


def weight_kernel(out_factor, grad_ref, mod_ref, out_ref):
    out_ref[...] = (readout_grad(grad_ref[...], mod_ref) * out_factor).astype(BF16)


def weight_call(grad, modulated, out_factor):
    return pl.pallas_call(
        functools.partial(weight_kernel, out_factor),
        out_shape=jax.ShapeDtypeStruct((CH, modulated.shape[2]), BF16),
        in_specs=[VMEM_SPEC] * 2,
        out_specs=VMEM_SPEC,
        compiler_params=limits(),
    )(grad, modulated)


def finish_kernel(in_ref, out_ref):
    count, _, width = in_ref.shape
    for group in range(count):
        out_ref[:, pl.ds(group * width, width)] = in_ref[group].astype(F32)


def finish(blocks):
    return pl.pallas_call(
        finish_kernel,
        out_shape=jax.ShapeDtypeStruct((CH, HEADS * HD), F32),
        in_specs=[VMEM_SPEC],
        out_specs=VMEM_SPEC,
        compiler_params=limits(),
    )(blocks)


def swap(x, axis, mask):
    count = lax.axis_size(axis)
    return lax.ppermute(x, axis, [(i, i ^ mask) for i in range(count)])


def all_to_all(x, groups=None):
    return lax.all_to_all(
        x, "seq", split_axis=0, concat_axis=0, tiled=True, axis_index_groups=groups
    )


def after_kernel(*refs):
    del refs


def after(x, others):
    return pl.pallas_call(
        after_kernel,
        out_shape=jax.ShapeDtypeStruct(x.shape, x.dtype),
        in_specs=[ANY_SPEC] * (1 + len(others)),
        out_specs=ANY_SPEC,
        input_output_aliases={0: 0},
    )(x, *others)


def on_device(
    queries,
    keys,
    values,
    shifts,
    scales,
    proj_out,
    patch_embed,
    pos_embed,
    pre_gain,
    post_gain,
    prompt,
    cotangent,
):
    seq_count = lax.axis_size("seq")
    data_count = lax.axis_size("dp")
    tok_rows = queries.shape[1]
    sizes = Sizes(seq_count, data_count, tok_rows, patch_embed)
    query_parts, head_count, part_rows = sizes.query_parts, sizes.heads, sizes.part_rows
    group_count = HEADS // head_count
    seq_index = lax.axis_index("seq")
    head_group = seq_index // query_parts
    query_part = seq_index % query_parts
    half = part_rows // 2
    lat_rows = seq_count * tok_rows
    grid_rows = lat_rows // GW
    canonical = part_rows == 2 * GW
    place = jnp.stack([seq_index, lax.axis_index("dp"), head_group]).astype(jnp.int32)
    proj_turned = proj_out.T
    out_factor = 1.0 / math.sqrt(data_count * lat_rows)

    masks = [1, 2] + list(range(seq_count - 1, 2, -1)) + [0]
    pieces = pack(
        sizes, masks, place, in_hbm(queries), in_hbm(keys), in_hbm(values), in_hbm(patch_embed)
    )
    received = [swap(piece, "seq", mask) if mask else piece for mask, piece in zip(masks, pieces)]
    bits = [1 << b for b in reversed(range(data_count.bit_length() - 1))]
    shared = sizes.share < patch_embed.shape[0]
    if sizes.riding:
        even = [slot for slot, mask in enumerate(masks) if mask % 2 == 0]
        others = [slot for slot, mask in enumerate(masks) if mask % 2]
        held = collect(
            sizes, [received[slot] for slot in even], [received[slot] for slot in others]
        )
        got = swap(held, "seq", 1)
        far_held = swap(held, "dp", bits[0]) if shared else None

    modulated, latent_part = attend(
        sizes, masks, place, received, in_hbm(scales), in_hbm(shifts), in_hbm(proj_turned)
    )

    if sizes.riding:
        got = after(got, [modulated])
        even_masks = [masks[slot] for slot in even]
        embed = [(arrange(sizes, even_masks, place, held, got, modulated), 0)]
        far_got = swap(got, "dp", bits[0]) if shared else None
    else:
        mine = patch_embed
        if shared:
            mine = lax.dynamic_slice_in_dim(
                patch_embed, lax.axis_index("dp") * sizes.share, sizes.share, 0
            )
        mine = lax.all_gather(mine, "seq", axis=1, tiled=True).reshape(-1, VW)
        embed = [(mine, 0)]
        if shared:
            embed = embed + [(swap(mine, "dp", bits[0]), bits[0])]

    groups = None
    if query_parts > 1:
        groups = [[g * query_parts + r for g in range(group_count)] for r in range(query_parts)]
    per_share = seq_count // group_count
    pieces = all_to_all(latent_part.reshape(group_count, per_share * half, 2 * CH), groups)
    if sizes.riding and shared:
        embed.append((arrange(sizes, even_masks, place, far_held, far_got, pieces), bits[0]))
    for bit in bits[1:] if shared else []:
        embed = embed + [(swap(x, "dp", bit), m ^ bit) for x, m in embed]
    latent = all_to_all(total_copies([pieces], seq_count))
    if canonical:
        latent = latent.reshape(lat_rows // 2, 2 * CH)
    else:
        latent = latent.reshape(group_count, query_parts, per_share, half, 2, CH)
        latent = latent.transpose(0, 2, 1, 4, 3, 5).reshape(grid_rows // 2, 2, GW, CH)
        latent = latent.transpose(0, 2, 1, 3).reshape(lat_rows // 2, 2 * CH)

    reward, grad, weight = reward_head(
        place, latent, embed, in_hbm(pos_embed), pre_gain[None], post_gain[None], in_hbm(prompt),
        cotangent, modulated, grid_rows, canonical, out_factor,
    )
    if not canonical:
        tokens = grad.reshape(grid_rows // 2, GW, 2, CH).transpose(0, 2, 1, 3)
        tokens = tokens.reshape(seq_count, query_parts, 2, half, CH)
        tokens = lax.dynamic_index_in_dim(tokens, query_part, 1, keepdims=False)
        grad = tokens.transpose(0, 2, 1, 3).reshape(seq_count * half, 2 * CH)
        weight = weight_call(grad, modulated, out_factor)

    parts = [weight] + [swap(weight, "dp", mask) for mask in range(1, data_count)]
    attn_grad = spread(place, grad, scales, proj_turned, seq_count, half, head_count)
    if query_parts > 1:
        total = total_copies(parts, 1)[0]
        parts = [total] + [swap(total, "seq", mask) for mask in range(1, query_parts)]
    blocks = all_to_all(total_copies(parts, group_count), groups)
    return (reward[0, :1], attn_grad, finish(blocks).T)


def solution(mesh):
    return jax.shard_map(
        on_device,
        mesh=mesh,
        in_specs=(
            P("dp", "seq", None),
            P("dp", "seq", None),
            P("dp", "seq", None),
            P("dp", None),
            P("dp", None),
            P(),
            P(None, "seq", None),
            P(),
            P(),
            P(),
            P("dp", None),
            P("dp"),
        ),
        out_specs=(P("dp"), P("dp", "seq", None, None), P()),
        check_vma=False,
    )
```

```python
import functools
import math

import jax
import jax.numpy as jnp
from jax import lax
from jax.experimental import pallas as pl
from jax.experimental.pallas import tpu as pltpu
from jax.sharding import PartitionSpec as P

HEADS = 16
HD = 128
CH = 64
GW = 64
VW = 1280
EPS = 1e-05
BF16 = jnp.bfloat16
F32 = jnp.float32
VMEM_LIMIT = 20 * 1024 * 1024


def mm(a, b):
    return jnp.dot(a, b, preferred_element_type=F32)


def mm_nt(a, b):
    return lax.dot_general(a, b, (((1,), (1,)), ((), ())), preferred_element_type=F32)


def mm_tn(a, b):
    return lax.dot_general(a, b, (((0,), (0,)), ((), ())), preferred_element_type=F32)


SMEM_SPEC = pl.BlockSpec(memory_space=pltpu.SMEM)
VMEM_SPEC = pl.BlockSpec(memory_space=pltpu.VMEM)
HBM_SPEC = pl.BlockSpec(memory_space=pltpu.HBM)
ANY_SPEC = pl.BlockSpec(memory_space=pl.ANY)


def in_hbm(x):
    return pltpu.with_memory_space_constraint(x, pltpu.HBM)


def limits():
    return pltpu.CompilerParams(vmem_limit_bytes=VMEM_LIMIT)


class Sizes:
    def __init__(self, seq_count, data_count, tok_rows, patch_embed):
        self.count = seq_count
        self.query_parts = max(1, seq_count // HEADS)
        self.heads = max(1, HEADS // seq_count)
        self.width = self.heads * HD
        self.tok_rows = tok_rows
        self.part_rows = tok_rows // self.query_parts
        positions, self.local, _ = patch_embed.shape
        self.share = positions // data_count if positions % data_count == 0 else positions
        self.rows = self.part_rows + 2 * tok_rows
        self.share_rows = self.share * self.local
        self.chunks = VW // HD
        self.riding = self.local % 8 == 0 and self.share_rows % 16 == 0 and seq_count >= 4
        self.ride_rows = self.chunks * self.share_rows if self.riding else 0

    def pieces(self):
        middle = self.count // 2
        far, near = range(self.count - 1, middle - 1, -1), range(1, middle)
        every = tuple(range(self.heads))
        listed = [(mask, (0,)) for mask in far] + [(mask, every) for mask in near]
        for head in every[1:]:
            listed += [(mask, (head,)) for mask in far]
        return listed + [(0, every)]

    def rides(self, piece):
        return self.riding and piece[0] % 2 == 0 and 0 in piece[1]

    def piece_shape(self, piece):
        wide = len(piece[1])
        return (self.rows + (self.ride_rows // wide if self.rides(piece) else 0), wide * HD)

    def ride_slices(self, piece):
        wide = len(piece[1])
        deep = self.ride_rows // wide
        return [
            (pl.ds(self.rows, deep), pl.ds(at * HD, HD), pl.ds(at * deep, deep)) for at in range(wide)
        ]


def pack_kernel(sizes, place_ref, q_ref, k_ref, v_ref, embed_ref, *refs):
    pieces = sizes.pieces()
    out_refs = refs[: len(pieces)]
    q_scr, k_scr, v_scr, embed_scr, share_scr, in_sems, out_sems = refs[len(pieces) :]
    me = place_ref[0]
    tok_rows, part_rows, width = sizes.tok_rows, sizes.part_rows, sizes.width
    share = pl.ds(place_ref[1] * sizes.share, sizes.share)
    loads = [
        pltpu.make_async_copy(embed_ref.at[share], embed_scr, in_sems.at[3]),
        pltpu.make_async_copy(q_ref.at[0], q_scr, in_sems.at[0]),
        pltpu.make_async_copy(k_ref.at[0], k_scr, in_sems.at[1]),
        pltpu.make_async_copy(v_ref.at[0], v_scr, in_sems.at[2]),
    ]
    for load in loads:
        load.start()
    stores = []
    sent = [[], [], [], []]
    for slot, (piece, out) in enumerate(zip(pieces, out_refs)):
        mask, some = piece
        dest = jnp.bitwise_xor(me, mask)
        group, part = dest // sizes.query_parts, dest % sizes.query_parts
        cols = pl.ds(pl.multiple_of(group * width + some[0] * HD, HD), len(some) * HD)
        first = pl.ds(pl.multiple_of(part * part_rows, part_rows), part_rows)
        for kind, source, rows in (
            (0, q_scr.at[first, cols], pl.ds(0, part_rows)),
            (1, k_scr.at[:, cols], pl.ds(part_rows, tok_rows)),
            (2, v_scr.at[:, cols], pl.ds(part_rows + tok_rows, tok_rows)),
        ):
            sent[kind].append(pltpu.make_async_copy(source, out.at[rows], out_sems.at[kind, slot]))
        if sizes.rides(piece):
            for at, (rows, place, from_rows) in enumerate(sizes.ride_slices(piece)):
                sent[3].append(
                    pltpu.make_async_copy(
                        share_scr.at[from_rows], out.at[rows, place], out_sems.at[3 + at, slot]
                    )
                )
    loads[0].wait()
    if sizes.riding:
        for chunk in range(sizes.chunks):
            cols = embed_scr[:, :, pl.ds(chunk * HD, HD)].astype(F32)
            share_scr[pl.ds(chunk * sizes.share_rows, sizes.share_rows), :] = cols.reshape(
                sizes.share_rows, HD
            ).astype(BF16)
    for store in sent[3]:
        store.start()
    for kind in range(3):
        loads[kind + 1].wait()
        for store in sent[kind]:
            store.start()
    for stores in sent:
        for store in stores:
            store.wait()


def pack(sizes, place, queries, keys, values, patch_embed):
    tok_rows, full = queries.shape[1:]
    pieces = sizes.pieces()
    return pl.pallas_call(
        functools.partial(pack_kernel, sizes),
        out_shape=[jax.ShapeDtypeStruct(sizes.piece_shape(piece), BF16) for piece in pieces],
        in_specs=[SMEM_SPEC] + [HBM_SPEC] * 4,
        out_specs=[HBM_SPEC] * len(pieces),
        scratch_shapes=[pltpu.VMEM((tok_rows, full), BF16)] * 3
        + [
            pltpu.VMEM((sizes.share,) + patch_embed.shape[1:], BF16),
            pltpu.VMEM((max(16, sizes.ride_rows), HD), BF16),
            pltpu.SemaphoreType.DMA((4,)),
            pltpu.SemaphoreType.DMA((3 + sizes.heads, len(pieces))),
        ],
        compiler_params=limits(),
        cost_estimate=pl.CostEstimate(
            flops=0, bytes_accessed=12 * tok_rows * full, transcendentals=0
        ),
    )(place, queries, keys, values, patch_embed)


def collect_kernel(sizes, pieces, *refs):
    in_refs, out_ref, sems = refs[: len(pieces)], refs[-2], refs[-1]
    copies = []
    for slot, (piece, ref) in enumerate(zip(pieces, in_refs)):
        for at, (rows, cols, to_rows) in enumerate(sizes.ride_slices(piece)):
            copies.append(
                pltpu.make_async_copy(
                    ref.at[rows, cols], out_ref.at[slot, to_rows], sems.at[at, slot]
                )
            )
    for copy in copies:
        copy.start()
    for copy in copies:
        copy.wait()


def collect(sizes, pieces, arrays, others):
    return pl.pallas_call(
        functools.partial(collect_kernel, sizes, pieces),
        out_shape=jax.ShapeDtypeStruct((len(pieces), sizes.ride_rows, HD), BF16),
        in_specs=[ANY_SPEC] * (len(arrays) + len(others)),
        out_specs=VMEM_SPEC,
        scratch_shapes=[pltpu.SemaphoreType.DMA((sizes.heads, len(pieces)))],
        compiler_params=limits(),
    )(*arrays, *others)


def arrange_kernel(sizes, masks, place_ref, held_ref, got_ref, wait_ref, out_ref):
    del wait_ref
    me = place_ref[0]
    odd = me % 2 == 1
    local, width = sizes.local, HD
    for slot, mask in enumerate(masks):
        pair = jnp.bitwise_xor(me, mask) // 2
        for chunk in range(sizes.chunks):
            rows = pl.ds(chunk * sizes.share_rows, sizes.share_rows)
            held = held_ref[slot, rows, :].astype(F32)
            got = got_ref[slot, rows, :].astype(F32)
            first = jnp.where(odd, got, held)
            second = jnp.where(odd, held, got)
            for at in range(sizes.share):
                part = slice(at * local, (at + 1) * local)
                both = jnp.concatenate([first[part], second[part]], axis=0).astype(BF16)
                start = pl.multiple_of(at * sizes.count * local + pair * 2 * local, 2 * local)
                out_ref[pl.ds(start, 2 * local), pl.ds(chunk * width, width)] = both


def arrange(sizes, masks, place, held, got, wait):
    rows = sizes.share * sizes.count * sizes.local
    return pl.pallas_call(
        functools.partial(arrange_kernel, sizes, masks),
        out_shape=jax.ShapeDtypeStruct((rows, VW), BF16),
        in_specs=[SMEM_SPEC, VMEM_SPEC, VMEM_SPEC, ANY_SPEC],
        out_specs=VMEM_SPEC,
        compiler_params=limits(),
    )(place, held, got, wait)


def attend_kernel(sizes, head, pieces, place_ref, *refs):
    count, width = sizes.count, sizes.width
    tok_rows, part_rows = sizes.tok_rows, sizes.part_rows
    in_refs, refs = refs[:count], refs[count:]
    scale_ref, shift_ref, proj_ref, *refs = refs
    before_ref = None
    if head:
        before_ref, *refs = refs
    mod_ref, lat_ref, query_scr, key_scr, value_scr, scale_scr, shift_scr, proj_scr, *refs = refs
    sems, side_sems = refs
    half = part_rows // 2
    lat_rows = count * tok_rows
    factor = HD ** (-0.5) * math.log2(math.e)
    me = place_ref[0]
    mine = pl.ds(pl.multiple_of(place_ref[2] * width + head * HD, HD), HD)
    copies = []
    for src, (piece, ref) in enumerate(zip(pieces, in_refs)):
        cols = pl.ds(piece[1].index(head) * HD, HD)
        for kind, start, rows, scr in (
            (0, 0, part_rows, query_scr),
            (1, part_rows, tok_rows, key_scr),
            (2, part_rows + tok_rows, tok_rows, value_scr),
        ):
            to = scr.at[pl.ds(src * rows, rows)]
            if kind == 2:
                to = scr.at[pl.ds(src * rows, rows), pl.ds(0, HD)]
            copies.append(
                pltpu.make_async_copy(ref.at[pl.ds(start, rows), cols], to, sems.at[kind, src])
            )
    copies += [
        pltpu.make_async_copy(scale_ref.at[:, mine], scale_scr, side_sems.at[0]),
        pltpu.make_async_copy(shift_ref.at[:, mine], shift_scr, side_sems.at[1]),
        pltpu.make_async_copy(proj_ref.at[:, mine], proj_scr, side_sems.at[2]),
    ]
    for copy in copies:
        copy.start()
    value_scr[:, pl.ds(HD, HD)] = jnp.ones((lat_rows, HD), BF16)
    for copy in copies:
        copy.wait()
    gain = 1.0 + scale_scr[...]
    shift = shift_scr[...]
    proj = proj_scr[...]
    zero = jnp.zeros_like(proj)
    proj_pair = jnp.concatenate(
        [jnp.concatenate([proj, zero], axis=1), jnp.concatenate([zero, proj], axis=1)], axis=0
    )
    block = min(count * part_rows, max(part_rows, min(256, (1 << 18) // lat_rows)))
    for first in range(0, count * part_rows, block):
        logits = mm_nt(query_scr[pl.ds(first, block), :], key_scr[...])
        top = jnp.max(logits, axis=-1, keepdims=True)
        weights = jnp.exp2((logits - top) * factor).astype(BF16)
        both = mm(weights, value_scr[...])
        modulated = (both[:, :HD] / both[:, HD:] * gain + shift).astype(BF16)
        for at in range(0, block, part_rows):
            place = jnp.bitwise_xor(me, pieces[(first + at) // part_rows][0])
            mod_ref[place] = modulated[at : at + part_rows]
            pair = jnp.concatenate(
                [modulated[at : at + half], modulated[at + half : at + part_rows]], axis=1
            )
            latent = mm_nt(pair, proj_pair)
            if head:
                latent = latent + before_ref[place]
            lat_ref[place] = latent.astype(lat_ref.dtype)


def attend(sizes, head, place, pieces, received, scales, shifts, proj, before):
    count = sizes.count
    lat_rows = count * sizes.tok_rows
    query_rows = count * sizes.part_rows
    last = head == sizes.heads - 1
    return pl.pallas_call(
        functools.partial(attend_kernel, sizes, head, pieces),
        out_shape=(
            jax.ShapeDtypeStruct((count, sizes.part_rows, HD), BF16),
            jax.ShapeDtypeStruct((count, sizes.part_rows // 2, 2 * CH), BF16 if last else F32),
        ),
        in_specs=[SMEM_SPEC] + [ANY_SPEC] * count + [HBM_SPEC] * 3 + [VMEM_SPEC] * len(before),
        out_specs=(VMEM_SPEC, VMEM_SPEC),
        scratch_shapes=[
            pltpu.VMEM((query_rows, HD), BF16),
            pltpu.VMEM((lat_rows, HD), BF16),
            pltpu.VMEM((lat_rows, 2 * HD), BF16),
            pltpu.VMEM((1, HD), F32),
            pltpu.VMEM((1, HD), F32),
            pltpu.VMEM((CH, HD), BF16),
            pltpu.SemaphoreType.DMA((3, count)),
            pltpu.SemaphoreType.DMA((3,)),
        ],
        compiler_params=limits(),
        cost_estimate=pl.CostEstimate(
            flops=4 * query_rows * lat_rows * HD,
            bytes_accessed=2 * (query_rows * 2 + lat_rows * 2) * HD,
            transcendentals=query_rows * lat_rows,
        ),
    )(place, *received, scales, shifts, proj, *before)


def total_kernel(copies, *refs):
    out_ref = refs[-1]
    if len(refs) == 2:
        parts = [refs[0][i].astype(F32) for i in range(refs[0].shape[0])]
    else:
        parts = [ref[...].astype(F32) for ref in refs[:-1]]
    while len(parts) > 1:
        parts = [parts[i] + parts[i + 1] for i in range(0, len(parts), 2)]
    for copy in range(copies):
        out_ref[copy] = parts[0].astype(BF16)


def total_copies(arrays, copies):
    return pl.pallas_call(
        functools.partial(total_kernel, copies),
        out_shape=jax.ShapeDtypeStruct((copies,) + arrays[0].shape[-2:], BF16),
        in_specs=[VMEM_SPEC] * len(arrays),
        out_specs=VMEM_SPEC,
        compiler_params=limits(),
    )(*arrays)


def lane_mean(x, count):
    return jnp.sum(x, axis=-1, keepdims=True) * (1.0 / count)


def head_kernel(grid_rows, heads, fused, embed_masks, out_factor, place_ref, lat_ref, *refs):
    embed_refs, refs = refs[: len(embed_masks)], refs[len(embed_masks) :]
    sides, refs = refs[:4], refs[4:]
    cot_ref, refs = refs[0], refs[1:]
    mod_refs, refs = refs[:heads], refs[heads:]
    reward_ref, grad_ref, weight_ref, lat_scr, grad_scr, embed_ref, *refs = refs
    pos_ref, pre_ref, post_ref, prompt_ref, sems, side_sems = refs
    patch_rows = grid_rows // 4
    patch_cols = GW // 4
    patches = patch_rows * patch_cols
    copies = []
    for slot, mask in enumerate(embed_masks):
        rows = embed_refs[slot].shape[0]
        first = pl.multiple_of(jnp.bitwise_xor(place_ref[1], mask) * rows, rows)
        copies.append(
            pltpu.make_async_copy(embed_refs[slot], embed_ref.at[pl.ds(first, rows)], sems.at[slot])
        )
    for slot, (side, scr) in enumerate(zip(sides, (pos_ref, pre_ref, post_ref, prompt_ref))):
        copies.append(pltpu.make_async_copy(side, scr, side_sems.at[slot]))
    for copy in copies:
        copy.start()
    lat_scr[...] = lat_ref[...].astype(F32)

    def position_rows(ty):
        return embed_ref[pl.ds(4 * ty * CH, 4 * CH), :]

    blocks = []
    for hi in range(2):
        wide = []
        for tx in range(4):
            rows = [
                lat_scr[pl.ds((2 * pr + hi) * GW + tx, patch_cols, stride=4), :]
                for pr in range(patch_rows)
            ]
            wide.append(jnp.concatenate(rows, axis=0))
        for side in range(2):
            lanes = slice(side * CH, (side + 1) * CH)
            blocks.append(jnp.concatenate([x[:, lanes] for x in wide], axis=1).astype(BF16))
    for copy in copies:
        copy.wait()
    embedded = pos_ref[...].astype(F32)
    for ty in range(4):
        embedded = embedded + mm(blocks[ty], position_rows(ty))
    pre = pre_ref[...].reshape(1, VW)
    post = post_ref[...].reshape(1, VW)
    prompt = prompt_ref[...]
    center = embedded - lane_mean(embedded, VW)
    rstd = lax.rsqrt(lane_mean(center * center, VW) + EPS)
    unit = center * rstd
    pooled = jnp.sum(unit, axis=0, keepdims=True) * (1.0 / patches) * pre
    pooled_center = pooled - lane_mean(pooled, VW)
    pooled_rstd = lax.rsqrt(lane_mean(pooled_center * pooled_center, VW) + EPS)
    pooled_unit = pooled_center * pooled_rstd
    final = pooled_unit * post
    dot = jnp.sum(final * prompt, axis=-1, keepdims=True)
    final_sq = jnp.sum(final * final, axis=-1, keepdims=True)
    prompt_sq = jnp.sum(prompt * prompt, axis=-1, keepdims=True)
    final_len = jnp.sqrt(final_sq)
    prompt_len = jnp.sqrt(prompt_sq)
    cosine = dot / (final_len * prompt_len)
    reward_ref[...] = jnp.broadcast_to(100.0 * cosine, reward_ref.shape)
    cot = cot_ref[0]
    final_grad = (100.0 * cot) * (prompt / (final_len * prompt_len) - final * (cosine / final_sq))
    unit_grad = final_grad * post
    pooled_grad = pooled_rstd * (
        unit_grad
        - lane_mean(unit_grad, VW)
        - pooled_unit * lane_mean(unit_grad * pooled_unit, VW)
    )
    flow = pooled_grad * pre * (1.0 / patches)
    embed_grad = rstd * (flow - lane_mean(flow, VW) - unit * lane_mean(flow * unit, VW))
    high = embed_grad.astype(BF16)
    low = (embed_grad - high.astype(F32)).astype(BF16)
    stacked = jnp.concatenate([high, low], axis=0)
    for hi in range(2):
        sides = []
        for side in range(2):
            both = mm_nt(stacked, position_rows(2 * hi + side))
            sides.append(both[:patches] + both[patches:])
        for tx in range(4):
            lanes = slice(tx * CH, (tx + 1) * CH)
            piece = jnp.concatenate([sides[0][:, lanes], sides[1][:, lanes]], axis=1)
            for pr in range(patch_rows):
                grad_scr[pl.ds((2 * pr + hi) * GW + tx, patch_cols, stride=4), :] = piece[
                    pr * patch_cols : (pr + 1) * patch_cols
                ]
    grad = grad_scr[...].astype(BF16)
    grad_ref[...] = grad
    if fused:
        store_readout_grad(grad, mod_refs, out_factor, weight_ref)
    else:
        weight_ref[...] = jnp.zeros_like(weight_ref)


def store_readout_grad(grad, mod_refs, out_factor, out_ref):
    for head, mod_ref in enumerate(mod_refs):
        count, rows, width = mod_ref.shape
        half = rows // 2
        first = mod_ref[:, :half, :].reshape(count * half, width)
        second = mod_ref[:, half:, :].reshape(count * half, width)
        total = mm_tn(grad, first)[:CH] + mm_tn(grad, second)[CH:]
        out_ref[:, pl.ds(head * width, width)] = (total * out_factor).astype(BF16)


def reward_head(
    place, latent, embed, pos, pre, post, prompt, cot, modulated, grid_rows, fused, out_factor
):
    patches = grid_rows * GW // 16
    rows = grid_rows * GW // 2
    width = HD * len(modulated)
    embed_arrays, embed_masks = [x for x, _ in embed], [mask for _, mask in embed]
    return pl.pallas_call(
        functools.partial(
            head_kernel, grid_rows, len(modulated), fused, embed_masks, out_factor
        ),
        out_shape=(
            jax.ShapeDtypeStruct((1, 128), F32),
            jax.ShapeDtypeStruct((rows, 2 * CH), BF16),
            jax.ShapeDtypeStruct((CH, width), BF16),
        ),
        in_specs=[SMEM_SPEC, VMEM_SPEC]
        + [ANY_SPEC] * len(embed_arrays)
        + [HBM_SPEC] * 4
        + [SMEM_SPEC]
        + [VMEM_SPEC] * len(modulated),
        out_specs=(VMEM_SPEC, VMEM_SPEC, VMEM_SPEC),
        scratch_shapes=[
            pltpu.VMEM((rows, 2 * CH), F32),
            pltpu.VMEM((rows, 2 * CH), F32),
            pltpu.VMEM((16 * CH, VW), BF16),
            pltpu.VMEM((patches, VW), BF16),
            pltpu.VMEM((VW,), F32),
            pltpu.VMEM((VW,), F32),
            pltpu.VMEM((1, VW), F32),
            pltpu.SemaphoreType.DMA((len(embed_arrays),)),
            pltpu.SemaphoreType.DMA((4,)),
        ],
        compiler_params=limits(),
        cost_estimate=pl.CostEstimate(
            flops=6 * patches * 16 * CH * VW,
            bytes_accessed=2 * 16 * CH * VW + 2 * patches * VW,
            transcendentals=0,
        ),
    )(place, latent, *embed_arrays, pos, pre, post, prompt, cot, *modulated)


def spread_kernel(
    count, half, heads, place_ref, grad_ref, scale_ref, proj_ref, out_ref, scale_scr, proj_scr, sems
):
    width = heads * HD
    mine = pl.ds(pl.multiple_of(place_ref[2] * width, HD), width)
    copies = [
        pltpu.make_async_copy(scale_ref.at[:, mine], scale_scr, sems.at[0]),
        pltpu.make_async_copy(proj_ref.at[:, mine], proj_scr, sems.at[1]),
    ]
    for copy in copies:
        copy.start()
    for copy in copies:
        copy.wait()
    gain = 1.0 + scale_scr[...]
    proj = proj_scr[...]
    zero = jnp.zeros_like(proj)
    sides = (jnp.concatenate([proj, zero], axis=0), jnp.concatenate([zero, proj], axis=0))
    for src in range(count):
        grad = grad_ref[pl.ds(src * half, half), :]
        for side in range(2):
            rows = (mm(grad, sides[side]) * gain).astype(BF16)
            for head in range(heads):
                out_ref[0, head, pl.ds((2 * src + side) * half, half), :] = rows[
                    :, head * HD : (head + 1) * HD
                ]


def spread(place, grad, scales, proj, count, half, heads):
    return pl.pallas_call(
        functools.partial(spread_kernel, count, half, heads),
        out_shape=jax.ShapeDtypeStruct((1, heads, 2 * count * half, HD), BF16),
        in_specs=[SMEM_SPEC, VMEM_SPEC, HBM_SPEC, HBM_SPEC],
        out_specs=VMEM_SPEC,
        scratch_shapes=[
            pltpu.VMEM((1, heads * HD), F32),
            pltpu.VMEM((CH, heads * HD), BF16),
            pltpu.SemaphoreType.DMA((2,)),
        ],
        compiler_params=limits(),
        cost_estimate=pl.CostEstimate(
            flops=8 * count * half * CH * heads * HD,
            bytes_accessed=4 * count * half * heads * HD,
            transcendentals=0,
        ),
    )(place, grad, scales, proj)


def weight_kernel(out_factor, grad_ref, *refs):
    store_readout_grad(grad_ref[...], refs[:-1], out_factor, refs[-1])


def weight_call(grad, modulated, out_factor):
    return pl.pallas_call(
        functools.partial(weight_kernel, out_factor),
        out_shape=jax.ShapeDtypeStruct((CH, HD * len(modulated)), BF16),
        in_specs=[VMEM_SPEC] * (1 + len(modulated)),
        out_specs=VMEM_SPEC,
        compiler_params=limits(),
    )(grad, *modulated)


def finish_kernel(in_ref, out_ref):
    count, _, width = in_ref.shape
    for group in range(count):
        out_ref[:, pl.ds(group * width, width)] = in_ref[group].astype(F32)


def finish(blocks):
    return pl.pallas_call(
        finish_kernel,
        out_shape=jax.ShapeDtypeStruct((CH, HEADS * HD), F32),
        in_specs=[VMEM_SPEC],
        out_specs=VMEM_SPEC,
        compiler_params=limits(),
    )(blocks)


def swap(x, axis, mask):
    count = lax.axis_size(axis)
    return lax.ppermute(x, axis, [(i, i ^ mask) for i in range(count)])


def all_to_all(x, groups=None):
    return lax.all_to_all(
        x, "seq", split_axis=0, concat_axis=0, tiled=True, axis_index_groups=groups
    )


def after_kernel(*refs):
    del refs


def after(x, others):
    return pl.pallas_call(
        after_kernel,
        out_shape=jax.ShapeDtypeStruct(x.shape, x.dtype),
        in_specs=[ANY_SPEC] * (1 + len(others)),
        out_specs=ANY_SPEC,
        input_output_aliases={0: 0},
    )(x, *others)


def on_device(
    queries,
    keys,
    values,
    shifts,
    scales,
    proj_out,
    patch_embed,
    pos_embed,
    pre_gain,
    post_gain,
    prompt,
    cotangent,
):
    seq_count = lax.axis_size("seq")
    data_count = lax.axis_size("dp")
    tok_rows = queries.shape[1]
    sizes = Sizes(seq_count, data_count, tok_rows, patch_embed)
    query_parts, head_count, part_rows = sizes.query_parts, sizes.heads, sizes.part_rows
    group_count = HEADS // head_count
    seq_index = lax.axis_index("seq")
    head_group = seq_index // query_parts
    query_part = seq_index % query_parts
    half = part_rows // 2
    lat_rows = seq_count * tok_rows
    grid_rows = lat_rows // GW
    canonical = part_rows == 2 * GW
    place = jnp.stack([seq_index, lax.axis_index("dp"), head_group]).astype(jnp.int32)
    proj_turned = proj_out.T
    out_factor = 1.0 / math.sqrt(data_count * lat_rows)

    pieces = sizes.pieces()
    packed = pack(
        sizes, place, in_hbm(queries), in_hbm(keys), in_hbm(values), in_hbm(patch_embed)
    )
    received = [swap(x, "seq", piece[0]) if piece[0] else x for piece, x in zip(pieces, packed)]
    bits = [1 << b for b in reversed(range(data_count.bit_length() - 1))]
    shared = sizes.share < patch_embed.shape[0]

    modulated, latent_part = [], []
    for head in range(head_count):
        slots = [slot for slot, piece in enumerate(pieces) if head in piece[1]]
        if head == head_count - 1 and sizes.riding:
            even = [slot for slot, piece in enumerate(pieces) if sizes.rides(piece)]
            rest = [x for slot, x in enumerate(received) if slot not in even]
            held = collect(
                sizes, [pieces[slot] for slot in even], [received[slot] for slot in even],
                rest + modulated,
            )
            got = swap(held, "seq", 1)
            far_held = swap(held, "dp", bits[0]) if shared else None
        mod, latent_sum = attend(
            sizes, head, place, [pieces[slot] for slot in slots], [received[slot] for slot in slots],
            in_hbm(scales), in_hbm(shifts), in_hbm(proj_turned), latent_part,
        )
        modulated, latent_part = modulated + [mod], [latent_sum]
    latent_part = latent_part[0]

    if sizes.riding:
        got = after(got, [modulated[-1]])
        even_masks = [pieces[slot][0] for slot in even]
        embed = [(arrange(sizes, even_masks, place, held, got, modulated[-1]), 0)]
        far_got = swap(got, "dp", bits[0]) if shared else None
    else:
        mine = patch_embed
        if shared:
            mine = lax.dynamic_slice_in_dim(
                patch_embed, lax.axis_index("dp") * sizes.share, sizes.share, 0
            )
        mine = lax.all_gather(mine, "seq", axis=1, tiled=True).reshape(-1, VW)
        embed = [(mine, 0)]
        if shared:
            embed = embed + [(swap(mine, "dp", bits[0]), bits[0])]

    groups = None
    if query_parts > 1:
        groups = [[g * query_parts + r for g in range(group_count)] for r in range(query_parts)]
    per_share = seq_count // group_count
    parts = all_to_all(latent_part.reshape(group_count, per_share * half, 2 * CH), groups)
    if sizes.riding and shared:
        embed.append((arrange(sizes, even_masks, place, far_held, far_got, parts), bits[0]))
    for bit in bits[1:] if shared else []:
        embed = embed + [(swap(x, "dp", bit), m ^ bit) for x, m in embed]
    latent = all_to_all(total_copies([parts], seq_count))
    if canonical:
        latent = latent.reshape(lat_rows // 2, 2 * CH)
    else:
        latent = latent.reshape(group_count, query_parts, per_share, half, 2, CH)
        latent = latent.transpose(0, 2, 1, 4, 3, 5).reshape(grid_rows // 2, 2, GW, CH)
        latent = latent.transpose(0, 2, 1, 3).reshape(lat_rows // 2, 2 * CH)

    reward, grad, weight = reward_head(
        place, latent, embed, in_hbm(pos_embed), in_hbm(pre_gain), in_hbm(post_gain), in_hbm(prompt),
        cotangent, modulated, grid_rows, canonical, out_factor,
    )
    if not canonical:
        tokens = grad.reshape(grid_rows // 2, GW, 2, CH).transpose(0, 2, 1, 3)
        tokens = tokens.reshape(seq_count, query_parts, 2, half, CH)
        tokens = lax.dynamic_index_in_dim(tokens, query_part, 1, keepdims=False)
        grad = tokens.transpose(0, 2, 1, 3).reshape(seq_count * half, 2 * CH)
        weight = weight_call(grad, modulated, out_factor)

    parts = [weight] + [swap(weight, "dp", mask) for mask in range(1, data_count)]
    attn_grad = spread(place, grad, in_hbm(scales), in_hbm(proj_turned), seq_count, half, head_count)
    if query_parts > 1:
        total = total_copies(parts, 1)[0]
        parts = [total] + [swap(total, "seq", mask) for mask in range(1, query_parts)]
    blocks = all_to_all(total_copies(parts, group_count), groups)
    return (reward[0, :1], attn_grad, finish(blocks).T)


def solution(mesh):
    return jax.shard_map(
        on_device,
        mesh=mesh,
        in_specs=(
            P("dp", "seq", None),
            P("dp", "seq", None),
            P("dp", "seq", None),
            P("dp", None),
            P("dp", None),
            P(),
            P(None, "seq", None),
            P(),
            P(),
            P(),
            P("dp", None),
            P("dp"),
        ),
        out_specs=(P("dp"), P("dp", "seq", None, None), P()),
        check_vma=False,
    )
```

```python
import functools
import math

import jax
import jax.numpy as jnp
from jax import lax
from jax.experimental import pallas as pl
from jax.experimental.pallas import tpu as pltpu
from jax.sharding import PartitionSpec as P

HEADS = 16
HD = 128
CH = 64
GW = 64
VW = 1280
EPS = 1e-05
BF16 = jnp.bfloat16
F32 = jnp.float32
VMEM_LIMIT = 20 * 1024 * 1024


def mm(a, b):
    return jnp.dot(a, b, preferred_element_type=F32)


def mm_nt(a, b):
    return lax.dot_general(a, b, (((1,), (1,)), ((), ())), preferred_element_type=F32)


def mm_tn(a, b):
    return lax.dot_general(a, b, (((0,), (0,)), ((), ())), preferred_element_type=F32)


SMEM_SPEC = pl.BlockSpec(memory_space=pltpu.SMEM)
VMEM_SPEC = pl.BlockSpec(memory_space=pltpu.VMEM)
HBM_SPEC = pl.BlockSpec(memory_space=pltpu.HBM)
ANY_SPEC = pl.BlockSpec(memory_space=pl.ANY)


def in_hbm(x):
    return pltpu.with_memory_space_constraint(x, pltpu.HBM)


def limits():
    return pltpu.CompilerParams(vmem_limit_bytes=VMEM_LIMIT)


class Sizes:
    def __init__(self, seq_count, data_count, tok_rows, patch_embed):
        self.count = seq_count
        self.query_parts = max(1, seq_count // HEADS)
        self.heads = max(1, HEADS // seq_count)
        self.width = self.heads * HD
        self.tok_rows = tok_rows
        self.part_rows = tok_rows // self.query_parts
        positions, self.local, _ = patch_embed.shape
        self.share = positions // data_count if positions % data_count == 0 else positions
        self.rows = self.part_rows + 2 * tok_rows
        self.share_rows = self.share * self.local
        self.chunks = VW // HD
        self.riding = self.local % 8 == 0 and self.share_rows % 16 == 0 and seq_count == 8
        self.ride_rows = self.chunks * self.share_rows if self.riding else 0

    def pieces(self):
        middle = self.count // 2
        far, near = range(self.count - 1, middle - 1, -1), range(1, middle)
        every = tuple(range(self.heads))
        listed = [(mask, (0,)) for mask in far] + [(mask, every) for mask in near]
        for head in every[1:]:
            listed += [(mask, (head,)) for mask in far]
        return listed + [(0, every)]

    def rides(self, piece):
        return self.riding and piece[0] in (0, 4) and 0 in piece[1]

    def piece_shape(self, piece):
        wide = len(piece[1])
        return (self.rows + (self.ride_rows // wide if self.rides(piece) else 0), wide * HD)

    def ride_slices(self, piece):
        wide = len(piece[1])
        deep = self.ride_rows // wide
        return [
            (pl.ds(self.rows, deep), pl.ds(at * HD, HD), pl.ds(at * deep, deep)) for at in range(wide)
        ]


def pack_kernel(sizes, place_ref, q_ref, k_ref, v_ref, embed_ref, *refs):
    pieces = sizes.pieces()
    out_refs = refs[: len(pieces)]
    q_scr, k_scr, v_scr, embed_scr, share_scr, in_sems, out_sems = refs[len(pieces) :]
    me = place_ref[0]
    tok_rows, part_rows, width = sizes.tok_rows, sizes.part_rows, sizes.width
    share = pl.ds(place_ref[1] * sizes.share, sizes.share)
    loads = [
        pltpu.make_async_copy(embed_ref.at[share], embed_scr, in_sems.at[3]),
        pltpu.make_async_copy(q_ref.at[0], q_scr, in_sems.at[0]),
        pltpu.make_async_copy(k_ref.at[0], k_scr, in_sems.at[1]),
        pltpu.make_async_copy(v_ref.at[0], v_scr, in_sems.at[2]),
    ]
    for load in loads:
        load.start()
    stores = []
    sent = [[], [], [], []]
    for slot, (piece, out) in enumerate(zip(pieces, out_refs)):
        mask, some = piece
        dest = jnp.bitwise_xor(me, mask)
        group, part = dest // sizes.query_parts, dest % sizes.query_parts
        cols = pl.ds(pl.multiple_of(group * width + some[0] * HD, HD), len(some) * HD)
        first = pl.ds(pl.multiple_of(part * part_rows, part_rows), part_rows)
        for kind, source, rows in (
            (0, q_scr.at[first, cols], pl.ds(0, part_rows)),
            (1, k_scr.at[:, cols], pl.ds(part_rows, tok_rows)),
            (2, v_scr.at[:, cols], pl.ds(part_rows + tok_rows, tok_rows)),
        ):
            sent[kind].append(pltpu.make_async_copy(source, out.at[rows], out_sems.at[kind, slot]))
        if sizes.rides(piece):
            for at, (rows, place, from_rows) in enumerate(sizes.ride_slices(piece)):
                sent[3].append(
                    pltpu.make_async_copy(
                        share_scr.at[from_rows], out.at[rows, place], out_sems.at[3 + at, slot]
                    )
                )
    loads[0].wait()
    if sizes.riding:
        for chunk in range(sizes.chunks):
            cols = embed_scr[:, :, pl.ds(chunk * HD, HD)].astype(F32)
            share_scr[pl.ds(chunk * sizes.share_rows, sizes.share_rows), :] = cols.reshape(
                sizes.share_rows, HD
            ).astype(BF16)
    for store in sent[3]:
        store.start()
    for kind in range(3):
        loads[kind + 1].wait()
        for store in sent[kind]:
            store.start()
    for stores in sent:
        for store in stores:
            store.wait()


def pack(sizes, place, queries, keys, values, patch_embed):
    tok_rows, full = queries.shape[1:]
    pieces = sizes.pieces()
    return pl.pallas_call(
        functools.partial(pack_kernel, sizes),
        out_shape=[jax.ShapeDtypeStruct(sizes.piece_shape(piece), BF16) for piece in pieces],
        in_specs=[SMEM_SPEC] + [HBM_SPEC] * 4,
        out_specs=[HBM_SPEC] * len(pieces),
        scratch_shapes=[pltpu.VMEM((tok_rows, full), BF16)] * 3
        + [
            pltpu.VMEM((sizes.share,) + patch_embed.shape[1:], BF16),
            pltpu.VMEM((max(16, sizes.ride_rows), HD), BF16),
            pltpu.SemaphoreType.DMA((4,)),
            pltpu.SemaphoreType.DMA((3 + sizes.heads, len(pieces))),
        ],
        compiler_params=limits(),
        cost_estimate=pl.CostEstimate(
            flops=0, bytes_accessed=12 * tok_rows * full, transcendentals=0
        ),
    )(place, queries, keys, values, patch_embed)


def collect_kernel(sizes, pieces, *refs):
    in_refs, out_ref, sems = refs[: len(pieces)], refs[-2], refs[-1]
    copies = []
    for slot, (piece, ref) in enumerate(zip(pieces, in_refs)):
        for at, (rows, cols, to_rows) in enumerate(sizes.ride_slices(piece)):
            copies.append(
                pltpu.make_async_copy(
                    ref.at[rows, cols], out_ref.at[slot, to_rows], sems.at[at, slot]
                )
            )
    for copy in copies:
        copy.start()
    for copy in copies:
        copy.wait()


def collect(sizes, pieces, arrays, others):
    return pl.pallas_call(
        functools.partial(collect_kernel, sizes, pieces),
        out_shape=jax.ShapeDtypeStruct((len(pieces), sizes.ride_rows, HD), BF16),
        in_specs=[ANY_SPEC] * (len(arrays) + len(others)),
        out_specs=VMEM_SPEC,
        scratch_shapes=[pltpu.SemaphoreType.DMA((sizes.heads, len(pieces)))],
        compiler_params=limits(),
    )(*arrays, *others)


def join_kernel(first_ref, second_ref, *refs):
    out_ref = refs[-1]
    count = first_ref.shape[0]
    out_ref[:count] = first_ref[...]
    out_ref[count:] = second_ref[...]


def join(first, second, others):
    return pl.pallas_call(
        join_kernel,
        out_shape=jax.ShapeDtypeStruct((2 * first.shape[0],) + first.shape[1:], BF16),
        in_specs=[VMEM_SPEC] * 2 + [ANY_SPEC] * len(others),
        out_specs=VMEM_SPEC,
        compiler_params=limits(),
    )(first, second, *others)


def arrange_kernel(sizes, masks, place_ref, held_ref, got_ref, wait_ref, out_ref):
    del wait_ref
    me = place_ref[0]
    odd = me % 2 == 1
    local, width = sizes.local, HD
    for slot, mask in enumerate(masks):
        pair = jnp.bitwise_xor(me, mask) // 2
        for chunk in range(sizes.chunks):
            rows = pl.ds(chunk * sizes.share_rows, sizes.share_rows)
            held = held_ref[slot, rows, :].astype(F32)
            got = got_ref[slot, rows, :].astype(F32)
            first = jnp.where(odd, got, held)
            second = jnp.where(odd, held, got)
            for at in range(sizes.share):
                part = slice(at * local, (at + 1) * local)
                both = jnp.concatenate([first[part], second[part]], axis=0).astype(BF16)
                start = pl.multiple_of(at * sizes.count * local + pair * 2 * local, 2 * local)
                out_ref[pl.ds(start, 2 * local), pl.ds(chunk * width, width)] = both


def arrange(sizes, masks, place, held, got, wait):
    rows = sizes.share * sizes.count * sizes.local
    return pl.pallas_call(
        functools.partial(arrange_kernel, sizes, masks),
        out_shape=jax.ShapeDtypeStruct((rows, VW), BF16),
        in_specs=[SMEM_SPEC, VMEM_SPEC, VMEM_SPEC, VMEM_SPEC],
        out_specs=VMEM_SPEC,
        compiler_params=limits(),
    )(place, held, got, wait)


def attend_kernel(sizes, head, pieces, place_ref, *refs):
    count, width = sizes.count, sizes.width
    tok_rows, part_rows = sizes.tok_rows, sizes.part_rows
    in_refs, refs = refs[:count], refs[count:]
    scale_ref, shift_ref, proj_ref, *refs = refs
    before_ref = None
    if head:
        before_ref, *refs = refs
    mod_ref, lat_ref, query_scr, key_scr, turned_scr, value_scr, *refs = refs
    scale_scr, shift_scr, proj_scr, sems, side_sems = refs
    half = part_rows // 2
    lat_rows = count * tok_rows
    factor = HD ** (-0.5)
    me = place_ref[0]
    mine = pl.ds(pl.multiple_of(place_ref[2] * width + head * HD, HD), HD)
    copies = []
    for src, (piece, ref) in enumerate(zip(pieces, in_refs)):
        cols = pl.ds(piece[1].index(head) * HD, HD)
        for kind, start, rows, scr in (
            (0, 0, part_rows, query_scr),
            (1, part_rows, tok_rows, key_scr),
            (2, part_rows + tok_rows, tok_rows, value_scr),
        ):
            to = scr.at[pl.ds(src * rows, rows)]
            if kind == 2:
                to = scr.at[pl.ds(src * rows, rows), pl.ds(0, HD)]
            copies.append(
                pltpu.make_async_copy(ref.at[pl.ds(start, rows), cols], to, sems.at[kind, src])
            )
    copies += [
        pltpu.make_async_copy(scale_ref.at[:, mine], scale_scr, side_sems.at[0]),
        pltpu.make_async_copy(shift_ref.at[:, mine], shift_scr, side_sems.at[1]),
        pltpu.make_async_copy(proj_ref.at[:, mine], proj_scr, side_sems.at[2]),
    ]
    for copy in copies:
        copy.start()
    value_scr[:, pl.ds(HD, HD)] = jnp.ones((lat_rows, HD), BF16)
    for copy in copies:
        copy.wait()
    gain = 1.0 + scale_scr[...]
    shift = shift_scr[...]
    turned_scr[...] = key_scr[...].astype(F32).T.astype(BF16)
    proj = proj_scr[...].astype(F32).T.astype(BF16)
    zero = jnp.zeros_like(proj)
    proj_pair = jnp.concatenate(
        [jnp.concatenate([proj, zero], axis=1), jnp.concatenate([zero, proj], axis=1)], axis=0
    )
    block = min(count * part_rows, max(part_rows, min(128, (1 << 18) // lat_rows)))
    for first in range(0, count * part_rows, block):
        logits = mm(query_scr[pl.ds(first, block), :], turned_scr[...])
        top = jnp.max(logits, axis=-1, keepdims=True)
        weights = jnp.exp((logits - top) * factor).astype(BF16)
        both = mm(weights, value_scr[...])
        modulated = (both[:, :HD] / both[:, HD:] * gain + shift).astype(BF16)
        for at in range(0, block, part_rows):
            place = jnp.bitwise_xor(me, pieces[(first + at) // part_rows][0])
            mod_ref[place] = modulated[at : at + part_rows]
            pair = jnp.concatenate(
                [modulated[at : at + half], modulated[at + half : at + part_rows]], axis=1
            )
            latent = mm(pair, proj_pair)
            if head:
                latent = latent + before_ref[place]
            lat_ref[place] = latent.astype(lat_ref.dtype)


def attend(sizes, head, place, pieces, received, scales, shifts, proj, before):
    count = sizes.count
    lat_rows = count * sizes.tok_rows
    query_rows = count * sizes.part_rows
    last = head == sizes.heads - 1
    return pl.pallas_call(
        functools.partial(attend_kernel, sizes, head, pieces),
        out_shape=(
            jax.ShapeDtypeStruct((count, sizes.part_rows, HD), BF16),
            jax.ShapeDtypeStruct((count, sizes.part_rows // 2, 2 * CH), BF16 if last else F32),
        ),
        in_specs=[SMEM_SPEC] + [ANY_SPEC] * count + [HBM_SPEC] * 3 + [VMEM_SPEC] * len(before),
        out_specs=(VMEM_SPEC, VMEM_SPEC),
        scratch_shapes=[
            pltpu.VMEM((query_rows, HD), BF16),
            pltpu.VMEM((lat_rows, HD), BF16),
            pltpu.VMEM((HD, lat_rows), BF16),
            pltpu.VMEM((lat_rows, 2 * HD), BF16),
            pltpu.VMEM((1, HD), F32),
            pltpu.VMEM((1, HD), F32),
            pltpu.VMEM((CH, HD), BF16),
            pltpu.SemaphoreType.DMA((3, count)),
            pltpu.SemaphoreType.DMA((3,)),
        ],
        compiler_params=limits(),
        cost_estimate=pl.CostEstimate(
            flops=4 * query_rows * lat_rows * HD,
            bytes_accessed=2 * (query_rows * 2 + lat_rows * 2) * HD,
            transcendentals=query_rows * lat_rows,
        ),
    )(place, *received, scales, shifts, proj, *before)


def total_kernel(copies, *refs):
    out_ref = refs[-1]
    if len(refs) == 2:
        parts = [refs[0][i].astype(F32) for i in range(refs[0].shape[0])]
    else:
        parts = [ref[...].astype(F32) for ref in refs[:-1]]
    while len(parts) > 1:
        parts = [parts[i] + parts[i + 1] for i in range(0, len(parts), 2)]
    for copy in range(copies):
        out_ref[copy] = parts[0].astype(BF16)


def total_copies(arrays, copies):
    return pl.pallas_call(
        functools.partial(total_kernel, copies),
        out_shape=jax.ShapeDtypeStruct((copies,) + arrays[0].shape[-2:], BF16),
        in_specs=[VMEM_SPEC] * len(arrays),
        out_specs=VMEM_SPEC,
        compiler_params=limits(),
    )(*arrays)


def lane_mean(x, count):
    return jnp.sum(x, axis=-1, keepdims=True) * (1.0 / count)


def head_kernel(grid_rows, heads, fused, embed_masks, out_factor, place_ref, lat_ref, *refs):
    embed_refs, refs = refs[: len(embed_masks)], refs[len(embed_masks) :]
    sides, refs = refs[:4], refs[4:]
    cot_ref, refs = refs[0], refs[1:]
    mod_refs, refs = refs[:heads], refs[heads:]
    reward_ref, grad_ref, weight_ref, lat_scr, grad_scr, embed_ref, *refs = refs
    pos_ref, pre_ref, post_ref, prompt_ref, sems, side_sems = refs
    patch_rows = grid_rows // 4
    patch_cols = GW // 4
    patches = patch_rows * patch_cols
    copies = []
    for slot, mask in enumerate(embed_masks):
        rows = embed_refs[slot].shape[0]
        first = pl.multiple_of(jnp.bitwise_xor(place_ref[1], mask) * rows, rows)
        copies.append(
            pltpu.make_async_copy(embed_refs[slot], embed_ref.at[pl.ds(first, rows)], sems.at[slot])
        )
    for slot, (side, scr) in enumerate(zip(sides, (pos_ref, pre_ref, post_ref, prompt_ref))):
        copies.append(pltpu.make_async_copy(side, scr, side_sems.at[slot]))
    for copy in copies:
        copy.start()
    lat_scr[...] = lat_ref[...].astype(F32)

    def position_rows(ty):
        return embed_ref[pl.ds(4 * ty * CH, 4 * CH), :]

    blocks = []
    for hi in range(2):
        wide = []
        for tx in range(4):
            rows = [
                lat_scr[pl.ds((2 * pr + hi) * GW + tx, patch_cols, stride=4), :]
                for pr in range(patch_rows)
            ]
            wide.append(jnp.concatenate(rows, axis=0))
        for side in range(2):
            lanes = slice(side * CH, (side + 1) * CH)
            blocks.append(jnp.concatenate([x[:, lanes] for x in wide], axis=1).astype(BF16))
    for copy in copies:
        copy.wait()
    embedded = pos_ref[...].astype(F32)
    for ty in range(4):
        embedded = embedded + mm(blocks[ty], position_rows(ty))
    pre = pre_ref[...].reshape(1, VW)
    post = post_ref[...].reshape(1, VW)
    prompt = prompt_ref[...]
    center = embedded - lane_mean(embedded, VW)
    rstd = lax.rsqrt(lane_mean(center * center, VW) + EPS)
    unit = center * rstd
    pooled = jnp.sum(unit, axis=0, keepdims=True) * (1.0 / patches) * pre
    pooled_center = pooled - lane_mean(pooled, VW)
    pooled_rstd = lax.rsqrt(lane_mean(pooled_center * pooled_center, VW) + EPS)
    pooled_unit = pooled_center * pooled_rstd
    final = pooled_unit * post
    dot = jnp.sum(final * prompt, axis=-1, keepdims=True)
    final_sq = jnp.sum(final * final, axis=-1, keepdims=True)
    prompt_sq = jnp.sum(prompt * prompt, axis=-1, keepdims=True)
    final_len = jnp.sqrt(final_sq)
    prompt_len = jnp.sqrt(prompt_sq)
    cosine = dot / (final_len * prompt_len)
    reward_ref[...] = jnp.broadcast_to(100.0 * cosine, reward_ref.shape)
    cot = cot_ref[0]
    final_grad = (100.0 * cot) * (prompt / (final_len * prompt_len) - final * (cosine / final_sq))
    unit_grad = final_grad * post
    pooled_grad = pooled_rstd * (
        unit_grad
        - lane_mean(unit_grad, VW)
        - pooled_unit * lane_mean(unit_grad * pooled_unit, VW)
    )
    flow = pooled_grad * pre * (1.0 / patches)
    embed_grad = rstd * (flow - lane_mean(flow, VW) - unit * lane_mean(flow * unit, VW))
    turned = embed_grad.T
    high = turned.astype(BF16)
    low = (turned - high.astype(F32)).astype(BF16)
    both = mm(embed_ref[...], jnp.concatenate([high, low], axis=1))
    position_grad = both[:, :patches] + both[:, patches:]
    for hi in range(2):
        for tx in range(4):
            first = ((2 * hi) * 4 + tx) * CH
            second = ((2 * hi + 1) * 4 + tx) * CH
            piece = jnp.concatenate(
                [position_grad[first : first + CH], position_grad[second : second + CH]], axis=0
            ).T
            for pr in range(patch_rows):
                grad_scr[pl.ds((2 * pr + hi) * GW + tx, patch_cols, stride=4), :] = piece[
                    pr * patch_cols : (pr + 1) * patch_cols
                ]
    grad = grad_scr[...].astype(BF16)
    grad_ref[...] = grad
    if fused:
        store_readout_grad(grad, mod_refs, out_factor, weight_ref)
    else:
        weight_ref[...] = jnp.zeros_like(weight_ref)


def store_readout_grad(grad, mod_refs, out_factor, out_ref):
    turned = grad.astype(F32).T.astype(BF16)
    for head, mod_ref in enumerate(mod_refs):
        count, rows, width = mod_ref.shape
        half = rows // 2
        first = mod_ref[:, :half, :].reshape(count * half, width)
        second = mod_ref[:, half:, :].reshape(count * half, width)
        total = mm(turned[:CH], first) + mm(turned[CH:], second)
        out_ref[:, pl.ds(head * width, width)] = (total * out_factor).astype(BF16)


def reward_head(
    place, latent, embed, pos, pre, post, prompt, cot, modulated, grid_rows, fused, out_factor
):
    patches = grid_rows * GW // 16
    rows = grid_rows * GW // 2
    width = HD * len(modulated)
    embed_arrays, embed_masks = [x for x, _ in embed], [mask for _, mask in embed]
    return pl.pallas_call(
        functools.partial(
            head_kernel, grid_rows, len(modulated), fused, embed_masks, out_factor
        ),
        out_shape=(
            jax.ShapeDtypeStruct((1, 128), F32),
            jax.ShapeDtypeStruct((rows, 2 * CH), BF16),
            jax.ShapeDtypeStruct((CH, width), BF16),
        ),
        in_specs=[SMEM_SPEC, VMEM_SPEC]
        + [ANY_SPEC] * len(embed_arrays)
        + [HBM_SPEC] * 4
        + [SMEM_SPEC]
        + [VMEM_SPEC] * len(modulated),
        out_specs=(VMEM_SPEC, VMEM_SPEC, VMEM_SPEC),
        scratch_shapes=[
            pltpu.VMEM((rows, 2 * CH), F32),
            pltpu.VMEM((rows, 2 * CH), F32),
            pltpu.VMEM((16 * CH, VW), BF16),
            pltpu.VMEM((patches, VW), BF16),
            pltpu.VMEM((VW,), F32),
            pltpu.VMEM((VW,), F32),
            pltpu.VMEM((1, VW), F32),
            pltpu.SemaphoreType.DMA((len(embed_arrays),)),
            pltpu.SemaphoreType.DMA((4,)),
        ],
        compiler_params=limits(),
        cost_estimate=pl.CostEstimate(
            flops=6 * patches * 16 * CH * VW,
            bytes_accessed=2 * 16 * CH * VW + 2 * patches * VW,
            transcendentals=0,
        ),
    )(place, latent, *embed_arrays, pos, pre, post, prompt, cot, *modulated)


def spread_kernel(
    count, half, heads, place_ref, grad_ref, scale_ref, proj_ref, out_ref, scale_scr, proj_scr, sems
):
    width = heads * HD
    mine = pl.ds(pl.multiple_of(place_ref[2] * width, HD), width)
    copies = [
        pltpu.make_async_copy(scale_ref.at[:, mine], scale_scr, sems.at[0]),
        pltpu.make_async_copy(proj_ref.at[:, mine], proj_scr, sems.at[1]),
    ]
    for copy in copies:
        copy.start()
    for copy in copies:
        copy.wait()
    gain = 1.0 + scale_scr[...]
    proj = proj_scr[...]
    zero = jnp.zeros_like(proj)
    sides = (jnp.concatenate([proj, zero], axis=0), jnp.concatenate([zero, proj], axis=0))
    for src in range(count):
        grad = grad_ref[pl.ds(src * half, half), :]
        for side in range(2):
            rows = (mm(grad, sides[side]) * gain).astype(BF16)
            for head in range(heads):
                out_ref[0, head, pl.ds((2 * src + side) * half, half), :] = rows[
                    :, head * HD : (head + 1) * HD
                ]


def spread(place, grad, scales, proj, count, half, heads):
    return pl.pallas_call(
        functools.partial(spread_kernel, count, half, heads),
        out_shape=jax.ShapeDtypeStruct((1, heads, 2 * count * half, HD), BF16),
        in_specs=[SMEM_SPEC, VMEM_SPEC, HBM_SPEC, HBM_SPEC],
        out_specs=VMEM_SPEC,
        scratch_shapes=[
            pltpu.VMEM((1, heads * HD), F32),
            pltpu.VMEM((CH, heads * HD), BF16),
            pltpu.SemaphoreType.DMA((2,)),
        ],
        compiler_params=limits(),
        cost_estimate=pl.CostEstimate(
            flops=8 * count * half * CH * heads * HD,
            bytes_accessed=4 * count * half * heads * HD,
            transcendentals=0,
        ),
    )(place, grad, scales, proj)


def weight_kernel(out_factor, grad_ref, *refs):
    store_readout_grad(grad_ref[...], refs[:-1], out_factor, refs[-1])


def weight_call(grad, modulated, out_factor):
    return pl.pallas_call(
        functools.partial(weight_kernel, out_factor),
        out_shape=jax.ShapeDtypeStruct((CH, HD * len(modulated)), BF16),
        in_specs=[VMEM_SPEC] * (1 + len(modulated)),
        out_specs=VMEM_SPEC,
        compiler_params=limits(),
    )(grad, *modulated)


def finish_kernel(in_ref, out_ref):
    count, _, width = in_ref.shape
    for group in range(count):
        out_ref[:, pl.ds(group * width, width)] = in_ref[group].astype(F32)


def finish(blocks):
    return pl.pallas_call(
        finish_kernel,
        out_shape=jax.ShapeDtypeStruct((CH, HEADS * HD), F32),
        in_specs=[VMEM_SPEC],
        out_specs=VMEM_SPEC,
        compiler_params=limits(),
    )(blocks)


def swap(x, axis, mask):
    count = lax.axis_size(axis)
    return lax.ppermute(x, axis, [(i, i ^ mask) for i in range(count)])


def all_to_all(x, groups=None):
    return lax.all_to_all(
        x, "seq", split_axis=0, concat_axis=0, tiled=True, axis_index_groups=groups
    )


def after_kernel(*refs):
    refs[-1][...] = refs[0][...]


def after(x, others):
    return pl.pallas_call(
        after_kernel,
        out_shape=jax.ShapeDtypeStruct(x.shape, x.dtype),
        in_specs=[VMEM_SPEC] * (1 + len(others)),
        out_specs=VMEM_SPEC,
    )(x, *others)


def on_device(
    queries,
    keys,
    values,
    shifts,
    scales,
    proj_out,
    patch_embed,
    pos_embed,
    pre_gain,
    post_gain,
    prompt,
    cotangent,
):
    seq_count = lax.axis_size("seq")
    data_count = lax.axis_size("dp")
    tok_rows = queries.shape[1]
    sizes = Sizes(seq_count, data_count, tok_rows, patch_embed)
    query_parts, head_count, part_rows = sizes.query_parts, sizes.heads, sizes.part_rows
    group_count = HEADS // head_count
    seq_index = lax.axis_index("seq")
    head_group = seq_index // query_parts
    query_part = seq_index % query_parts
    half = part_rows // 2
    lat_rows = seq_count * tok_rows
    grid_rows = lat_rows // GW
    canonical = part_rows == 2 * GW
    place = jnp.stack([seq_index, lax.axis_index("dp"), head_group]).astype(jnp.int32)
    proj_turned = proj_out.T
    out_factor = 1.0 / math.sqrt(data_count * lat_rows)

    pieces = sizes.pieces()
    packed = pack(
        sizes, place, in_hbm(queries), in_hbm(keys), in_hbm(values), in_hbm(patch_embed)
    )
    received = [swap(x, "seq", piece[0]) if piece[0] else x for piece, x in zip(pieces, packed)]
    bits = [1 << b for b in reversed(range(data_count.bit_length() - 1))]
    shared = sizes.share < patch_embed.shape[0]

    modulated, latent_part = [], []
    for head in range(head_count):
        slots = [slot for slot, piece in enumerate(pieces) if head in piece[1]]
        if head == 0 and sizes.riding:
            ride = [slot for slot, piece in enumerate(pieces) if sizes.rides(piece)]
            two = collect(
                sizes, [pieces[slot] for slot in ride], [received[slot] for slot in ride], []
            )
            other_two = swap(two, "seq", 2)
        if head == head_count - 1 and sizes.riding:
            rest = [received[slot] for slot in slots if slot not in ride]
            held = join(two, other_two, rest + modulated)
            got = swap(held, "seq", 1)
            far_held = swap(held, "dp", bits[0]) if shared else None
        mod, latent_sum = attend(
            sizes, head, place, [pieces[slot] for slot in slots], [received[slot] for slot in slots],
            in_hbm(scales), in_hbm(shifts), in_hbm(proj_turned), latent_part,
        )
        modulated, latent_part = modulated + [mod], [latent_sum]
    latent_part = latent_part[0]

    if sizes.riding:
        got = after(got, [modulated[-1]])
        even_masks = [pieces[slot][0] for slot in ride]
        even_masks = even_masks + [mask ^ 2 for mask in even_masks]
        embed = [(arrange(sizes, even_masks, place, held, got, modulated[-1]), 0)]
        far_got = swap(got, "dp", bits[0]) if shared else None
    else:
        mine = patch_embed
        if shared:
            mine = lax.dynamic_slice_in_dim(
                patch_embed, lax.axis_index("dp") * sizes.share, sizes.share, 0
            )
        mine = lax.all_gather(mine, "seq", axis=1, tiled=True).reshape(-1, VW)
        embed = [(mine, 0)]
        if shared:
            embed = embed + [(swap(mine, "dp", bits[0]), bits[0])]

    groups = None
    if query_parts > 1:
        groups = [[g * query_parts + r for g in range(group_count)] for r in range(query_parts)]
    per_share = seq_count // group_count
    parts = all_to_all(latent_part.reshape(group_count, per_share * half, 2 * CH), groups)
    if sizes.riding and shared:
        embed.append((arrange(sizes, even_masks, place, far_held, far_got, parts), bits[0]))
    for bit in bits[1:] if shared else []:
        embed = embed + [(swap(x, "dp", bit), m ^ bit) for x, m in embed]
    latent = all_to_all(total_copies([parts], seq_count))
    if canonical:
        latent = latent.reshape(lat_rows // 2, 2 * CH)
    else:
        latent = latent.reshape(group_count, query_parts, per_share, half, 2, CH)
        latent = latent.transpose(0, 2, 1, 4, 3, 5).reshape(grid_rows // 2, 2, GW, CH)
        latent = latent.transpose(0, 2, 1, 3).reshape(lat_rows // 2, 2 * CH)

    reward, grad, weight = reward_head(
        place, latent, embed, in_hbm(pos_embed), in_hbm(pre_gain), in_hbm(post_gain), in_hbm(prompt),
        cotangent, modulated, grid_rows, canonical, out_factor,
    )
    if not canonical:
        tokens = grad.reshape(grid_rows // 2, GW, 2, CH).transpose(0, 2, 1, 3)
        tokens = tokens.reshape(seq_count, query_parts, 2, half, CH)
        tokens = lax.dynamic_index_in_dim(tokens, query_part, 1, keepdims=False)
        grad = tokens.transpose(0, 2, 1, 3).reshape(seq_count * half, 2 * CH)
        weight = weight_call(grad, modulated, out_factor)

    parts = [weight] + [swap(weight, "dp", mask) for mask in range(1, data_count)]
    attn_grad = spread(place, grad, in_hbm(scales), in_hbm(proj_turned), seq_count, half, head_count)
    if query_parts > 1:
        total = total_copies(parts, 1)[0]
        parts = [total] + [swap(total, "seq", mask) for mask in range(1, query_parts)]
    blocks = all_to_all(total_copies(parts, group_count), groups)
    return (reward[0, :1], attn_grad, finish(blocks).T)


def solution(mesh):
    return jax.shard_map(
        on_device,
        mesh=mesh,
        in_specs=(
            P("dp", "seq", None),
            P("dp", "seq", None),
            P("dp", "seq", None),
            P("dp", None),
            P("dp", None),
            P(),
            P(None, "seq", None),
            P(),
            P(),
            P(),
            P("dp", None),
            P("dp"),
        ),
        out_specs=(P("dp"), P("dp", "seq", None, None), P()),
        check_vma=False,
    )
```

```python
import functools
import math

import jax
import jax.numpy as jnp
from jax import lax
from jax.experimental import pallas as pl
from jax.experimental.pallas import tpu as pltpu
from jax.sharding import PartitionSpec as P

HEADS = 16
HD = 128
CH = 64
GW = 64
VW = 1280
EPS = 1e-05
BF16 = jnp.bfloat16
F32 = jnp.float32


def mm(a, b):
    return jnp.dot(a, b, preferred_element_type=F32)


def mm_nt(a, b):
    return lax.dot_general(a, b, (((1,), (1,)), ((), ())), preferred_element_type=F32)


def mm_tn(a, b):
    return lax.dot_general(a, b, (((0,), (0,)), ((), ())), preferred_element_type=F32)


SMEM_SPEC = pl.BlockSpec(memory_space=pltpu.SMEM)
VMEM_SPEC = pl.BlockSpec(memory_space=pltpu.VMEM)
HBM_SPEC = pl.BlockSpec(memory_space=pltpu.HBM)
ANY_SPEC = pl.BlockSpec(memory_space=pl.ANY)


def in_hbm(x):
    return pltpu.with_memory_space_constraint(x, pltpu.HBM)


def limits(mib=4):
    return pltpu.CompilerParams(vmem_limit_bytes=mib * 1024 * 1024)


class Sizes:
    def __init__(self, seq_count, data_count, tok_rows, patch_embed):
        self.count = seq_count
        self.query_parts = max(1, seq_count // HEADS)
        self.heads = max(1, HEADS // seq_count)
        self.width = self.heads * HD
        self.tok_rows = tok_rows
        self.part_rows = tok_rows // self.query_parts
        positions, self.local, _ = patch_embed.shape
        self.share = positions // data_count if positions % data_count == 0 else positions
        self.rows = self.part_rows + 2 * tok_rows
        self.share_rows = self.share * self.local
        self.chunks = VW // HD
        self.riding = self.local % 8 == 0 and self.share_rows % 16 == 0 and seq_count == 8
        self.ride_rows = self.chunks * self.share_rows if self.riding else 0

    def pieces(self):
        return list(range(1, self.count)) + [0]

    def rides(self, mask):
        return self.riding and mask in (0, 4)

    def piece_shape(self, mask):
        return (self.rows + (self.ride_rows // self.heads if self.rides(mask) else 0), self.width)

    def ride_slices(self):
        deep = self.ride_rows // self.heads
        return [
            (pl.ds(self.rows, deep), pl.ds(at * HD, HD), pl.ds(at * deep, deep))
            for at in range(self.heads)
        ]


def pack_kernel(sizes, place_ref, q_ref, k_ref, v_ref, embed_ref, *refs):
    pieces = sizes.pieces()
    out_refs = refs[: len(pieces)]
    q_scr, k_scr, v_scr, embed_scr, share_scr, in_sems, out_sems = refs[len(pieces) :]
    me = place_ref[0]
    tok_rows, part_rows, width = sizes.tok_rows, sizes.part_rows, sizes.width
    share = pl.ds(place_ref[1] * sizes.share, sizes.share)
    loads = [
        pltpu.make_async_copy(embed_ref.at[share], embed_scr, in_sems.at[3]),
        pltpu.make_async_copy(q_ref.at[0], q_scr, in_sems.at[0]),
        pltpu.make_async_copy(k_ref.at[0], k_scr, in_sems.at[1]),
        pltpu.make_async_copy(v_ref.at[0], v_scr, in_sems.at[2]),
    ]
    for load in loads:
        load.start()
    sent = [[], [], [], []]
    for slot, (mask, out) in enumerate(zip(pieces, out_refs)):
        dest = jnp.bitwise_xor(me, mask)
        group, part = dest // sizes.query_parts, dest % sizes.query_parts
        cols = pl.ds(pl.multiple_of(group * width, HD), width)
        first = pl.ds(pl.multiple_of(part * part_rows, part_rows), part_rows)
        for kind, source, rows in (
            (0, q_scr.at[first, cols], pl.ds(0, part_rows)),
            (1, k_scr.at[:, cols], pl.ds(part_rows, tok_rows)),
            (2, v_scr.at[:, cols], pl.ds(part_rows + tok_rows, tok_rows)),
        ):
            sent[kind].append(pltpu.make_async_copy(source, out.at[rows], out_sems.at[kind, slot]))
        if sizes.rides(mask):
            for at, (rows, place, from_rows) in enumerate(sizes.ride_slices()):
                sent[3].append(
                    pltpu.make_async_copy(
                        share_scr.at[from_rows], out.at[rows, place], out_sems.at[3 + at, slot]
                    )
                )
    loads[0].wait()
    if sizes.riding:
        for chunk in range(sizes.chunks):
            cols = embed_scr[:, :, pl.ds(chunk * HD, HD)].astype(F32)
            share_scr[pl.ds(chunk * sizes.share_rows, sizes.share_rows), :] = cols.reshape(
                sizes.share_rows, HD
            ).astype(BF16)
    for store in sent[3]:
        store.start()
    for kind in range(3):
        loads[kind + 1].wait()
        for store in sent[kind]:
            store.start()
    for stores in sent:
        for store in stores:
            store.wait()


def pack(sizes, place, queries, keys, values, patch_embed):
    tok_rows, full = queries.shape[1:]
    pieces = sizes.pieces()
    return pl.pallas_call(
        functools.partial(pack_kernel, sizes),
        out_shape=[jax.ShapeDtypeStruct(sizes.piece_shape(mask), BF16) for mask in pieces],
        in_specs=[SMEM_SPEC] + [HBM_SPEC] * 4,
        out_specs=[HBM_SPEC] * len(pieces),
        scratch_shapes=[pltpu.VMEM((tok_rows, full), BF16)] * 3
        + [
            pltpu.VMEM((sizes.share,) + patch_embed.shape[1:], BF16),
            pltpu.VMEM((max(16, sizes.ride_rows), HD), BF16),
            pltpu.SemaphoreType.DMA((4,)),
            pltpu.SemaphoreType.DMA((3 + sizes.heads, len(pieces))),
        ],
        compiler_params=limits(),
        cost_estimate=pl.CostEstimate(
            flops=0, bytes_accessed=12 * tok_rows * full, transcendentals=0
        ),
    )(place, queries, keys, values, patch_embed)


def collect_kernel(sizes, *refs):
    *in_refs, out_ref, sems = refs
    copies = []
    for slot, ref in enumerate(in_refs):
        for at, (rows, cols, to_rows) in enumerate(sizes.ride_slices()):
            copies.append(
                pltpu.make_async_copy(
                    ref.at[rows, cols], out_ref.at[slot, to_rows], sems.at[at, slot]
                )
            )
    for copy in copies:
        copy.start()
    for copy in copies:
        copy.wait()


def collect(sizes, arrays):
    return pl.pallas_call(
        functools.partial(collect_kernel, sizes),
        out_shape=jax.ShapeDtypeStruct((len(arrays), sizes.ride_rows, HD), BF16),
        in_specs=[ANY_SPEC] * len(arrays),
        out_specs=VMEM_SPEC,
        scratch_shapes=[pltpu.SemaphoreType.DMA((sizes.heads, len(arrays)))],
        compiler_params=limits(),
    )(*arrays)


def join_kernel(first_ref, second_ref, *refs):
    out_ref = refs[-1]
    count = first_ref.shape[0]
    out_ref[:count] = first_ref[...]
    out_ref[count:] = second_ref[...]


def join(first, second, others):
    return pl.pallas_call(
        join_kernel,
        out_shape=jax.ShapeDtypeStruct((2 * first.shape[0],) + first.shape[1:], BF16),
        in_specs=[VMEM_SPEC] * 2 + [ANY_SPEC] * len(others),
        out_specs=VMEM_SPEC,
        compiler_params=limits(),
    )(first, second, *others)


def arrange_kernel(sizes, masks, place_ref, held_ref, got_ref, wait_ref, out_ref):
    del wait_ref
    me = place_ref[0]
    odd = me % 2 == 1
    local, width = sizes.local, HD
    for slot, mask in enumerate(masks):
        pair = jnp.bitwise_xor(me, mask) // 2
        for chunk in range(sizes.chunks):
            rows = pl.ds(chunk * sizes.share_rows, sizes.share_rows)
            held = held_ref[slot, rows, :].astype(F32)
            got = got_ref[slot, rows, :].astype(F32)
            first = jnp.where(odd, got, held)
            second = jnp.where(odd, held, got)
            for at in range(sizes.share):
                part = slice(at * local, (at + 1) * local)
                both = jnp.concatenate([first[part], second[part]], axis=0).astype(BF16)
                start = pl.multiple_of(at * sizes.count * local + pair * 2 * local, 2 * local)
                out_ref[pl.ds(start, 2 * local), pl.ds(chunk * width, width)] = both


def arrange(sizes, masks, place, held, got, wait):
    rows = sizes.share * sizes.count * sizes.local
    return pl.pallas_call(
        functools.partial(arrange_kernel, sizes, masks),
        out_shape=jax.ShapeDtypeStruct((rows, VW), BF16),
        in_specs=[SMEM_SPEC, VMEM_SPEC, VMEM_SPEC, VMEM_SPEC],
        out_specs=VMEM_SPEC,
        compiler_params=limits(),
    )(place, held, got, wait)


def attend_kernel(sizes, masks, place_ref, *refs):
    count, heads, width = sizes.count, sizes.heads, sizes.width
    tok_rows, part_rows = sizes.tok_rows, sizes.part_rows
    in_refs, refs = refs[:count], refs[count:]
    scale_ref, shift_ref, proj_ref, mod_ref, lat_ref, token_ref, *refs = refs
    query_scr, key_scr, value_scr, scale_scr, shift_scr, proj_scr, sems, side_sems = refs
    half = part_rows // 2
    factor = HD ** (-0.5) * math.log2(math.e)
    me = place_ref[0]
    mine = pl.ds(pl.multiple_of(place_ref[2] * width, HD), width)
    logit_copies, value_copies = [], []
    for src, ref in enumerate(in_refs):
        rows = pl.ds(src * tok_rows, tok_rows)
        logit_copies += [
            pltpu.make_async_copy(ref.at[pl.ds(0, part_rows)], query_scr.at[src], sems.at[0, src]),
            pltpu.make_async_copy(
                ref.at[pl.ds(part_rows, tok_rows)], key_scr.at[rows], sems.at[1, src]
            ),
        ]
        for head in range(heads):
            value_copies.append(
                pltpu.make_async_copy(
                    ref.at[pl.ds(part_rows + tok_rows, tok_rows), pl.ds(head * HD, HD)],
                    value_scr.at[rows, pl.ds(2 * head * HD, HD)],
                    sems.at[2 + head, src],
                )
            )
    value_copies += [
        pltpu.make_async_copy(scale_ref.at[:, mine], scale_scr, side_sems.at[0]),
        pltpu.make_async_copy(shift_ref.at[:, mine], shift_scr, side_sems.at[1]),
        pltpu.make_async_copy(proj_ref.at[:, mine], proj_scr, side_sems.at[2]),
    ]
    for copy in logit_copies + value_copies:
        copy.start()
    token_ref[...] = jnp.zeros_like(token_ref)
    ones = jnp.ones((count * tok_rows, HD), BF16)
    for head in range(heads):
        value_scr[:, pl.ds((2 * head + 1) * HD, HD)] = ones
    for copy in logit_copies + value_copies:
        copy.wait()
    gain = 1.0 + scale_scr[...]
    shift = shift_scr[...]
    proj = proj_scr[...]
    zero = jnp.zeros_like(proj)
    proj_pair = jnp.concatenate(
        [jnp.concatenate([proj, zero], axis=1), jnp.concatenate([zero, proj], axis=1)], axis=0
    )
    together = 2
    for first in range(0, count, together):
        results = []
        for src in range(first, first + together):
            mixed = []
            for head in range(heads):
                cols = pl.ds(head * HD, HD)
                logits = mm_nt(query_scr[src, :, cols], key_scr[:, cols])
                top = jnp.max(logits, axis=-1, keepdims=True)
                weights = jnp.exp2((logits - top) * factor).astype(BF16)
                both = mm(weights, value_scr[:, pl.ds(2 * head * HD, 2 * HD)])
                mixed.append(both[:, :HD] / both[:, HD:])
            attended = jnp.concatenate(mixed, axis=1) if heads > 1 else mixed[0]
            modulated = (attended * gain + shift).astype(BF16)
            pair = jnp.concatenate([modulated[:half], modulated[half:]], axis=1)
            results.append((modulated, mm_nt(pair, proj_pair).astype(BF16)))
        for at, (modulated, latent) in enumerate(results):
            place = jnp.bitwise_xor(me, masks[first + at])
            mod_ref[place] = modulated
            lat_ref[place] = latent


def attend(sizes, masks, place, received, scales, shifts, proj):
    count, width, heads = sizes.count, sizes.width, sizes.heads
    lat_rows = count * sizes.tok_rows
    query_rows = count * sizes.part_rows
    return pl.pallas_call(
        functools.partial(attend_kernel, sizes, masks),
        out_shape=(
            jax.ShapeDtypeStruct((count, sizes.part_rows, width), BF16),
            jax.ShapeDtypeStruct((count, sizes.part_rows // 2, 2 * CH), BF16),
            jax.ShapeDtypeStruct((8, 128), F32),
        ),
        in_specs=[SMEM_SPEC] + [ANY_SPEC] * count + [HBM_SPEC] * 3,
        out_specs=(VMEM_SPEC, VMEM_SPEC, VMEM_SPEC),
        scratch_shapes=[
            pltpu.VMEM((count, sizes.part_rows, width), BF16),
            pltpu.VMEM((lat_rows, width), BF16),
            pltpu.VMEM((lat_rows, 2 * width), BF16),
            pltpu.VMEM((1, width), F32),
            pltpu.VMEM((1, width), F32),
            pltpu.VMEM((CH, width), BF16),
            pltpu.SemaphoreType.DMA((2 + heads, count)),
            pltpu.SemaphoreType.DMA((3,)),
        ],
        compiler_params=limits(16),
        cost_estimate=pl.CostEstimate(
            flops=4 * query_rows * lat_rows * width,
            bytes_accessed=2 * (query_rows * 2 + lat_rows * 2) * width,
            transcendentals=query_rows * lat_rows * heads,
        ),
    )(place, *received, scales, shifts, proj)


def total_kernel(copies, *refs):
    out_ref = refs[-1]
    if len(refs) == 2:
        parts = [refs[0][i].astype(F32) for i in range(refs[0].shape[0])]
    else:
        parts = [ref[...].astype(F32) for ref in refs[:-1]]
    while len(parts) > 1:
        parts = [parts[i] + parts[i + 1] for i in range(0, len(parts), 2)]
    for copy in range(copies):
        out_ref[copy] = parts[0].astype(BF16)


def total_copies(arrays, copies):
    return pl.pallas_call(
        functools.partial(total_kernel, copies),
        out_shape=jax.ShapeDtypeStruct((copies,) + arrays[0].shape[-2:], BF16),
        in_specs=[VMEM_SPEC] * len(arrays),
        out_specs=VMEM_SPEC,
        compiler_params=limits(),
    )(*arrays)


def lane_mean(x, count):
    return jnp.sum(x, axis=-1, keepdims=True) * (1.0 / count)


def head_kernel(grid_rows, fused, embed_masks, out_factor, place_ref, lat_ref, *refs):
    embed_refs, refs = refs[: len(embed_masks)], refs[len(embed_masks) :]
    sides, refs = refs[:4], refs[4:]
    cot_ref, refs = refs[0], refs[1:]
    mod_ref, refs = refs[0], refs[1:]
    reward_ref, grad_ref, weight_ref, lat_scr, grad_scr, embed_ref, *refs = refs
    pos_ref, pre_ref, post_ref, prompt_ref, sems, side_sems = refs
    patch_rows = grid_rows // 4
    patch_cols = GW // 4
    patches = patch_rows * patch_cols
    copies = []
    for slot, mask in enumerate(embed_masks):
        rows = embed_refs[slot].shape[0]
        first = pl.multiple_of(jnp.bitwise_xor(place_ref[1], mask) * rows, rows)
        copies.append(
            pltpu.make_async_copy(embed_refs[slot], embed_ref.at[pl.ds(first, rows)], sems.at[slot])
        )
    for slot, (side, scr) in enumerate(zip(sides, (pos_ref, pre_ref, post_ref, prompt_ref))):
        copies.append(pltpu.make_async_copy(side, scr, side_sems.at[slot]))
    for copy in copies:
        copy.start()
    lat_scr[...] = lat_ref[...].astype(F32)

    def position_rows(ty):
        return embed_ref[pl.ds(4 * ty * CH, 4 * CH), :]

    blocks = []
    for hi in range(2):
        wide = []
        for tx in range(4):
            rows = [
                lat_scr[pl.ds((2 * pr + hi) * GW + tx, patch_cols, stride=4), :]
                for pr in range(patch_rows)
            ]
            wide.append(jnp.concatenate(rows, axis=0))
        for side in range(2):
            lanes = slice(side * CH, (side + 1) * CH)
            blocks.append(jnp.concatenate([x[:, lanes] for x in wide], axis=1).astype(BF16))
    for copy in copies:
        copy.wait()
    embedded = pos_ref[...].astype(F32)
    for ty in range(4):
        embedded = embedded + mm(blocks[ty], position_rows(ty))
    pre = pre_ref[...].reshape(1, VW)
    post = post_ref[...].reshape(1, VW)
    prompt = prompt_ref[...]
    center = embedded - lane_mean(embedded, VW)
    rstd = lax.rsqrt(lane_mean(center * center, VW) + EPS)
    unit = center * rstd
    pooled = jnp.sum(unit, axis=0, keepdims=True) * (1.0 / patches) * pre
    pooled_center = pooled - lane_mean(pooled, VW)
    pooled_rstd = lax.rsqrt(lane_mean(pooled_center * pooled_center, VW) + EPS)
    pooled_unit = pooled_center * pooled_rstd
    final = pooled_unit * post
    dot = jnp.sum(final * prompt, axis=-1, keepdims=True)
    final_sq = jnp.sum(final * final, axis=-1, keepdims=True)
    prompt_sq = jnp.sum(prompt * prompt, axis=-1, keepdims=True)
    final_len = jnp.sqrt(final_sq)
    prompt_len = jnp.sqrt(prompt_sq)
    cosine = dot / (final_len * prompt_len)
    reward_ref[...] = jnp.broadcast_to(100.0 * cosine, reward_ref.shape)
    cot = cot_ref[0]
    final_grad = (100.0 * cot) * (prompt / (final_len * prompt_len) - final * (cosine / final_sq))
    unit_grad = final_grad * post
    pooled_grad = pooled_rstd * (
        unit_grad
        - lane_mean(unit_grad, VW)
        - pooled_unit * lane_mean(unit_grad * pooled_unit, VW)
    )
    flow = pooled_grad * pre * (1.0 / patches)
    embed_grad = rstd * (flow - lane_mean(flow, VW) - unit * lane_mean(flow * unit, VW))
    high = embed_grad.astype(BF16)
    low = (embed_grad - high.astype(F32)).astype(BF16)
    stacked = jnp.concatenate([high, low], axis=0)
    for hi in range(2):
        sides = []
        for side in range(2):
            both = mm_nt(stacked, position_rows(2 * hi + side))
            sides.append(both[:patches] + both[patches:])
        for tx in range(4):
            lanes = slice(tx * CH, (tx + 1) * CH)
            piece = jnp.concatenate([sides[0][:, lanes], sides[1][:, lanes]], axis=1)
            for pr in range(patch_rows):
                grad_scr[pl.ds((2 * pr + hi) * GW + tx, patch_cols, stride=4), :] = piece[
                    pr * patch_cols : (pr + 1) * patch_cols
                ]
    grad = grad_scr[...].astype(BF16)
    grad_ref[...] = grad
    if fused:
        store_readout_grad(grad, mod_ref, out_factor, weight_ref)
    else:
        weight_ref[...] = jnp.zeros_like(weight_ref)


def store_readout_grad(grad, mod_ref, out_factor, out_ref):
    turned = grad.astype(F32).T.astype(BF16)
    count, rows, width = mod_ref.shape
    half = rows // 2
    first = mod_ref[:, :half, :].reshape(count * half, width)
    second = mod_ref[:, half:, :].reshape(count * half, width)
    total = mm(turned[:CH], first) + mm(turned[CH:], second)
    out_ref[...] = (total * out_factor).astype(BF16)


def reward_head(
    place, latent, embed, pos, pre, post, prompt, cot, modulated, grid_rows, fused, out_factor
):
    patches = grid_rows * GW // 16
    rows = grid_rows * GW // 2
    width = modulated.shape[2]
    embed_arrays, embed_masks = [x for x, _ in embed], [mask for _, mask in embed]
    return pl.pallas_call(
        functools.partial(head_kernel, grid_rows, fused, embed_masks, out_factor),
        out_shape=(
            jax.ShapeDtypeStruct((1, 128), F32),
            jax.ShapeDtypeStruct((rows, 2 * CH), BF16),
            jax.ShapeDtypeStruct((CH, width), BF16),
        ),
        in_specs=[SMEM_SPEC, VMEM_SPEC]
        + [ANY_SPEC] * len(embed_arrays)
        + [HBM_SPEC] * 4
        + [SMEM_SPEC, VMEM_SPEC],
        out_specs=(VMEM_SPEC, VMEM_SPEC, VMEM_SPEC),
        scratch_shapes=[
            pltpu.VMEM((rows, 2 * CH), F32),
            pltpu.VMEM((rows, 2 * CH), F32),
            pltpu.VMEM((16 * CH, VW), BF16),
            pltpu.VMEM((patches, VW), BF16),
            pltpu.VMEM((VW,), F32),
            pltpu.VMEM((VW,), F32),
            pltpu.VMEM((1, VW), F32),
            pltpu.SemaphoreType.DMA((len(embed_arrays),)),
            pltpu.SemaphoreType.DMA((4,)),
        ],
        compiler_params=limits(16),
        cost_estimate=pl.CostEstimate(
            flops=6 * patches * 16 * CH * VW,
            bytes_accessed=2 * 16 * CH * VW + 2 * patches * VW,
            transcendentals=0,
        ),
    )(place, latent, *embed_arrays, pos, pre, post, prompt, cot, modulated)


def spread_kernel(
    count, half, heads, place_ref, grad_ref, scale_ref, proj_ref, out_ref, scale_scr, proj_scr, sems
):
    width = heads * HD
    mine = pl.ds(pl.multiple_of(place_ref[2] * width, HD), width)
    copies = [
        pltpu.make_async_copy(scale_ref.at[:, mine], scale_scr, sems.at[0]),
        pltpu.make_async_copy(proj_ref.at[:, mine], proj_scr, sems.at[1]),
    ]
    for copy in copies:
        copy.start()
    for copy in copies:
        copy.wait()
    gain = 1.0 + scale_scr[...]
    proj = proj_scr[...]
    zero = jnp.zeros_like(proj)
    sides = (jnp.concatenate([proj, zero], axis=0), jnp.concatenate([zero, proj], axis=0))
    for src in range(count):
        grad = grad_ref[pl.ds(src * half, half), :]
        for side in range(2):
            rows = (mm(grad, sides[side]) * gain).astype(BF16)
            for head in range(heads):
                out_ref[0, head, pl.ds((2 * src + side) * half, half), :] = rows[
                    :, head * HD : (head + 1) * HD
                ]


def spread(place, grad, scales, proj, count, half, heads):
    return pl.pallas_call(
        functools.partial(spread_kernel, count, half, heads),
        out_shape=jax.ShapeDtypeStruct((1, heads, 2 * count * half, HD), BF16),
        in_specs=[SMEM_SPEC, VMEM_SPEC, HBM_SPEC, HBM_SPEC],
        out_specs=VMEM_SPEC,
        scratch_shapes=[
            pltpu.VMEM((1, heads * HD), F32),
            pltpu.VMEM((CH, heads * HD), BF16),
            pltpu.SemaphoreType.DMA((2,)),
        ],
        compiler_params=limits(),
        cost_estimate=pl.CostEstimate(
            flops=8 * count * half * CH * heads * HD,
            bytes_accessed=4 * count * half * heads * HD,
            transcendentals=0,
        ),
    )(place, grad, scales, proj)


def weight_kernel(out_factor, grad_ref, *refs):
    store_readout_grad(grad_ref[...], refs[0], out_factor, refs[1])


def weight_call(grad, modulated, out_factor):
    return pl.pallas_call(
        functools.partial(weight_kernel, out_factor),
        out_shape=jax.ShapeDtypeStruct((CH, modulated.shape[2]), BF16),
        in_specs=[VMEM_SPEC] * 2,
        out_specs=VMEM_SPEC,
        compiler_params=limits(),
    )(grad, modulated)


def finish_kernel(in_ref, out_ref):
    count, _, width = in_ref.shape
    for group in range(count):
        out_ref[:, pl.ds(group * width, width)] = in_ref[group].astype(F32)


def finish(blocks):
    return pl.pallas_call(
        finish_kernel,
        out_shape=jax.ShapeDtypeStruct((CH, HEADS * HD), F32),
        in_specs=[VMEM_SPEC],
        out_specs=VMEM_SPEC,
        compiler_params=limits(),
    )(blocks)


def swap(x, axis, mask):
    count = lax.axis_size(axis)
    return lax.ppermute(x, axis, [(i, i ^ mask) for i in range(count)])


def all_to_all(x, groups=None):
    return lax.all_to_all(
        x, "seq", split_axis=0, concat_axis=0, tiled=True, axis_index_groups=groups
    )


def after_kernel(*refs):
    refs[-1][...] = refs[0][...]


def after(x, others):
    return pl.pallas_call(
        after_kernel,
        out_shape=jax.ShapeDtypeStruct(x.shape, x.dtype),
        in_specs=[VMEM_SPEC] * (1 + len(others)),
        out_specs=VMEM_SPEC,
    )(x, *others)


def on_device(
    queries,
    keys,
    values,
    shifts,
    scales,
    proj_out,
    patch_embed,
    pos_embed,
    pre_gain,
    post_gain,
    prompt,
    cotangent,
):
    seq_count = lax.axis_size("seq")
    data_count = lax.axis_size("dp")
    tok_rows = queries.shape[1]
    sizes = Sizes(seq_count, data_count, tok_rows, patch_embed)
    query_parts, head_count, part_rows = sizes.query_parts, sizes.heads, sizes.part_rows
    group_count = HEADS // head_count
    seq_index = lax.axis_index("seq")
    head_group = seq_index // query_parts
    query_part = seq_index % query_parts
    half = part_rows // 2
    lat_rows = seq_count * tok_rows
    grid_rows = lat_rows // GW
    canonical = part_rows == 2 * GW
    place = jnp.stack([seq_index, lax.axis_index("dp"), head_group]).astype(jnp.int32)
    proj_turned = proj_out.T
    out_factor = 1.0 / math.sqrt(data_count * lat_rows)

    masks = sizes.pieces()
    packed = pack(
        sizes, place, in_hbm(queries), in_hbm(keys), in_hbm(values), in_hbm(patch_embed)
    )
    received = [swap(x, "seq", mask) if mask else x for mask, x in zip(masks, packed)]
    bits = [1 << b for b in reversed(range(data_count.bit_length() - 1))]
    shared = sizes.share < patch_embed.shape[0]
    if sizes.riding:
        ride = [slot for slot, mask in enumerate(masks) if sizes.rides(mask)]
        two = collect(sizes, [received[slot] for slot in ride])
        held = join(two, swap(two, "seq", 2), received)
        ride_masks = [masks[slot] for slot in ride]
        ride_masks = ride_masks + [mask ^ 2 for mask in ride_masks]
        got = swap(held, "seq", 1)
        far_held = swap(held, "dp", bits[0]) if shared else None

    modulated, latent_part, token = attend(
        sizes, masks, place, received, in_hbm(scales), in_hbm(shifts), in_hbm(proj_turned)
    )

    if sizes.riding:
        got = after(got, [token])
        embed = [(arrange(sizes, ride_masks, place, held, got, token), 0)]
        far_got = swap(got, "dp", bits[0]) if shared else None
    else:
        mine = patch_embed
        if shared:
            mine = lax.dynamic_slice_in_dim(
                patch_embed, lax.axis_index("dp") * sizes.share, sizes.share, 0
            )
        mine = lax.all_gather(mine, "seq", axis=1, tiled=True).reshape(-1, VW)
        embed = [(mine, 0)]
        if shared:
            embed = embed + [(swap(mine, "dp", bits[0]), bits[0])]

    groups = None
    if query_parts > 1:
        groups = [[g * query_parts + r for g in range(group_count)] for r in range(query_parts)]
    per_share = seq_count // group_count
    parts = all_to_all(latent_part.reshape(group_count, per_share * half, 2 * CH), groups)
    if sizes.riding and shared:
        embed.append((arrange(sizes, ride_masks, place, far_held, far_got, parts), bits[0]))
    for bit in bits[1:] if shared else []:
        embed = embed + [(swap(x, "dp", bit), m ^ bit) for x, m in embed]
    latent = all_to_all(total_copies([parts], seq_count))
    if canonical:
        latent = latent.reshape(lat_rows // 2, 2 * CH)
    else:
        latent = latent.reshape(group_count, query_parts, per_share, half, 2, CH)
        latent = latent.transpose(0, 2, 1, 4, 3, 5).reshape(grid_rows // 2, 2, GW, CH)
        latent = latent.transpose(0, 2, 1, 3).reshape(lat_rows // 2, 2 * CH)

    reward, grad, weight = reward_head(
        place, latent, embed, in_hbm(pos_embed), in_hbm(pre_gain), in_hbm(post_gain), in_hbm(prompt),
        cotangent, modulated, grid_rows, canonical, out_factor,
    )
    if not canonical:
        tokens = grad.reshape(grid_rows // 2, GW, 2, CH).transpose(0, 2, 1, 3)
        tokens = tokens.reshape(seq_count, query_parts, 2, half, CH)
        tokens = lax.dynamic_index_in_dim(tokens, query_part, 1, keepdims=False)
        grad = tokens.transpose(0, 2, 1, 3).reshape(seq_count * half, 2 * CH)
        weight = weight_call(grad, modulated, out_factor)

    parts = [weight] + [swap(weight, "dp", mask) for mask in range(1, data_count)]
    attn_grad = spread(place, grad, in_hbm(scales), in_hbm(proj_turned), seq_count, half, head_count)
    if query_parts > 1:
        total = total_copies(parts, 1)[0]
        parts = [total] + [swap(total, "seq", mask) for mask in range(1, query_parts)]
    blocks = all_to_all(total_copies(parts, group_count), groups)
    return (reward[0, :1], attn_grad, finish(blocks).T)


def solution(mesh):
    return jax.shard_map(
        on_device,
        mesh=mesh,
        in_specs=(
            P("dp", "seq", None),
            P("dp", "seq", None),
            P("dp", "seq", None),
            P("dp", None),
            P("dp", None),
            P(),
            P(None, "seq", None),
            P(),
            P(),
            P(),
            P("dp", None),
            P("dp"),
        ),
        out_specs=(P("dp"), P("dp", "seq", None, None), P()),
        check_vma=False,
    )
```

```python
import functools
import math

import jax
import jax.numpy as jnp
from jax import lax
from jax.experimental import pallas as pl
from jax.experimental.pallas import tpu as pltpu
from jax.sharding import PartitionSpec as P

HEADS = 16
HD = 128
CH = 64
GW = 64
VW = 1280
EPS = 1e-05
BF16 = jnp.bfloat16
F32 = jnp.float32


def mm(a, b):
    return jnp.dot(a, b, preferred_element_type=F32)


def mm_nt(a, b):
    return lax.dot_general(a, b, (((1,), (1,)), ((), ())), preferred_element_type=F32)


def mm_tn(a, b):
    return lax.dot_general(a, b, (((0,), (0,)), ((), ())), preferred_element_type=F32)


SMEM_SPEC = pl.BlockSpec(memory_space=pltpu.SMEM)
VMEM_SPEC = pl.BlockSpec(memory_space=pltpu.VMEM)
HBM_SPEC = pl.BlockSpec(memory_space=pltpu.HBM)
ANY_SPEC = pl.BlockSpec(memory_space=pl.ANY)


def in_hbm(x):
    return pltpu.with_memory_space_constraint(x, pltpu.HBM)


def limits(mib=4):
    return pltpu.CompilerParams(vmem_limit_bytes=mib * 1024 * 1024)


class Sizes:
    def __init__(self, seq_count, data_count, tok_rows, patch_embed):
        self.count = seq_count
        self.query_parts = max(1, seq_count // HEADS)
        self.heads = max(1, HEADS // seq_count)
        self.width = self.heads * HD
        self.tok_rows = tok_rows
        self.part_rows = tok_rows // self.query_parts
        positions, self.local, _ = patch_embed.shape
        self.share = positions // data_count if positions % data_count == 0 else positions
        self.rows = self.part_rows + 2 * tok_rows
        self.share_rows = self.share * self.local
        self.chunks = VW // HD
        self.riding = self.local % 8 == 0 and self.share_rows % 16 == 0 and seq_count == 8
        self.riding = self.riding and 1 < data_count <= positions
        self.ride_rows = self.chunks * self.share_rows if self.riding else 0

    def pieces(self):
        return list(range(1, self.count)) + [0]

    def rides(self, mask):
        return self.riding and mask in (0, 4)

    def piece_shape(self, mask):
        return (self.rows + (self.ride_rows // self.heads if self.rides(mask) else 0), self.width)

    def ride_slices(self):
        deep = self.ride_rows // self.heads
        return [
            (pl.ds(self.rows, deep), pl.ds(at * HD, HD), pl.ds(at * deep, deep))
            for at in range(self.heads)
        ]


def pack_kernel(sizes, place_ref, q_ref, k_ref, v_ref, embed_ref, *refs):
    pieces = sizes.pieces()
    out_refs = refs[: len(pieces)]
    q_scr, k_scr, v_scr, embed_scr, share_scr, in_sems, out_sems = refs[len(pieces) :]
    me = place_ref[0]
    tok_rows, part_rows, width = sizes.tok_rows, sizes.part_rows, sizes.width
    share = pl.ds(place_ref[1] * sizes.share, sizes.share)
    loads = [
        pltpu.make_async_copy(embed_ref.at[share], embed_scr, in_sems.at[3]),
        pltpu.make_async_copy(q_ref.at[0], q_scr, in_sems.at[0]),
        pltpu.make_async_copy(k_ref.at[0], k_scr, in_sems.at[1]),
        pltpu.make_async_copy(v_ref.at[0], v_scr, in_sems.at[2]),
    ]
    for load in loads:
        load.start()
    sent = [[], [], [], []]
    for slot, (mask, out) in enumerate(zip(pieces, out_refs)):
        dest = jnp.bitwise_xor(me, mask)
        group, part = dest // sizes.query_parts, dest % sizes.query_parts
        cols = pl.ds(pl.multiple_of(group * width, HD), width)
        first = pl.ds(pl.multiple_of(part * part_rows, part_rows), part_rows)
        for kind, source, rows in (
            (0, q_scr.at[first, cols], pl.ds(0, part_rows)),
            (1, k_scr.at[:, cols], pl.ds(part_rows, tok_rows)),
            (2, v_scr.at[:, cols], pl.ds(part_rows + tok_rows, tok_rows)),
        ):
            sent[kind].append(pltpu.make_async_copy(source, out.at[rows], out_sems.at[kind, slot]))
        if sizes.rides(mask):
            for at, (rows, place, from_rows) in enumerate(sizes.ride_slices()):
                sent[3].append(
                    pltpu.make_async_copy(
                        share_scr.at[from_rows], out.at[rows, place], out_sems.at[3 + at, slot]
                    )
                )
    loads[0].wait()
    if sizes.riding:
        for chunk in range(sizes.chunks):
            cols = embed_scr[:, :, pl.ds(chunk * HD, HD)].astype(F32)
            share_scr[pl.ds(chunk * sizes.share_rows, sizes.share_rows), :] = cols.reshape(
                sizes.share_rows, HD
            ).astype(BF16)
    for store in sent[3]:
        store.start()
    for kind in range(3):
        loads[kind + 1].wait()
        for store in sent[kind]:
            store.start()
    for stores in sent:
        for store in stores:
            store.wait()


def pack(sizes, place, queries, keys, values, patch_embed):
    tok_rows, full = queries.shape[1:]
    pieces = sizes.pieces()
    return pl.pallas_call(
        functools.partial(pack_kernel, sizes),
        out_shape=[jax.ShapeDtypeStruct(sizes.piece_shape(mask), BF16) for mask in pieces],
        in_specs=[SMEM_SPEC] + [HBM_SPEC] * 4,
        out_specs=[HBM_SPEC] * len(pieces),
        scratch_shapes=[pltpu.VMEM((tok_rows, full), BF16)] * 3
        + [
            pltpu.VMEM((sizes.share,) + patch_embed.shape[1:], BF16),
            pltpu.VMEM((max(16, sizes.ride_rows), HD), BF16),
            pltpu.SemaphoreType.DMA((4,)),
            pltpu.SemaphoreType.DMA((3 + sizes.heads, len(pieces))),
        ],
        compiler_params=limits(),
        cost_estimate=pl.CostEstimate(
            flops=0, bytes_accessed=12 * tok_rows * full, transcendentals=0
        ),
    )(place, queries, keys, values, patch_embed)


def collect_kernel(sizes, *refs):
    *in_refs, out_ref, sems = refs
    copies = []
    for slot, ref in enumerate(in_refs):
        for at, (rows, cols, to_rows) in enumerate(sizes.ride_slices()):
            copies.append(
                pltpu.make_async_copy(
                    ref.at[rows, cols], out_ref.at[slot, to_rows], sems.at[at, slot]
                )
            )
    for copy in copies:
        copy.start()
    for copy in copies:
        copy.wait()


def collect(sizes, arrays):
    return pl.pallas_call(
        functools.partial(collect_kernel, sizes),
        out_shape=jax.ShapeDtypeStruct((len(arrays), sizes.ride_rows, HD), BF16),
        in_specs=[ANY_SPEC] * len(arrays),
        out_specs=VMEM_SPEC,
        scratch_shapes=[pltpu.SemaphoreType.DMA((sizes.heads, len(arrays)))],
        compiler_params=limits(),
    )(*arrays)


def join_kernel(first_ref, second_ref, *refs):
    out_ref = refs[-1]
    count = first_ref.shape[0]
    out_ref[:count] = first_ref[...]
    out_ref[count:] = second_ref[...]


def join(first, second, others):
    return pl.pallas_call(
        join_kernel,
        out_shape=jax.ShapeDtypeStruct((2 * first.shape[0],) + first.shape[1:], BF16),
        in_specs=[VMEM_SPEC] * 2 + [ANY_SPEC] * len(others),
        out_specs=VMEM_SPEC,
        compiler_params=limits(),
    )(first, second, *others)


def arrange_kernel(sizes, masks, place_ref, *refs):
    *pair_refs, out_ref = refs[:-2] + refs[-1:]
    me = place_ref[0]
    odd = me % 2 == 1
    local = sizes.local
    for quarter in range(len(pair_refs) // 2):
        held_ref, got_ref = pair_refs[2 * quarter], pair_refs[2 * quarter + 1]
        for slot, mask in enumerate(masks):
            pair = jnp.bitwise_xor(me, mask) // 2
            for chunk in range(sizes.chunks):
                rows = pl.ds(chunk * sizes.share_rows, sizes.share_rows)
                held = held_ref[slot, rows, :].astype(F32)
                got = got_ref[slot, rows, :].astype(F32)
                first = jnp.where(odd, got, held)
                second = jnp.where(odd, held, got)
                for at in range(sizes.share):
                    part = slice(at * local, (at + 1) * local)
                    both = jnp.concatenate([first[part], second[part]], axis=0).astype(BF16)
                    start = pl.multiple_of(at * sizes.count * local + pair * 2 * local, 2 * local)
                    out_ref[quarter, pl.ds(start, 2 * local), pl.ds(chunk * HD, HD)] = both


def arrange(sizes, masks, place, pairs, wait):
    rows = sizes.share * sizes.count * sizes.local
    flat = [x for pair in pairs for x in pair]
    return pl.pallas_call(
        functools.partial(arrange_kernel, sizes, masks),
        out_shape=jax.ShapeDtypeStruct((len(pairs), rows, VW), BF16),
        in_specs=[SMEM_SPEC] + [VMEM_SPEC] * (len(flat) + 1),
        out_specs=VMEM_SPEC,
        compiler_params=limits(),
    )(place, *flat, wait)


def attend_kernel(sizes, masks, place_ref, *refs):
    count, heads, width = sizes.count, sizes.heads, sizes.width
    tok_rows, part_rows = sizes.tok_rows, sizes.part_rows
    in_refs, refs = refs[:count], refs[count:]
    scale_ref, shift_ref, proj_ref, mod_ref, lat_ref, token_ref, *refs = refs
    query_scr, key_scr, value_scr, scale_scr, shift_scr, proj_scr, sems, side_sems = refs
    half = part_rows // 2
    factor = HD ** (-0.5) * math.log2(math.e)
    me = place_ref[0]
    mine = pl.ds(pl.multiple_of(place_ref[2] * width, HD), width)
    logit_copies, value_copies = [], []
    for src, ref in enumerate(in_refs):
        rows = pl.ds(src * tok_rows, tok_rows)
        logit_copies += [
            pltpu.make_async_copy(ref.at[pl.ds(0, part_rows)], query_scr.at[src], sems.at[0, src]),
            pltpu.make_async_copy(
                ref.at[pl.ds(part_rows, tok_rows)], key_scr.at[rows], sems.at[1, src]
            ),
        ]
        for head in range(heads):
            value_copies.append(
                pltpu.make_async_copy(
                    ref.at[pl.ds(part_rows + tok_rows, tok_rows), pl.ds(head * HD, HD)],
                    value_scr.at[rows, pl.ds(2 * head * HD, HD)],
                    sems.at[2 + head, src],
                )
            )
    value_copies += [
        pltpu.make_async_copy(scale_ref.at[:, mine], scale_scr, side_sems.at[0]),
        pltpu.make_async_copy(shift_ref.at[:, mine], shift_scr, side_sems.at[1]),
        pltpu.make_async_copy(proj_ref.at[:, mine], proj_scr, side_sems.at[2]),
    ]
    for copy in logit_copies + value_copies:
        copy.start()
    token_ref[...] = jnp.zeros_like(token_ref)
    ones = jnp.ones((count * tok_rows, HD), BF16)
    for head in range(heads):
        value_scr[:, pl.ds((2 * head + 1) * HD, HD)] = ones
    for copy in logit_copies + value_copies:
        copy.wait()
    gain = 1.0 + scale_scr[...]
    shift = shift_scr[...]
    proj = proj_scr[...]
    zero = jnp.zeros_like(proj)
    proj_pair = jnp.concatenate(
        [jnp.concatenate([proj, zero], axis=1), jnp.concatenate([zero, proj], axis=1)], axis=0
    )
    together = 2
    for first in range(0, count, together):
        results = []
        for src in range(first, first + together):
            mixed = []
            for head in range(heads):
                cols = pl.ds(head * HD, HD)
                logits = mm_nt(query_scr[src, :, cols], key_scr[:, cols])
                top = jnp.max(logits, axis=-1, keepdims=True)
                weights = jnp.exp2((logits - top) * factor).astype(BF16)
                both = mm(weights, value_scr[:, pl.ds(2 * head * HD, 2 * HD)])
                mixed.append(both[:, :HD] / both[:, HD:])
            attended = jnp.concatenate(mixed, axis=1) if heads > 1 else mixed[0]
            modulated = (attended * gain + shift).astype(BF16)
            pair = jnp.concatenate([modulated[:half], modulated[half:]], axis=1)
            results.append((modulated, mm_nt(pair, proj_pair).astype(BF16)))
        for at, (modulated, latent) in enumerate(results):
            place = jnp.bitwise_xor(me, masks[first + at])
            mod_ref[place] = modulated
            lat_ref[place] = latent


def attend(sizes, masks, place, received, scales, shifts, proj):
    count, width, heads = sizes.count, sizes.width, sizes.heads
    lat_rows = count * sizes.tok_rows
    query_rows = count * sizes.part_rows
    return pl.pallas_call(
        functools.partial(attend_kernel, sizes, masks),
        out_shape=(
            jax.ShapeDtypeStruct((count, sizes.part_rows, width), BF16),
            jax.ShapeDtypeStruct((count, sizes.part_rows // 2, 2 * CH), BF16),
            jax.ShapeDtypeStruct((8, 128), F32),
        ),
        in_specs=[SMEM_SPEC] + [ANY_SPEC] * count + [HBM_SPEC] * 3,
        out_specs=(VMEM_SPEC, VMEM_SPEC, VMEM_SPEC),
        scratch_shapes=[
            pltpu.VMEM((count, sizes.part_rows, width), BF16),
            pltpu.VMEM((lat_rows, width), BF16),
            pltpu.VMEM((lat_rows, 2 * width), BF16),
            pltpu.VMEM((1, width), F32),
            pltpu.VMEM((1, width), F32),
            pltpu.VMEM((CH, width), BF16),
            pltpu.SemaphoreType.DMA((2 + heads, count)),
            pltpu.SemaphoreType.DMA((3,)),
        ],
        compiler_params=limits(16),
        cost_estimate=pl.CostEstimate(
            flops=4 * query_rows * lat_rows * width,
            bytes_accessed=2 * (query_rows * 2 + lat_rows * 2) * width,
            transcendentals=query_rows * lat_rows * heads,
        ),
    )(place, *received, scales, shifts, proj)


def total_kernel(copies, *refs):
    out_ref = refs[-1]
    if len(refs) == 2:
        parts = [refs[0][i].astype(F32) for i in range(refs[0].shape[0])]
    else:
        parts = [ref[...].astype(F32) for ref in refs[:-1]]
    while len(parts) > 1:
        parts = [parts[i] + parts[i + 1] for i in range(0, len(parts), 2)]
    for copy in range(copies):
        out_ref[copy] = parts[0].astype(BF16)


def total_copies(arrays, copies):
    return pl.pallas_call(
        functools.partial(total_kernel, copies),
        out_shape=jax.ShapeDtypeStruct((copies,) + arrays[0].shape[-2:], BF16),
        in_specs=[VMEM_SPEC] * len(arrays),
        out_specs=VMEM_SPEC,
        compiler_params=limits(),
    )(*arrays)


def lane_mean(x, count):
    return jnp.sum(x, axis=-1, keepdims=True) * (1.0 / count)


def head_kernel(grid_rows, fused, embed_masks, out_factor, place_ref, lat_ref, *refs):
    embed_refs, refs = refs[: len(embed_masks)], refs[len(embed_masks) :]
    sides, refs = refs[:4], refs[4:]
    cot_ref, refs = refs[0], refs[1:]
    mod_ref, refs = refs[0], refs[1:]
    reward_ref, grad_ref, weight_ref, lat_scr, grad_scr, embed_ref, *refs = refs
    pos_ref, pre_ref, post_ref, prompt_ref, sems, side_sems = refs
    patch_rows = grid_rows // 4
    patch_cols = GW // 4
    patches = patch_rows * patch_cols
    copies = []
    for ref, masks in zip(embed_refs, embed_masks):
        for slot, mask in enumerate(masks):
            rows = ref.shape[1]
            first = pl.multiple_of(jnp.bitwise_xor(place_ref[1], mask) * rows, rows)
            to = embed_ref.at[pl.ds(first, rows)]
            copies.append(pltpu.make_async_copy(ref.at[slot], to, sems.at[len(copies)]))
    for slot, (side, scr) in enumerate(zip(sides, (pos_ref, pre_ref, post_ref, prompt_ref))):
        copies.append(pltpu.make_async_copy(side, scr, side_sems.at[slot]))
    for copy in copies:
        copy.start()
    lat_scr[...] = lat_ref[...].astype(F32)

    def position_rows(ty):
        return embed_ref[pl.ds(4 * ty * CH, 4 * CH), :]

    blocks = []
    for hi in range(2):
        wide = []
        for tx in range(4):
            rows = [
                lat_scr[pl.ds((2 * pr + hi) * GW + tx, patch_cols, stride=4), :]
                for pr in range(patch_rows)
            ]
            wide.append(jnp.concatenate(rows, axis=0))
        for side in range(2):
            lanes = slice(side * CH, (side + 1) * CH)
            blocks.append(jnp.concatenate([x[:, lanes] for x in wide], axis=1).astype(BF16))
    for copy in copies:
        copy.wait()
    embedded = pos_ref[...].astype(F32)
    for ty in range(4):
        embedded = embedded + mm(blocks[ty], position_rows(ty))
    pre = pre_ref[...].reshape(1, VW)
    post = post_ref[...].reshape(1, VW)
    prompt = prompt_ref[...]
    center = embedded - lane_mean(embedded, VW)
    rstd = lax.rsqrt(lane_mean(center * center, VW) + EPS)
    unit = center * rstd
    pooled = jnp.sum(unit, axis=0, keepdims=True) * (1.0 / patches) * pre
    pooled_center = pooled - lane_mean(pooled, VW)
    pooled_rstd = lax.rsqrt(lane_mean(pooled_center * pooled_center, VW) + EPS)
    pooled_unit = pooled_center * pooled_rstd
    final = pooled_unit * post
    dot = jnp.sum(final * prompt, axis=-1, keepdims=True)
    final_sq = jnp.sum(final * final, axis=-1, keepdims=True)
    prompt_sq = jnp.sum(prompt * prompt, axis=-1, keepdims=True)
    final_len = jnp.sqrt(final_sq)
    prompt_len = jnp.sqrt(prompt_sq)
    cosine = dot / (final_len * prompt_len)
    reward_ref[...] = jnp.broadcast_to(100.0 * cosine, reward_ref.shape)
    cot = cot_ref[0]
    final_grad = (100.0 * cot) * (prompt / (final_len * prompt_len) - final * (cosine / final_sq))
    unit_grad = final_grad * post
    pooled_grad = pooled_rstd * (
        unit_grad
        - lane_mean(unit_grad, VW)
        - pooled_unit * lane_mean(unit_grad * pooled_unit, VW)
    )
    flow = pooled_grad * pre * (1.0 / patches)
    embed_grad = rstd * (flow - lane_mean(flow, VW) - unit * lane_mean(flow * unit, VW))
    high = embed_grad.astype(BF16)
    low = (embed_grad - high.astype(F32)).astype(BF16)
    stacked = jnp.concatenate([high, low], axis=0)
    for hi in range(2):
        sides = []
        for side in range(2):
            both = mm_nt(stacked, position_rows(2 * hi + side))
            sides.append(both[:patches] + both[patches:])
        for tx in range(4):
            lanes = slice(tx * CH, (tx + 1) * CH)
            piece = jnp.concatenate([sides[0][:, lanes], sides[1][:, lanes]], axis=1)
            for pr in range(patch_rows):
                grad_scr[pl.ds((2 * pr + hi) * GW + tx, patch_cols, stride=4), :] = piece[
                    pr * patch_cols : (pr + 1) * patch_cols
                ]
    grad = grad_scr[...].astype(BF16)
    grad_ref[...] = grad
    if fused:
        store_readout_grad(grad, mod_ref, out_factor, weight_ref)
    else:
        weight_ref[...] = jnp.zeros_like(weight_ref)


def store_readout_grad(grad, mod_ref, out_factor, out_ref):
    turned = grad.astype(F32).T.astype(BF16)
    count, rows, width = mod_ref.shape
    half = rows // 2
    first = mod_ref[:, :half, :].reshape(count * half, width)
    second = mod_ref[:, half:, :].reshape(count * half, width)
    total = mm(turned[:CH], first) + mm(turned[CH:], second)
    out_ref[...] = (total * out_factor).astype(BF16)


def reward_head(
    place, latent, embed, pos, pre, post, prompt, cot, modulated, grid_rows, fused, out_factor
):
    patches = grid_rows * GW // 16
    rows = grid_rows * GW // 2
    width = modulated.shape[2]
    embed_arrays, embed_masks = [x for x, _ in embed], [masks for _, masks in embed]
    return pl.pallas_call(
        functools.partial(head_kernel, grid_rows, fused, embed_masks, out_factor),
        out_shape=(
            jax.ShapeDtypeStruct((1, 128), F32),
            jax.ShapeDtypeStruct((rows, 2 * CH), BF16),
            jax.ShapeDtypeStruct((CH, width), BF16),
        ),
        in_specs=[SMEM_SPEC, VMEM_SPEC]
        + [ANY_SPEC] * len(embed_arrays)
        + [HBM_SPEC] * 4
        + [SMEM_SPEC, VMEM_SPEC],
        out_specs=(VMEM_SPEC, VMEM_SPEC, VMEM_SPEC),
        scratch_shapes=[
            pltpu.VMEM((rows, 2 * CH), F32),
            pltpu.VMEM((rows, 2 * CH), F32),
            pltpu.VMEM((16 * CH, VW), BF16),
            pltpu.VMEM((patches, VW), BF16),
            pltpu.VMEM((VW,), F32),
            pltpu.VMEM((VW,), F32),
            pltpu.VMEM((1, VW), F32),
            pltpu.SemaphoreType.DMA((sum(len(masks) for masks in embed_masks),)),
            pltpu.SemaphoreType.DMA((4,)),
        ],
        compiler_params=limits(16),
        cost_estimate=pl.CostEstimate(
            flops=6 * patches * 16 * CH * VW,
            bytes_accessed=2 * 16 * CH * VW + 2 * patches * VW,
            transcendentals=0,
        ),
    )(place, latent, *embed_arrays, pos, pre, post, prompt, cot, modulated)


def spread_kernel(
    count, half, heads, place_ref, grad_ref, scale_ref, proj_ref, out_ref, scale_scr, proj_scr, sems
):
    width = heads * HD
    mine = pl.ds(pl.multiple_of(place_ref[2] * width, HD), width)
    copies = [
        pltpu.make_async_copy(scale_ref.at[:, mine], scale_scr, sems.at[0]),
        pltpu.make_async_copy(proj_ref.at[:, mine], proj_scr, sems.at[1]),
    ]
    for copy in copies:
        copy.start()
    for copy in copies:
        copy.wait()
    gain = 1.0 + scale_scr[...]
    proj = proj_scr[...]
    zero = jnp.zeros_like(proj)
    sides = (jnp.concatenate([proj, zero], axis=0), jnp.concatenate([zero, proj], axis=0))
    for src in range(count):
        grad = grad_ref[pl.ds(src * half, half), :]
        for side in range(2):
            rows = (mm(grad, sides[side]) * gain).astype(BF16)
            for head in range(heads):
                out_ref[0, head, pl.ds((2 * src + side) * half, half), :] = rows[
                    :, head * HD : (head + 1) * HD
                ]


def spread(place, grad, scales, proj, count, half, heads):
    return pl.pallas_call(
        functools.partial(spread_kernel, count, half, heads),
        out_shape=jax.ShapeDtypeStruct((1, heads, 2 * count * half, HD), BF16),
        in_specs=[SMEM_SPEC, VMEM_SPEC, HBM_SPEC, HBM_SPEC],
        out_specs=VMEM_SPEC,
        scratch_shapes=[
            pltpu.VMEM((1, heads * HD), F32),
            pltpu.VMEM((CH, heads * HD), BF16),
            pltpu.SemaphoreType.DMA((2,)),
        ],
        compiler_params=limits(),
        cost_estimate=pl.CostEstimate(
            flops=8 * count * half * CH * heads * HD,
            bytes_accessed=4 * count * half * heads * HD,
            transcendentals=0,
        ),
    )(place, grad, scales, proj)


def weight_kernel(out_factor, grad_ref, *refs):
    store_readout_grad(grad_ref[...], refs[0], out_factor, refs[1])


def weight_call(grad, modulated, out_factor):
    return pl.pallas_call(
        functools.partial(weight_kernel, out_factor),
        out_shape=jax.ShapeDtypeStruct((CH, modulated.shape[2]), BF16),
        in_specs=[VMEM_SPEC] * 2,
        out_specs=VMEM_SPEC,
        compiler_params=limits(),
    )(grad, modulated)


def finish_kernel(in_ref, out_ref):
    count, _, width = in_ref.shape
    for group in range(count):
        out_ref[:, pl.ds(group * width, width)] = in_ref[group].astype(F32)


def finish(blocks):
    return pl.pallas_call(
        finish_kernel,
        out_shape=jax.ShapeDtypeStruct((CH, HEADS * HD), F32),
        in_specs=[VMEM_SPEC],
        out_specs=VMEM_SPEC,
        compiler_params=limits(),
    )(blocks)


def swap(x, axis, mask):
    count = lax.axis_size(axis)
    return lax.ppermute(x, axis, [(i, i ^ mask) for i in range(count)])


def all_to_all(x, groups=None):
    return lax.all_to_all(
        x, "seq", split_axis=0, concat_axis=0, tiled=True, axis_index_groups=groups
    )


def swap_both(x, seq_mask, data_mask):
    seq_count, data_count = lax.axis_size("seq"), lax.axis_size("dp")
    pairs = [
        (i * data_count + j, (i ^ seq_mask) * data_count + (j ^ data_mask))
        for i in range(seq_count)
        for j in range(data_count)
    ]
    return lax.ppermute(x, ("seq", "dp"), pairs)


def on_device(
    queries,
    keys,
    values,
    shifts,
    scales,
    proj_out,
    patch_embed,
    pos_embed,
    pre_gain,
    post_gain,
    prompt,
    cotangent,
):
    seq_count = lax.axis_size("seq")
    data_count = lax.axis_size("dp")
    tok_rows = queries.shape[1]
    sizes = Sizes(seq_count, data_count, tok_rows, patch_embed)
    query_parts, head_count, part_rows = sizes.query_parts, sizes.heads, sizes.part_rows
    group_count = HEADS // head_count
    seq_index = lax.axis_index("seq")
    head_group = seq_index // query_parts
    query_part = seq_index % query_parts
    half = part_rows // 2
    lat_rows = seq_count * tok_rows
    grid_rows = lat_rows // GW
    canonical = part_rows == 2 * GW
    place = jnp.stack([seq_index, lax.axis_index("dp"), head_group]).astype(jnp.int32)
    proj_turned = proj_out.T
    out_factor = 1.0 / math.sqrt(data_count * lat_rows)

    masks = sizes.pieces()
    packed = pack(
        sizes, place, in_hbm(queries), in_hbm(keys), in_hbm(values), in_hbm(patch_embed)
    )
    received = [swap(x, "seq", mask) if mask else x for mask, x in zip(masks, packed)]
    bits = [1 << b for b in reversed(range(data_count.bit_length() - 1))]
    shared = sizes.share < patch_embed.shape[0]
    if sizes.riding:
        ride = [slot for slot, mask in enumerate(masks) if sizes.rides(mask)]
        two = collect(sizes, [received[slot] for slot in ride])
        held = join(two, swap(two, "seq", 2), received[:-1])
        ride_masks = [masks[slot] for slot in ride]
        ride_masks = ride_masks + [mask ^ 2 for mask in ride_masks]
        pairs = [
            (held, swap(held, "seq", 1)),
            (swap(held, "dp", bits[0]), swap_both(held, 1, bits[0])),
        ]

    modulated, latent_part, token = attend(
        sizes, masks, place, received, in_hbm(scales), in_hbm(shifts), in_hbm(proj_turned)
    )

    if sizes.riding:
        embed = [(arrange(sizes, ride_masks, place, pairs, token), [0, bits[0]])]
    else:
        mine = patch_embed
        if shared:
            mine = lax.dynamic_slice_in_dim(
                patch_embed, lax.axis_index("dp") * sizes.share, sizes.share, 0
            )
        mine = lax.all_gather(mine, "seq", axis=1, tiled=True).reshape(-1, VW)
        embed = [(mine[None], [0])]
        if shared:
            embed = embed + [(swap(mine[None], "dp", bits[0]), [bits[0]])]

    groups = None
    if query_parts > 1:
        groups = [[g * query_parts + r for g in range(group_count)] for r in range(query_parts)]
    per_share = seq_count // group_count
    parts = all_to_all(latent_part.reshape(group_count, per_share * half, 2 * CH), groups)
    for bit in bits[1:] if shared else []:
        embed = embed + [(swap(x, "dp", bit), [m ^ bit for m in some]) for x, some in embed]
    latent = all_to_all(total_copies([parts], seq_count))
    if canonical:
        latent = latent.reshape(lat_rows // 2, 2 * CH)
    else:
        latent = latent.reshape(group_count, query_parts, per_share, half, 2, CH)
        latent = latent.transpose(0, 2, 1, 4, 3, 5).reshape(grid_rows // 2, 2, GW, CH)
        latent = latent.transpose(0, 2, 1, 3).reshape(lat_rows // 2, 2 * CH)

    reward, grad, weight = reward_head(
        place, latent, embed, in_hbm(pos_embed), in_hbm(pre_gain), in_hbm(post_gain), in_hbm(prompt),
        cotangent, modulated, grid_rows, canonical, out_factor,
    )
    if not canonical:
        tokens = grad.reshape(grid_rows // 2, GW, 2, CH).transpose(0, 2, 1, 3)
        tokens = tokens.reshape(seq_count, query_parts, 2, half, CH)
        tokens = lax.dynamic_index_in_dim(tokens, query_part, 1, keepdims=False)
        grad = tokens.transpose(0, 2, 1, 3).reshape(seq_count * half, 2 * CH)
        weight = weight_call(grad, modulated, out_factor)

    parts = [weight] + [swap(weight, "dp", mask) for mask in range(1, data_count)]
    attn_grad = spread(place, grad, in_hbm(scales), in_hbm(proj_turned), seq_count, half, head_count)
    if query_parts > 1:
        total = total_copies(parts, 1)[0]
        parts = [total] + [swap(total, "seq", mask) for mask in range(1, query_parts)]
    blocks = all_to_all(total_copies(parts, group_count), groups)
    return (reward[0, :1], attn_grad, finish(blocks).T)


def solution(mesh):
    return jax.shard_map(
        on_device,
        mesh=mesh,
        in_specs=(
            P("dp", "seq", None),
            P("dp", "seq", None),
            P("dp", "seq", None),
            P("dp", None),
            P("dp", None),
            P(),
            P(None, "seq", None),
            P(),
            P(),
            P(),
            P("dp", None),
            P("dp"),
        ),
        out_specs=(P("dp"), P("dp", "seq", None, None), P()),
        check_vma=False,
    )
```

```python
import functools
import math

import jax
import jax.numpy as jnp
from jax import lax
from jax.experimental import pallas as pl
from jax.experimental.pallas import tpu as pltpu
from jax.sharding import PartitionSpec as P

HEADS = 16
HD = 128
CH = 64
GW = 64
VW = 1280
EPS = 1e-05
BF16 = jnp.bfloat16
F32 = jnp.float32


def mm(a, b):
    return jnp.dot(a, b, preferred_element_type=F32)


def mm_nt(a, b):
    return lax.dot_general(a, b, (((1,), (1,)), ((), ())), preferred_element_type=F32)


def mm_tn(a, b):
    return lax.dot_general(a, b, (((0,), (0,)), ((), ())), preferred_element_type=F32)


SMEM_SPEC = pl.BlockSpec(memory_space=pltpu.SMEM)
VMEM_SPEC = pl.BlockSpec(memory_space=pltpu.VMEM)
HBM_SPEC = pl.BlockSpec(memory_space=pltpu.HBM)
ANY_SPEC = pl.BlockSpec(memory_space=pl.ANY)


def in_hbm(x):
    return pltpu.with_memory_space_constraint(x, pltpu.HBM)


def limits(mib=4):
    return pltpu.CompilerParams(vmem_limit_bytes=mib * 1024 * 1024)


class Sizes:
    def __init__(self, seq_count, data_count, tok_rows, patch_embed):
        self.count = seq_count
        self.query_parts = max(1, seq_count // HEADS)
        self.heads = max(1, HEADS // seq_count)
        self.width = self.heads * HD
        self.tok_rows = tok_rows
        self.part_rows = tok_rows // self.query_parts
        positions, self.local, _ = patch_embed.shape
        self.share = positions // data_count if positions % data_count == 0 else positions
        self.rows = self.part_rows + 2 * tok_rows
        self.share_rows = self.share * self.local
        self.chunks = VW // HD
        self.riding = self.local % 8 == 0 and self.share_rows % 16 == 0 and seq_count == 8
        self.riding = self.riding and 1 < data_count <= positions
        self.ride_rows = self.chunks * self.share_rows if self.riding else 0

    def pieces(self):
        return list(range(1, self.count)) + [0]

    def rides(self, mask):
        return self.riding and mask in (0, 4)

    def piece_shape(self, mask):
        return (self.rows + (self.ride_rows // self.heads if self.rides(mask) else 0), self.width)

    def ride_slices(self):
        deep = self.ride_rows // self.heads
        return [
            (pl.ds(self.rows, deep), pl.ds(at * HD, HD), pl.ds(at * deep, deep))
            for at in range(self.heads)
        ]


def pack_kernel(sizes, q_ref, k_ref, v_ref, embed_ref, *refs):
    pieces = sizes.pieces()
    out_refs = refs[: len(pieces)]
    q_scr, k_scr, v_scr, embed_scr, share_scr, in_sems, out_sems = refs[len(pieces) :]
    me = lax.axis_index("seq")
    tok_rows, part_rows, width = sizes.tok_rows, sizes.part_rows, sizes.width
    share = pl.ds(lax.axis_index("dp") * sizes.share, sizes.share)
    loads = [
        pltpu.make_async_copy(embed_ref.at[share], embed_scr, in_sems.at[3]),
        pltpu.make_async_copy(q_ref.at[0], q_scr, in_sems.at[0]),
        pltpu.make_async_copy(k_ref.at[0], k_scr, in_sems.at[1]),
        pltpu.make_async_copy(v_ref.at[0], v_scr, in_sems.at[2]),
    ]
    for load in loads:
        load.start()
    sent = [[], [], [], []]
    for slot, (mask, out) in enumerate(zip(pieces, out_refs)):
        dest = jnp.bitwise_xor(me, mask)
        group, part = dest // sizes.query_parts, dest % sizes.query_parts
        cols = pl.ds(pl.multiple_of(group * width, HD), width)
        first = pl.ds(pl.multiple_of(part * part_rows, part_rows), part_rows)
        for kind, source, rows in (
            (0, q_scr.at[first, cols], pl.ds(0, part_rows)),
            (1, k_scr.at[:, cols], pl.ds(part_rows, tok_rows)),
            (2, v_scr.at[:, cols], pl.ds(part_rows + tok_rows, tok_rows)),
        ):
            sent[kind].append(pltpu.make_async_copy(source, out.at[rows], out_sems.at[kind, slot]))
        if sizes.rides(mask):
            for at, (rows, place, from_rows) in enumerate(sizes.ride_slices()):
                sent[3].append(
                    pltpu.make_async_copy(
                        share_scr.at[from_rows], out.at[rows, place], out_sems.at[3 + at, slot]
                    )
                )
    loads[0].wait()
    if sizes.riding:
        for chunk in range(sizes.chunks):
            cols = embed_scr[:, :, pl.ds(chunk * HD, HD)].astype(F32)
            share_scr[pl.ds(chunk * sizes.share_rows, sizes.share_rows), :] = cols.reshape(
                sizes.share_rows, HD
            ).astype(BF16)
    for store in sent[3]:
        store.start()
    for kind in range(3):
        loads[kind + 1].wait()
        for store in sent[kind]:
            store.start()
    for stores in sent:
        for store in stores:
            store.wait()


def pack(sizes, queries, keys, values, patch_embed):
    tok_rows, full = queries.shape[1:]
    pieces = sizes.pieces()
    return pl.pallas_call(
        functools.partial(pack_kernel, sizes),
        out_shape=[jax.ShapeDtypeStruct(sizes.piece_shape(mask), BF16) for mask in pieces],
        in_specs=[HBM_SPEC] * 4,
        out_specs=[HBM_SPEC] * len(pieces),
        scratch_shapes=[pltpu.VMEM((tok_rows, full), BF16)] * 3
        + [
            pltpu.VMEM((sizes.share,) + patch_embed.shape[1:], BF16),
            pltpu.VMEM((max(16, sizes.ride_rows), HD), BF16),
            pltpu.SemaphoreType.DMA((4,)),
            pltpu.SemaphoreType.DMA((3 + sizes.heads, len(pieces))),
        ],
        compiler_params=limits(),
        cost_estimate=pl.CostEstimate(
            flops=0, bytes_accessed=12 * tok_rows * full, transcendentals=0
        ),
    )(queries, keys, values, patch_embed)


def collect_kernel(sizes, *refs):
    *in_refs, out_ref, sems = refs
    copies = []
    for slot, ref in enumerate(in_refs):
        for at, (rows, cols, to_rows) in enumerate(sizes.ride_slices()):
            copies.append(
                pltpu.make_async_copy(
                    ref.at[rows, cols], out_ref.at[slot, to_rows], sems.at[at, slot]
                )
            )
    for copy in copies:
        copy.start()
    for copy in copies:
        copy.wait()


def collect(sizes, arrays):
    return pl.pallas_call(
        functools.partial(collect_kernel, sizes),
        out_shape=jax.ShapeDtypeStruct((len(arrays), sizes.ride_rows, HD), BF16),
        in_specs=[ANY_SPEC] * len(arrays),
        out_specs=VMEM_SPEC,
        scratch_shapes=[pltpu.SemaphoreType.DMA((sizes.heads, len(arrays)))],
        compiler_params=limits(),
    )(*arrays)


def join_kernel(first_ref, second_ref, *refs):
    out_ref = refs[-1]
    count = first_ref.shape[0]
    out_ref[:count] = first_ref[...]
    out_ref[count:] = second_ref[...]


def join(first, second, others):
    return pl.pallas_call(
        join_kernel,
        out_shape=jax.ShapeDtypeStruct((2 * first.shape[0],) + first.shape[1:], BF16),
        in_specs=[VMEM_SPEC] * 2 + [ANY_SPEC] * len(others),
        out_specs=VMEM_SPEC,
        compiler_params=limits(),
    )(first, second, *others)


def arrange_kernel(sizes, masks, place_ref, *refs):
    *pair_refs, out_ref = refs[:-2] + refs[-1:]
    me = place_ref[0]
    odd = me % 2 == 1
    local = sizes.local
    for quarter in range(len(pair_refs) // 2):
        held_ref, got_ref = pair_refs[2 * quarter], pair_refs[2 * quarter + 1]
        for slot, mask in enumerate(masks):
            pair = jnp.bitwise_xor(me, mask) // 2
            for chunk in range(sizes.chunks):
                rows = pl.ds(chunk * sizes.share_rows, sizes.share_rows)
                held = held_ref[slot, rows, :].astype(F32)
                got = got_ref[slot, rows, :].astype(F32)
                first = jnp.where(odd, got, held)
                second = jnp.where(odd, held, got)
                for at in range(sizes.share):
                    part = slice(at * local, (at + 1) * local)
                    both = jnp.concatenate([first[part], second[part]], axis=0).astype(BF16)
                    start = pl.multiple_of(at * sizes.count * local + pair * 2 * local, 2 * local)
                    out_ref[quarter, pl.ds(start, 2 * local), pl.ds(chunk * HD, HD)] = both


def arrange(sizes, masks, place, pairs, wait):
    rows = sizes.share * sizes.count * sizes.local
    flat = [x for pair in pairs for x in pair]
    return pl.pallas_call(
        functools.partial(arrange_kernel, sizes, masks),
        out_shape=jax.ShapeDtypeStruct((len(pairs), rows, VW), BF16),
        in_specs=[SMEM_SPEC] + [VMEM_SPEC] * (len(flat) + 1),
        out_specs=VMEM_SPEC,
        compiler_params=limits(),
    )(place, *flat, wait)


def attend_kernel(sizes, masks, place_ref, *refs):
    count, heads, width = sizes.count, sizes.heads, sizes.width
    tok_rows, part_rows = sizes.tok_rows, sizes.part_rows
    in_refs, refs = refs[:count], refs[count:]
    scale_ref, shift_ref, proj_ref, mod_ref, lat_ref, *refs = refs
    query_scr, key_scr, value_scr, scale_scr, shift_scr, proj_scr, sems, side_sems = refs
    half = part_rows // 2
    factor = HD ** (-0.5) * math.log2(math.e)
    me = place_ref[0]
    mine = pl.ds(pl.multiple_of(place_ref[2] * width, HD), width)
    logit_copies, value_copies = [], []
    for src, ref in enumerate(in_refs):
        rows = pl.ds(src * tok_rows, tok_rows)
        logit_copies += [
            pltpu.make_async_copy(ref.at[pl.ds(0, part_rows)], query_scr.at[src], sems.at[0, src]),
            pltpu.make_async_copy(
                ref.at[pl.ds(part_rows, tok_rows)], key_scr.at[rows], sems.at[1, src]
            ),
        ]
        for head in range(heads):
            value_copies.append(
                pltpu.make_async_copy(
                    ref.at[pl.ds(part_rows + tok_rows, tok_rows), pl.ds(head * HD, HD)],
                    value_scr.at[rows, pl.ds(2 * head * HD, HD)],
                    sems.at[2 + head, src],
                )
            )
    value_copies += [
        pltpu.make_async_copy(scale_ref.at[:, mine], scale_scr, side_sems.at[0]),
        pltpu.make_async_copy(shift_ref.at[:, mine], shift_scr, side_sems.at[1]),
        pltpu.make_async_copy(proj_ref.at[:, mine], proj_scr, side_sems.at[2]),
    ]
    for copy in logit_copies + value_copies:
        copy.start()
    ones = jnp.ones((count * tok_rows, HD), BF16)
    for head in range(heads):
        value_scr[:, pl.ds((2 * head + 1) * HD, HD)] = ones
    for copy in logit_copies + value_copies:
        copy.wait()
    gain = 1.0 + scale_scr[...]
    shift = shift_scr[...]
    proj = proj_scr[...]
    zero = jnp.zeros_like(proj)
    proj_pair = jnp.concatenate(
        [jnp.concatenate([proj, zero], axis=1), jnp.concatenate([zero, proj], axis=1)], axis=0
    )
    together = 2
    for first in range(0, count, together):
        results = []
        for src in range(first, first + together):
            mixed = []
            for head in range(heads):
                cols = pl.ds(head * HD, HD)
                logits = mm_nt(query_scr[src, :, cols], key_scr[:, cols])
                top = jnp.max(logits, axis=-1, keepdims=True)
                weights = jnp.exp2((logits - top) * factor).astype(BF16)
                both = mm(weights, value_scr[:, pl.ds(2 * head * HD, 2 * HD)])
                mixed.append(both[:, :HD] / both[:, HD:])
            attended = jnp.concatenate(mixed, axis=1) if heads > 1 else mixed[0]
            modulated = (attended * gain + shift).astype(BF16)
            pair = jnp.concatenate([modulated[:half], modulated[half:]], axis=1)
            results.append((modulated, mm_nt(pair, proj_pair).astype(BF16)))
        for at, (modulated, latent) in enumerate(results):
            place = jnp.bitwise_xor(me, masks[first + at])
            mod_ref[place] = modulated
            lat_ref[place] = latent


def attend(sizes, masks, place, received, scales, shifts, proj):
    count, width, heads = sizes.count, sizes.width, sizes.heads
    lat_rows = count * sizes.tok_rows
    query_rows = count * sizes.part_rows
    return pl.pallas_call(
        functools.partial(attend_kernel, sizes, masks),
        out_shape=(
            jax.ShapeDtypeStruct((count, sizes.part_rows, width), BF16),
            jax.ShapeDtypeStruct((count, sizes.part_rows // 2, 2 * CH), BF16),
        ),
        in_specs=[SMEM_SPEC] + [ANY_SPEC] * count + [HBM_SPEC] * 3,
        out_specs=(VMEM_SPEC, VMEM_SPEC),
        scratch_shapes=[
            pltpu.VMEM((count, sizes.part_rows, width), BF16),
            pltpu.VMEM((lat_rows, width), BF16),
            pltpu.VMEM((lat_rows, 2 * width), BF16),
            pltpu.VMEM((1, width), F32),
            pltpu.VMEM((1, width), F32),
            pltpu.VMEM((CH, width), BF16),
            pltpu.SemaphoreType.DMA((2 + heads, count)),
            pltpu.SemaphoreType.DMA((3,)),
        ],
        compiler_params=limits(16),
        cost_estimate=pl.CostEstimate(
            flops=4 * query_rows * lat_rows * width,
            bytes_accessed=2 * (query_rows * 2 + lat_rows * 2) * width,
            transcendentals=query_rows * lat_rows * heads,
        ),
    )(place, *received, scales, shifts, proj)


def total_kernel(copies, *refs):
    out_ref = refs[-1]
    if len(refs) == 2:
        parts = [refs[0][i].astype(F32) for i in range(refs[0].shape[0])]
    else:
        parts = [ref[...].astype(F32) for ref in refs[:-1]]
    while len(parts) > 1:
        parts = [parts[i] + parts[i + 1] for i in range(0, len(parts), 2)]
    for copy in range(copies):
        out_ref[copy] = parts[0].astype(BF16)


def total_copies(arrays, copies):
    return pl.pallas_call(
        functools.partial(total_kernel, copies),
        out_shape=jax.ShapeDtypeStruct((copies,) + arrays[0].shape[-2:], BF16),
        in_specs=[VMEM_SPEC] * len(arrays),
        out_specs=VMEM_SPEC,
        compiler_params=limits(),
    )(*arrays)


def lane_mean(x, count):
    return jnp.sum(x, axis=-1, keepdims=True) * (1.0 / count)


def head_kernel(grid_rows, fused, embed_masks, out_factor, place_ref, lat_ref, *refs):
    embed_refs, refs = refs[: len(embed_masks)], refs[len(embed_masks) :]
    sides, refs = refs[:4], refs[4:]
    cot_ref, refs = refs[0], refs[1:]
    mod_ref, refs = refs[0], refs[1:]
    reward_ref, grad_ref, weight_ref, lat_scr, grad_scr, block_scr, back_scr, *refs = refs
    pos_ref, pre_ref, post_ref, prompt_ref, side_sems = refs
    patch_rows = grid_rows // 4
    patch_cols = GW // 4
    patches = patch_rows * patch_cols
    copies = []
    for slot, (side, scr) in enumerate(zip(sides, (pos_ref, pre_ref, post_ref, prompt_ref))):
        copies.append(pltpu.make_async_copy(side, scr, side_sems.at[slot]))
    for copy in copies:
        copy.start()
    lat_scr[...] = lat_ref[...].astype(F32)

    data = place_ref[1]
    shares = [
        (jnp.bitwise_xor(data, mask), ref, slot)
        for ref, masks in zip(embed_refs, embed_masks)
        for slot, mask in enumerate(masks)
    ]
    share_rows = embed_refs[0].shape[1]
    for hi in range(2):
        wide = []
        for tx in range(4):
            rows = [
                lat_scr[pl.ds((2 * pr + hi) * GW + tx, patch_cols, stride=4), :]
                for pr in range(patch_rows)
            ]
            wide.append(jnp.concatenate(rows, axis=0))
        for side in range(2):
            lanes = slice(side * CH, (side + 1) * CH)
            line = jnp.concatenate([x[:, lanes] for x in wide], axis=1).astype(BF16)
            first = (2 * hi + side) * 4 * CH
            if share_rows >= 4 * CH:
                at = first % share_rows
                block_scr[first // share_rows, :, pl.ds(at, 4 * CH)] = line
            else:
                for at in range(0, 4 * CH, share_rows):
                    block_scr[(first + at) // share_rows] = line[:, at : at + share_rows]
    for copy in copies:
        copy.wait()
    embedded = pos_ref[...].astype(F32)
    for number, ref, slot in shares:
        embedded = embedded + mm(block_scr[number], ref[slot])
    pre = pre_ref[...].reshape(1, VW)
    post = post_ref[...].reshape(1, VW)
    prompt = prompt_ref[...]
    center = embedded - lane_mean(embedded, VW)
    rstd = lax.rsqrt(lane_mean(center * center, VW) + EPS)
    unit = center * rstd
    pooled = jnp.sum(unit, axis=0, keepdims=True) * (1.0 / patches) * pre
    pooled_center = pooled - lane_mean(pooled, VW)
    pooled_rstd = lax.rsqrt(lane_mean(pooled_center * pooled_center, VW) + EPS)
    pooled_unit = pooled_center * pooled_rstd
    final = pooled_unit * post
    dot = jnp.sum(final * prompt, axis=-1, keepdims=True)
    final_sq = jnp.sum(final * final, axis=-1, keepdims=True)
    prompt_sq = jnp.sum(prompt * prompt, axis=-1, keepdims=True)
    final_len = jnp.sqrt(final_sq)
    prompt_len = jnp.sqrt(prompt_sq)
    cosine = dot / (final_len * prompt_len)
    reward_ref[...] = jnp.broadcast_to(100.0 * cosine, reward_ref.shape)
    cot = cot_ref[0]
    final_grad = (100.0 * cot) * (prompt / (final_len * prompt_len) - final * (cosine / final_sq))
    unit_grad = final_grad * post
    pooled_grad = pooled_rstd * (
        unit_grad
        - lane_mean(unit_grad, VW)
        - pooled_unit * lane_mean(unit_grad * pooled_unit, VW)
    )
    flow = pooled_grad * pre * (1.0 / patches)
    embed_grad = rstd * (flow - lane_mean(flow, VW) - unit * lane_mean(flow * unit, VW))
    high = embed_grad.astype(BF16)
    low = (embed_grad - high.astype(F32)).astype(BF16)
    stacked = jnp.concatenate([high, low], axis=0)
    for number, ref, slot in shares:
        both = mm_nt(stacked, ref[slot])
        back_scr[number] = both[:patches] + both[patches:]
    back = jnp.concatenate([back_scr[i] for i in range(16 * CH // share_rows)], axis=1)
    for hi in range(2):
        for tx in range(4):
            first = (4 * (2 * hi) + tx) * CH
            second = (4 * (2 * hi + 1) + tx) * CH
            piece = jnp.concatenate(
                [back[:, first : first + CH], back[:, second : second + CH]], axis=1
            )
            for pr in range(patch_rows):
                grad_scr[pl.ds((2 * pr + hi) * GW + tx, patch_cols, stride=4), :] = piece[
                    pr * patch_cols : (pr + 1) * patch_cols
                ]
    grad = grad_scr[...].astype(BF16)
    grad_ref[...] = grad
    if fused:
        store_readout_grad(grad, mod_ref, out_factor, weight_ref)
    else:
        weight_ref[...] = jnp.zeros_like(weight_ref)


def store_readout_grad(grad, mod_ref, out_factor, out_ref):
    turned = grad.astype(F32).T.astype(BF16)
    count, rows, width = mod_ref.shape
    half = rows // 2
    first = mod_ref[:, :half, :].reshape(count * half, width)
    second = mod_ref[:, half:, :].reshape(count * half, width)
    total = mm(turned[:CH], first) + mm(turned[CH:], second)
    out_ref[...] = (total * out_factor).astype(BF16)


def reward_head(
    place, latent, embed, pos, pre, post, prompt, cot, modulated, grid_rows, fused, out_factor
):
    patches = grid_rows * GW // 16
    rows = grid_rows * GW // 2
    width = modulated.shape[2]
    embed_arrays, embed_masks = [x for x, _ in embed], [masks for _, masks in embed]
    share_rows = embed_arrays[0].shape[1]
    return pl.pallas_call(
        functools.partial(head_kernel, grid_rows, fused, embed_masks, out_factor),
        out_shape=(
            jax.ShapeDtypeStruct((1, 128), F32),
            jax.ShapeDtypeStruct((rows, 2 * CH), BF16),
            jax.ShapeDtypeStruct((CH, width), BF16),
        ),
        in_specs=[SMEM_SPEC, VMEM_SPEC]
        + [VMEM_SPEC] * len(embed_arrays)
        + [HBM_SPEC] * 4
        + [SMEM_SPEC, VMEM_SPEC],
        out_specs=(VMEM_SPEC, VMEM_SPEC, VMEM_SPEC),
        scratch_shapes=[
            pltpu.VMEM((rows, 2 * CH), F32),
            pltpu.VMEM((rows, 2 * CH), F32),
            pltpu.VMEM((16 * CH // share_rows, patches, share_rows), BF16),
            pltpu.VMEM((16 * CH // share_rows, patches, share_rows), F32),
            pltpu.VMEM((patches, VW), BF16),
            pltpu.VMEM((VW,), F32),
            pltpu.VMEM((VW,), F32),
            pltpu.VMEM((1, VW), F32),
            pltpu.SemaphoreType.DMA((4,)),
        ],
        compiler_params=limits(16),
        cost_estimate=pl.CostEstimate(
            flops=6 * patches * 16 * CH * VW,
            bytes_accessed=2 * 16 * CH * VW + 2 * patches * VW,
            transcendentals=0,
        ),
    )(place, latent, *embed_arrays, pos, pre, post, prompt, cot, modulated)


def spread_kernel(
    count, half, heads, place_ref, grad_ref, scale_ref, proj_ref, out_ref, scale_scr, proj_scr, sems
):
    width = heads * HD
    mine = pl.ds(pl.multiple_of(place_ref[2] * width, HD), width)
    copies = [
        pltpu.make_async_copy(scale_ref.at[:, mine], scale_scr, sems.at[0]),
        pltpu.make_async_copy(proj_ref.at[:, mine], proj_scr, sems.at[1]),
    ]
    for copy in copies:
        copy.start()
    for copy in copies:
        copy.wait()
    gain = 1.0 + scale_scr[...]
    proj = proj_scr[...]
    zero = jnp.zeros_like(proj)
    sides = (jnp.concatenate([proj, zero], axis=0), jnp.concatenate([zero, proj], axis=0))
    for src in range(count):
        grad = grad_ref[pl.ds(src * half, half), :]
        for side in range(2):
            rows = (mm(grad, sides[side]) * gain).astype(BF16)
            for head in range(heads):
                out_ref[0, head, pl.ds((2 * src + side) * half, half), :] = rows[
                    :, head * HD : (head + 1) * HD
                ]


def spread(place, grad, scales, proj, count, half, heads):
    return pl.pallas_call(
        functools.partial(spread_kernel, count, half, heads),
        out_shape=jax.ShapeDtypeStruct((1, heads, 2 * count * half, HD), BF16),
        in_specs=[SMEM_SPEC, VMEM_SPEC, HBM_SPEC, HBM_SPEC],
        out_specs=VMEM_SPEC,
        scratch_shapes=[
            pltpu.VMEM((1, heads * HD), F32),
            pltpu.VMEM((CH, heads * HD), BF16),
            pltpu.SemaphoreType.DMA((2,)),
        ],
        compiler_params=limits(),
        cost_estimate=pl.CostEstimate(
            flops=8 * count * half * CH * heads * HD,
            bytes_accessed=4 * count * half * heads * HD,
            transcendentals=0,
        ),
    )(place, grad, scales, proj)


def weight_kernel(out_factor, grad_ref, *refs):
    store_readout_grad(grad_ref[...], refs[0], out_factor, refs[1])


def weight_call(grad, modulated, out_factor):
    return pl.pallas_call(
        functools.partial(weight_kernel, out_factor),
        out_shape=jax.ShapeDtypeStruct((CH, modulated.shape[2]), BF16),
        in_specs=[VMEM_SPEC] * 2,
        out_specs=VMEM_SPEC,
        compiler_params=limits(),
    )(grad, modulated)


def finish_kernel(in_ref, out_ref):
    count, _, width = in_ref.shape
    for group in range(count):
        out_ref[:, pl.ds(group * width, width)] = in_ref[group].astype(F32)


def finish(blocks):
    return pl.pallas_call(
        finish_kernel,
        out_shape=jax.ShapeDtypeStruct((CH, HEADS * HD), F32),
        in_specs=[VMEM_SPEC],
        out_specs=VMEM_SPEC,
        compiler_params=limits(),
    )(blocks)


def swap(x, axis, mask):
    count = lax.axis_size(axis)
    return lax.ppermute(x, axis, [(i, i ^ mask) for i in range(count)])


def all_to_all(x, groups=None):
    return lax.all_to_all(
        x, "seq", split_axis=0, concat_axis=0, tiled=True, axis_index_groups=groups
    )


def swap_both(x, seq_mask, data_mask):
    seq_count, data_count = lax.axis_size("seq"), lax.axis_size("dp")
    pairs = [
        (i * data_count + j, (i ^ seq_mask) * data_count + (j ^ data_mask))
        for i in range(seq_count)
        for j in range(data_count)
    ]
    return lax.ppermute(x, ("seq", "dp"), pairs)


def on_device(
    queries,
    keys,
    values,
    shifts,
    scales,
    proj_out,
    patch_embed,
    pos_embed,
    pre_gain,
    post_gain,
    prompt,
    cotangent,
):
    seq_count = lax.axis_size("seq")
    data_count = lax.axis_size("dp")
    tok_rows = queries.shape[1]
    sizes = Sizes(seq_count, data_count, tok_rows, patch_embed)
    query_parts, head_count, part_rows = sizes.query_parts, sizes.heads, sizes.part_rows
    group_count = HEADS // head_count
    seq_index = lax.axis_index("seq")
    head_group = seq_index // query_parts
    query_part = seq_index % query_parts
    half = part_rows // 2
    lat_rows = seq_count * tok_rows
    grid_rows = lat_rows // GW
    canonical = part_rows == 2 * GW
    place = jnp.stack([seq_index, lax.axis_index("dp"), head_group]).astype(jnp.int32)
    proj_turned = proj_out.T
    out_factor = 1.0 / math.sqrt(data_count * lat_rows)

    masks = sizes.pieces()
    packed = pack(
        sizes, in_hbm(queries), in_hbm(keys), in_hbm(values), in_hbm(patch_embed)
    )
    received = [swap(x, "seq", mask) if mask else x for mask, x in zip(masks, packed)]
    bits = [1 << b for b in reversed(range(data_count.bit_length() - 1))]
    shared = sizes.share < patch_embed.shape[0]
    if sizes.riding:
        ride = [slot for slot, mask in enumerate(masks) if sizes.rides(mask)]
        two = collect(sizes, [received[slot] for slot in ride])
        held = join(two, swap(two, "seq", 2), received[:-1])
        ride_masks = [masks[slot] for slot in ride]
        ride_masks = ride_masks + [mask ^ 2 for mask in ride_masks]
        pairs = [
            (held, swap(held, "seq", 1)),
            (swap(held, "dp", bits[0]), swap_both(held, 1, bits[0])),
        ]

    modulated, latent_part = attend(
        sizes, masks, place, received, in_hbm(scales), in_hbm(shifts), in_hbm(proj_turned)
    )

    if not sizes.riding:
        mine = patch_embed
        if shared:
            mine = lax.dynamic_slice_in_dim(
                patch_embed, lax.axis_index("dp") * sizes.share, sizes.share, 0
            )
        mine = lax.all_gather(mine, "seq", axis=1, tiled=True).reshape(-1, VW)
        embed = [(mine[None], [0])]
        if shared:
            embed = embed + [(swap(mine[None], "dp", bits[0]), [bits[0]])]

    groups = None
    if query_parts > 1:
        groups = [[g * query_parts + r for g in range(group_count)] for r in range(query_parts)]
    per_share = seq_count // group_count
    parts = all_to_all(latent_part.reshape(group_count, per_share * half, 2 * CH), groups)
    summed = total_copies([parts], seq_count)
    if sizes.riding:
        embed = [(arrange(sizes, ride_masks, place, pairs, summed), [0, bits[0]])]
    for bit in bits[1:] if shared else []:
        embed = embed + [(swap(x, "dp", bit), [m ^ bit for m in some]) for x, some in embed]
    latent = all_to_all(summed)
    if canonical:
        latent = latent.reshape(lat_rows // 2, 2 * CH)
    else:
        latent = latent.reshape(group_count, query_parts, per_share, half, 2, CH)
        latent = latent.transpose(0, 2, 1, 4, 3, 5).reshape(grid_rows // 2, 2, GW, CH)
        latent = latent.transpose(0, 2, 1, 3).reshape(lat_rows // 2, 2 * CH)

    reward, grad, weight = reward_head(
        place, latent, embed, in_hbm(pos_embed), in_hbm(pre_gain), in_hbm(post_gain), in_hbm(prompt),
        cotangent, modulated, grid_rows, canonical, out_factor,
    )
    if not canonical:
        tokens = grad.reshape(grid_rows // 2, GW, 2, CH).transpose(0, 2, 1, 3)
        tokens = tokens.reshape(seq_count, query_parts, 2, half, CH)
        tokens = lax.dynamic_index_in_dim(tokens, query_part, 1, keepdims=False)
        grad = tokens.transpose(0, 2, 1, 3).reshape(seq_count * half, 2 * CH)
        weight = weight_call(grad, modulated, out_factor)

    parts = [weight] + [swap(weight, "dp", mask) for mask in range(1, data_count)]
    attn_grad = spread(place, grad, in_hbm(scales), in_hbm(proj_turned), seq_count, half, head_count)
    if query_parts > 1:
        total = total_copies(parts, 1)[0]
        parts = [total] + [swap(total, "seq", mask) for mask in range(1, query_parts)]
    blocks = all_to_all(total_copies(parts, group_count), groups)
    return (reward[0, :1], attn_grad, finish(blocks).T)


def solution(mesh):
    return jax.shard_map(
        on_device,
        mesh=mesh,
        in_specs=(
            P("dp", "seq", None),
            P("dp", "seq", None),
            P("dp", "seq", None),
            P("dp", None),
            P("dp", None),
            P(),
            P(None, "seq", None),
            P(),
            P(),
            P(),
            P("dp", None),
            P("dp"),
        ),
        out_specs=(P("dp"), P("dp", "seq", None, None), P()),
        check_vma=False,
    )
```

```python
import functools
import math

import jax
import jax.numpy as jnp
from jax import lax
from jax.experimental import pallas as pl
from jax.experimental.pallas import tpu as pltpu
from jax.sharding import PartitionSpec as P

HEADS = 16
HD = 128
CH = 64
GW = 64
VW = 1280
EPS = 1e-05
BF16 = jnp.bfloat16
F32 = jnp.float32


def mm(a, b):
    return jnp.dot(a, b, preferred_element_type=F32)


def mm_nt(a, b):
    return lax.dot_general(a, b, (((1,), (1,)), ((), ())), preferred_element_type=F32)


def mm_tn(a, b):
    return lax.dot_general(a, b, (((0,), (0,)), ((), ())), preferred_element_type=F32)


SMEM_SPEC = pl.BlockSpec(memory_space=pltpu.SMEM)
VMEM_SPEC = pl.BlockSpec(memory_space=pltpu.VMEM)
HBM_SPEC = pl.BlockSpec(memory_space=pltpu.HBM)
ANY_SPEC = pl.BlockSpec(memory_space=pl.ANY)


def in_hbm(x):
    return pltpu.with_memory_space_constraint(x, pltpu.HBM)


def limits(mib=4):
    return pltpu.CompilerParams(vmem_limit_bytes=mib * 1024 * 1024)


class Sizes:
    def __init__(self, seq_count, data_count, tok_rows, patch_embed):
        self.count = seq_count
        self.query_parts = max(1, seq_count // HEADS)
        self.heads = max(1, HEADS // seq_count)
        self.width = self.heads * HD
        self.tok_rows = tok_rows
        self.part_rows = tok_rows // self.query_parts
        positions, self.local, _ = patch_embed.shape
        self.share = positions // data_count if positions % data_count == 0 else positions
        self.rows = self.part_rows + 2 * tok_rows
        self.share_rows = self.share * self.local
        self.chunks = VW // HD
        self.riding = self.local % 8 == 0 and self.share_rows % 16 == 0 and seq_count == 8
        self.riding = self.riding and 1 < data_count <= positions
        self.ride_rows = self.chunks * self.share_rows if self.riding else 0

    def pieces(self):
        return list(range(1, self.count)) + [0]

    def rides(self, mask):
        return self.riding and mask in (0, 4)

    def piece_shape(self, mask):
        return (self.rows + (self.ride_rows // self.heads if self.rides(mask) else 0), self.width)

    def ride_slices(self):
        deep = self.ride_rows // self.heads
        return [
            (pl.ds(self.rows, deep), pl.ds(at * HD, HD), pl.ds(at * deep, deep))
            for at in range(self.heads)
        ]


def pack_kernel(sizes, q_ref, k_ref, v_ref, embed_ref, *refs):
    pieces = sizes.pieces()
    out_refs = refs[: len(pieces)]
    q_scr, k_scr, v_scr, embed_scr, share_scr, in_sems, out_sems = refs[len(pieces) :]
    me = lax.axis_index("seq")
    tok_rows, part_rows, width = sizes.tok_rows, sizes.part_rows, sizes.width
    share = pl.ds(lax.axis_index("dp") * sizes.share, sizes.share)
    loads = [
        pltpu.make_async_copy(embed_ref.at[share], embed_scr, in_sems.at[3]),
        pltpu.make_async_copy(q_ref.at[0], q_scr, in_sems.at[0]),
        pltpu.make_async_copy(k_ref.at[0], k_scr, in_sems.at[1]),
        pltpu.make_async_copy(v_ref.at[0], v_scr, in_sems.at[2]),
    ]
    for load in loads:
        load.start()
    sent = [[], [], [], []]
    for slot, (mask, out) in enumerate(zip(pieces, out_refs)):
        dest = jnp.bitwise_xor(me, mask)
        group, part = dest // sizes.query_parts, dest % sizes.query_parts
        cols = pl.ds(pl.multiple_of(group * width, HD), width)
        first = pl.ds(pl.multiple_of(part * part_rows, part_rows), part_rows)
        for kind, source, rows in (
            (0, q_scr.at[first, cols], pl.ds(0, part_rows)),
            (1, k_scr.at[:, cols], pl.ds(part_rows, tok_rows)),
            (2, v_scr.at[:, cols], pl.ds(part_rows + tok_rows, tok_rows)),
        ):
            sent[kind].append(pltpu.make_async_copy(source, out.at[rows], out_sems.at[kind, slot]))
        if sizes.rides(mask):
            for at, (rows, place, from_rows) in enumerate(sizes.ride_slices()):
                sent[3].append(
                    pltpu.make_async_copy(
                        share_scr.at[from_rows], out.at[rows, place], out_sems.at[3 + at, slot]
                    )
                )
    loads[0].wait()
    if sizes.riding:
        for chunk in range(sizes.chunks):
            cols = embed_scr[:, :, pl.ds(chunk * HD, HD)].astype(F32)
            share_scr[pl.ds(chunk * sizes.share_rows, sizes.share_rows), :] = cols.reshape(
                sizes.share_rows, HD
            ).astype(BF16)
    for store in sent[3]:
        store.start()
    for kind in range(3):
        loads[kind + 1].wait()
        for store in sent[kind]:
            store.start()
    for stores in sent:
        for store in stores:
            store.wait()


def pack(sizes, queries, keys, values, patch_embed):
    tok_rows, full = queries.shape[1:]
    pieces = sizes.pieces()
    return pl.pallas_call(
        functools.partial(pack_kernel, sizes),
        out_shape=[jax.ShapeDtypeStruct(sizes.piece_shape(mask), BF16) for mask in pieces],
        in_specs=[HBM_SPEC] * 4,
        out_specs=[HBM_SPEC] * len(pieces),
        scratch_shapes=[pltpu.VMEM((tok_rows, full), BF16)] * 3
        + [
            pltpu.VMEM((sizes.share,) + patch_embed.shape[1:], BF16),
            pltpu.VMEM((max(16, sizes.ride_rows), HD), BF16),
            pltpu.SemaphoreType.DMA((4,)),
            pltpu.SemaphoreType.DMA((3 + sizes.heads, len(pieces))),
        ],
        compiler_params=limits(),
        cost_estimate=pl.CostEstimate(
            flops=0, bytes_accessed=12 * tok_rows * full, transcendentals=0
        ),
    )(queries, keys, values, patch_embed)


def collect_kernel(sizes, *refs):
    *in_refs, out_ref, sems = refs
    copies = []
    for slot, ref in enumerate(in_refs):
        for at, (rows, cols, to_rows) in enumerate(sizes.ride_slices()):
            copies.append(
                pltpu.make_async_copy(
                    ref.at[rows, cols], out_ref.at[slot, to_rows], sems.at[at, slot]
                )
            )
    for copy in copies:
        copy.start()
    for copy in copies:
        copy.wait()


def collect(sizes, arrays):
    return pl.pallas_call(
        functools.partial(collect_kernel, sizes),
        out_shape=jax.ShapeDtypeStruct((len(arrays), sizes.ride_rows, HD), BF16),
        in_specs=[ANY_SPEC] * len(arrays),
        out_specs=VMEM_SPEC,
        scratch_shapes=[pltpu.SemaphoreType.DMA((sizes.heads, len(arrays)))],
        compiler_params=limits(),
    )(*arrays)


def join_kernel(first_ref, second_ref, *refs):
    out_ref = refs[-1]
    count = first_ref.shape[0]
    out_ref[:count] = first_ref[...]
    out_ref[count:] = second_ref[...]


def join(first, second, others):
    return pl.pallas_call(
        join_kernel,
        out_shape=jax.ShapeDtypeStruct((2 * first.shape[0],) + first.shape[1:], BF16),
        in_specs=[VMEM_SPEC] * 2 + [ANY_SPEC] * len(others),
        out_specs=VMEM_SPEC,
        compiler_params=limits(),
    )(first, second, *others)


def arrange_kernel(sizes, masks, place_ref, *refs):
    *pair_refs, out_ref = refs[:-2] + refs[-1:]
    me = place_ref[0]
    odd = me % 2 == 1
    local = sizes.local
    for quarter in range(len(pair_refs) // 2):
        held_ref, got_ref = pair_refs[2 * quarter], pair_refs[2 * quarter + 1]
        for slot, mask in enumerate(masks):
            pair = jnp.bitwise_xor(me, mask) // 2
            for chunk in range(sizes.chunks):
                rows = pl.ds(chunk * sizes.share_rows, sizes.share_rows)
                held = held_ref[slot, rows, :].astype(F32)
                got = got_ref[slot, rows, :].astype(F32)
                first = jnp.where(odd, got, held)
                second = jnp.where(odd, held, got)
                for at in range(sizes.share):
                    part = slice(at * local, (at + 1) * local)
                    both = jnp.concatenate([first[part], second[part]], axis=0).astype(BF16)
                    start = pl.multiple_of(at * sizes.count * local + pair * 2 * local, 2 * local)
                    out_ref[quarter, pl.ds(start, 2 * local), pl.ds(chunk * HD, HD)] = both


def arrange(sizes, masks, place, pairs, wait):
    rows = sizes.share * sizes.count * sizes.local
    flat = [x for pair in pairs for x in pair]
    return pl.pallas_call(
        functools.partial(arrange_kernel, sizes, masks),
        out_shape=jax.ShapeDtypeStruct((len(pairs), rows, VW), BF16),
        in_specs=[SMEM_SPEC] + [VMEM_SPEC] * (len(flat) + 1),
        out_specs=VMEM_SPEC,
        compiler_params=limits(),
    )(place, *flat, wait)


FACTOR = HD ** (-0.5) * math.log2(math.e)


def load_pieces(sizes, in_refs, query_scr, key_scr, value_scr, sems):
    tok_rows, part_rows = sizes.tok_rows, sizes.part_rows
    copies = []
    for src, ref in enumerate(in_refs):
        rows = pl.ds(src * tok_rows, tok_rows)
        copies += [
            pltpu.make_async_copy(ref.at[pl.ds(0, part_rows)], query_scr.at[src], sems.at[0, src]),
            pltpu.make_async_copy(
                ref.at[pl.ds(part_rows, tok_rows)], key_scr.at[rows], sems.at[1, src]
            ),
        ]
        for head in range(sizes.heads):
            copies.append(
                pltpu.make_async_copy(
                    ref.at[pl.ds(part_rows + tok_rows, tok_rows), pl.ds(head * HD, HD)],
                    value_scr.at[rows, pl.ds(2 * head * HD, HD)],
                    sems.at[2 + head, src],
                )
            )
    for copy in copies:
        copy.start()
    ones = jnp.ones((len(in_refs) * tok_rows, HD), BF16)
    for head in range(sizes.heads):
        value_scr[:, pl.ds((2 * head + 1) * HD, HD)] = ones
    return copies


def soft_part(query, key_scr, value_scr, rows, head, before):
    logits = mm_nt(query, key_scr[rows, pl.ds(head * HD, HD)])
    top = jnp.max(logits, axis=-1, keepdims=True)
    if before:
        top = jnp.maximum(top, before[2])
    weights = jnp.exp2((logits - top) * FACTOR).astype(BF16)
    both = mm(weights, value_scr[rows, pl.ds(2 * head * HD, 2 * HD)])
    mixed, total = both[:, :HD], both[:, HD:]
    if before:
        shrink = jnp.exp2((before[2] - top) * FACTOR)
        mixed, total = mixed + before[0] * shrink, total + before[1] * shrink
    return mixed, total, top


def piece_scratch(sizes, count):
    lat_rows = count * sizes.tok_rows
    return [
        pltpu.VMEM((count, sizes.part_rows, sizes.width), BF16),
        pltpu.VMEM((lat_rows, sizes.width), BF16),
        pltpu.VMEM((lat_rows, 2 * sizes.width), BF16),
        pltpu.SemaphoreType.DMA((2 + sizes.heads, count)),
    ]


def early_kernel(sizes, count, *refs):
    in_refs, refs = refs[:count], refs[count:]
    sum_ref, stat_ref, query_scr, key_scr, value_scr, sems = refs
    for copy in load_pieces(sizes, in_refs, query_scr, key_scr, value_scr, sems):
        copy.wait()
    left = lax.broadcasted_iota(jnp.int32, (sizes.part_rows, HD), 1) < HD // 2
    rows = pl.ds(0, count * sizes.tok_rows)
    for src in range(count):
        results = [
            soft_part(
                query_scr[src, :, pl.ds(head * HD, HD)], key_scr, value_scr, rows, head, None
            )
            for head in range(sizes.heads)
        ]
        for head, (mixed, total, top) in enumerate(results):
            sum_ref[src, head] = mixed
            stat_ref[src, head] = jnp.where(left, top, total)


def attend_early(sizes, received):
    count = len(received)
    shape = jax.ShapeDtypeStruct((count, sizes.heads, sizes.part_rows, HD), F32)
    return pl.pallas_call(
        functools.partial(early_kernel, sizes, count),
        out_shape=(shape, shape),
        in_specs=[ANY_SPEC] * count,
        out_specs=(VMEM_SPEC, VMEM_SPEC),
        scratch_shapes=piece_scratch(sizes, count),
        compiler_params=limits(12),
        cost_estimate=pl.CostEstimate(flops=1, bytes_accessed=1, transcendentals=0),
    )(*received)


def attend_kernel(sizes, masks, early, place_ref, *refs):
    count, heads, width = sizes.count, sizes.heads, sizes.width
    tok_rows, part_rows = sizes.tok_rows, sizes.part_rows
    in_refs, refs = refs[:count], refs[count:]
    kept_refs, refs = refs[: 2 if early else 0], refs[2 if early else 0 :]
    scale_ref, shift_ref, proj_ref, mod_ref, lat_ref, *refs = refs
    query_scr, key_scr, value_scr, sems, scale_scr, shift_scr, proj_scr, side_sems, *kept_scr = refs
    half = part_rows // 2
    me = place_ref[0]
    mine = pl.ds(pl.multiple_of(place_ref[2] * width, HD), width)
    copies = load_pieces(sizes, in_refs, query_scr, key_scr, value_scr, sems)
    others = [
        pltpu.make_async_copy(scale_ref.at[:, mine], scale_scr, side_sems.at[0]),
        pltpu.make_async_copy(shift_ref.at[:, mine], shift_scr, side_sems.at[1]),
        pltpu.make_async_copy(proj_ref.at[:, mine], proj_scr, side_sems.at[2]),
    ]
    for slot, (ref, scr) in enumerate(zip(kept_refs, kept_scr)):
        others.append(pltpu.make_async_copy(ref, scr, side_sems.at[3 + slot]))
    for copy in others:
        copy.start()
    for copy in copies + others:
        copy.wait()
    gain = 1.0 + scale_scr[...]
    shift = shift_scr[...]
    proj = proj_scr[...]
    zero = jnp.zeros_like(proj)
    proj_pair = jnp.concatenate(
        [jnp.concatenate([proj, zero], axis=1), jnp.concatenate([zero, proj], axis=1)], axis=0
    )
    together = 2
    for first in range(0, count, together):
        results = []
        for src in range(first, first + together):
            mixed = []
            for head in range(heads):
                before = None
                rows = pl.ds(0, count * tok_rows)
                if src < early:
                    rows = pl.ds(early * tok_rows, (count - early) * tok_rows)
                    stat = kept_scr[1][src, head]
                    before = (kept_scr[0][src, head], stat[:, HD - 1 :], stat[:, :1])
                query = query_scr[src, :, pl.ds(head * HD, HD)]
                value, total, _ = soft_part(query, key_scr, value_scr, rows, head, before)
                mixed.append(value / total)
            attended = jnp.concatenate(mixed, axis=1) if heads > 1 else mixed[0]
            modulated = (attended * gain + shift).astype(BF16)
            pair = jnp.concatenate([modulated[:half], modulated[half:]], axis=1)
            results.append((modulated, mm_nt(pair, proj_pair).astype(BF16)))
        for at, (modulated, latent) in enumerate(results):
            place = jnp.bitwise_xor(me, masks[first + at])
            mod_ref[place] = modulated
            lat_ref[place] = latent


def attend(sizes, masks, place, received, kept, scales, shifts, proj):
    count, width, heads = sizes.count, sizes.width, sizes.heads
    lat_rows = count * sizes.tok_rows
    query_rows = count * sizes.part_rows
    early = kept[0].shape[0] if kept else 0
    return pl.pallas_call(
        functools.partial(attend_kernel, sizes, masks, early),
        out_shape=(
            jax.ShapeDtypeStruct((count, sizes.part_rows, width), BF16),
            jax.ShapeDtypeStruct((count, sizes.part_rows // 2, 2 * CH), BF16),
        ),
        in_specs=[SMEM_SPEC] + [ANY_SPEC] * (count + len(kept)) + [HBM_SPEC] * 3,
        out_specs=(VMEM_SPEC, VMEM_SPEC),
        scratch_shapes=piece_scratch(sizes, count)
        + [
            pltpu.VMEM((1, width), F32),
            pltpu.VMEM((1, width), F32),
            pltpu.VMEM((CH, width), BF16),
            pltpu.SemaphoreType.DMA((5,)),
        ]
        + [pltpu.VMEM(x.shape, F32) for x in kept],
        compiler_params=limits(16),
        cost_estimate=pl.CostEstimate(
            flops=4 * query_rows * lat_rows * width,
            bytes_accessed=2 * (query_rows * 2 + lat_rows * 2) * width,
            transcendentals=query_rows * lat_rows * heads,
        ),
    )(place, *received, *kept, scales, shifts, proj)


def total_kernel(copies, *refs):
    out_ref = refs[-1]
    if len(refs) == 2:
        parts = [refs[0][i].astype(F32) for i in range(refs[0].shape[0])]
    else:
        parts = [ref[...].astype(F32) for ref in refs[:-1]]
    while len(parts) > 1:
        parts = [parts[i] + parts[i + 1] for i in range(0, len(parts), 2)]
    for copy in range(copies):
        out_ref[copy] = parts[0].astype(BF16)


def total_copies(arrays, copies):
    return pl.pallas_call(
        functools.partial(total_kernel, copies),
        out_shape=jax.ShapeDtypeStruct((copies,) + arrays[0].shape[-2:], BF16),
        in_specs=[VMEM_SPEC] * len(arrays),
        out_specs=VMEM_SPEC,
        compiler_params=limits(),
    )(*arrays)


def lane_mean(x, count):
    return jnp.sum(x, axis=-1, keepdims=True) * (1.0 / count)


def head_kernel(grid_rows, fused, embed_masks, out_factor, place_ref, lat_ref, *refs):
    embed_refs, refs = refs[: len(embed_masks)], refs[len(embed_masks) :]
    sides, refs = refs[:4], refs[4:]
    cot_ref, refs = refs[0], refs[1:]
    mod_ref, refs = refs[0], refs[1:]
    reward_ref, grad_ref, weight_ref, lat_scr, grad_scr, block_scr, back_scr, *refs = refs
    pos_ref, pre_ref, post_ref, prompt_ref, side_sems = refs
    patch_rows = grid_rows // 4
    patch_cols = GW // 4
    patches = patch_rows * patch_cols
    copies = []
    for slot, (side, scr) in enumerate(zip(sides, (pos_ref, pre_ref, post_ref, prompt_ref))):
        copies.append(pltpu.make_async_copy(side, scr, side_sems.at[slot]))
    for copy in copies:
        copy.start()
    lat_scr[...] = lat_ref[...].astype(F32)

    data = place_ref[1]
    shares = [
        (jnp.bitwise_xor(data, mask), ref, slot)
        for ref, masks in zip(embed_refs, embed_masks)
        for slot, mask in enumerate(masks)
    ]
    share_rows = embed_refs[0].shape[1]
    for hi in range(2):
        wide = []
        for tx in range(4):
            rows = [
                lat_scr[pl.ds((2 * pr + hi) * GW + tx, patch_cols, stride=4), :]
                for pr in range(patch_rows)
            ]
            wide.append(jnp.concatenate(rows, axis=0))
        for side in range(2):
            lanes = slice(side * CH, (side + 1) * CH)
            line = jnp.concatenate([x[:, lanes] for x in wide], axis=1).astype(BF16)
            first = (2 * hi + side) * 4 * CH
            if share_rows >= 4 * CH:
                at = first % share_rows
                block_scr[first // share_rows, :, pl.ds(at, 4 * CH)] = line
            else:
                for at in range(0, 4 * CH, share_rows):
                    block_scr[(first + at) // share_rows] = line[:, at : at + share_rows]
    for copy in copies:
        copy.wait()
    embedded = pos_ref[...].astype(F32)
    for number, ref, slot in shares:
        embedded = embedded + mm(block_scr[number], ref[slot])
    pre = pre_ref[...].reshape(1, VW)
    post = post_ref[...].reshape(1, VW)
    prompt = prompt_ref[...]
    center = embedded - lane_mean(embedded, VW)
    rstd = lax.rsqrt(lane_mean(center * center, VW) + EPS)
    unit = center * rstd
    pooled = jnp.sum(unit, axis=0, keepdims=True) * (1.0 / patches) * pre
    pooled_center = pooled - lane_mean(pooled, VW)
    pooled_rstd = lax.rsqrt(lane_mean(pooled_center * pooled_center, VW) + EPS)
    pooled_unit = pooled_center * pooled_rstd
    final = pooled_unit * post
    dot = jnp.sum(final * prompt, axis=-1, keepdims=True)
    final_sq = jnp.sum(final * final, axis=-1, keepdims=True)
    prompt_sq = jnp.sum(prompt * prompt, axis=-1, keepdims=True)
    final_len = jnp.sqrt(final_sq)
    prompt_len = jnp.sqrt(prompt_sq)
    cosine = dot / (final_len * prompt_len)
    reward_ref[...] = jnp.broadcast_to(100.0 * cosine, reward_ref.shape)
    cot = cot_ref[0]
    final_grad = (100.0 * cot) * (prompt / (final_len * prompt_len) - final * (cosine / final_sq))
    unit_grad = final_grad * post
    pooled_grad = pooled_rstd * (
        unit_grad
        - lane_mean(unit_grad, VW)
        - pooled_unit * lane_mean(unit_grad * pooled_unit, VW)
    )
    flow = pooled_grad * pre * (1.0 / patches)
    embed_grad = rstd * (flow - lane_mean(flow, VW) - unit * lane_mean(flow * unit, VW))
    high = embed_grad.astype(BF16)
    low = (embed_grad - high.astype(F32)).astype(BF16)
    stacked = jnp.concatenate([high, low], axis=0)
    for number, ref, slot in shares:
        both = mm_nt(stacked, ref[slot])
        back_scr[number] = both[:patches] + both[patches:]
    back = jnp.concatenate([back_scr[i] for i in range(16 * CH // share_rows)], axis=1)
    for hi in range(2):
        for tx in range(4):
            first = (4 * (2 * hi) + tx) * CH
            second = (4 * (2 * hi + 1) + tx) * CH
            piece = jnp.concatenate(
                [back[:, first : first + CH], back[:, second : second + CH]], axis=1
            )
            for pr in range(patch_rows):
                grad_scr[pl.ds((2 * pr + hi) * GW + tx, patch_cols, stride=4), :] = piece[
                    pr * patch_cols : (pr + 1) * patch_cols
                ]
    grad = grad_scr[...].astype(BF16)
    grad_ref[...] = grad
    if fused:
        store_readout_grad(grad, mod_ref, out_factor, weight_ref)
    else:
        weight_ref[...] = jnp.zeros_like(weight_ref)


def store_readout_grad(grad, mod_ref, out_factor, out_ref):
    turned = grad.astype(F32).T.astype(BF16)
    count, rows, width = mod_ref.shape
    half = rows // 2
    first = mod_ref[:, :half, :].reshape(count * half, width)
    second = mod_ref[:, half:, :].reshape(count * half, width)
    total = mm(turned[:CH], first) + mm(turned[CH:], second)
    out_ref[...] = (total * out_factor).astype(BF16)


def reward_head(
    place, latent, embed, pos, pre, post, prompt, cot, modulated, grid_rows, fused, out_factor
):
    patches = grid_rows * GW // 16
    rows = grid_rows * GW // 2
    width = modulated.shape[2]
    embed_arrays, embed_masks = [x for x, _ in embed], [masks for _, masks in embed]
    share_rows = embed_arrays[0].shape[1]
    return pl.pallas_call(
        functools.partial(head_kernel, grid_rows, fused, embed_masks, out_factor),
        out_shape=(
            jax.ShapeDtypeStruct((1, 128), F32),
            jax.ShapeDtypeStruct((rows, 2 * CH), BF16),
            jax.ShapeDtypeStruct((CH, width), BF16),
        ),
        in_specs=[SMEM_SPEC, VMEM_SPEC]
        + [VMEM_SPEC] * len(embed_arrays)
        + [HBM_SPEC] * 4
        + [SMEM_SPEC, VMEM_SPEC],
        out_specs=(VMEM_SPEC, VMEM_SPEC, VMEM_SPEC),
        scratch_shapes=[
            pltpu.VMEM((rows, 2 * CH), F32),
            pltpu.VMEM((rows, 2 * CH), F32),
            pltpu.VMEM((16 * CH // share_rows, patches, share_rows), BF16),
            pltpu.VMEM((16 * CH // share_rows, patches, share_rows), F32),
            pltpu.VMEM((patches, VW), BF16),
            pltpu.VMEM((VW,), F32),
            pltpu.VMEM((VW,), F32),
            pltpu.VMEM((1, VW), F32),
            pltpu.SemaphoreType.DMA((4,)),
        ],
        compiler_params=limits(16),
        cost_estimate=pl.CostEstimate(
            flops=6 * patches * 16 * CH * VW,
            bytes_accessed=2 * 16 * CH * VW + 2 * patches * VW,
            transcendentals=0,
        ),
    )(place, latent, *embed_arrays, pos, pre, post, prompt, cot, modulated)


def spread_kernel(
    count, half, heads, place_ref, grad_ref, scale_ref, proj_ref, out_ref, scale_scr, proj_scr, sems
):
    width = heads * HD
    mine = pl.ds(pl.multiple_of(place_ref[2] * width, HD), width)
    copies = [
        pltpu.make_async_copy(scale_ref.at[:, mine], scale_scr, sems.at[0]),
        pltpu.make_async_copy(proj_ref.at[:, mine], proj_scr, sems.at[1]),
    ]
    for copy in copies:
        copy.start()
    for copy in copies:
        copy.wait()
    gain = 1.0 + scale_scr[...]
    proj = proj_scr[...]
    zero = jnp.zeros_like(proj)
    sides = (jnp.concatenate([proj, zero], axis=0), jnp.concatenate([zero, proj], axis=0))
    for src in range(count):
        grad = grad_ref[pl.ds(src * half, half), :]
        for side in range(2):
            rows = (mm(grad, sides[side]) * gain).astype(BF16)
            for head in range(heads):
                out_ref[0, head, pl.ds((2 * src + side) * half, half), :] = rows[
                    :, head * HD : (head + 1) * HD
                ]


def spread(place, grad, scales, proj, count, half, heads):
    return pl.pallas_call(
        functools.partial(spread_kernel, count, half, heads),
        out_shape=jax.ShapeDtypeStruct((1, heads, 2 * count * half, HD), BF16),
        in_specs=[SMEM_SPEC, VMEM_SPEC, HBM_SPEC, HBM_SPEC],
        out_specs=VMEM_SPEC,
        scratch_shapes=[
            pltpu.VMEM((1, heads * HD), F32),
            pltpu.VMEM((CH, heads * HD), BF16),
            pltpu.SemaphoreType.DMA((2,)),
        ],
        compiler_params=limits(),
        cost_estimate=pl.CostEstimate(
            flops=8 * count * half * CH * heads * HD,
            bytes_accessed=4 * count * half * heads * HD,
            transcendentals=0,
        ),
    )(place, grad, scales, proj)


def weight_kernel(out_factor, grad_ref, *refs):
    store_readout_grad(grad_ref[...], refs[0], out_factor, refs[1])


def weight_call(grad, modulated, out_factor):
    return pl.pallas_call(
        functools.partial(weight_kernel, out_factor),
        out_shape=jax.ShapeDtypeStruct((CH, modulated.shape[2]), BF16),
        in_specs=[VMEM_SPEC] * 2,
        out_specs=VMEM_SPEC,
        compiler_params=limits(),
    )(grad, modulated)


def finish_kernel(in_ref, out_ref):
    count, _, width = in_ref.shape
    for group in range(count):
        out_ref[:, pl.ds(group * width, width)] = in_ref[group].astype(F32)


def finish(blocks):
    return pl.pallas_call(
        finish_kernel,
        out_shape=jax.ShapeDtypeStruct((CH, HEADS * HD), F32),
        in_specs=[VMEM_SPEC],
        out_specs=VMEM_SPEC,
        compiler_params=limits(),
    )(blocks)


def swap(x, axis, mask):
    count = lax.axis_size(axis)
    return lax.ppermute(x, axis, [(i, i ^ mask) for i in range(count)])


def all_to_all(x, groups=None):
    return lax.all_to_all(
        x, "seq", split_axis=0, concat_axis=0, tiled=True, axis_index_groups=groups
    )


def swap_both(x, seq_mask, data_mask):
    seq_count, data_count = lax.axis_size("seq"), lax.axis_size("dp")
    pairs = [
        (i * data_count + j, (i ^ seq_mask) * data_count + (j ^ data_mask))
        for i in range(seq_count)
        for j in range(data_count)
    ]
    return lax.ppermute(x, ("seq", "dp"), pairs)


def on_device(
    queries,
    keys,
    values,
    shifts,
    scales,
    proj_out,
    patch_embed,
    pos_embed,
    pre_gain,
    post_gain,
    prompt,
    cotangent,
):
    seq_count = lax.axis_size("seq")
    data_count = lax.axis_size("dp")
    tok_rows = queries.shape[1]
    sizes = Sizes(seq_count, data_count, tok_rows, patch_embed)
    query_parts, head_count, part_rows = sizes.query_parts, sizes.heads, sizes.part_rows
    group_count = HEADS // head_count
    seq_index = lax.axis_index("seq")
    head_group = seq_index // query_parts
    query_part = seq_index % query_parts
    half = part_rows // 2
    lat_rows = seq_count * tok_rows
    grid_rows = lat_rows // GW
    canonical = part_rows == 2 * GW
    place = jnp.stack([seq_index, lax.axis_index("dp"), head_group]).astype(jnp.int32)
    proj_turned = proj_out.T
    out_factor = 1.0 / math.sqrt(data_count * lat_rows)

    masks = sizes.pieces()
    packed = pack(
        sizes, in_hbm(queries), in_hbm(keys), in_hbm(values), in_hbm(patch_embed)
    )
    received = [swap(x, "seq", mask) if mask else x for mask, x in zip(masks, packed)]
    bits = [1 << b for b in reversed(range(data_count.bit_length() - 1))]
    shared = sizes.share < patch_embed.shape[0]
    if sizes.riding:
        ride = [slot for slot, mask in enumerate(masks) if sizes.rides(mask)]
        two = collect(sizes, [received[slot] for slot in ride])
        held = join(two, swap(two, "seq", 2), received[:-1])
        ride_masks = [masks[slot] for slot in ride]
        ride_masks = ride_masks + [mask ^ 2 for mask in ride_masks]
        pairs = [
            (held, swap(held, "seq", 1)),
            (swap(held, "dp", bits[0]), swap_both(held, 1, bits[0])),
        ]

    kept, order = [], list(range(seq_count))
    if seq_count == 8:
        late = [slot for slot, mask in enumerate(masks) if mask in (6, 7)]
        order = [slot for slot in order if slot not in late]
        kept = attend_early(sizes, [received[slot] for slot in order])
        order = order + late
    modulated, latent_part = attend(
        sizes, [masks[slot] for slot in order], place, [received[slot] for slot in order], kept,
        in_hbm(scales), in_hbm(shifts), in_hbm(proj_turned)
    )

    if not sizes.riding:
        mine = patch_embed
        if shared:
            mine = lax.dynamic_slice_in_dim(
                patch_embed, lax.axis_index("dp") * sizes.share, sizes.share, 0
            )
        mine = lax.all_gather(mine, "seq", axis=1, tiled=True).reshape(-1, VW)
        embed = [(mine[None], [0])]
        if shared:
            embed = embed + [(swap(mine[None], "dp", bits[0]), [bits[0]])]

    groups = None
    if query_parts > 1:
        groups = [[g * query_parts + r for g in range(group_count)] for r in range(query_parts)]
    per_share = seq_count // group_count
    parts = all_to_all(latent_part.reshape(group_count, per_share * half, 2 * CH), groups)
    summed = total_copies([parts], seq_count)
    if sizes.riding:
        embed = [(arrange(sizes, ride_masks, place, pairs, summed), [0, bits[0]])]
    for bit in bits[1:] if shared else []:
        embed = embed + [(swap(x, "dp", bit), [m ^ bit for m in some]) for x, some in embed]
    latent = all_to_all(summed)
    if canonical:
        latent = latent.reshape(lat_rows // 2, 2 * CH)
    else:
        latent = latent.reshape(group_count, query_parts, per_share, half, 2, CH)
        latent = latent.transpose(0, 2, 1, 4, 3, 5).reshape(grid_rows // 2, 2, GW, CH)
        latent = latent.transpose(0, 2, 1, 3).reshape(lat_rows // 2, 2 * CH)

    reward, grad, weight = reward_head(
        place, latent, embed, in_hbm(pos_embed), in_hbm(pre_gain), in_hbm(post_gain), in_hbm(prompt),
        cotangent, modulated, grid_rows, canonical, out_factor,
    )
    if not canonical:
        tokens = grad.reshape(grid_rows // 2, GW, 2, CH).transpose(0, 2, 1, 3)
        tokens = tokens.reshape(seq_count, query_parts, 2, half, CH)
        tokens = lax.dynamic_index_in_dim(tokens, query_part, 1, keepdims=False)
        grad = tokens.transpose(0, 2, 1, 3).reshape(seq_count * half, 2 * CH)
        weight = weight_call(grad, modulated, out_factor)

    parts = [weight] + [swap(weight, "dp", mask) for mask in range(1, data_count)]
    attn_grad = spread(place, grad, in_hbm(scales), in_hbm(proj_turned), seq_count, half, head_count)
    if query_parts > 1:
        total = total_copies(parts, 1)[0]
        parts = [total] + [swap(total, "seq", mask) for mask in range(1, query_parts)]
    blocks = all_to_all(total_copies(parts, group_count), groups)
    return (reward[0, :1], attn_grad, finish(blocks).T)


def solution(mesh):
    return jax.shard_map(
        on_device,
        mesh=mesh,
        in_specs=(
            P("dp", "seq", None),
            P("dp", "seq", None),
            P("dp", "seq", None),
            P("dp", None),
            P("dp", None),
            P(),
            P(None, "seq", None),
            P(),
            P(),
            P(),
            P("dp", None),
            P("dp"),
        ),
        out_specs=(P("dp"), P("dp", "seq", None, None), P()),
        check_vma=False,
    )
```

```python
import functools
import math

import jax
import jax.numpy as jnp
from jax import lax
from jax.experimental import pallas as pl
from jax.experimental.pallas import tpu as pltpu
from jax.sharding import PartitionSpec as P

HEADS = 16
HD = 128
CH = 64
GW = 64
VW = 1280
EPS = 1e-05
BF16 = jnp.bfloat16
F32 = jnp.float32


def mm(a, b):
    return jnp.dot(a, b, preferred_element_type=F32)


def mm_nt(a, b):
    return lax.dot_general(a, b, (((1,), (1,)), ((), ())), preferred_element_type=F32)


def mm_tn(a, b):
    return lax.dot_general(a, b, (((0,), (0,)), ((), ())), preferred_element_type=F32)


SMEM_SPEC = pl.BlockSpec(memory_space=pltpu.SMEM)
VMEM_SPEC = pl.BlockSpec(memory_space=pltpu.VMEM)
HBM_SPEC = pl.BlockSpec(memory_space=pltpu.HBM)
ANY_SPEC = pl.BlockSpec(memory_space=pl.ANY)


def in_hbm(x):
    return pltpu.with_memory_space_constraint(x, pltpu.HBM)


def limits(mib=4):
    return pltpu.CompilerParams(vmem_limit_bytes=mib * 1024 * 1024)


class Sizes:
    def __init__(self, seq_count, data_count, tok_rows, patch_embed):
        self.count = seq_count
        self.query_parts = max(1, seq_count // HEADS)
        self.heads = max(1, HEADS // seq_count)
        self.width = self.heads * HD
        self.tok_rows = tok_rows
        self.part_rows = tok_rows // self.query_parts
        positions, self.local, _ = patch_embed.shape
        self.share = positions // data_count if positions % data_count == 0 else positions
        self.rows = self.part_rows + 2 * tok_rows
        self.share_rows = self.share * self.local
        self.chunks = VW // HD
        self.riding = self.local % 8 == 0 and self.share_rows % 16 == 0 and seq_count == 8
        self.riding = self.riding and 1 < data_count <= positions
        self.ride_rows = self.chunks * self.share_rows if self.riding else 0

    def pieces(self):
        return list(range(1, self.count)) + [0]

    def rides(self, mask):
        return self.riding and mask in (0, 4)

    def piece_shape(self, mask):
        return (self.rows + (self.ride_rows // self.heads if self.rides(mask) else 0), self.width)

    def ride_slices(self):
        deep = self.ride_rows // self.heads
        return [
            (pl.ds(self.rows, deep), pl.ds(at * HD, HD), pl.ds(at * deep, deep))
            for at in range(self.heads)
        ]


def pack_kernel(sizes, q_ref, k_ref, v_ref, embed_ref, *refs):
    pieces = sizes.pieces()
    out_refs = refs[: len(pieces)]
    q_scr, k_scr, v_scr, embed_scr, share_scr, in_sems, out_sems = refs[len(pieces) :]
    me = lax.axis_index("seq")
    tok_rows, part_rows, width = sizes.tok_rows, sizes.part_rows, sizes.width
    share = pl.ds(lax.axis_index("dp") * sizes.share, sizes.share)
    loads = [
        pltpu.make_async_copy(embed_ref.at[share], embed_scr, in_sems.at[3]),
        pltpu.make_async_copy(q_ref.at[0], q_scr, in_sems.at[0]),
        pltpu.make_async_copy(k_ref.at[0], k_scr, in_sems.at[1]),
        pltpu.make_async_copy(v_ref.at[0], v_scr, in_sems.at[2]),
    ]
    for load in loads:
        load.start()
    sent = [[], [], [], []]
    for slot, (mask, out) in enumerate(zip(pieces, out_refs)):
        dest = jnp.bitwise_xor(me, mask)
        group, part = dest // sizes.query_parts, dest % sizes.query_parts
        cols = pl.ds(pl.multiple_of(group * width, HD), width)
        first = pl.ds(pl.multiple_of(part * part_rows, part_rows), part_rows)
        for kind, source, rows in (
            (0, q_scr.at[first, cols], pl.ds(0, part_rows)),
            (1, k_scr.at[:, cols], pl.ds(part_rows, tok_rows)),
            (2, v_scr.at[:, cols], pl.ds(part_rows + tok_rows, tok_rows)),
        ):
            sent[kind].append(pltpu.make_async_copy(source, out.at[rows], out_sems.at[kind, slot]))
        if sizes.rides(mask):
            for at, (rows, place, from_rows) in enumerate(sizes.ride_slices()):
                sent[3].append(
                    pltpu.make_async_copy(
                        share_scr.at[from_rows], out.at[rows, place], out_sems.at[3 + at, slot]
                    )
                )
    loads[0].wait()
    if sizes.riding:
        for chunk in range(sizes.chunks):
            cols = embed_scr[:, :, pl.ds(chunk * HD, HD)].astype(F32)
            share_scr[pl.ds(chunk * sizes.share_rows, sizes.share_rows), :] = cols.reshape(
                sizes.share_rows, HD
            ).astype(BF16)
    for store in sent[3]:
        store.start()
    for kind in range(3):
        loads[kind + 1].wait()
        for store in sent[kind]:
            store.start()
    for stores in sent:
        for store in stores:
            store.wait()


def pack(sizes, queries, keys, values, patch_embed):
    tok_rows, full = queries.shape[1:]
    pieces = sizes.pieces()
    return pl.pallas_call(
        functools.partial(pack_kernel, sizes),
        out_shape=[jax.ShapeDtypeStruct(sizes.piece_shape(mask), BF16) for mask in pieces],
        in_specs=[HBM_SPEC] * 4,
        out_specs=[HBM_SPEC] * len(pieces),
        scratch_shapes=[pltpu.VMEM((tok_rows, full), BF16)] * 3
        + [
            pltpu.VMEM((sizes.share,) + patch_embed.shape[1:], BF16),
            pltpu.VMEM((max(16, sizes.ride_rows), HD), BF16),
            pltpu.SemaphoreType.DMA((4,)),
            pltpu.SemaphoreType.DMA((3 + sizes.heads, len(pieces))),
        ],
        compiler_params=limits(),
        cost_estimate=pl.CostEstimate(
            flops=0, bytes_accessed=12 * tok_rows * full, transcendentals=0
        ),
    )(queries, keys, values, patch_embed)


def collect_kernel(sizes, *refs):
    *in_refs, out_ref, sems = refs
    copies = []
    for slot, ref in enumerate(in_refs):
        for at, (rows, cols, to_rows) in enumerate(sizes.ride_slices()):
            copies.append(
                pltpu.make_async_copy(
                    ref.at[rows, cols], out_ref.at[slot, to_rows], sems.at[at, slot]
                )
            )
    for copy in copies:
        copy.start()
    for copy in copies:
        copy.wait()


def collect(sizes, arrays):
    return pl.pallas_call(
        functools.partial(collect_kernel, sizes),
        out_shape=jax.ShapeDtypeStruct((len(arrays), sizes.ride_rows, HD), BF16),
        in_specs=[ANY_SPEC] * len(arrays),
        out_specs=VMEM_SPEC,
        scratch_shapes=[pltpu.SemaphoreType.DMA((sizes.heads, len(arrays)))],
        compiler_params=limits(),
    )(*arrays)


def join_kernel(first_ref, second_ref, *refs):
    out_ref = refs[-1]
    count = first_ref.shape[0]
    out_ref[:count] = first_ref[...]
    out_ref[count:] = second_ref[...]


def join(first, second, others):
    return pl.pallas_call(
        join_kernel,
        out_shape=jax.ShapeDtypeStruct((2 * first.shape[0],) + first.shape[1:], BF16),
        in_specs=[VMEM_SPEC] * 2 + [ANY_SPEC] * len(others),
        out_specs=VMEM_SPEC,
        compiler_params=limits(),
    )(first, second, *others)


def arrange_kernel(sizes, masks, place_ref, *refs):
    *pair_refs, out_ref = refs[:-2] + refs[-1:]
    me = place_ref[0]
    odd = me % 2 == 1
    local = sizes.local
    for quarter in range(len(pair_refs) // 2):
        held_ref, got_ref = pair_refs[2 * quarter], pair_refs[2 * quarter + 1]
        for slot, mask in enumerate(masks):
            pair = jnp.bitwise_xor(me, mask) // 2
            for chunk in range(sizes.chunks):
                rows = pl.ds(chunk * sizes.share_rows, sizes.share_rows)
                held = held_ref[slot, rows, :].astype(F32)
                got = got_ref[slot, rows, :].astype(F32)
                first = jnp.where(odd, got, held)
                second = jnp.where(odd, held, got)
                for at in range(sizes.share):
                    part = slice(at * local, (at + 1) * local)
                    both = jnp.concatenate([first[part], second[part]], axis=0).astype(BF16)
                    start = pl.multiple_of(at * sizes.count * local + pair * 2 * local, 2 * local)
                    out_ref[quarter, pl.ds(start, 2 * local), pl.ds(chunk * HD, HD)] = both


def arrange(sizes, masks, place, pairs, wait):
    rows = sizes.share * sizes.count * sizes.local
    flat = [x for pair in pairs for x in pair]
    return pl.pallas_call(
        functools.partial(arrange_kernel, sizes, masks),
        out_shape=jax.ShapeDtypeStruct((len(pairs), rows, VW), BF16),
        in_specs=[SMEM_SPEC] + [VMEM_SPEC] * (len(flat) + 1),
        out_specs=VMEM_SPEC,
        compiler_params=limits(),
    )(place, *flat, wait)


FACTOR = HD ** (-0.5) * math.log2(math.e)


def load_pieces(sizes, in_refs, query_scr, key_scr, value_scr, sems):
    tok_rows, part_rows = sizes.tok_rows, sizes.part_rows
    copies = []
    for src, ref in enumerate(in_refs):
        rows = pl.ds(src * tok_rows, tok_rows)
        copies += [
            pltpu.make_async_copy(ref.at[pl.ds(0, part_rows)], query_scr.at[src], sems.at[0, src]),
            pltpu.make_async_copy(
                ref.at[pl.ds(part_rows, tok_rows)], key_scr.at[rows], sems.at[1, src]
            ),
        ]
        for head in range(sizes.heads):
            copies.append(
                pltpu.make_async_copy(
                    ref.at[pl.ds(part_rows + tok_rows, tok_rows), pl.ds(head * HD, HD)],
                    value_scr.at[rows, pl.ds(2 * head * HD, HD)],
                    sems.at[2 + head, src],
                )
            )
    for copy in copies:
        copy.start()
    ones = jnp.ones((len(in_refs) * tok_rows, HD), BF16)
    for head in range(sizes.heads):
        value_scr[:, pl.ds((2 * head + 1) * HD, HD)] = ones
    return copies


def soft_part(query, key_scr, value_scr, rows, head, before):
    logits = mm_nt(query, key_scr[rows, pl.ds(head * HD, HD)])
    top = jnp.max(logits, axis=-1, keepdims=True)
    if before:
        top = jnp.maximum(top, before[2])
    weights = jnp.exp2((logits - top) * FACTOR).astype(BF16)
    both = mm(weights, value_scr[rows, pl.ds(2 * head * HD, 2 * HD)])
    mixed, total = both[:, :HD], both[:, HD:]
    if before:
        shrink = jnp.exp2((before[2] - top) * FACTOR)
        mixed, total = mixed + before[0] * shrink, total + before[1] * shrink
    return mixed, total, top


def piece_scratch(sizes, count):
    lat_rows = count * sizes.tok_rows
    return [
        pltpu.VMEM((count, sizes.part_rows, sizes.width), BF16),
        pltpu.VMEM((lat_rows, sizes.width), BF16),
        pltpu.VMEM((lat_rows, 2 * sizes.width), BF16),
        pltpu.SemaphoreType.DMA((2 + sizes.heads, count)),
    ]


def early_kernel(sizes, count, *refs):
    in_refs, refs = refs[:count], refs[count:]
    sum_ref, stat_ref, query_scr, key_scr, value_scr, sems = refs
    for copy in load_pieces(sizes, in_refs, query_scr, key_scr, value_scr, sems):
        copy.wait()
    left = lax.broadcasted_iota(jnp.int32, (sizes.part_rows, HD), 1) < HD // 2
    rows = pl.ds(0, count * sizes.tok_rows)
    for src in range(count):
        results = [
            soft_part(
                query_scr[src, :, pl.ds(head * HD, HD)], key_scr, value_scr, rows, head, None
            )
            for head in range(sizes.heads)
        ]
        for head, (mixed, total, top) in enumerate(results):
            sum_ref[src, head] = mixed
            stat_ref[src, head] = jnp.where(left, top, total)


def attend_early(sizes, received):
    count = len(received)
    shape = jax.ShapeDtypeStruct((count, sizes.heads, sizes.part_rows, HD), F32)
    return pl.pallas_call(
        functools.partial(early_kernel, sizes, count),
        out_shape=(shape, shape),
        in_specs=[ANY_SPEC] * count,
        out_specs=(VMEM_SPEC, VMEM_SPEC),
        scratch_shapes=piece_scratch(sizes, count),
        compiler_params=limits(12),
        cost_estimate=pl.CostEstimate(flops=1, bytes_accessed=1, transcendentals=0),
    )(*received)


def attend_kernel(sizes, masks, early, place_ref, *refs):
    count, heads, width = sizes.count, sizes.heads, sizes.width
    tok_rows, part_rows = sizes.tok_rows, sizes.part_rows
    in_refs, refs = refs[:count], refs[count:]
    kept_refs, refs = refs[: 2 if early else 0], refs[2 if early else 0 :]
    scale_ref, shift_ref, proj_ref, mod_ref, lat_ref, *refs = refs
    query_scr, key_scr, value_scr, sems, scale_scr, shift_scr, proj_scr, side_sems, *kept_scr = refs
    half = part_rows // 2
    me = place_ref[0]
    mine = pl.ds(pl.multiple_of(place_ref[2] * width, HD), width)
    copies = load_pieces(sizes, in_refs, query_scr, key_scr, value_scr, sems)
    others = [
        pltpu.make_async_copy(scale_ref.at[:, mine], scale_scr, side_sems.at[0]),
        pltpu.make_async_copy(shift_ref.at[:, mine], shift_scr, side_sems.at[1]),
        pltpu.make_async_copy(proj_ref.at[:, mine], proj_scr, side_sems.at[2]),
    ]
    for slot, (ref, scr) in enumerate(zip(kept_refs, kept_scr)):
        others.append(pltpu.make_async_copy(ref, scr, side_sems.at[3 + slot]))
    for copy in others:
        copy.start()
    for copy in copies + others:
        copy.wait()
    gain = 1.0 + scale_scr[...]
    shift = shift_scr[...]
    together = 2
    for first in range(0, count, together):
        results = []
        for src in range(first, first + together):
            mixed = []
            for head in range(heads):
                before = None
                rows = pl.ds(0, count * tok_rows)
                if src < early:
                    rows = pl.ds(early * tok_rows, (count - early) * tok_rows)
                    stat = kept_scr[1][src, head]
                    before = (kept_scr[0][src, head], stat[:, HD - 1 :], stat[:, :1])
                query = query_scr[src, :, pl.ds(head * HD, HD)]
                value, total, _ = soft_part(query, key_scr, value_scr, rows, head, before)
                mixed.append(value / total)
            attended = jnp.concatenate(mixed, axis=1) if heads > 1 else mixed[0]
            results.append((attended * gain + shift).astype(BF16))
        for at, modulated in enumerate(results):
            mod_ref[jnp.bitwise_xor(me, masks[first + at])] = modulated
    sides = [
        mm_nt(mod_ref[:, rows, :].reshape(count * half, width), proj_scr[...])
        for rows in (slice(0, half), slice(half, part_rows))
    ]
    latent = jnp.concatenate(sides, axis=1).astype(BF16)
    lat_ref[...] = latent.reshape(count, half, 2 * CH)


def attend(sizes, masks, place, received, kept, scales, shifts, proj):
    count, width, heads = sizes.count, sizes.width, sizes.heads
    lat_rows = count * sizes.tok_rows
    query_rows = count * sizes.part_rows
    early = kept[0].shape[0] if kept else 0
    return pl.pallas_call(
        functools.partial(attend_kernel, sizes, masks, early),
        out_shape=(
            jax.ShapeDtypeStruct((count, sizes.part_rows, width), BF16),
            jax.ShapeDtypeStruct((count, sizes.part_rows // 2, 2 * CH), BF16),
        ),
        in_specs=[SMEM_SPEC] + [ANY_SPEC] * (count + len(kept)) + [HBM_SPEC] * 3,
        out_specs=(VMEM_SPEC, VMEM_SPEC),
        scratch_shapes=piece_scratch(sizes, count)
        + [
            pltpu.VMEM((1, width), F32),
            pltpu.VMEM((1, width), F32),
            pltpu.VMEM((CH, width), BF16),
            pltpu.SemaphoreType.DMA((5,)),
        ]
        + [pltpu.VMEM(x.shape, F32) for x in kept],
        compiler_params=limits(16),
        cost_estimate=pl.CostEstimate(
            flops=4 * query_rows * lat_rows * width,
            bytes_accessed=2 * (query_rows * 2 + lat_rows * 2) * width,
            transcendentals=query_rows * lat_rows * heads,
        ),
    )(place, *received, *kept, scales, shifts, proj)


def total_kernel(copies, *refs):
    out_ref = refs[-1]
    if len(refs) == 2:
        parts = [refs[0][i].astype(F32) for i in range(refs[0].shape[0])]
    else:
        parts = [ref[...].astype(F32) for ref in refs[:-1]]
    while len(parts) > 1:
        parts = [parts[i] + parts[i + 1] for i in range(0, len(parts), 2)]
    for copy in range(copies):
        out_ref[copy] = parts[0].astype(BF16)


def total_copies(arrays, copies):
    return pl.pallas_call(
        functools.partial(total_kernel, copies),
        out_shape=jax.ShapeDtypeStruct((copies,) + arrays[0].shape[-2:], BF16),
        in_specs=[VMEM_SPEC] * len(arrays),
        out_specs=VMEM_SPEC,
        compiler_params=limits(),
    )(*arrays)


def lane_mean(x, count):
    return jnp.sum(x, axis=-1, keepdims=True) * (1.0 / count)


def head_kernel(grid_rows, fused, embed_masks, out_factor, place_ref, lat_ref, *refs):
    embed_refs, refs = refs[: len(embed_masks)], refs[len(embed_masks) :]
    sides, refs = refs[:4], refs[4:]
    cot_ref, refs = refs[0], refs[1:]
    mod_ref, refs = refs[0], refs[1:]
    reward_ref, grad_ref, weight_ref, lat_scr, grad_scr, block_scr, back_scr, *refs = refs
    pos_ref, pre_ref, post_ref, prompt_ref, side_sems = refs
    patch_rows = grid_rows // 4
    patch_cols = GW // 4
    patches = patch_rows * patch_cols
    copies = []
    for slot, (side, scr) in enumerate(zip(sides, (pos_ref, pre_ref, post_ref, prompt_ref))):
        copies.append(pltpu.make_async_copy(side, scr, side_sems.at[slot]))
    for copy in copies:
        copy.start()
    lat_scr[...] = lat_ref[...].astype(F32)

    data = place_ref[1]
    shares = [
        (jnp.bitwise_xor(data, mask), ref, slot)
        for ref, masks in zip(embed_refs, embed_masks)
        for slot, mask in enumerate(masks)
    ]
    share_rows = embed_refs[0].shape[1]
    for hi in range(2):
        wide = []
        for tx in range(4):
            rows = [
                lat_scr[pl.ds((2 * pr + hi) * GW + tx, patch_cols, stride=4), :]
                for pr in range(patch_rows)
            ]
            wide.append(jnp.concatenate(rows, axis=0))
        for side in range(2):
            lanes = slice(side * CH, (side + 1) * CH)
            line = jnp.concatenate([x[:, lanes] for x in wide], axis=1).astype(BF16)
            first = (2 * hi + side) * 4 * CH
            if share_rows >= 4 * CH:
                at = first % share_rows
                block_scr[first // share_rows, :, pl.ds(at, 4 * CH)] = line
            else:
                for at in range(0, 4 * CH, share_rows):
                    block_scr[(first + at) // share_rows] = line[:, at : at + share_rows]
    for copy in copies:
        copy.wait()
    embedded = pos_ref[...].astype(F32)
    for number, ref, slot in shares:
        embedded = embedded + mm(block_scr[number], ref[slot])
    pre = pre_ref[...].reshape(1, VW)
    post = post_ref[...].reshape(1, VW)
    prompt = prompt_ref[...]
    center = embedded - lane_mean(embedded, VW)
    rstd = lax.rsqrt(lane_mean(center * center, VW) + EPS)
    unit = center * rstd
    pooled = jnp.sum(unit, axis=0, keepdims=True) * (1.0 / patches) * pre
    pooled_center = pooled - lane_mean(pooled, VW)
    pooled_rstd = lax.rsqrt(lane_mean(pooled_center * pooled_center, VW) + EPS)
    pooled_unit = pooled_center * pooled_rstd
    final = pooled_unit * post
    dot = jnp.sum(final * prompt, axis=-1, keepdims=True)
    final_sq = jnp.sum(final * final, axis=-1, keepdims=True)
    prompt_sq = jnp.sum(prompt * prompt, axis=-1, keepdims=True)
    final_len = jnp.sqrt(final_sq)
    prompt_len = jnp.sqrt(prompt_sq)
    cosine = dot / (final_len * prompt_len)
    reward_ref[...] = jnp.broadcast_to(100.0 * cosine, reward_ref.shape)
    cot = cot_ref[0]
    final_grad = (100.0 * cot) * (prompt / (final_len * prompt_len) - final * (cosine / final_sq))
    unit_grad = final_grad * post
    pooled_grad = pooled_rstd * (
        unit_grad
        - lane_mean(unit_grad, VW)
        - pooled_unit * lane_mean(unit_grad * pooled_unit, VW)
    )
    flow = pooled_grad * pre * (1.0 / patches)
    embed_grad = rstd * (flow - lane_mean(flow, VW) - unit * lane_mean(flow * unit, VW))
    high = embed_grad.astype(BF16)
    low = (embed_grad - high.astype(F32)).astype(BF16)
    stacked = jnp.concatenate([high, low], axis=0)
    for number, ref, slot in shares:
        both = mm_nt(stacked, ref[slot])
        back_scr[number] = both[:patches] + both[patches:]
    back = jnp.concatenate([back_scr[i] for i in range(16 * CH // share_rows)], axis=1)
    for hi in range(2):
        for tx in range(4):
            first = (4 * (2 * hi) + tx) * CH
            second = (4 * (2 * hi + 1) + tx) * CH
            piece = jnp.concatenate(
                [back[:, first : first + CH], back[:, second : second + CH]], axis=1
            )
            for pr in range(patch_rows):
                grad_scr[pl.ds((2 * pr + hi) * GW + tx, patch_cols, stride=4), :] = piece[
                    pr * patch_cols : (pr + 1) * patch_cols
                ]
    grad = grad_scr[...].astype(BF16)
    grad_ref[...] = grad
    if fused:
        store_readout_grad(grad, mod_ref, out_factor, weight_ref)
    else:
        weight_ref[...] = jnp.zeros_like(weight_ref)


def store_readout_grad(grad, mod_ref, out_factor, out_ref):
    turned = grad.astype(F32).T.astype(BF16)
    count, rows, width = mod_ref.shape
    half = rows // 2
    first = mod_ref[:, :half, :].reshape(count * half, width)
    second = mod_ref[:, half:, :].reshape(count * half, width)
    total = mm(turned[:CH], first) + mm(turned[CH:], second)
    out_ref[...] = (total * out_factor).astype(BF16)


def reward_head(
    place, latent, embed, pos, pre, post, prompt, cot, modulated, grid_rows, fused, out_factor
):
    patches = grid_rows * GW // 16
    rows = grid_rows * GW // 2
    width = modulated.shape[2]
    embed_arrays, embed_masks = [x for x, _ in embed], [masks for _, masks in embed]
    share_rows = embed_arrays[0].shape[1]
    return pl.pallas_call(
        functools.partial(head_kernel, grid_rows, fused, embed_masks, out_factor),
        out_shape=(
            jax.ShapeDtypeStruct((1, 128), F32),
            jax.ShapeDtypeStruct((rows, 2 * CH), BF16),
            jax.ShapeDtypeStruct((CH, width), BF16),
        ),
        in_specs=[SMEM_SPEC, VMEM_SPEC]
        + [VMEM_SPEC] * len(embed_arrays)
        + [HBM_SPEC] * 4
        + [SMEM_SPEC, VMEM_SPEC],
        out_specs=(VMEM_SPEC, VMEM_SPEC, VMEM_SPEC),
        scratch_shapes=[
            pltpu.VMEM((rows, 2 * CH), F32),
            pltpu.VMEM((rows, 2 * CH), F32),
            pltpu.VMEM((16 * CH // share_rows, patches, share_rows), BF16),
            pltpu.VMEM((16 * CH // share_rows, patches, share_rows), F32),
            pltpu.VMEM((patches, VW), BF16),
            pltpu.VMEM((VW,), F32),
            pltpu.VMEM((VW,), F32),
            pltpu.VMEM((1, VW), F32),
            pltpu.SemaphoreType.DMA((4,)),
        ],
        compiler_params=limits(16),
        cost_estimate=pl.CostEstimate(
            flops=6 * patches * 16 * CH * VW,
            bytes_accessed=2 * 16 * CH * VW + 2 * patches * VW,
            transcendentals=0,
        ),
    )(place, latent, *embed_arrays, pos, pre, post, prompt, cot, modulated)


def spread_kernel(
    count, half, heads, place_ref, grad_ref, scale_ref, proj_ref, out_ref, scale_scr, proj_scr, sems
):
    width = heads * HD
    mine = pl.ds(pl.multiple_of(place_ref[2] * width, HD), width)
    copies = [
        pltpu.make_async_copy(scale_ref.at[:, mine], scale_scr, sems.at[0]),
        pltpu.make_async_copy(proj_ref.at[:, mine], proj_scr, sems.at[1]),
    ]
    for copy in copies:
        copy.start()
    for copy in copies:
        copy.wait()
    gain = 1.0 + scale_scr[...]
    proj = proj_scr[...]
    zero = jnp.zeros_like(proj)
    sides = (jnp.concatenate([proj, zero], axis=0), jnp.concatenate([zero, proj], axis=0))
    for src in range(count):
        grad = grad_ref[pl.ds(src * half, half), :]
        for side in range(2):
            rows = (mm(grad, sides[side]) * gain).astype(BF16)
            for head in range(heads):
                out_ref[0, head, pl.ds((2 * src + side) * half, half), :] = rows[
                    :, head * HD : (head + 1) * HD
                ]


def spread(place, grad, scales, proj, count, half, heads):
    return pl.pallas_call(
        functools.partial(spread_kernel, count, half, heads),
        out_shape=jax.ShapeDtypeStruct((1, heads, 2 * count * half, HD), BF16),
        in_specs=[SMEM_SPEC, VMEM_SPEC, HBM_SPEC, HBM_SPEC],
        out_specs=VMEM_SPEC,
        scratch_shapes=[
            pltpu.VMEM((1, heads * HD), F32),
            pltpu.VMEM((CH, heads * HD), BF16),
            pltpu.SemaphoreType.DMA((2,)),
        ],
        compiler_params=limits(),
        cost_estimate=pl.CostEstimate(
            flops=8 * count * half * CH * heads * HD,
            bytes_accessed=4 * count * half * heads * HD,
            transcendentals=0,
        ),
    )(place, grad, scales, proj)


def weight_kernel(out_factor, grad_ref, *refs):
    store_readout_grad(grad_ref[...], refs[0], out_factor, refs[1])


def weight_call(grad, modulated, out_factor):
    return pl.pallas_call(
        functools.partial(weight_kernel, out_factor),
        out_shape=jax.ShapeDtypeStruct((CH, modulated.shape[2]), BF16),
        in_specs=[VMEM_SPEC] * 2,
        out_specs=VMEM_SPEC,
        compiler_params=limits(),
    )(grad, modulated)


def finish_kernel(in_ref, out_ref):
    count, _, width = in_ref.shape
    for group in range(count):
        out_ref[:, pl.ds(group * width, width)] = in_ref[group].astype(F32)


def finish(blocks):
    return pl.pallas_call(
        finish_kernel,
        out_shape=jax.ShapeDtypeStruct((CH, HEADS * HD), F32),
        in_specs=[VMEM_SPEC],
        out_specs=VMEM_SPEC,
        compiler_params=limits(),
    )(blocks)


def swap(x, axis, mask):
    count = lax.axis_size(axis)
    return lax.ppermute(x, axis, [(i, i ^ mask) for i in range(count)])


def all_to_all(x, groups=None):
    return lax.all_to_all(
        x, "seq", split_axis=0, concat_axis=0, tiled=True, axis_index_groups=groups
    )


def swap_both(x, seq_mask, data_mask):
    seq_count, data_count = lax.axis_size("seq"), lax.axis_size("dp")
    pairs = [
        (i * data_count + j, (i ^ seq_mask) * data_count + (j ^ data_mask))
        for i in range(seq_count)
        for j in range(data_count)
    ]
    return lax.ppermute(x, ("seq", "dp"), pairs)


def on_device(
    queries,
    keys,
    values,
    shifts,
    scales,
    proj_out,
    patch_embed,
    pos_embed,
    pre_gain,
    post_gain,
    prompt,
    cotangent,
):
    seq_count = lax.axis_size("seq")
    data_count = lax.axis_size("dp")
    tok_rows = queries.shape[1]
    sizes = Sizes(seq_count, data_count, tok_rows, patch_embed)
    query_parts, head_count, part_rows = sizes.query_parts, sizes.heads, sizes.part_rows
    group_count = HEADS // head_count
    seq_index = lax.axis_index("seq")
    head_group = seq_index // query_parts
    query_part = seq_index % query_parts
    half = part_rows // 2
    lat_rows = seq_count * tok_rows
    grid_rows = lat_rows // GW
    canonical = part_rows == 2 * GW
    place = jnp.stack([seq_index, lax.axis_index("dp"), head_group]).astype(jnp.int32)
    proj_turned = proj_out.T
    out_factor = 1.0 / math.sqrt(data_count * lat_rows)

    masks = sizes.pieces()
    packed = pack(
        sizes, in_hbm(queries), in_hbm(keys), in_hbm(values), in_hbm(patch_embed)
    )
    received = [swap(x, "seq", mask) if mask else x for mask, x in zip(masks, packed)]
    bits = [1 << b for b in reversed(range(data_count.bit_length() - 1))]
    shared = sizes.share < patch_embed.shape[0]
    kept, order = [], list(range(seq_count))
    if seq_count == 8:
        late = [slot for slot, mask in enumerate(masks) if mask in (6, 7)]
        order = [slot for slot in order if slot not in late]
        kept = attend_early(sizes, [received[slot] for slot in order])
        order = order + late
    if sizes.riding:
        ride = [slot for slot, mask in enumerate(masks) if sizes.rides(mask)]
        two = collect(sizes, [received[slot] for slot in ride])
        held = join(two, swap(two, "seq", 2), kept)
        ride_masks = [masks[slot] for slot in ride]
        ride_masks = ride_masks + [mask ^ 2 for mask in ride_masks]
        pairs = [
            (held, swap(held, "seq", 1)),
            (swap(held, "dp", bits[0]), swap_both(held, 1, bits[0])),
        ]

    modulated, latent_part = attend(
        sizes, [masks[slot] for slot in order], place, [received[slot] for slot in order], kept,
        in_hbm(scales), in_hbm(shifts), in_hbm(proj_turned)
    )

    if not sizes.riding:
        mine = patch_embed
        if shared:
            mine = lax.dynamic_slice_in_dim(
                patch_embed, lax.axis_index("dp") * sizes.share, sizes.share, 0
            )
        mine = lax.all_gather(mine, "seq", axis=1, tiled=True).reshape(-1, VW)
        embed = [(mine[None], [0])]
        if shared:
            embed = embed + [(swap(mine[None], "dp", bits[0]), [bits[0]])]

    groups = None
    if query_parts > 1:
        groups = [[g * query_parts + r for g in range(group_count)] for r in range(query_parts)]
    per_share = seq_count // group_count
    parts = all_to_all(latent_part.reshape(group_count, per_share * half, 2 * CH), groups)
    summed = total_copies([parts], seq_count)
    if sizes.riding:
        embed = [(arrange(sizes, ride_masks, place, pairs, summed), [0, bits[0]])]
    for bit in bits[1:] if shared else []:
        embed = embed + [(swap(x, "dp", bit), [m ^ bit for m in some]) for x, some in embed]
    latent = all_to_all(summed)
    if canonical:
        latent = latent.reshape(lat_rows // 2, 2 * CH)
    else:
        latent = latent.reshape(group_count, query_parts, per_share, half, 2, CH)
        latent = latent.transpose(0, 2, 1, 4, 3, 5).reshape(grid_rows // 2, 2, GW, CH)
        latent = latent.transpose(0, 2, 1, 3).reshape(lat_rows // 2, 2 * CH)

    reward, grad, weight = reward_head(
        place, latent, embed, in_hbm(pos_embed), in_hbm(pre_gain), in_hbm(post_gain), in_hbm(prompt),
        cotangent, modulated, grid_rows, canonical, out_factor,
    )
    if not canonical:
        tokens = grad.reshape(grid_rows // 2, GW, 2, CH).transpose(0, 2, 1, 3)
        tokens = tokens.reshape(seq_count, query_parts, 2, half, CH)
        tokens = lax.dynamic_index_in_dim(tokens, query_part, 1, keepdims=False)
        grad = tokens.transpose(0, 2, 1, 3).reshape(seq_count * half, 2 * CH)
        weight = weight_call(grad, modulated, out_factor)

    parts = [weight] + [swap(weight, "dp", mask) for mask in range(1, data_count)]
    attn_grad = spread(place, grad, in_hbm(scales), in_hbm(proj_turned), seq_count, half, head_count)
    if query_parts > 1:
        total = total_copies(parts, 1)[0]
        parts = [total] + [swap(total, "seq", mask) for mask in range(1, query_parts)]
    blocks = all_to_all(total_copies(parts, group_count), groups)
    return (reward[0, :1], attn_grad, finish(blocks).T)


def solution(mesh):
    return jax.shard_map(
        on_device,
        mesh=mesh,
        in_specs=(
            P("dp", "seq", None),
            P("dp", "seq", None),
            P("dp", "seq", None),
            P("dp", None),
            P("dp", None),
            P(),
            P(None, "seq", None),
            P(),
            P(),
            P(),
            P("dp", None),
            P("dp"),
        ),
        out_specs=(P("dp"), P("dp", "seq", None, None), P()),
        check_vma=False,
    )
```

```python
import functools
import math

import jax
import jax.numpy as jnp
from jax import lax
from jax.experimental import pallas as pl
from jax.experimental.pallas import tpu as pltpu
from jax.sharding import PartitionSpec as P

HEADS = 16
HD = 128
CH = 64
GW = 64
VW = 1280
EPS = 1e-05
BF16 = jnp.bfloat16
F32 = jnp.float32


def mm(a, b):
    return jnp.dot(a, b, preferred_element_type=F32)


def mm_nt(a, b):
    return lax.dot_general(a, b, (((1,), (1,)), ((), ())), preferred_element_type=F32)


def mm_tn(a, b):
    return lax.dot_general(a, b, (((0,), (0,)), ((), ())), preferred_element_type=F32)


SMEM_SPEC = pl.BlockSpec(memory_space=pltpu.SMEM)
VMEM_SPEC = pl.BlockSpec(memory_space=pltpu.VMEM)
HBM_SPEC = pl.BlockSpec(memory_space=pltpu.HBM)
ANY_SPEC = pl.BlockSpec(memory_space=pl.ANY)


def in_hbm(x):
    return pltpu.with_memory_space_constraint(x, pltpu.HBM)


def limits(mib=4):
    return pltpu.CompilerParams(vmem_limit_bytes=mib * 1024 * 1024)


class Sizes:
    def __init__(self, seq_count, data_count, tok_rows, patch_embed):
        self.count = seq_count
        self.query_parts = max(1, seq_count // HEADS)
        self.heads = max(1, HEADS // seq_count)
        self.width = self.heads * HD
        self.tok_rows = tok_rows
        self.part_rows = tok_rows // self.query_parts
        positions, self.local, _ = patch_embed.shape
        self.share = positions // data_count if positions % data_count == 0 else positions
        self.rows = self.part_rows + 2 * tok_rows
        self.share_rows = self.share * self.local
        self.chunks = VW // HD
        self.riding = self.local % 8 == 0 and self.share_rows % 16 == 0 and seq_count == 8
        self.riding = self.riding and 1 < data_count <= positions
        self.ride_rows = self.chunks * self.share_rows if self.riding else 0

    def pieces(self):
        return list(range(1, self.count)) + [0]

    def rides(self, mask):
        return self.riding and mask in (0, 4)

    def piece_shape(self, mask):
        return (self.rows + (self.ride_rows // self.heads if self.rides(mask) else 0), self.width)

    def ride_slices(self):
        deep = self.ride_rows // self.heads
        return [
            (pl.ds(self.rows, deep), pl.ds(at * HD, HD), pl.ds(at * deep, deep))
            for at in range(self.heads)
        ]


def pack_kernel(sizes, q_ref, k_ref, v_ref, embed_ref, *refs):
    pieces = sizes.pieces()
    out_refs = refs[: len(pieces)]
    q_scr, k_scr, v_scr, embed_scr, share_scr, in_sems, out_sems = refs[len(pieces) :]
    me = lax.axis_index("seq")
    tok_rows, part_rows, width = sizes.tok_rows, sizes.part_rows, sizes.width
    share = pl.ds(lax.axis_index("dp") * sizes.share, sizes.share)
    loads = [
        pltpu.make_async_copy(embed_ref.at[share], embed_scr, in_sems.at[3]),
        pltpu.make_async_copy(q_ref.at[0], q_scr, in_sems.at[0]),
        pltpu.make_async_copy(k_ref.at[0], k_scr, in_sems.at[1]),
        pltpu.make_async_copy(v_ref.at[0], v_scr, in_sems.at[2]),
    ]
    for load in loads:
        load.start()
    sent = [[], [], [], []]
    for slot, (mask, out) in enumerate(zip(pieces, out_refs)):
        dest = jnp.bitwise_xor(me, mask)
        group, part = dest // sizes.query_parts, dest % sizes.query_parts
        cols = pl.ds(pl.multiple_of(group * width, HD), width)
        first = pl.ds(pl.multiple_of(part * part_rows, part_rows), part_rows)
        for kind, source, rows in (
            (0, q_scr.at[first, cols], pl.ds(0, part_rows)),
            (1, k_scr.at[:, cols], pl.ds(part_rows, tok_rows)),
            (2, v_scr.at[:, cols], pl.ds(part_rows + tok_rows, tok_rows)),
        ):
            sent[kind].append(pltpu.make_async_copy(source, out.at[rows], out_sems.at[kind, slot]))
        if sizes.rides(mask):
            for at, (rows, place, from_rows) in enumerate(sizes.ride_slices()):
                sent[3].append(
                    pltpu.make_async_copy(
                        share_scr.at[from_rows], out.at[rows, place], out_sems.at[3 + at, slot]
                    )
                )
    loads[0].wait()
    if sizes.riding:
        for chunk in range(sizes.chunks):
            cols = embed_scr[:, :, pl.ds(chunk * HD, HD)].astype(F32)
            share_scr[pl.ds(chunk * sizes.share_rows, sizes.share_rows), :] = cols.reshape(
                sizes.share_rows, HD
            ).astype(BF16)
    for store in sent[3]:
        store.start()
    for kind in range(3):
        loads[kind + 1].wait()
        for store in sent[kind]:
            store.start()
    for stores in sent:
        for store in stores:
            store.wait()


def pack(sizes, queries, keys, values, patch_embed):
    tok_rows, full = queries.shape[1:]
    pieces = sizes.pieces()
    return pl.pallas_call(
        functools.partial(pack_kernel, sizes),
        out_shape=[jax.ShapeDtypeStruct(sizes.piece_shape(mask), BF16) for mask in pieces],
        in_specs=[HBM_SPEC] * 4,
        out_specs=[HBM_SPEC] * len(pieces),
        scratch_shapes=[pltpu.VMEM((tok_rows, full), BF16)] * 3
        + [
            pltpu.VMEM((sizes.share,) + patch_embed.shape[1:], BF16),
            pltpu.VMEM((max(16, sizes.ride_rows), HD), BF16),
            pltpu.SemaphoreType.DMA((4,)),
            pltpu.SemaphoreType.DMA((3 + sizes.heads, len(pieces))),
        ],
        compiler_params=limits(),
        cost_estimate=pl.CostEstimate(
            flops=0, bytes_accessed=12 * tok_rows * full, transcendentals=0
        ),
    )(queries, keys, values, patch_embed)


def collect_kernel(sizes, *refs):
    *in_refs, out_ref, sems = refs
    copies = []
    for slot, ref in enumerate(in_refs):
        for at, (rows, cols, to_rows) in enumerate(sizes.ride_slices()):
            copies.append(
                pltpu.make_async_copy(
                    ref.at[rows, cols], out_ref.at[slot, to_rows], sems.at[at, slot]
                )
            )
    for copy in copies:
        copy.start()
    for copy in copies:
        copy.wait()


def collect(sizes, arrays):
    return pl.pallas_call(
        functools.partial(collect_kernel, sizes),
        out_shape=jax.ShapeDtypeStruct((len(arrays), sizes.ride_rows, HD), BF16),
        in_specs=[ANY_SPEC] * len(arrays),
        out_specs=VMEM_SPEC,
        scratch_shapes=[pltpu.SemaphoreType.DMA((sizes.heads, len(arrays)))],
        compiler_params=limits(),
    )(*arrays)


def join_kernel(first_ref, second_ref, *refs):
    out_ref = refs[-1]
    count = first_ref.shape[0]
    out_ref[:count] = first_ref[...]
    out_ref[count:] = second_ref[...]


def join(first, second, others):
    return pl.pallas_call(
        join_kernel,
        out_shape=jax.ShapeDtypeStruct((2 * first.shape[0],) + first.shape[1:], BF16),
        in_specs=[VMEM_SPEC] * 2 + [ANY_SPEC] * len(others),
        out_specs=VMEM_SPEC,
        compiler_params=limits(),
    )(first, second, *others)


def arrange_kernel(sizes, masks, place_ref, *refs):
    *pair_refs, out_ref = refs[:-2] + refs[-1:]
    me = place_ref[0]
    odd = me % 2 == 1
    local = sizes.local
    for quarter in range(len(pair_refs) // 2):
        held_ref, got_ref = pair_refs[2 * quarter], pair_refs[2 * quarter + 1]
        for slot, mask in enumerate(masks):
            pair = jnp.bitwise_xor(me, mask) // 2
            for chunk in range(sizes.chunks):
                rows = pl.ds(chunk * sizes.share_rows, sizes.share_rows)
                held = held_ref[slot, rows, :].astype(F32)
                got = got_ref[slot, rows, :].astype(F32)
                first = jnp.where(odd, got, held)
                second = jnp.where(odd, held, got)
                for at in range(sizes.share):
                    part = slice(at * local, (at + 1) * local)
                    both = jnp.concatenate([first[part], second[part]], axis=0).astype(BF16)
                    start = pl.multiple_of(at * sizes.count * local + pair * 2 * local, 2 * local)
                    out_ref[quarter, pl.ds(start, 2 * local), pl.ds(chunk * HD, HD)] = both


def arrange(sizes, masks, place, pairs, wait):
    rows = sizes.share * sizes.count * sizes.local
    flat = [x for pair in pairs for x in pair]
    return pl.pallas_call(
        functools.partial(arrange_kernel, sizes, masks),
        out_shape=jax.ShapeDtypeStruct((len(pairs), rows, VW), BF16),
        in_specs=[SMEM_SPEC] + [VMEM_SPEC] * (len(flat) + 1),
        out_specs=VMEM_SPEC,
        compiler_params=limits(),
    )(place, *flat, wait)


FACTOR = HD ** (-0.5) * math.log2(math.e)


def load_pieces(sizes, in_refs, key_scr, value_scr):
    tok_rows, part_rows = sizes.tok_rows, sizes.part_rows
    for src, ref in enumerate(in_refs):
        rows = pl.ds(src * tok_rows, tok_rows)
        key_scr[rows, :] = ref[pl.ds(part_rows, tok_rows), :]
        for head in range(sizes.heads):
            value_scr[rows, pl.ds(2 * head * HD, HD)] = ref[
                pl.ds(part_rows + tok_rows, tok_rows), pl.ds(head * HD, HD)
            ]
    ones = jnp.ones((len(in_refs) * tok_rows, HD), BF16)
    for head in range(sizes.heads):
        value_scr[:, pl.ds((2 * head + 1) * HD, HD)] = ones


def soft_part(query, key_scr, value_scr, rows, head, before):
    logits = mm_nt(query, key_scr[rows, pl.ds(head * HD, HD)])
    top = jnp.max(logits, axis=-1, keepdims=True)
    if before:
        top = jnp.maximum(top, before[2])
    weights = jnp.exp2((logits - top) * FACTOR).astype(BF16)
    both = mm(weights, value_scr[rows, pl.ds(2 * head * HD, 2 * HD)])
    mixed, total = both[:, :HD], both[:, HD:]
    if before:
        shrink = jnp.exp2((before[2] - top) * FACTOR)
        mixed, total = mixed + before[0] * shrink, total + before[1] * shrink
    return mixed, total, top


def piece_scratch(sizes, count):
    lat_rows = count * sizes.tok_rows
    return [
        pltpu.VMEM((lat_rows, sizes.width), BF16),
        pltpu.VMEM((lat_rows, 2 * sizes.width), BF16),
    ]


def early_kernel(sizes, count, *refs):
    in_refs, refs = refs[:count], refs[count:]
    sum_ref, stat_ref, key_scr, value_scr = refs
    load_pieces(sizes, in_refs, key_scr, value_scr)
    left = lax.broadcasted_iota(jnp.int32, (sizes.part_rows, HD), 1) < HD // 2
    rows = pl.ds(0, count * sizes.tok_rows)
    for src in range(count):
        results = [
            soft_part(
                in_refs[src][pl.ds(0, sizes.part_rows), pl.ds(head * HD, HD)],
                key_scr, value_scr, rows, head, None,
            )
            for head in range(sizes.heads)
        ]
        for head, (mixed, total, top) in enumerate(results):
            sum_ref[src, head] = mixed
            stat_ref[src, head] = jnp.where(left, top, total)


def attend_early(sizes, received):
    count = len(received)
    shape = jax.ShapeDtypeStruct((count, sizes.heads, sizes.part_rows, HD), F32)
    return pl.pallas_call(
        functools.partial(early_kernel, sizes, count),
        out_shape=(shape, shape),
        in_specs=[VMEM_SPEC] * count,
        out_specs=(VMEM_SPEC, VMEM_SPEC),
        scratch_shapes=piece_scratch(sizes, count),
        compiler_params=limits(12),
        cost_estimate=pl.CostEstimate(flops=1, bytes_accessed=1, transcendentals=0),
    )(*received)


def attend_kernel(sizes, masks, early, place_ref, *refs):
    count, heads, width = sizes.count, sizes.heads, sizes.width
    tok_rows, part_rows = sizes.tok_rows, sizes.part_rows
    in_refs, refs = refs[:count], refs[count:]
    kept_refs, refs = refs[: 2 if early else 0], refs[2 if early else 0 :]
    scale_ref, shift_ref, proj_ref, mod_ref, lat_ref, *refs = refs
    key_scr, value_scr, scale_scr, shift_scr, proj_scr, side_sems = refs
    half = part_rows // 2
    me = place_ref[0]
    mine = pl.ds(pl.multiple_of(place_ref[2] * width, HD), width)
    copies = [
        pltpu.make_async_copy(scale_ref.at[:, mine], scale_scr, side_sems.at[0]),
        pltpu.make_async_copy(shift_ref.at[:, mine], shift_scr, side_sems.at[1]),
        pltpu.make_async_copy(proj_ref.at[:, mine], proj_scr, side_sems.at[2]),
    ]
    for copy in copies:
        copy.start()
    load_pieces(sizes, in_refs, key_scr, value_scr)
    together = 2
    for first in range(0, count, together):
        results = []
        for src in range(first, first + together):
            mixed = []
            for head in range(heads):
                before = None
                rows = pl.ds(0, count * tok_rows)
                if src < early:
                    rows = pl.ds(early * tok_rows, (count - early) * tok_rows)
                    stat = kept_refs[1][src, head]
                    before = (kept_refs[0][src, head], stat[:, HD - 1 :], stat[:, :1])
                query = in_refs[src][pl.ds(0, part_rows), pl.ds(head * HD, HD)]
                value, total, _ = soft_part(query, key_scr, value_scr, rows, head, before)
                mixed.append(value / total)
            results.append(jnp.concatenate(mixed, axis=1) if heads > 1 else mixed[0])
        if first == 0:
            for copy in copies:
                copy.wait()
            gain = 1.0 + scale_scr[...]
            shift = shift_scr[...]
        for at, attended in enumerate(results):
            modulated = (attended * gain + shift).astype(BF16)
            mod_ref[jnp.bitwise_xor(me, masks[first + at])] = modulated
    sides = [
        mm_nt(mod_ref[:, rows, :].reshape(count * half, width), proj_scr[...])
        for rows in (slice(0, half), slice(half, part_rows))
    ]
    latent = jnp.concatenate(sides, axis=1).astype(BF16)
    lat_ref[...] = latent.reshape(count, half, 2 * CH)


def attend(sizes, masks, place, received, kept, scales, shifts, proj):
    count, width, heads = sizes.count, sizes.width, sizes.heads
    lat_rows = count * sizes.tok_rows
    query_rows = count * sizes.part_rows
    early = kept[0].shape[0] if kept else 0
    return pl.pallas_call(
        functools.partial(attend_kernel, sizes, masks, early),
        out_shape=(
            jax.ShapeDtypeStruct((count, sizes.part_rows, width), BF16),
            jax.ShapeDtypeStruct((count, sizes.part_rows // 2, 2 * CH), BF16),
        ),
        in_specs=[SMEM_SPEC] + [VMEM_SPEC] * (count + len(kept)) + [HBM_SPEC] * 3,
        out_specs=(VMEM_SPEC, VMEM_SPEC),
        scratch_shapes=piece_scratch(sizes, count)
        + [
            pltpu.VMEM((1, width), F32),
            pltpu.VMEM((1, width), F32),
            pltpu.VMEM((CH, width), BF16),
            pltpu.SemaphoreType.DMA((3,)),
        ],
        compiler_params=limits(16),
        cost_estimate=pl.CostEstimate(
            flops=4 * query_rows * lat_rows * width,
            bytes_accessed=2 * (query_rows * 2 + lat_rows * 2) * width,
            transcendentals=query_rows * lat_rows * heads,
        ),
    )(place, *received, *kept, scales, shifts, proj)


def total_kernel(copies, *refs):
    out_ref = refs[-1]
    if len(refs) == 2:
        parts = [refs[0][i].astype(F32) for i in range(refs[0].shape[0])]
    else:
        parts = [ref[...].astype(F32) for ref in refs[:-1]]
    while len(parts) > 1:
        parts = [parts[i] + parts[i + 1] for i in range(0, len(parts), 2)]
    for copy in range(copies):
        out_ref[copy] = parts[0].astype(BF16)


def total_copies(arrays, copies):
    return pl.pallas_call(
        functools.partial(total_kernel, copies),
        out_shape=jax.ShapeDtypeStruct((copies,) + arrays[0].shape[-2:], BF16),
        in_specs=[VMEM_SPEC] * len(arrays),
        out_specs=VMEM_SPEC,
        compiler_params=limits(),
    )(*arrays)


def lane_mean(x, count):
    return jnp.sum(x, axis=-1, keepdims=True) * (1.0 / count)


def head_kernel(grid_rows, fused, embed_masks, out_factor, place_ref, lat_ref, *refs):
    embed_refs, refs = refs[: len(embed_masks)], refs[len(embed_masks) :]
    sides, refs = refs[:4], refs[4:]
    cot_ref, refs = refs[0], refs[1:]
    mod_ref, refs = refs[0], refs[1:]
    reward_ref, grad_ref, weight_ref, lat_scr, grad_scr, block_scr, back_scr, *refs = refs
    pos_ref, pre_ref, post_ref, prompt_ref, side_sems = refs
    patch_rows = grid_rows // 4
    patch_cols = GW // 4
    patches = patch_rows * patch_cols
    copies = []
    for slot, (side, scr) in enumerate(zip(sides, (pos_ref, pre_ref, post_ref, prompt_ref))):
        copies.append(pltpu.make_async_copy(side, scr, side_sems.at[slot]))
    for copy in copies:
        copy.start()
    lat_scr[...] = lat_ref[...].astype(F32)

    data = place_ref[1]
    shares = [
        (jnp.bitwise_xor(data, mask), ref, slot)
        for ref, masks in zip(embed_refs, embed_masks)
        for slot, mask in enumerate(masks)
    ]
    share_rows = embed_refs[0].shape[1]
    for hi in range(2):
        wide = []
        for tx in range(4):
            rows = [
                lat_scr[pl.ds((2 * pr + hi) * GW + tx, patch_cols, stride=4), :]
                for pr in range(patch_rows)
            ]
            wide.append(jnp.concatenate(rows, axis=0))
        for side in range(2):
            lanes = slice(side * CH, (side + 1) * CH)
            line = jnp.concatenate([x[:, lanes] for x in wide], axis=1).astype(BF16)
            first = (2 * hi + side) * 4 * CH
            if share_rows >= 4 * CH:
                at = first % share_rows
                block_scr[first // share_rows, :, pl.ds(at, 4 * CH)] = line
            else:
                for at in range(0, 4 * CH, share_rows):
                    block_scr[(first + at) // share_rows] = line[:, at : at + share_rows]
    for copy in copies:
        copy.wait()
    embedded = pos_ref[...].astype(F32)
    for number, ref, slot in shares:
        embedded = embedded + mm(block_scr[number], ref[slot])
    pre = pre_ref[...].reshape(1, VW)
    post = post_ref[...].reshape(1, VW)
    prompt = prompt_ref[...]
    center = embedded - lane_mean(embedded, VW)
    rstd = lax.rsqrt(lane_mean(center * center, VW) + EPS)
    unit = center * rstd
    pooled = jnp.sum(unit, axis=0, keepdims=True) * (1.0 / patches) * pre
    pooled_center = pooled - lane_mean(pooled, VW)
    pooled_rstd = lax.rsqrt(lane_mean(pooled_center * pooled_center, VW) + EPS)
    pooled_unit = pooled_center * pooled_rstd
    final = pooled_unit * post
    dot = jnp.sum(final * prompt, axis=-1, keepdims=True)
    final_sq = jnp.sum(final * final, axis=-1, keepdims=True)
    prompt_sq = jnp.sum(prompt * prompt, axis=-1, keepdims=True)
    final_len = jnp.sqrt(final_sq)
    prompt_len = jnp.sqrt(prompt_sq)
    cosine = dot / (final_len * prompt_len)
    reward_ref[...] = jnp.broadcast_to(100.0 * cosine, reward_ref.shape)
    cot = cot_ref[0]
    final_grad = (100.0 * cot) * (prompt / (final_len * prompt_len) - final * (cosine / final_sq))
    unit_grad = final_grad * post
    pooled_grad = pooled_rstd * (
        unit_grad
        - lane_mean(unit_grad, VW)
        - pooled_unit * lane_mean(unit_grad * pooled_unit, VW)
    )
    flow = pooled_grad * pre * (1.0 / patches)
    embed_grad = rstd * (flow - lane_mean(flow, VW) - unit * lane_mean(flow * unit, VW))
    high = embed_grad.astype(BF16)
    low = (embed_grad - high.astype(F32)).astype(BF16)
    stacked = jnp.concatenate([high, low], axis=0)
    for number, ref, slot in shares:
        both = mm_nt(stacked, ref[slot])
        back_scr[number] = both[:patches] + both[patches:]
    back = jnp.concatenate([back_scr[i] for i in range(16 * CH // share_rows)], axis=1)
    for hi in range(2):
        for tx in range(4):
            first = (4 * (2 * hi) + tx) * CH
            second = (4 * (2 * hi + 1) + tx) * CH
            piece = jnp.concatenate(
                [back[:, first : first + CH], back[:, second : second + CH]], axis=1
            )
            for pr in range(patch_rows):
                grad_scr[pl.ds((2 * pr + hi) * GW + tx, patch_cols, stride=4), :] = piece[
                    pr * patch_cols : (pr + 1) * patch_cols
                ]
    grad = grad_scr[...].astype(BF16)
    grad_ref[...] = grad
    if fused:
        store_readout_grad(grad, mod_ref, out_factor, weight_ref)
    else:
        weight_ref[...] = jnp.zeros_like(weight_ref)


def store_readout_grad(grad, mod_ref, out_factor, out_ref):
    turned = grad.astype(F32).T.astype(BF16)
    count, rows, width = mod_ref.shape
    half = rows // 2
    first = mod_ref[:, :half, :].reshape(count * half, width)
    second = mod_ref[:, half:, :].reshape(count * half, width)
    total = mm(turned[:CH], first) + mm(turned[CH:], second)
    out_ref[...] = (total * out_factor).astype(BF16)


def reward_head(
    place, latent, embed, pos, pre, post, prompt, cot, modulated, grid_rows, fused, out_factor
):
    patches = grid_rows * GW // 16
    rows = grid_rows * GW // 2
    width = modulated.shape[2]
    embed_arrays, embed_masks = [x for x, _ in embed], [masks for _, masks in embed]
    share_rows = embed_arrays[0].shape[1]
    return pl.pallas_call(
        functools.partial(head_kernel, grid_rows, fused, embed_masks, out_factor),
        out_shape=(
            jax.ShapeDtypeStruct((1, 128), F32),
            jax.ShapeDtypeStruct((rows, 2 * CH), BF16),
            jax.ShapeDtypeStruct((CH, width), BF16),
        ),
        in_specs=[SMEM_SPEC, VMEM_SPEC]
        + [VMEM_SPEC] * len(embed_arrays)
        + [HBM_SPEC] * 4
        + [SMEM_SPEC, VMEM_SPEC],
        out_specs=(VMEM_SPEC, VMEM_SPEC, VMEM_SPEC),
        scratch_shapes=[
            pltpu.VMEM((rows, 2 * CH), F32),
            pltpu.VMEM((rows, 2 * CH), F32),
            pltpu.VMEM((16 * CH // share_rows, patches, share_rows), BF16),
            pltpu.VMEM((16 * CH // share_rows, patches, share_rows), F32),
            pltpu.VMEM((patches, VW), BF16),
            pltpu.VMEM((VW,), F32),
            pltpu.VMEM((VW,), F32),
            pltpu.VMEM((1, VW), F32),
            pltpu.SemaphoreType.DMA((4,)),
        ],
        compiler_params=limits(16),
        cost_estimate=pl.CostEstimate(
            flops=6 * patches * 16 * CH * VW,
            bytes_accessed=2 * 16 * CH * VW + 2 * patches * VW,
            transcendentals=0,
        ),
    )(place, latent, *embed_arrays, pos, pre, post, prompt, cot, modulated)


def spread_kernel(
    count, half, heads, place_ref, grad_ref, scale_ref, proj_ref, out_ref, scale_scr, proj_scr, sems
):
    width = heads * HD
    mine = pl.ds(pl.multiple_of(place_ref[2] * width, HD), width)
    copies = [
        pltpu.make_async_copy(scale_ref.at[:, mine], scale_scr, sems.at[0]),
        pltpu.make_async_copy(proj_ref.at[:, mine], proj_scr, sems.at[1]),
    ]
    for copy in copies:
        copy.start()
    for copy in copies:
        copy.wait()
    gain = 1.0 + scale_scr[...]
    proj = proj_scr[...]
    zero = jnp.zeros_like(proj)
    sides = (jnp.concatenate([proj, zero], axis=0), jnp.concatenate([zero, proj], axis=0))
    for src in range(count):
        grad = grad_ref[pl.ds(src * half, half), :]
        for side in range(2):
            rows = (mm(grad, sides[side]) * gain).astype(BF16)
            for head in range(heads):
                out_ref[0, head, pl.ds((2 * src + side) * half, half), :] = rows[
                    :, head * HD : (head + 1) * HD
                ]


def spread(place, grad, scales, proj, count, half, heads):
    return pl.pallas_call(
        functools.partial(spread_kernel, count, half, heads),
        out_shape=jax.ShapeDtypeStruct((1, heads, 2 * count * half, HD), BF16),
        in_specs=[SMEM_SPEC, VMEM_SPEC, HBM_SPEC, HBM_SPEC],
        out_specs=VMEM_SPEC,
        scratch_shapes=[
            pltpu.VMEM((1, heads * HD), F32),
            pltpu.VMEM((CH, heads * HD), BF16),
            pltpu.SemaphoreType.DMA((2,)),
        ],
        compiler_params=limits(),
        cost_estimate=pl.CostEstimate(
            flops=8 * count * half * CH * heads * HD,
            bytes_accessed=4 * count * half * heads * HD,
            transcendentals=0,
        ),
    )(place, grad, scales, proj)


def weight_kernel(out_factor, grad_ref, *refs):
    store_readout_grad(grad_ref[...], refs[0], out_factor, refs[1])


def weight_call(grad, modulated, out_factor):
    return pl.pallas_call(
        functools.partial(weight_kernel, out_factor),
        out_shape=jax.ShapeDtypeStruct((CH, modulated.shape[2]), BF16),
        in_specs=[VMEM_SPEC] * 2,
        out_specs=VMEM_SPEC,
        compiler_params=limits(),
    )(grad, modulated)


def finish_kernel(in_ref, out_ref):
    count, _, width = in_ref.shape
    for group in range(count):
        out_ref[:, pl.ds(group * width, width)] = in_ref[group].astype(F32)


def finish(blocks):
    return pl.pallas_call(
        finish_kernel,
        out_shape=jax.ShapeDtypeStruct((CH, HEADS * HD), F32),
        in_specs=[VMEM_SPEC],
        out_specs=VMEM_SPEC,
        compiler_params=limits(),
    )(blocks)


def swap(x, axis, mask):
    count = lax.axis_size(axis)
    return lax.ppermute(x, axis, [(i, i ^ mask) for i in range(count)])


def all_to_all(x, groups=None):
    return lax.all_to_all(
        x, "seq", split_axis=0, concat_axis=0, tiled=True, axis_index_groups=groups
    )


def swap_both(x, seq_mask, data_mask):
    seq_count, data_count = lax.axis_size("seq"), lax.axis_size("dp")
    pairs = [
        (i * data_count + j, (i ^ seq_mask) * data_count + (j ^ data_mask))
        for i in range(seq_count)
        for j in range(data_count)
    ]
    return lax.ppermute(x, ("seq", "dp"), pairs)


def on_device(
    queries,
    keys,
    values,
    shifts,
    scales,
    proj_out,
    patch_embed,
    pos_embed,
    pre_gain,
    post_gain,
    prompt,
    cotangent,
):
    seq_count = lax.axis_size("seq")
    data_count = lax.axis_size("dp")
    tok_rows = queries.shape[1]
    sizes = Sizes(seq_count, data_count, tok_rows, patch_embed)
    query_parts, head_count, part_rows = sizes.query_parts, sizes.heads, sizes.part_rows
    group_count = HEADS // head_count
    seq_index = lax.axis_index("seq")
    head_group = seq_index // query_parts
    query_part = seq_index % query_parts
    half = part_rows // 2
    lat_rows = seq_count * tok_rows
    grid_rows = lat_rows // GW
    canonical = part_rows == 2 * GW
    place = jnp.stack([seq_index, lax.axis_index("dp"), head_group]).astype(jnp.int32)
    proj_turned = proj_out.T
    out_factor = 1.0 / math.sqrt(data_count * lat_rows)

    masks = sizes.pieces()
    packed = pack(
        sizes, in_hbm(queries), in_hbm(keys), in_hbm(values), in_hbm(patch_embed)
    )
    received = [swap(x, "seq", mask) if mask else x for mask, x in zip(masks, packed)]
    bits = [1 << b for b in reversed(range(data_count.bit_length() - 1))]
    shared = sizes.share < patch_embed.shape[0]
    kept, order = [], list(range(seq_count))
    if seq_count == 8:
        late = [slot for slot, mask in enumerate(masks) if mask in (6, 7)]
        order = [slot for slot in order if slot not in late]
        kept = attend_early(sizes, [received[slot] for slot in order])
        order = order + late
    if sizes.riding:
        ride = [slot for slot, mask in enumerate(masks) if sizes.rides(mask)]
        two = collect(sizes, [received[slot] for slot in ride])
        held = join(two, swap(two, "seq", 2), kept)
        ride_masks = [masks[slot] for slot in ride]
        ride_masks = ride_masks + [mask ^ 2 for mask in ride_masks]
        pairs = [
            (held, swap(held, "seq", 1)),
            (swap(held, "dp", bits[0]), swap_both(held, 1, bits[0])),
        ]

    modulated, latent_part = attend(
        sizes, [masks[slot] for slot in order], place, [received[slot] for slot in order], kept,
        in_hbm(scales), in_hbm(shifts), in_hbm(proj_turned)
    )

    if not sizes.riding:
        mine = patch_embed
        if shared:
            mine = lax.dynamic_slice_in_dim(
                patch_embed, lax.axis_index("dp") * sizes.share, sizes.share, 0
            )
        mine = lax.all_gather(mine, "seq", axis=1, tiled=True).reshape(-1, VW)
        embed = [(mine[None], [0])]
        if shared:
            embed = embed + [(swap(mine[None], "dp", bits[0]), [bits[0]])]

    groups = None
    if query_parts > 1:
        groups = [[g * query_parts + r for g in range(group_count)] for r in range(query_parts)]
    per_share = seq_count // group_count
    parts = all_to_all(latent_part.reshape(group_count, per_share * half, 2 * CH), groups)
    summed = total_copies([parts], seq_count)
    if sizes.riding:
        embed = [(arrange(sizes, ride_masks, place, pairs, summed), [0, bits[0]])]
    for bit in bits[1:] if shared else []:
        embed = embed + [(swap(x, "dp", bit), [m ^ bit for m in some]) for x, some in embed]
    latent = all_to_all(summed)
    if canonical:
        latent = latent.reshape(lat_rows // 2, 2 * CH)
    else:
        latent = latent.reshape(group_count, query_parts, per_share, half, 2, CH)
        latent = latent.transpose(0, 2, 1, 4, 3, 5).reshape(grid_rows // 2, 2, GW, CH)
        latent = latent.transpose(0, 2, 1, 3).reshape(lat_rows // 2, 2 * CH)

    reward, grad, weight = reward_head(
        place, latent, embed, in_hbm(pos_embed), in_hbm(pre_gain), in_hbm(post_gain), in_hbm(prompt),
        cotangent, modulated, grid_rows, canonical, out_factor,
    )
    if not canonical:
        tokens = grad.reshape(grid_rows // 2, GW, 2, CH).transpose(0, 2, 1, 3)
        tokens = tokens.reshape(seq_count, query_parts, 2, half, CH)
        tokens = lax.dynamic_index_in_dim(tokens, query_part, 1, keepdims=False)
        grad = tokens.transpose(0, 2, 1, 3).reshape(seq_count * half, 2 * CH)
        weight = weight_call(grad, modulated, out_factor)

    parts = [weight] + [swap(weight, "dp", mask) for mask in range(1, data_count)]
    attn_grad = spread(place, grad, in_hbm(scales), in_hbm(proj_turned), seq_count, half, head_count)
    if query_parts > 1:
        total = total_copies(parts, 1)[0]
        parts = [total] + [swap(total, "seq", mask) for mask in range(1, query_parts)]
    blocks = all_to_all(total_copies(parts, group_count), groups)
    return (reward[0, :1], attn_grad, finish(blocks).T)


def solution(mesh):
    return jax.shard_map(
        on_device,
        mesh=mesh,
        in_specs=(
            P("dp", "seq", None),
            P("dp", "seq", None),
            P("dp", "seq", None),
            P("dp", None),
            P("dp", None),
            P(),
            P(None, "seq", None),
            P(),
            P(),
            P(),
            P("dp", None),
            P("dp"),
        ),
        out_specs=(P("dp"), P("dp", "seq", None, None), P()),
        check_vma=False,
    )
```

```python
import functools
import math

import jax
import jax.numpy as jnp
from jax import lax
from jax.experimental import pallas as pl
from jax.experimental.pallas import tpu as pltpu
from jax.sharding import PartitionSpec as P

HEADS = 16
HD = 128
CH = 64
GW = 64
VW = 1280
EPS = 1e-05
BF16 = jnp.bfloat16
F32 = jnp.float32


def mm(a, b):
    return jnp.dot(a, b, preferred_element_type=F32)


def mm_nt(a, b):
    return lax.dot_general(a, b, (((1,), (1,)), ((), ())), preferred_element_type=F32)


def mm_tn(a, b):
    return lax.dot_general(a, b, (((0,), (0,)), ((), ())), preferred_element_type=F32)


SMEM_SPEC = pl.BlockSpec(memory_space=pltpu.SMEM)
VMEM_SPEC = pl.BlockSpec(memory_space=pltpu.VMEM)
HBM_SPEC = pl.BlockSpec(memory_space=pltpu.HBM)
ANY_SPEC = pl.BlockSpec(memory_space=pl.ANY)


def in_hbm(x):
    return pltpu.with_memory_space_constraint(x, pltpu.HBM)


def limits(mib=4):
    return pltpu.CompilerParams(vmem_limit_bytes=mib * 1024 * 1024)


class Sizes:
    def __init__(self, seq_count, data_count, tok_rows, patch_embed):
        self.count = seq_count
        self.query_parts = max(1, seq_count // HEADS)
        self.heads = max(1, HEADS // seq_count)
        self.width = self.heads * HD
        self.tok_rows = tok_rows
        self.part_rows = tok_rows // self.query_parts
        positions, self.local, _ = patch_embed.shape
        self.share = positions // data_count if positions % data_count == 0 else positions
        self.rows = self.part_rows + 2 * tok_rows
        self.share_rows = self.share * self.local
        self.chunks = VW // HD
        self.riding = self.local % 8 == 0 and self.share_rows % 16 == 0 and seq_count == 8
        self.riding = self.riding and 1 < data_count <= positions
        self.ride_rows = self.chunks * self.share_rows if self.riding else 0

    def pieces(self):
        return list(range(1, self.count)) + [0]

    def rides(self, mask):
        return self.riding and mask in (0, 4)

    def piece_shape(self, mask):
        return (self.rows + (self.ride_rows // self.heads if self.rides(mask) else 0), self.width)

    def ride_slices(self):
        deep = self.ride_rows // self.heads
        return [
            (pl.ds(self.rows, deep), pl.ds(at * HD, HD), pl.ds(at * deep, deep))
            for at in range(self.heads)
        ]


def pack_kernel(sizes, q_ref, k_ref, v_ref, embed_ref, *refs):
    pieces = sizes.pieces()
    out_refs = refs[: len(pieces)]
    q_scr, k_scr, v_scr, embed_scr, share_scr, in_sems, out_sems = refs[len(pieces) :]
    me = lax.axis_index("seq")
    tok_rows, part_rows, width = sizes.tok_rows, sizes.part_rows, sizes.width
    share = pl.ds(lax.axis_index("dp") * sizes.share, sizes.share)
    loads = [
        pltpu.make_async_copy(embed_ref.at[share], embed_scr, in_sems.at[3]),
        pltpu.make_async_copy(q_ref.at[0], q_scr, in_sems.at[0]),
        pltpu.make_async_copy(k_ref.at[0], k_scr, in_sems.at[1]),
        pltpu.make_async_copy(v_ref.at[0], v_scr, in_sems.at[2]),
    ]
    for load in loads:
        load.start()
    sent = [[], [], [], []]
    for slot, (mask, out) in enumerate(zip(pieces, out_refs)):
        dest = jnp.bitwise_xor(me, mask)
        group, part = dest // sizes.query_parts, dest % sizes.query_parts
        cols = pl.ds(pl.multiple_of(group * width, HD), width)
        first = pl.ds(pl.multiple_of(part * part_rows, part_rows), part_rows)
        for kind, source, rows in (
            (0, q_scr.at[first, cols], pl.ds(0, part_rows)),
            (1, k_scr.at[:, cols], pl.ds(part_rows, tok_rows)),
            (2, v_scr.at[:, cols], pl.ds(part_rows + tok_rows, tok_rows)),
        ):
            sent[kind].append(pltpu.make_async_copy(source, out.at[rows], out_sems.at[kind, slot]))
        if sizes.rides(mask):
            for at, (rows, place, from_rows) in enumerate(sizes.ride_slices()):
                sent[3].append(
                    pltpu.make_async_copy(
                        share_scr.at[from_rows], out.at[rows, place], out_sems.at[3 + at, slot]
                    )
                )
    loads[0].wait()
    if sizes.riding:
        for chunk in range(sizes.chunks):
            cols = embed_scr[:, :, pl.ds(chunk * HD, HD)].astype(F32)
            share_scr[pl.ds(chunk * sizes.share_rows, sizes.share_rows), :] = cols.reshape(
                sizes.share_rows, HD
            ).astype(BF16)
    for store in sent[3]:
        store.start()
    for kind in range(3):
        loads[kind + 1].wait()
        for store in sent[kind]:
            store.start()
    for stores in sent:
        for store in stores:
            store.wait()


def pack(sizes, queries, keys, values, patch_embed):
    tok_rows, full = queries.shape[1:]
    pieces = sizes.pieces()
    return pl.pallas_call(
        functools.partial(pack_kernel, sizes),
        out_shape=[jax.ShapeDtypeStruct(sizes.piece_shape(mask), BF16) for mask in pieces],
        in_specs=[HBM_SPEC] * 4,
        out_specs=[HBM_SPEC] * len(pieces),
        scratch_shapes=[pltpu.VMEM((tok_rows, full), BF16)] * 3
        + [
            pltpu.VMEM((sizes.share,) + patch_embed.shape[1:], BF16),
            pltpu.VMEM((max(16, sizes.ride_rows), HD), BF16),
            pltpu.SemaphoreType.DMA((4,)),
            pltpu.SemaphoreType.DMA((3 + sizes.heads, len(pieces))),
        ],
        compiler_params=limits(),
        cost_estimate=pl.CostEstimate(
            flops=0, bytes_accessed=12 * tok_rows * full, transcendentals=0
        ),
    )(queries, keys, values, patch_embed)


def collect_kernel(sizes, *refs):
    *in_refs, out_ref, sems = refs
    copies = []
    for slot, ref in enumerate(in_refs):
        for at, (rows, cols, to_rows) in enumerate(sizes.ride_slices()):
            copies.append(
                pltpu.make_async_copy(
                    ref.at[rows, cols], out_ref.at[slot, to_rows], sems.at[at, slot]
                )
            )
    for copy in copies:
        copy.start()
    for copy in copies:
        copy.wait()


def collect(sizes, arrays):
    return pl.pallas_call(
        functools.partial(collect_kernel, sizes),
        out_shape=jax.ShapeDtypeStruct((len(arrays), sizes.ride_rows, HD), BF16),
        in_specs=[ANY_SPEC] * len(arrays),
        out_specs=VMEM_SPEC,
        scratch_shapes=[pltpu.SemaphoreType.DMA((sizes.heads, len(arrays)))],
        compiler_params=limits(),
    )(*arrays)


def join_kernel(first_ref, second_ref, *refs):
    out_ref = refs[-1]
    count = first_ref.shape[0]
    out_ref[:count] = first_ref[...]
    out_ref[count:] = second_ref[...]


def join(first, second, others):
    return pl.pallas_call(
        join_kernel,
        out_shape=jax.ShapeDtypeStruct((2 * first.shape[0],) + first.shape[1:], BF16),
        in_specs=[VMEM_SPEC] * 2 + [ANY_SPEC] * len(others),
        out_specs=VMEM_SPEC,
        compiler_params=limits(),
    )(first, second, *others)


def arrange_kernel(sizes, masks, place_ref, *refs):
    *pair_refs, out_ref = refs[:-2] + refs[-1:]
    me = place_ref[0]
    odd = me % 2 == 1
    local = sizes.local
    for quarter in range(len(pair_refs) // 2):
        held_ref, got_ref = pair_refs[2 * quarter], pair_refs[2 * quarter + 1]
        for slot, mask in enumerate(masks):
            pair = jnp.bitwise_xor(me, mask) // 2
            for chunk in range(sizes.chunks):
                rows = pl.ds(chunk * sizes.share_rows, sizes.share_rows)
                held = held_ref[slot, rows, :].astype(F32)
                got = got_ref[slot, rows, :].astype(F32)
                first = jnp.where(odd, got, held)
                second = jnp.where(odd, held, got)
                for at in range(sizes.share):
                    part = slice(at * local, (at + 1) * local)
                    both = jnp.concatenate([first[part], second[part]], axis=0).astype(BF16)
                    start = pl.multiple_of(at * sizes.count * local + pair * 2 * local, 2 * local)
                    out_ref[quarter, pl.ds(start, 2 * local), pl.ds(chunk * HD, HD)] = both


def arrange(sizes, masks, place, pairs, wait):
    rows = sizes.share * sizes.count * sizes.local
    flat = [x for pair in pairs for x in pair]
    return pl.pallas_call(
        functools.partial(arrange_kernel, sizes, masks),
        out_shape=jax.ShapeDtypeStruct((len(pairs), rows, VW), BF16),
        in_specs=[SMEM_SPEC] + [VMEM_SPEC] * (len(flat) + 1),
        out_specs=VMEM_SPEC,
        compiler_params=limits(),
    )(place, *flat, wait)


def fetch_kernel(sizes, place_ref, *refs):
    count = len(refs) // 2
    sems = refs[-1]
    mine = pl.ds(pl.multiple_of(place_ref[2] * sizes.width, HD), sizes.width)
    copies = []
    for slot in range(count):
        source = refs[slot].at[:, mine] if slot < 3 else refs[slot]
        copies.append(pltpu.make_async_copy(source, refs[count + slot], sems.at[slot]))
        copies[-1].start()
    for copy in copies:
        copy.wait()


def fetch(sizes, place, arrays):
    shapes = [x.shape if slot >= 3 else (x.shape[0], sizes.width) for slot, x in enumerate(arrays)]
    return pl.pallas_call(
        functools.partial(fetch_kernel, sizes),
        out_shape=[jax.ShapeDtypeStruct(shape, x.dtype) for shape, x in zip(shapes, arrays)],
        in_specs=[SMEM_SPEC] + [HBM_SPEC] * len(arrays),
        out_specs=[VMEM_SPEC] * len(arrays),
        scratch_shapes=[pltpu.SemaphoreType.DMA((len(arrays),))],
        compiler_params=limits(),
        cost_estimate=pl.CostEstimate(flops=1, bytes_accessed=1, transcendentals=0),
    )(place, *[in_hbm(x) for x in arrays])


FACTOR = HD ** (-0.5) * math.log2(math.e)


def load_pieces(sizes, in_refs, key_scr, value_scr):
    tok_rows, part_rows = sizes.tok_rows, sizes.part_rows
    for src, ref in enumerate(in_refs):
        rows = pl.ds(src * tok_rows, tok_rows)
        key_scr[rows, :] = ref[pl.ds(part_rows, tok_rows), :]
        for head in range(sizes.heads):
            value_scr[rows, pl.ds(2 * head * HD, HD)] = ref[
                pl.ds(part_rows + tok_rows, tok_rows), pl.ds(head * HD, HD)
            ]
    ones = jnp.ones((len(in_refs) * tok_rows, HD), BF16)
    for head in range(sizes.heads):
        value_scr[:, pl.ds((2 * head + 1) * HD, HD)] = ones


def soft_part(query, key_scr, value_scr, rows, head, before):
    logits = mm_nt(query, key_scr[rows, pl.ds(head * HD, HD)])
    top = jnp.max(logits, axis=-1, keepdims=True)
    if before:
        top = jnp.maximum(top, before[2])
    weights = jnp.exp2((logits - top) * FACTOR).astype(BF16)
    both = mm(weights, value_scr[rows, pl.ds(2 * head * HD, 2 * HD)])
    mixed, total = both[:, :HD], both[:, HD:]
    if before:
        shrink = jnp.exp2((before[2] - top) * FACTOR)
        mixed, total = mixed + before[0] * shrink, total + before[1] * shrink
    return mixed, total, top


def piece_scratch(sizes, count):
    lat_rows = count * sizes.tok_rows
    return [
        pltpu.VMEM((lat_rows, sizes.width), BF16),
        pltpu.VMEM((lat_rows, 2 * sizes.width), BF16),
    ]


def early_kernel(sizes, count, *refs):
    in_refs, refs = refs[:count], refs[count + 1 :]
    sum_ref, stat_ref, key_scr, value_scr = refs
    load_pieces(sizes, in_refs, key_scr, value_scr)
    left = lax.broadcasted_iota(jnp.int32, (sizes.part_rows, HD), 1) < HD // 2
    rows = pl.ds(0, count * sizes.tok_rows)
    for src in range(count):
        results = [
            soft_part(
                in_refs[src][pl.ds(0, sizes.part_rows), pl.ds(head * HD, HD)],
                key_scr, value_scr, rows, head, None,
            )
            for head in range(sizes.heads)
        ]
        for head, (mixed, total, top) in enumerate(results):
            sum_ref[src, head] = mixed
            stat_ref[src, head] = jnp.where(left, top, total)


def attend_early(sizes, received, wait):
    count = len(received)
    shape = jax.ShapeDtypeStruct((count, sizes.heads, sizes.part_rows, HD), F32)
    return pl.pallas_call(
        functools.partial(early_kernel, sizes, count),
        out_shape=(shape, shape),
        in_specs=[VMEM_SPEC] * (count + 1),
        out_specs=(VMEM_SPEC, VMEM_SPEC),
        scratch_shapes=piece_scratch(sizes, count),
        compiler_params=limits(12),
        cost_estimate=pl.CostEstimate(flops=1, bytes_accessed=1, transcendentals=0),
    )(*received, wait)


def attend_kernel(sizes, masks, early, place_ref, *refs):
    count, heads, width = sizes.count, sizes.heads, sizes.width
    tok_rows, part_rows = sizes.tok_rows, sizes.part_rows
    in_refs, refs = refs[:count], refs[count:]
    kept_refs, refs = refs[: 2 if early else 0], refs[2 if early else 0 :]
    scale_ref, shift_ref, proj_ref, mod_ref, lat_ref, *refs = refs
    key_scr, value_scr = refs
    half = part_rows // 2
    me = place_ref[0]
    gain = 1.0 + scale_ref[...]
    shift = shift_ref[...]
    load_pieces(sizes, in_refs, key_scr, value_scr)
    together = 2
    for first in range(0, count, together):
        results = []
        for src in range(first, first + together):
            mixed = []
            for head in range(heads):
                before = None
                rows = pl.ds(0, count * tok_rows)
                if src < early:
                    rows = pl.ds(early * tok_rows, (count - early) * tok_rows)
                    stat = kept_refs[1][src, head]
                    before = (kept_refs[0][src, head], stat[:, HD - 1 :], stat[:, :1])
                query = in_refs[src][pl.ds(0, part_rows), pl.ds(head * HD, HD)]
                value, total, _ = soft_part(query, key_scr, value_scr, rows, head, before)
                mixed.append(value / total)
            results.append(jnp.concatenate(mixed, axis=1) if heads > 1 else mixed[0])
        for at, attended in enumerate(results):
            modulated = (attended * gain + shift).astype(BF16)
            mod_ref[jnp.bitwise_xor(me, masks[first + at])] = modulated
    sides = [
        mm_nt(mod_ref[:, rows, :].reshape(count * half, width), proj_ref[...])
        for rows in (slice(0, half), slice(half, part_rows))
    ]
    latent = jnp.concatenate(sides, axis=1).astype(BF16)
    lat_ref[...] = latent.reshape(count, half, 2 * CH)


def attend(sizes, masks, place, received, kept, scales, shifts, proj):
    count, width, heads = sizes.count, sizes.width, sizes.heads
    lat_rows = count * sizes.tok_rows
    query_rows = count * sizes.part_rows
    early = kept[0].shape[0] if kept else 0
    return pl.pallas_call(
        functools.partial(attend_kernel, sizes, masks, early),
        out_shape=(
            jax.ShapeDtypeStruct((count, sizes.part_rows, width), BF16),
            jax.ShapeDtypeStruct((count, sizes.part_rows // 2, 2 * CH), BF16),
        ),
        in_specs=[SMEM_SPEC] + [VMEM_SPEC] * (count + len(kept) + 3),
        out_specs=(VMEM_SPEC, VMEM_SPEC),
        scratch_shapes=piece_scratch(sizes, count),
        compiler_params=limits(16),
        cost_estimate=pl.CostEstimate(
            flops=4 * query_rows * lat_rows * width,
            bytes_accessed=2 * (query_rows * 2 + lat_rows * 2) * width,
            transcendentals=query_rows * lat_rows * heads,
        ),
    )(place, *received, *kept, scales, shifts, proj)


def total_kernel(copies, *refs):
    out_ref = refs[-1]
    if len(refs) == 2:
        parts = [refs[0][i].astype(F32) for i in range(refs[0].shape[0])]
    else:
        parts = [ref[...].astype(F32) for ref in refs[:-1]]
    while len(parts) > 1:
        parts = [parts[i] + parts[i + 1] for i in range(0, len(parts), 2)]
    for copy in range(copies):
        out_ref[copy] = parts[0].astype(BF16)


def total_copies(arrays, copies):
    return pl.pallas_call(
        functools.partial(total_kernel, copies),
        out_shape=jax.ShapeDtypeStruct((copies,) + arrays[0].shape[-2:], BF16),
        in_specs=[VMEM_SPEC] * len(arrays),
        out_specs=VMEM_SPEC,
        compiler_params=limits(),
    )(*arrays)


def lane_mean(x, count):
    return jnp.sum(x, axis=-1, keepdims=True) * (1.0 / count)


def head_kernel(grid_rows, fused, embed_masks, out_factor, place_ref, lat_ref, *refs):
    embed_refs, refs = refs[: len(embed_masks)], refs[len(embed_masks) :]
    pos_ref, pre_ref, post_ref, prompt_ref, cot_ref, mod_ref, *refs = refs
    reward_ref, grad_ref, weight_ref, lat_scr, grad_scr, block_scr, back_scr = refs
    patch_rows = grid_rows // 4
    patch_cols = GW // 4
    patches = patch_rows * patch_cols
    lat_scr[...] = lat_ref[...].astype(F32)

    data = place_ref[1]
    shares = [
        (jnp.bitwise_xor(data, mask), ref, slot)
        for ref, masks in zip(embed_refs, embed_masks)
        for slot, mask in enumerate(masks)
    ]
    share_rows = embed_refs[0].shape[1]
    for hi in range(2):
        wide = []
        for tx in range(4):
            rows = [
                lat_scr[pl.ds((2 * pr + hi) * GW + tx, patch_cols, stride=4), :]
                for pr in range(patch_rows)
            ]
            wide.append(jnp.concatenate(rows, axis=0))
        for side in range(2):
            lanes = slice(side * CH, (side + 1) * CH)
            line = jnp.concatenate([x[:, lanes] for x in wide], axis=1).astype(BF16)
            first = (2 * hi + side) * 4 * CH
            if share_rows >= 4 * CH:
                at = first % share_rows
                block_scr[first // share_rows, :, pl.ds(at, 4 * CH)] = line
            else:
                for at in range(0, 4 * CH, share_rows):
                    block_scr[(first + at) // share_rows] = line[:, at : at + share_rows]
    embedded = pos_ref[...].astype(F32)
    for number, ref, slot in shares:
        embedded = embedded + mm(block_scr[number], ref[slot])
    pre = pre_ref[...].reshape(1, VW)
    post = post_ref[...].reshape(1, VW)
    prompt = prompt_ref[...]
    center = embedded - lane_mean(embedded, VW)
    rstd = lax.rsqrt(lane_mean(center * center, VW) + EPS)
    unit = center * rstd
    pooled = jnp.sum(unit, axis=0, keepdims=True) * (1.0 / patches) * pre
    pooled_center = pooled - lane_mean(pooled, VW)
    pooled_rstd = lax.rsqrt(lane_mean(pooled_center * pooled_center, VW) + EPS)
    pooled_unit = pooled_center * pooled_rstd
    final = pooled_unit * post
    dot = jnp.sum(final * prompt, axis=-1, keepdims=True)
    final_sq = jnp.sum(final * final, axis=-1, keepdims=True)
    prompt_sq = jnp.sum(prompt * prompt, axis=-1, keepdims=True)
    final_len = jnp.sqrt(final_sq)
    prompt_len = jnp.sqrt(prompt_sq)
    cosine = dot / (final_len * prompt_len)
    reward_ref[...] = jnp.broadcast_to(100.0 * cosine, reward_ref.shape)
    cot = cot_ref[0]
    final_grad = (100.0 * cot) * (prompt / (final_len * prompt_len) - final * (cosine / final_sq))
    unit_grad = final_grad * post
    pooled_grad = pooled_rstd * (
        unit_grad
        - lane_mean(unit_grad, VW)
        - pooled_unit * lane_mean(unit_grad * pooled_unit, VW)
    )
    flow = pooled_grad * pre * (1.0 / patches)
    embed_grad = rstd * (flow - lane_mean(flow, VW) - unit * lane_mean(flow * unit, VW))
    high = embed_grad.astype(BF16)
    low = (embed_grad - high.astype(F32)).astype(BF16)
    stacked = jnp.concatenate([high, low], axis=0)
    for number, ref, slot in shares:
        both = mm_nt(stacked, ref[slot])
        back_scr[number] = both[:patches] + both[patches:]
    back = jnp.concatenate([back_scr[i] for i in range(16 * CH // share_rows)], axis=1)
    for hi in range(2):
        for tx in range(4):
            first = (4 * (2 * hi) + tx) * CH
            second = (4 * (2 * hi + 1) + tx) * CH
            piece = jnp.concatenate(
                [back[:, first : first + CH], back[:, second : second + CH]], axis=1
            )
            for pr in range(patch_rows):
                grad_scr[pl.ds((2 * pr + hi) * GW + tx, patch_cols, stride=4), :] = piece[
                    pr * patch_cols : (pr + 1) * patch_cols
                ]
    grad = grad_scr[...].astype(BF16)
    grad_ref[...] = grad
    if fused:
        store_readout_grad(grad, mod_ref, out_factor, weight_ref)
    else:
        weight_ref[...] = jnp.zeros_like(weight_ref)


def store_readout_grad(grad, mod_ref, out_factor, out_ref):
    turned = grad.astype(F32).T.astype(BF16)
    count, rows, width = mod_ref.shape
    half = rows // 2
    first = mod_ref[:, :half, :].reshape(count * half, width)
    second = mod_ref[:, half:, :].reshape(count * half, width)
    total = mm(turned[:CH], first) + mm(turned[CH:], second)
    out_ref[...] = (total * out_factor).astype(BF16)


def reward_head(
    place, latent, embed, pos, pre, post, prompt, cot, modulated, grid_rows, fused, out_factor
):
    patches = grid_rows * GW // 16
    rows = grid_rows * GW // 2
    width = modulated.shape[2]
    embed_arrays, embed_masks = [x for x, _ in embed], [masks for _, masks in embed]
    share_rows = embed_arrays[0].shape[1]
    return pl.pallas_call(
        functools.partial(head_kernel, grid_rows, fused, embed_masks, out_factor),
        out_shape=(
            jax.ShapeDtypeStruct((1, 128), F32),
            jax.ShapeDtypeStruct((rows, 2 * CH), BF16),
            jax.ShapeDtypeStruct((CH, width), BF16),
        ),
        in_specs=[SMEM_SPEC, VMEM_SPEC]
        + [VMEM_SPEC] * len(embed_arrays)
        + [VMEM_SPEC] * 4
        + [SMEM_SPEC, VMEM_SPEC],
        out_specs=(VMEM_SPEC, VMEM_SPEC, VMEM_SPEC),
        scratch_shapes=[
            pltpu.VMEM((rows, 2 * CH), F32),
            pltpu.VMEM((rows, 2 * CH), F32),
            pltpu.VMEM((16 * CH // share_rows, patches, share_rows), BF16),
            pltpu.VMEM((16 * CH // share_rows, patches, share_rows), F32),
        ],
        compiler_params=limits(16),
        cost_estimate=pl.CostEstimate(
            flops=6 * patches * 16 * CH * VW,
            bytes_accessed=2 * 16 * CH * VW + 2 * patches * VW,
            transcendentals=0,
        ),
    )(place, latent, *embed_arrays, pos, pre, post, prompt, cot, modulated)


def spread_kernel(count, half, heads, grad_ref, scale_ref, proj_ref, out_ref):
    gain = 1.0 + scale_ref[...]
    proj = proj_ref[...]
    zero = jnp.zeros_like(proj)
    sides = (jnp.concatenate([proj, zero], axis=0), jnp.concatenate([zero, proj], axis=0))
    for src in range(count):
        grad = grad_ref[pl.ds(src * half, half), :]
        for side in range(2):
            rows = (mm(grad, sides[side]) * gain).astype(BF16)
            for head in range(heads):
                out_ref[0, head, pl.ds((2 * src + side) * half, half), :] = rows[
                    :, head * HD : (head + 1) * HD
                ]


def spread(grad, scales, proj, count, half, heads):
    return pl.pallas_call(
        functools.partial(spread_kernel, count, half, heads),
        out_shape=jax.ShapeDtypeStruct((1, heads, 2 * count * half, HD), BF16),
        in_specs=[VMEM_SPEC] * 3,
        out_specs=VMEM_SPEC,
        compiler_params=limits(),
        cost_estimate=pl.CostEstimate(
            flops=8 * count * half * CH * heads * HD,
            bytes_accessed=4 * count * half * heads * HD,
            transcendentals=0,
        ),
    )(grad, scales, proj)


def weight_kernel(out_factor, grad_ref, *refs):
    store_readout_grad(grad_ref[...], refs[0], out_factor, refs[1])


def weight_call(grad, modulated, out_factor):
    return pl.pallas_call(
        functools.partial(weight_kernel, out_factor),
        out_shape=jax.ShapeDtypeStruct((CH, modulated.shape[2]), BF16),
        in_specs=[VMEM_SPEC] * 2,
        out_specs=VMEM_SPEC,
        compiler_params=limits(),
    )(grad, modulated)


def finish_kernel(in_ref, out_ref):
    count, _, width = in_ref.shape
    for group in range(count):
        out_ref[:, pl.ds(group * width, width)] = in_ref[group].astype(F32)


def finish(blocks):
    return pl.pallas_call(
        finish_kernel,
        out_shape=jax.ShapeDtypeStruct((CH, HEADS * HD), F32),
        in_specs=[VMEM_SPEC],
        out_specs=VMEM_SPEC,
        compiler_params=limits(),
    )(blocks)


def swap(x, axis, mask):
    count = lax.axis_size(axis)
    return lax.ppermute(x, axis, [(i, i ^ mask) for i in range(count)])


def all_to_all(x, groups=None):
    return lax.all_to_all(
        x, "seq", split_axis=0, concat_axis=0, tiled=True, axis_index_groups=groups
    )


def swap_both(x, seq_mask, data_mask):
    seq_count, data_count = lax.axis_size("seq"), lax.axis_size("dp")
    pairs = [
        (i * data_count + j, (i ^ seq_mask) * data_count + (j ^ data_mask))
        for i in range(seq_count)
        for j in range(data_count)
    ]
    return lax.ppermute(x, ("seq", "dp"), pairs)


def on_device(
    queries,
    keys,
    values,
    shifts,
    scales,
    proj_out,
    patch_embed,
    pos_embed,
    pre_gain,
    post_gain,
    prompt,
    cotangent,
):
    seq_count = lax.axis_size("seq")
    data_count = lax.axis_size("dp")
    tok_rows = queries.shape[1]
    sizes = Sizes(seq_count, data_count, tok_rows, patch_embed)
    query_parts, head_count, part_rows = sizes.query_parts, sizes.heads, sizes.part_rows
    group_count = HEADS // head_count
    seq_index = lax.axis_index("seq")
    head_group = seq_index // query_parts
    query_part = seq_index % query_parts
    half = part_rows // 2
    lat_rows = seq_count * tok_rows
    grid_rows = lat_rows // GW
    canonical = part_rows == 2 * GW
    place = jnp.stack([seq_index, lax.axis_index("dp"), head_group]).astype(jnp.int32)
    proj_turned = proj_out.T
    out_factor = 1.0 / math.sqrt(data_count * lat_rows)

    masks = sizes.pieces()
    packed = pack(
        sizes, in_hbm(queries), in_hbm(keys), in_hbm(values), in_hbm(patch_embed)
    )
    received = [swap(x, "seq", mask) if mask else x for mask, x in zip(masks, packed)]
    bits = [1 << b for b in reversed(range(data_count.bit_length() - 1))]
    shared = sizes.share < patch_embed.shape[0]
    scale, shift, proj, pos, pre, post, words = fetch(
        sizes, place, [scales, shifts, proj_turned, pos_embed, pre_gain, post_gain, prompt]
    )

    kept, order = [], list(range(seq_count))
    if seq_count == 8:
        late = [slot for slot, mask in enumerate(masks) if mask in (6, 7)]
        order = [slot for slot in order if slot not in late]
        kept = attend_early(sizes, [received[slot] for slot in order], scale)
        order = order + late
    if sizes.riding:
        ride = [slot for slot, mask in enumerate(masks) if sizes.rides(mask)]
        two = collect(sizes, [received[slot] for slot in ride])
        held = join(two, swap(two, "seq", 2), kept)
        ride_masks = [masks[slot] for slot in ride]
        ride_masks = ride_masks + [mask ^ 2 for mask in ride_masks]
        pairs = [
            (held, swap(held, "seq", 1)),
            (swap(held, "dp", bits[0]), swap_both(held, 1, bits[0])),
        ]

    modulated, latent_part = attend(
        sizes, [masks[slot] for slot in order], place, [received[slot] for slot in order], kept,
        scale, shift, proj,
    )

    if not sizes.riding:
        mine = patch_embed
        if shared:
            mine = lax.dynamic_slice_in_dim(
                patch_embed, lax.axis_index("dp") * sizes.share, sizes.share, 0
            )
        mine = lax.all_gather(mine, "seq", axis=1, tiled=True).reshape(-1, VW)
        embed = [(mine[None], [0])]
        if shared:
            embed = embed + [(swap(mine[None], "dp", bits[0]), [bits[0]])]

    groups = None
    if query_parts > 1:
        groups = [[g * query_parts + r for g in range(group_count)] for r in range(query_parts)]
    per_share = seq_count // group_count
    parts = all_to_all(latent_part.reshape(group_count, per_share * half, 2 * CH), groups)
    summed = total_copies([parts], seq_count)
    if sizes.riding:
        embed = [(arrange(sizes, ride_masks, place, pairs, summed), [0, bits[0]])]
    for bit in bits[1:] if shared else []:
        embed = embed + [(swap(x, "dp", bit), [m ^ bit for m in some]) for x, some in embed]
    latent = all_to_all(summed)
    if canonical:
        latent = latent.reshape(lat_rows // 2, 2 * CH)
    else:
        latent = latent.reshape(group_count, query_parts, per_share, half, 2, CH)
        latent = latent.transpose(0, 2, 1, 4, 3, 5).reshape(grid_rows // 2, 2, GW, CH)
        latent = latent.transpose(0, 2, 1, 3).reshape(lat_rows // 2, 2 * CH)

    reward, grad, weight = reward_head(
        place, latent, embed, pos, pre, post, words,
        cotangent, modulated, grid_rows, canonical, out_factor,
    )
    if not canonical:
        tokens = grad.reshape(grid_rows // 2, GW, 2, CH).transpose(0, 2, 1, 3)
        tokens = tokens.reshape(seq_count, query_parts, 2, half, CH)
        tokens = lax.dynamic_index_in_dim(tokens, query_part, 1, keepdims=False)
        grad = tokens.transpose(0, 2, 1, 3).reshape(seq_count * half, 2 * CH)
        weight = weight_call(grad, modulated, out_factor)

    parts = [weight] + [swap(weight, "dp", mask) for mask in range(1, data_count)]
    attn_grad = spread(grad, scale, proj, seq_count, half, head_count)
    if query_parts > 1:
        total = total_copies(parts, 1)[0]
        parts = [total] + [swap(total, "seq", mask) for mask in range(1, query_parts)]
    blocks = all_to_all(total_copies(parts, group_count), groups)
    return (reward[0, :1], attn_grad, finish(blocks).T)


def solution(mesh):
    return jax.shard_map(
        on_device,
        mesh=mesh,
        in_specs=(
            P("dp", "seq", None),
            P("dp", "seq", None),
            P("dp", "seq", None),
            P("dp", None),
            P("dp", None),
            P(),
            P(None, "seq", None),
            P(),
            P(),
            P(),
            P("dp", None),
            P("dp"),
        ),
        out_specs=(P("dp"), P("dp", "seq", None, None), P()),
        check_vma=False,
    )
```

```python
import functools
import math

import jax
import jax.numpy as jnp
from jax import lax
from jax.experimental import pallas as pl
from jax.experimental.pallas import tpu as pltpu
from jax.sharding import PartitionSpec as P

HEADS = 16
HD = 128
CH = 64
GW = 64
VW = 1280
EPS = 1e-05
BF16 = jnp.bfloat16
F32 = jnp.float32


def mm(a, b):
    return jnp.dot(a, b, preferred_element_type=F32)


def mm_nt(a, b):
    return lax.dot_general(a, b, (((1,), (1,)), ((), ())), preferred_element_type=F32)


def mm_tn(a, b):
    return lax.dot_general(a, b, (((0,), (0,)), ((), ())), preferred_element_type=F32)


SMEM_SPEC = pl.BlockSpec(memory_space=pltpu.SMEM)
VMEM_SPEC = pl.BlockSpec(memory_space=pltpu.VMEM)
HBM_SPEC = pl.BlockSpec(memory_space=pltpu.HBM)
ANY_SPEC = pl.BlockSpec(memory_space=pl.ANY)


def in_hbm(x):
    return pltpu.with_memory_space_constraint(x, pltpu.HBM)


def limits(mib=4):
    return pltpu.CompilerParams(vmem_limit_bytes=mib * 1024 * 1024)


class Sizes:
    def __init__(self, seq_count, data_count, tok_rows, patch_embed):
        self.count = seq_count
        self.query_parts = max(1, seq_count // HEADS)
        self.heads = max(1, HEADS // seq_count)
        self.width = self.heads * HD
        self.tok_rows = tok_rows
        self.part_rows = tok_rows // self.query_parts
        positions, self.local, _ = patch_embed.shape
        self.share = positions // data_count if positions % data_count == 0 else positions
        self.rows = self.part_rows + 2 * tok_rows
        self.share_rows = self.share * self.local
        self.chunks = VW // HD
        self.riding = self.local % 8 == 0 and self.share_rows % 16 == 0 and seq_count == 8
        self.riding = self.riding and 1 < data_count <= positions
        self.ride_rows = self.chunks * self.share_rows if self.riding else 0

    def pieces(self):
        return list(range(1, self.count)) + [0]

    def rides(self, mask):
        return self.riding and mask in (0, 4)

    def piece_shape(self, mask):
        return (self.rows + (self.ride_rows // self.heads if self.rides(mask) else 0), self.width)

    def ride_slices(self):
        deep = self.ride_rows // self.heads
        return [
            (pl.ds(self.rows, deep), pl.ds(at * HD, HD), pl.ds(at * deep, deep))
            for at in range(self.heads)
        ]


def pack_kernel(sizes, q_ref, k_ref, v_ref, embed_ref, *refs):
    pieces = sizes.pieces()
    out_refs = refs[: len(pieces)]
    q_scr, k_scr, v_scr, embed_scr, share_scr, in_sems, out_sems = refs[len(pieces) :]
    me = lax.axis_index("seq")
    tok_rows, part_rows, width = sizes.tok_rows, sizes.part_rows, sizes.width
    share = pl.ds(lax.axis_index("dp") * sizes.share, sizes.share)
    loads = [
        pltpu.make_async_copy(embed_ref.at[share], embed_scr, in_sems.at[3]),
        pltpu.make_async_copy(q_ref.at[0], q_scr, in_sems.at[0]),
        pltpu.make_async_copy(k_ref.at[0], k_scr, in_sems.at[1]),
        pltpu.make_async_copy(v_ref.at[0], v_scr, in_sems.at[2]),
    ]
    for load in loads:
        load.start()
    sent = [[], [], [], []]
    for slot, (mask, out) in enumerate(zip(pieces, out_refs)):
        dest = jnp.bitwise_xor(me, mask)
        group, part = dest // sizes.query_parts, dest % sizes.query_parts
        cols = pl.ds(pl.multiple_of(group * width, HD), width)
        first = pl.ds(pl.multiple_of(part * part_rows, part_rows), part_rows)
        for kind, source, rows in (
            (0, q_scr.at[first, cols], pl.ds(0, part_rows)),
            (1, k_scr.at[:, cols], pl.ds(part_rows, tok_rows)),
            (2, v_scr.at[:, cols], pl.ds(part_rows + tok_rows, tok_rows)),
        ):
            sent[kind].append(pltpu.make_async_copy(source, out.at[rows], out_sems.at[kind, slot]))
        if sizes.rides(mask):
            for at, (rows, place, from_rows) in enumerate(sizes.ride_slices()):
                sent[3].append(
                    pltpu.make_async_copy(
                        share_scr.at[from_rows], out.at[rows, place], out_sems.at[3 + at, slot]
                    )
                )
    loads[0].wait()
    if sizes.riding:
        for chunk in range(sizes.chunks):
            cols = embed_scr[:, :, pl.ds(chunk * HD, HD)].astype(F32)
            share_scr[pl.ds(chunk * sizes.share_rows, sizes.share_rows), :] = cols.reshape(
                sizes.share_rows, HD
            ).astype(BF16)
    for store in sent[3]:
        store.start()
    for kind in range(3):
        loads[kind + 1].wait()
        for store in sent[kind]:
            store.start()
    for stores in sent:
        for store in stores:
            store.wait()


def pack(sizes, queries, keys, values, patch_embed):
    tok_rows, full = queries.shape[1:]
    pieces = sizes.pieces()
    return pl.pallas_call(
        functools.partial(pack_kernel, sizes),
        out_shape=[jax.ShapeDtypeStruct(sizes.piece_shape(mask), BF16) for mask in pieces],
        in_specs=[HBM_SPEC] * 4,
        out_specs=[HBM_SPEC] * len(pieces),
        scratch_shapes=[pltpu.VMEM((tok_rows, full), BF16)] * 3
        + [
            pltpu.VMEM((sizes.share,) + patch_embed.shape[1:], BF16),
            pltpu.VMEM((max(16, sizes.ride_rows), HD), BF16),
            pltpu.SemaphoreType.DMA((4,)),
            pltpu.SemaphoreType.DMA((3 + sizes.heads, len(pieces))),
        ],
        compiler_params=limits(),
        cost_estimate=pl.CostEstimate(
            flops=0, bytes_accessed=12 * tok_rows * full, transcendentals=0
        ),
    )(queries, keys, values, patch_embed)


def collect_kernel(sizes, *refs):
    *in_refs, out_ref, sems = refs
    copies = []
    for slot, ref in enumerate(in_refs):
        for at, (rows, cols, to_rows) in enumerate(sizes.ride_slices()):
            copies.append(
                pltpu.make_async_copy(
                    ref.at[rows, cols], out_ref.at[slot, to_rows], sems.at[at, slot]
                )
            )
    for copy in copies:
        copy.start()
    for copy in copies:
        copy.wait()


def collect(sizes, arrays):
    return pl.pallas_call(
        functools.partial(collect_kernel, sizes),
        out_shape=jax.ShapeDtypeStruct((len(arrays), sizes.ride_rows, HD), BF16),
        in_specs=[ANY_SPEC] * len(arrays),
        out_specs=VMEM_SPEC,
        scratch_shapes=[pltpu.SemaphoreType.DMA((sizes.heads, len(arrays)))],
        compiler_params=limits(),
    )(*arrays)


def join_kernel(first_ref, second_ref, *refs):
    out_ref = refs[-1]
    count = first_ref.shape[0]
    out_ref[:count] = first_ref[...]
    out_ref[count:] = second_ref[...]


def join(first, second, others):
    return pl.pallas_call(
        join_kernel,
        out_shape=jax.ShapeDtypeStruct((2 * first.shape[0],) + first.shape[1:], BF16),
        in_specs=[VMEM_SPEC] * 2 + [ANY_SPEC] * len(others),
        out_specs=VMEM_SPEC,
        compiler_params=limits(),
    )(first, second, *others)


def arrange_kernel(sizes, masks, place_ref, *refs):
    *pair_refs, out_ref = refs[:-2] + refs[-1:]
    me = place_ref[0]
    odd = me % 2 == 1
    local = sizes.local
    for quarter in range(len(pair_refs) // 2):
        held_ref, got_ref = pair_refs[2 * quarter], pair_refs[2 * quarter + 1]
        for slot, mask in enumerate(masks):
            pair = jnp.bitwise_xor(me, mask) // 2
            for chunk in range(sizes.chunks):
                rows = pl.ds(chunk * sizes.share_rows, sizes.share_rows)
                held = held_ref[slot, rows, :].astype(F32)
                got = got_ref[slot, rows, :].astype(F32)
                first = jnp.where(odd, got, held)
                second = jnp.where(odd, held, got)
                for at in range(sizes.share):
                    part = slice(at * local, (at + 1) * local)
                    both = jnp.concatenate([first[part], second[part]], axis=0).astype(BF16)
                    start = pl.multiple_of(at * sizes.count * local + pair * 2 * local, 2 * local)
                    out_ref[quarter, pl.ds(start, 2 * local), pl.ds(chunk * HD, HD)] = both


def arrange(sizes, masks, place, pairs, wait):
    rows = sizes.share * sizes.count * sizes.local
    flat = [x for pair in pairs for x in pair]
    return pl.pallas_call(
        functools.partial(arrange_kernel, sizes, masks),
        out_shape=jax.ShapeDtypeStruct((len(pairs), rows, VW), BF16),
        in_specs=[SMEM_SPEC] + [VMEM_SPEC] * (len(flat) + 1),
        out_specs=VMEM_SPEC,
        compiler_params=limits(),
    )(place, *flat, wait)


def fetch_kernel(sizes, place_ref, *refs):
    count = len(refs) // 2
    sems = refs[-1]
    mine = pl.ds(pl.multiple_of(place_ref[2] * sizes.width, HD), sizes.width)
    copies = []
    for slot in range(count):
        source = refs[slot].at[:, mine] if slot < 3 else refs[slot]
        copies.append(pltpu.make_async_copy(source, refs[count + slot], sems.at[slot]))
        copies[-1].start()
    for copy in copies:
        copy.wait()


def fetch(sizes, place, arrays):
    shapes = [x.shape if slot >= 3 else (x.shape[0], sizes.width) for slot, x in enumerate(arrays)]
    return pl.pallas_call(
        functools.partial(fetch_kernel, sizes),
        out_shape=[jax.ShapeDtypeStruct(shape, x.dtype) for shape, x in zip(shapes, arrays)],
        in_specs=[SMEM_SPEC] + [HBM_SPEC] * len(arrays),
        out_specs=[VMEM_SPEC] * len(arrays),
        scratch_shapes=[pltpu.SemaphoreType.DMA((len(arrays),))],
        compiler_params=limits(),
        cost_estimate=pl.CostEstimate(flops=1, bytes_accessed=1, transcendentals=0),
    )(place, *[in_hbm(x) for x in arrays])


FACTOR = HD ** (-0.5) * math.log2(math.e)


def load_pieces(sizes, in_refs, key_scr, value_scr):
    tok_rows, part_rows = sizes.tok_rows, sizes.part_rows
    for src, ref in enumerate(in_refs):
        rows = pl.ds(src * tok_rows, tok_rows)
        key_scr[rows, :] = ref[pl.ds(part_rows, tok_rows), :]
        for head in range(sizes.heads):
            value_scr[rows, pl.ds(2 * head * HD, HD)] = ref[
                pl.ds(part_rows + tok_rows, tok_rows), pl.ds(head * HD, HD)
            ]
    ones = jnp.ones((len(in_refs) * tok_rows, HD), BF16)
    for head in range(sizes.heads):
        value_scr[:, pl.ds((2 * head + 1) * HD, HD)] = ones


def soft_part(query, key_scr, value_scr, rows, head, before):
    logits = mm_nt(query, key_scr[rows, pl.ds(head * HD, HD)])
    top = jnp.max(logits, axis=-1, keepdims=True)
    if before:
        top = jnp.maximum(top, before[2])
    weights = jnp.exp2((logits - top) * FACTOR).astype(BF16)
    both = mm(weights, value_scr[rows, pl.ds(2 * head * HD, 2 * HD)])
    mixed, total = both[:, :HD], both[:, HD:]
    if before:
        shrink = jnp.exp2((before[2] - top) * FACTOR)
        mixed, total = mixed + before[0] * shrink, total + before[1] * shrink
    return mixed, total, top


def piece_scratch(sizes, count):
    lat_rows = count * sizes.tok_rows
    return [
        pltpu.VMEM((lat_rows, sizes.width), BF16),
        pltpu.VMEM((lat_rows, 2 * sizes.width), BF16),
    ]


def early_kernel(sizes, count, *refs):
    in_refs, refs = refs[:count], refs[count + 1 :]
    sum_ref, stat_ref, key_scr, value_scr = refs
    load_pieces(sizes, in_refs, key_scr, value_scr)
    left = lax.broadcasted_iota(jnp.int32, (sizes.part_rows, HD), 1) < HD // 2
    rows = pl.ds(0, count * sizes.tok_rows)
    for src in range(count):
        results = [
            soft_part(
                in_refs[src][pl.ds(0, sizes.part_rows), pl.ds(head * HD, HD)],
                key_scr, value_scr, rows, head, None,
            )
            for head in range(sizes.heads)
        ]
        for head, (mixed, total, top) in enumerate(results):
            sum_ref[src, head] = mixed
            stat_ref[src, head] = jnp.where(left, top, total)


def attend_early(sizes, received, wait):
    count = len(received)
    shape = jax.ShapeDtypeStruct((count, sizes.heads, sizes.part_rows, HD), F32)
    return pl.pallas_call(
        functools.partial(early_kernel, sizes, count),
        out_shape=(shape, shape),
        in_specs=[VMEM_SPEC] * (count + 1),
        out_specs=(VMEM_SPEC, VMEM_SPEC),
        scratch_shapes=piece_scratch(sizes, count),
        compiler_params=limits(12),
        cost_estimate=pl.CostEstimate(flops=1, bytes_accessed=1, transcendentals=0),
    )(*received, wait)


def attend_kernel(sizes, masks, early, place_ref, *refs):
    count, heads, width = sizes.count, sizes.heads, sizes.width
    tok_rows, part_rows = sizes.tok_rows, sizes.part_rows
    in_refs, refs = refs[:count], refs[count:]
    kept_refs, refs = refs[: 2 if early else 0], refs[2 if early else 0 :]
    scale_ref, shift_ref, proj_ref, mod_ref, lat_ref, *refs = refs
    key_scr, value_scr, mod_scr = refs
    half = part_rows // 2
    me = place_ref[0]
    gain = 1.0 + scale_ref[...]
    shift = shift_ref[...]
    load_pieces(sizes, in_refs, key_scr, value_scr)
    for src in range(count):
        mixed = []
        for head in range(heads):
            before = None
            rows = pl.ds(0, count * tok_rows)
            if src < early:
                rows = pl.ds(early * tok_rows, (count - early) * tok_rows)
                stat = kept_refs[1][src, head]
                before = (kept_refs[0][src, head], stat[:, HD - 1 :], stat[:, :1])
            query = in_refs[src][pl.ds(0, part_rows), pl.ds(head * HD, HD)]
            value, total, _ = soft_part(query, key_scr, value_scr, rows, head, before)
            mixed.append(value / total)
        attended = jnp.concatenate(mixed, axis=1) if heads > 1 else mixed[0]
        mod_scr[src] = (attended * gain + shift).astype(BF16)
    sides = [
        mm_nt(mod_scr[:, rows, :].reshape(count * half, width), proj_ref[...])
        for rows in (slice(0, half), slice(half, part_rows))
    ]
    latent = jnp.concatenate(sides, axis=1).astype(BF16)
    for src in range(count):
        place = jnp.bitwise_xor(me, masks[src])
        mod_ref[place] = mod_scr[src]
        lat_ref[place] = latent[src * half : (src + 1) * half]


def attend(sizes, masks, place, received, kept, scales, shifts, proj):
    count, width, heads = sizes.count, sizes.width, sizes.heads
    lat_rows = count * sizes.tok_rows
    query_rows = count * sizes.part_rows
    early = kept[0].shape[0] if kept else 0
    return pl.pallas_call(
        functools.partial(attend_kernel, sizes, masks, early),
        out_shape=(
            jax.ShapeDtypeStruct((count, sizes.part_rows, width), BF16),
            jax.ShapeDtypeStruct((count, sizes.part_rows // 2, 2 * CH), BF16),
        ),
        in_specs=[SMEM_SPEC] + [VMEM_SPEC] * (count + len(kept) + 3),
        out_specs=(VMEM_SPEC, VMEM_SPEC),
        scratch_shapes=piece_scratch(sizes, count)
        + [pltpu.VMEM((count, sizes.part_rows, width), BF16)],
        compiler_params=limits(16),
        cost_estimate=pl.CostEstimate(
            flops=4 * query_rows * lat_rows * width,
            bytes_accessed=2 * (query_rows * 2 + lat_rows * 2) * width,
            transcendentals=query_rows * lat_rows * heads,
        ),
    )(place, *received, *kept, scales, shifts, proj)


def total_kernel(copies, *refs):
    out_ref = refs[-1]
    if len(refs) == 2:
        parts = [refs[0][i].astype(F32) for i in range(refs[0].shape[0])]
    else:
        parts = [ref[...].astype(F32) for ref in refs[:-1]]
    while len(parts) > 1:
        parts = [parts[i] + parts[i + 1] for i in range(0, len(parts), 2)]
    for copy in range(copies):
        out_ref[copy] = parts[0].astype(BF16)


def total_copies(arrays, copies):
    return pl.pallas_call(
        functools.partial(total_kernel, copies),
        out_shape=jax.ShapeDtypeStruct((copies,) + arrays[0].shape[-2:], BF16),
        in_specs=[VMEM_SPEC] * len(arrays),
        out_specs=VMEM_SPEC,
        compiler_params=limits(),
    )(*arrays)


def lane_mean(x, count):
    return jnp.sum(x, axis=-1, keepdims=True) * (1.0 / count)


def head_kernel(grid_rows, fused, embed_masks, out_factor, place_ref, lat_ref, *refs):
    embed_refs, refs = refs[: len(embed_masks)], refs[len(embed_masks) :]
    pos_ref, pre_ref, post_ref, prompt_ref, cot_ref, mod_ref, *refs = refs
    reward_ref, grad_ref, weight_ref, lat_scr, grad_scr, block_scr, back_scr = refs
    patch_rows = grid_rows // 4
    patch_cols = GW // 4
    patches = patch_rows * patch_cols
    lat_scr[...] = lat_ref[...].astype(F32)

    data = place_ref[1]
    shares = [
        (jnp.bitwise_xor(data, mask), ref, slot)
        for ref, masks in zip(embed_refs, embed_masks)
        for slot, mask in enumerate(masks)
    ]
    share_rows = embed_refs[0].shape[1]
    for hi in range(2):
        wide = []
        for tx in range(4):
            rows = [
                lat_scr[pl.ds((2 * pr + hi) * GW + tx, patch_cols, stride=4), :]
                for pr in range(patch_rows)
            ]
            wide.append(jnp.concatenate(rows, axis=0))
        for side in range(2):
            lanes = slice(side * CH, (side + 1) * CH)
            line = jnp.concatenate([x[:, lanes] for x in wide], axis=1).astype(BF16)
            first = (2 * hi + side) * 4 * CH
            if share_rows >= 4 * CH:
                at = first % share_rows
                block_scr[first // share_rows, :, pl.ds(at, 4 * CH)] = line
            else:
                for at in range(0, 4 * CH, share_rows):
                    block_scr[(first + at) // share_rows] = line[:, at : at + share_rows]
    embedded = pos_ref[...].astype(F32)
    for number, ref, slot in shares:
        embedded = embedded + mm(block_scr[number], ref[slot])
    pre = pre_ref[...].reshape(1, VW)
    post = post_ref[...].reshape(1, VW)
    prompt = prompt_ref[...]
    center = embedded - lane_mean(embedded, VW)
    rstd = lax.rsqrt(lane_mean(center * center, VW) + EPS)
    unit = center * rstd
    pooled = jnp.sum(unit, axis=0, keepdims=True) * (1.0 / patches) * pre
    pooled_center = pooled - lane_mean(pooled, VW)
    pooled_rstd = lax.rsqrt(lane_mean(pooled_center * pooled_center, VW) + EPS)
    pooled_unit = pooled_center * pooled_rstd
    final = pooled_unit * post
    dot = jnp.sum(final * prompt, axis=-1, keepdims=True)
    final_sq = jnp.sum(final * final, axis=-1, keepdims=True)
    prompt_sq = jnp.sum(prompt * prompt, axis=-1, keepdims=True)
    final_len = jnp.sqrt(final_sq)
    prompt_len = jnp.sqrt(prompt_sq)
    cosine = dot / (final_len * prompt_len)
    reward_ref[...] = jnp.broadcast_to(100.0 * cosine, reward_ref.shape)
    cot = cot_ref[0]
    final_grad = (100.0 * cot) * (prompt / (final_len * prompt_len) - final * (cosine / final_sq))
    unit_grad = final_grad * post
    pooled_grad = pooled_rstd * (
        unit_grad
        - lane_mean(unit_grad, VW)
        - pooled_unit * lane_mean(unit_grad * pooled_unit, VW)
    )
    flow = pooled_grad * pre * (1.0 / patches)
    embed_grad = rstd * (flow - lane_mean(flow, VW) - unit * lane_mean(flow * unit, VW))
    high = embed_grad.astype(BF16)
    low = (embed_grad - high.astype(F32)).astype(BF16)
    stacked = jnp.concatenate([high, low], axis=0)
    for number, ref, slot in shares:
        both = mm_nt(stacked, ref[slot])
        back_scr[number] = both[:patches] + both[patches:]
    back = jnp.concatenate([back_scr[i] for i in range(16 * CH // share_rows)], axis=1)
    for hi in range(2):
        for tx in range(4):
            first = (4 * (2 * hi) + tx) * CH
            second = (4 * (2 * hi + 1) + tx) * CH
            piece = jnp.concatenate(
                [back[:, first : first + CH], back[:, second : second + CH]], axis=1
            )
            for pr in range(patch_rows):
                grad_scr[pl.ds((2 * pr + hi) * GW + tx, patch_cols, stride=4), :] = piece[
                    pr * patch_cols : (pr + 1) * patch_cols
                ]
    grad = grad_scr[...].astype(BF16)
    grad_ref[...] = grad
    if fused:
        store_readout_grad(grad, mod_ref, out_factor, weight_ref)
    else:
        weight_ref[...] = jnp.zeros_like(weight_ref)


def store_readout_grad(grad, mod_ref, out_factor, out_ref):
    turned = grad.astype(F32).T.astype(BF16)
    count, rows, width = mod_ref.shape
    half = rows // 2
    first = mod_ref[:, :half, :].reshape(count * half, width)
    second = mod_ref[:, half:, :].reshape(count * half, width)
    total = mm(turned[:CH], first) + mm(turned[CH:], second)
    out_ref[...] = (total * out_factor).astype(BF16)


def reward_head(
    place, latent, embed, pos, pre, post, prompt, cot, modulated, grid_rows, fused, out_factor
):
    patches = grid_rows * GW // 16
    rows = grid_rows * GW // 2
    width = modulated.shape[2]
    embed_arrays, embed_masks = [x for x, _ in embed], [masks for _, masks in embed]
    share_rows = embed_arrays[0].shape[1]
    return pl.pallas_call(
        functools.partial(head_kernel, grid_rows, fused, embed_masks, out_factor),
        out_shape=(
            jax.ShapeDtypeStruct((1, 128), F32),
            jax.ShapeDtypeStruct((rows, 2 * CH), BF16),
            jax.ShapeDtypeStruct((CH, width), BF16),
        ),
        in_specs=[SMEM_SPEC, VMEM_SPEC]
        + [VMEM_SPEC] * len(embed_arrays)
        + [VMEM_SPEC] * 4
        + [SMEM_SPEC, VMEM_SPEC],
        out_specs=(VMEM_SPEC, VMEM_SPEC, VMEM_SPEC),
        scratch_shapes=[
            pltpu.VMEM((rows, 2 * CH), F32),
            pltpu.VMEM((rows, 2 * CH), F32),
            pltpu.VMEM((16 * CH // share_rows, patches, share_rows), BF16),
            pltpu.VMEM((16 * CH // share_rows, patches, share_rows), F32),
        ],
        compiler_params=limits(16),
        cost_estimate=pl.CostEstimate(
            flops=6 * patches * 16 * CH * VW,
            bytes_accessed=2 * 16 * CH * VW + 2 * patches * VW,
            transcendentals=0,
        ),
    )(place, latent, *embed_arrays, pos, pre, post, prompt, cot, modulated)


def spread_kernel(
    count, half, heads, place_ref, grad_ref, scale_ref, proj_ref, out_ref, scale_scr, proj_scr, sems
):
    width = heads * HD
    mine = pl.ds(pl.multiple_of(place_ref[2] * width, HD), width)
    copies = [
        pltpu.make_async_copy(scale_ref.at[:, mine], scale_scr, sems.at[0]),
        pltpu.make_async_copy(proj_ref.at[:, mine], proj_scr, sems.at[1]),
    ]
    for copy in copies:
        copy.start()
    for copy in copies:
        copy.wait()
    gain = 1.0 + scale_scr[...]
    proj = proj_scr[...]
    zero = jnp.zeros_like(proj)
    sides = (jnp.concatenate([proj, zero], axis=0), jnp.concatenate([zero, proj], axis=0))
    for src in range(count):
        grad = grad_ref[pl.ds(src * half, half), :]
        for side in range(2):
            rows = (mm(grad, sides[side]) * gain).astype(BF16)
            for head in range(heads):
                out_ref[0, head, pl.ds((2 * src + side) * half, half), :] = rows[
                    :, head * HD : (head + 1) * HD
                ]


def spread(place, grad, scales, proj, count, half, heads):
    return pl.pallas_call(
        functools.partial(spread_kernel, count, half, heads),
        out_shape=jax.ShapeDtypeStruct((1, heads, 2 * count * half, HD), BF16),
        in_specs=[SMEM_SPEC, VMEM_SPEC, HBM_SPEC, HBM_SPEC],
        out_specs=VMEM_SPEC,
        scratch_shapes=[
            pltpu.VMEM((1, heads * HD), F32),
            pltpu.VMEM((CH, heads * HD), BF16),
            pltpu.SemaphoreType.DMA((2,)),
        ],
        compiler_params=limits(),
        cost_estimate=pl.CostEstimate(
            flops=8 * count * half * CH * heads * HD,
            bytes_accessed=4 * count * half * heads * HD,
            transcendentals=0,
        ),
    )(place, grad, scales, proj)


def weight_kernel(out_factor, grad_ref, *refs):
    store_readout_grad(grad_ref[...], refs[0], out_factor, refs[1])


def weight_call(grad, modulated, out_factor):
    return pl.pallas_call(
        functools.partial(weight_kernel, out_factor),
        out_shape=jax.ShapeDtypeStruct((CH, modulated.shape[2]), BF16),
        in_specs=[VMEM_SPEC] * 2,
        out_specs=VMEM_SPEC,
        compiler_params=limits(),
    )(grad, modulated)


def finish_kernel(in_ref, out_ref):
    count, _, width = in_ref.shape
    for group in range(count):
        out_ref[:, pl.ds(group * width, width)] = in_ref[group].astype(F32)


def finish(blocks):
    return pl.pallas_call(
        finish_kernel,
        out_shape=jax.ShapeDtypeStruct((CH, HEADS * HD), F32),
        in_specs=[VMEM_SPEC],
        out_specs=VMEM_SPEC,
        compiler_params=limits(),
    )(blocks)


def swap(x, axis, mask):
    count = lax.axis_size(axis)
    return lax.ppermute(x, axis, [(i, i ^ mask) for i in range(count)])


def all_to_all(x, groups=None):
    return lax.all_to_all(
        x, "seq", split_axis=0, concat_axis=0, tiled=True, axis_index_groups=groups
    )


def swap_both(x, seq_mask, data_mask):
    seq_count, data_count = lax.axis_size("seq"), lax.axis_size("dp")
    pairs = [
        (i * data_count + j, (i ^ seq_mask) * data_count + (j ^ data_mask))
        for i in range(seq_count)
        for j in range(data_count)
    ]
    return lax.ppermute(x, ("seq", "dp"), pairs)


def on_device(
    queries,
    keys,
    values,
    shifts,
    scales,
    proj_out,
    patch_embed,
    pos_embed,
    pre_gain,
    post_gain,
    prompt,
    cotangent,
):
    seq_count = lax.axis_size("seq")
    data_count = lax.axis_size("dp")
    tok_rows = queries.shape[1]
    sizes = Sizes(seq_count, data_count, tok_rows, patch_embed)
    query_parts, head_count, part_rows = sizes.query_parts, sizes.heads, sizes.part_rows
    group_count = HEADS // head_count
    seq_index = lax.axis_index("seq")
    head_group = seq_index // query_parts
    query_part = seq_index % query_parts
    half = part_rows // 2
    lat_rows = seq_count * tok_rows
    grid_rows = lat_rows // GW
    canonical = part_rows == 2 * GW
    place = jnp.stack([seq_index, lax.axis_index("dp"), head_group]).astype(jnp.int32)
    proj_turned = proj_out.T
    out_factor = 1.0 / math.sqrt(data_count * lat_rows)

    masks = sizes.pieces()
    packed = pack(
        sizes, in_hbm(queries), in_hbm(keys), in_hbm(values), in_hbm(patch_embed)
    )
    received = [swap(x, "seq", mask) if mask else x for mask, x in zip(masks, packed)]
    bits = [1 << b for b in reversed(range(data_count.bit_length() - 1))]
    shared = sizes.share < patch_embed.shape[0]
    scale, shift, proj, pos, pre, post, words = fetch(
        sizes, place, [scales, shifts, proj_turned, pos_embed, pre_gain, post_gain, prompt]
    )

    kept, order = [], list(range(seq_count))
    if seq_count == 8:
        late = [slot for slot, mask in enumerate(masks) if mask in (6, 7)]
        order = [slot for slot in order if slot not in late]
        kept = attend_early(sizes, [received[slot] for slot in order], scale)
        order = order + late
    if sizes.riding:
        ride = [slot for slot, mask in enumerate(masks) if sizes.rides(mask)]
        two = collect(sizes, [received[slot] for slot in ride])
        held = join(two, swap(two, "seq", 2), kept)
        ride_masks = [masks[slot] for slot in ride]
        ride_masks = ride_masks + [mask ^ 2 for mask in ride_masks]
        pairs = [
            (held, swap(held, "seq", 1)),
            (swap(held, "dp", bits[0]), swap_both(held, 1, bits[0])),
        ]

    modulated, latent_part = attend(
        sizes, [masks[slot] for slot in order], place, [received[slot] for slot in order], kept,
        scale, shift, proj,
    )

    if not sizes.riding:
        mine = patch_embed
        if shared:
            mine = lax.dynamic_slice_in_dim(
                patch_embed, lax.axis_index("dp") * sizes.share, sizes.share, 0
            )
        mine = lax.all_gather(mine, "seq", axis=1, tiled=True).reshape(-1, VW)
        embed = [(mine[None], [0])]
        if shared:
            embed = embed + [(swap(mine[None], "dp", bits[0]), [bits[0]])]

    groups = None
    if query_parts > 1:
        groups = [[g * query_parts + r for g in range(group_count)] for r in range(query_parts)]
    per_share = seq_count // group_count
    parts = all_to_all(latent_part.reshape(group_count, per_share * half, 2 * CH), groups)
    summed = total_copies([parts], seq_count)
    if sizes.riding:
        embed = [(arrange(sizes, ride_masks, place, pairs, summed), [0, bits[0]])]
    for bit in bits[1:] if shared else []:
        embed = embed + [(swap(x, "dp", bit), [m ^ bit for m in some]) for x, some in embed]
    latent = all_to_all(summed)
    if canonical:
        latent = latent.reshape(lat_rows // 2, 2 * CH)
    else:
        latent = latent.reshape(group_count, query_parts, per_share, half, 2, CH)
        latent = latent.transpose(0, 2, 1, 4, 3, 5).reshape(grid_rows // 2, 2, GW, CH)
        latent = latent.transpose(0, 2, 1, 3).reshape(lat_rows // 2, 2 * CH)

    reward, grad, weight = reward_head(
        place, latent, embed, pos, pre, post, words,
        cotangent, modulated, grid_rows, canonical, out_factor,
    )
    if not canonical:
        tokens = grad.reshape(grid_rows // 2, GW, 2, CH).transpose(0, 2, 1, 3)
        tokens = tokens.reshape(seq_count, query_parts, 2, half, CH)
        tokens = lax.dynamic_index_in_dim(tokens, query_part, 1, keepdims=False)
        grad = tokens.transpose(0, 2, 1, 3).reshape(seq_count * half, 2 * CH)
        weight = weight_call(grad, modulated, out_factor)

    parts = [weight] + [swap(weight, "dp", mask) for mask in range(1, data_count)]
    attn_grad = spread(place, grad, in_hbm(scales), in_hbm(proj_turned), seq_count, half, head_count)
    if query_parts > 1:
        total = total_copies(parts, 1)[0]
        parts = [total] + [swap(total, "seq", mask) for mask in range(1, query_parts)]
    blocks = all_to_all(total_copies(parts, group_count), groups)
    return (reward[0, :1], attn_grad, finish(blocks).T)


def solution(mesh):
    return jax.shard_map(
        on_device,
        mesh=mesh,
        in_specs=(
            P("dp", "seq", None),
            P("dp", "seq", None),
            P("dp", "seq", None),
            P("dp", None),
            P("dp", None),
            P(),
            P(None, "seq", None),
            P(),
            P(),
            P(),
            P("dp", None),
            P("dp"),
        ),
        out_specs=(P("dp"), P("dp", "seq", None, None), P()),
        check_vma=False,
    )
```

```python
import functools
import math

import jax
import jax.numpy as jnp
from jax import lax
from jax.experimental import pallas as pl
from jax.experimental.pallas import tpu as pltpu
from jax.sharding import PartitionSpec as P

HEADS = 16
HD = 128
CH = 64
GW = 64
VW = 1280
EPS = 1e-05
BF16 = jnp.bfloat16
F32 = jnp.float32


def mm(a, b):
    return jnp.dot(a, b, preferred_element_type=F32)


def mm_nt(a, b):
    return lax.dot_general(a, b, (((1,), (1,)), ((), ())), preferred_element_type=F32)


def mm_tn(a, b):
    return lax.dot_general(a, b, (((0,), (0,)), ((), ())), preferred_element_type=F32)


SMEM_SPEC = pl.BlockSpec(memory_space=pltpu.SMEM)
VMEM_SPEC = pl.BlockSpec(memory_space=pltpu.VMEM)
HBM_SPEC = pl.BlockSpec(memory_space=pltpu.HBM)
ANY_SPEC = pl.BlockSpec(memory_space=pl.ANY)


def in_hbm(x):
    return pltpu.with_memory_space_constraint(x, pltpu.HBM)


def limits(mib=4):
    return pltpu.CompilerParams(vmem_limit_bytes=mib * 1024 * 1024)


class Sizes:
    def __init__(self, seq_count, data_count, tok_rows, patch_embed):
        self.count = seq_count
        self.query_parts = max(1, seq_count // HEADS)
        self.heads = max(1, HEADS // seq_count)
        self.width = self.heads * HD
        self.tok_rows = tok_rows
        self.part_rows = tok_rows // self.query_parts
        positions, self.local, _ = patch_embed.shape
        self.share = positions // data_count if positions % data_count == 0 else positions
        self.rows = self.part_rows + 2 * tok_rows
        self.share_rows = self.share * self.local
        self.chunks = VW // HD
        self.riding = self.local % 8 == 0 and self.share_rows % 16 == 0 and seq_count == 8
        self.riding = self.riding and 1 < data_count <= positions
        self.ride_rows = self.chunks * self.share_rows if self.riding else 0

    def pieces(self):
        return list(range(1, self.count)) + [0]

    def rides(self, mask):
        return self.riding and mask in (0, 4)

    def piece_shape(self, mask):
        return (self.rows + (self.ride_rows // self.heads if self.rides(mask) else 0), self.width)

    def ride_slices(self):
        deep = self.ride_rows // self.heads
        return [
            (pl.ds(self.rows, deep), pl.ds(at * HD, HD), pl.ds(at * deep, deep))
            for at in range(self.heads)
        ]


def pack_kernel(sizes, q_ref, k_ref, v_ref, embed_ref, *refs):
    pieces = sizes.pieces()
    out_refs = refs[: len(pieces)]
    q_scr, k_scr, v_scr, embed_scr, share_scr, in_sems, out_sems = refs[len(pieces) :]
    me = lax.axis_index("seq")
    tok_rows, part_rows, width = sizes.tok_rows, sizes.part_rows, sizes.width
    share = pl.ds(lax.axis_index("dp") * sizes.share, sizes.share)
    loads = [
        pltpu.make_async_copy(embed_ref.at[share], embed_scr, in_sems.at[3]),
        pltpu.make_async_copy(q_ref.at[0], q_scr, in_sems.at[0]),
        pltpu.make_async_copy(k_ref.at[0], k_scr, in_sems.at[1]),
        pltpu.make_async_copy(v_ref.at[0], v_scr, in_sems.at[2]),
    ]
    for load in loads:
        load.start()
    sent = [[], [], [], []]
    for slot, (mask, out) in enumerate(zip(pieces, out_refs)):
        dest = jnp.bitwise_xor(me, mask)
        group, part = dest // sizes.query_parts, dest % sizes.query_parts
        cols = pl.ds(pl.multiple_of(group * width, HD), width)
        first = pl.ds(pl.multiple_of(part * part_rows, part_rows), part_rows)
        for kind, source, rows in (
            (0, q_scr.at[first, cols], pl.ds(0, part_rows)),
            (1, k_scr.at[:, cols], pl.ds(part_rows, tok_rows)),
            (2, v_scr.at[:, cols], pl.ds(part_rows + tok_rows, tok_rows)),
        ):
            sent[kind].append(pltpu.make_async_copy(source, out.at[rows], out_sems.at[kind, slot]))
        if sizes.rides(mask):
            for at, (rows, place, from_rows) in enumerate(sizes.ride_slices()):
                sent[3].append(
                    pltpu.make_async_copy(
                        share_scr.at[from_rows], out.at[rows, place], out_sems.at[3 + at, slot]
                    )
                )
    loads[0].wait()
    if sizes.riding:
        for chunk in range(sizes.chunks):
            cols = embed_scr[:, :, pl.ds(chunk * HD, HD)].astype(F32)
            share_scr[pl.ds(chunk * sizes.share_rows, sizes.share_rows), :] = cols.reshape(
                sizes.share_rows, HD
            ).astype(BF16)
    for store in sent[3]:
        store.start()
    for kind in range(3):
        loads[kind + 1].wait()
        for store in sent[kind]:
            store.start()
    for stores in sent:
        for store in stores:
            store.wait()


def pack(sizes, queries, keys, values, patch_embed):
    tok_rows, full = queries.shape[1:]
    pieces = sizes.pieces()
    return pl.pallas_call(
        functools.partial(pack_kernel, sizes),
        out_shape=[jax.ShapeDtypeStruct(sizes.piece_shape(mask), BF16) for mask in pieces],
        in_specs=[HBM_SPEC] * 4,
        out_specs=[HBM_SPEC] * len(pieces),
        scratch_shapes=[pltpu.VMEM((tok_rows, full), BF16)] * 3
        + [
            pltpu.VMEM((sizes.share,) + patch_embed.shape[1:], BF16),
            pltpu.VMEM((max(16, sizes.ride_rows), HD), BF16),
            pltpu.SemaphoreType.DMA((4,)),
            pltpu.SemaphoreType.DMA((3 + sizes.heads, len(pieces))),
        ],
        compiler_params=limits(),
        cost_estimate=pl.CostEstimate(
            flops=0, bytes_accessed=12 * tok_rows * full, transcendentals=0
        ),
    )(queries, keys, values, patch_embed)


def collect_kernel(sizes, *refs):
    *in_refs, out_ref, sems = refs
    copies = []
    for slot, ref in enumerate(in_refs):
        for at, (rows, cols, to_rows) in enumerate(sizes.ride_slices()):
            copies.append(
                pltpu.make_async_copy(
                    ref.at[rows, cols], out_ref.at[slot, to_rows], sems.at[at, slot]
                )
            )
    for copy in copies:
        copy.start()
    for copy in copies:
        copy.wait()


def collect(sizes, arrays):
    return pl.pallas_call(
        functools.partial(collect_kernel, sizes),
        out_shape=jax.ShapeDtypeStruct((len(arrays), sizes.ride_rows, HD), BF16),
        in_specs=[ANY_SPEC] * len(arrays),
        out_specs=VMEM_SPEC,
        scratch_shapes=[pltpu.SemaphoreType.DMA((sizes.heads, len(arrays)))],
        compiler_params=limits(),
    )(*arrays)


def join_kernel(first_ref, second_ref, *refs):
    out_ref = refs[-1]
    count = first_ref.shape[0]
    out_ref[:count] = first_ref[...]
    out_ref[count:] = second_ref[...]


def join(first, second, others):
    return pl.pallas_call(
        join_kernel,
        out_shape=jax.ShapeDtypeStruct((2 * first.shape[0],) + first.shape[1:], BF16),
        in_specs=[VMEM_SPEC] * 2 + [ANY_SPEC] * len(others),
        out_specs=VMEM_SPEC,
        compiler_params=limits(),
    )(first, second, *others)


def arrange_kernel(sizes, masks, place_ref, *refs):
    *pair_refs, out_ref = refs[:-2] + refs[-1:]
    me = place_ref[0]
    odd = me % 2 == 1
    local = sizes.local
    for quarter in range(len(pair_refs) // 2):
        held_ref, got_ref = pair_refs[2 * quarter], pair_refs[2 * quarter + 1]
        for slot, mask in enumerate(masks):
            pair = jnp.bitwise_xor(me, mask) // 2
            for chunk in range(sizes.chunks):
                rows = pl.ds(chunk * sizes.share_rows, sizes.share_rows)
                held = held_ref[slot, rows, :].astype(F32)
                got = got_ref[slot, rows, :].astype(F32)
                first = jnp.where(odd, got, held)
                second = jnp.where(odd, held, got)
                for at in range(sizes.share):
                    part = slice(at * local, (at + 1) * local)
                    both = jnp.concatenate([first[part], second[part]], axis=0).astype(BF16)
                    start = pl.multiple_of(at * sizes.count * local + pair * 2 * local, 2 * local)
                    out_ref[quarter, pl.ds(start, 2 * local), pl.ds(chunk * HD, HD)] = both


def arrange(sizes, masks, place, pairs, wait):
    rows = sizes.share * sizes.count * sizes.local
    flat = [x for pair in pairs for x in pair]
    return pl.pallas_call(
        functools.partial(arrange_kernel, sizes, masks),
        out_shape=jax.ShapeDtypeStruct((len(pairs), rows, VW), BF16),
        in_specs=[SMEM_SPEC] + [VMEM_SPEC] * (len(flat) + 1),
        out_specs=VMEM_SPEC,
        compiler_params=limits(),
    )(place, *flat, wait)


def fetch_kernel(sizes, place_ref, cot_ref, *refs):
    *refs, row_ref, sems = refs
    count = len(refs) // 2
    row_ref[...] = jnp.full(row_ref.shape, cot_ref[0], F32)
    mine = pl.ds(pl.multiple_of(place_ref[2] * sizes.width, HD), sizes.width)
    copies = []
    for slot in range(count):
        source = refs[slot].at[:, mine] if slot < 3 else refs[slot]
        copies.append(pltpu.make_async_copy(source, refs[count + slot], sems.at[slot]))
        copies[-1].start()
    for copy in copies:
        copy.wait()


def fetch(sizes, place, cotangent, arrays):
    shapes = [x.shape if slot >= 3 else (x.shape[0], sizes.width) for slot, x in enumerate(arrays)]
    return pl.pallas_call(
        functools.partial(fetch_kernel, sizes),
        out_shape=[jax.ShapeDtypeStruct(shape, x.dtype) for shape, x in zip(shapes, arrays)]
        + [jax.ShapeDtypeStruct((1, 128), F32)],
        in_specs=[SMEM_SPEC] * 2 + [HBM_SPEC] * len(arrays),
        out_specs=[VMEM_SPEC] * (len(arrays) + 1),
        scratch_shapes=[pltpu.SemaphoreType.DMA((len(arrays),))],
        compiler_params=limits(),
        cost_estimate=pl.CostEstimate(flops=1, bytes_accessed=1, transcendentals=0),
    )(place, cotangent, *[in_hbm(x) for x in arrays])


FACTOR = HD ** (-0.5) * math.log2(math.e)


def load_pieces(sizes, in_refs, key_scr, value_scr):
    tok_rows, part_rows = sizes.tok_rows, sizes.part_rows
    for src, ref in enumerate(in_refs):
        rows = pl.ds(src * tok_rows, tok_rows)
        key_scr[rows, :] = ref[pl.ds(part_rows, tok_rows), :]
        for head in range(sizes.heads):
            value_scr[rows, pl.ds(2 * head * HD, HD)] = ref[
                pl.ds(part_rows + tok_rows, tok_rows), pl.ds(head * HD, HD)
            ]
    ones = jnp.ones((len(in_refs) * tok_rows, HD), BF16)
    for head in range(sizes.heads):
        value_scr[:, pl.ds((2 * head + 1) * HD, HD)] = ones


def soft_part(query, key_scr, value_scr, rows, head, before):
    logits = mm_nt(query, key_scr[rows, pl.ds(head * HD, HD)])
    top = jnp.max(logits, axis=-1, keepdims=True)
    if before:
        top = jnp.maximum(top, before[2])
    weights = jnp.exp2((logits - top) * FACTOR).astype(BF16)
    both = mm(weights, value_scr[rows, pl.ds(2 * head * HD, 2 * HD)])
    mixed, total = both[:, :HD], both[:, HD:]
    if before:
        shrink = jnp.exp2((before[2] - top) * FACTOR)
        mixed, total = mixed + before[0] * shrink, total + before[1] * shrink
    return mixed, total, top


def piece_scratch(sizes, count):
    lat_rows = count * sizes.tok_rows
    return [
        pltpu.VMEM((lat_rows, sizes.width), BF16),
        pltpu.VMEM((lat_rows, 2 * sizes.width), BF16),
    ]


def early_kernel(sizes, count, *refs):
    in_refs, refs = refs[:count], refs[count + 1 :]
    sum_ref, stat_ref, key_scr, value_scr = refs
    load_pieces(sizes, in_refs, key_scr, value_scr)
    left = lax.broadcasted_iota(jnp.int32, (sizes.part_rows, HD), 1) < HD // 2
    rows = pl.ds(0, count * sizes.tok_rows)
    for src in range(count):
        results = [
            soft_part(
                in_refs[src][pl.ds(0, sizes.part_rows), pl.ds(head * HD, HD)],
                key_scr, value_scr, rows, head, None,
            )
            for head in range(sizes.heads)
        ]
        for head, (mixed, total, top) in enumerate(results):
            sum_ref[src, head] = mixed
            stat_ref[src, head] = jnp.where(left, top, total)


def attend_early(sizes, received, wait):
    count = len(received)
    shape = jax.ShapeDtypeStruct((count, sizes.heads, sizes.part_rows, HD), F32)
    return pl.pallas_call(
        functools.partial(early_kernel, sizes, count),
        out_shape=(shape, shape),
        in_specs=[VMEM_SPEC] * (count + 1),
        out_specs=(VMEM_SPEC, VMEM_SPEC),
        scratch_shapes=piece_scratch(sizes, count),
        compiler_params=limits(12),
        cost_estimate=pl.CostEstimate(flops=1, bytes_accessed=1, transcendentals=0),
    )(*received, wait)


def attend_kernel(sizes, masks, early, place_ref, *refs):
    count, heads, width = sizes.count, sizes.heads, sizes.width
    tok_rows, part_rows = sizes.tok_rows, sizes.part_rows
    in_refs, refs = refs[:count], refs[count:]
    kept_refs, refs = refs[: 2 if early else 0], refs[2 if early else 0 :]
    scale_ref, shift_ref, proj_ref, mod_ref, lat_ref, *refs = refs
    key_scr, value_scr = refs
    half = part_rows // 2
    me = place_ref[0]
    gain = 1.0 + scale_ref[...]
    shift = shift_ref[...]
    load_pieces(sizes, in_refs, key_scr, value_scr)
    together = 2
    for first in range(0, count, together):
        results = []
        for src in range(first, first + together):
            mixed = []
            for head in range(heads):
                before = None
                rows = pl.ds(0, count * tok_rows)
                if src < early:
                    rows = pl.ds(early * tok_rows, (count - early) * tok_rows)
                    stat = kept_refs[1][src, head]
                    before = (kept_refs[0][src, head], stat[:, HD - 1 :], stat[:, :1])
                query = in_refs[src][pl.ds(0, part_rows), pl.ds(head * HD, HD)]
                value, total, _ = soft_part(query, key_scr, value_scr, rows, head, before)
                mixed.append(value / total)
            results.append(jnp.concatenate(mixed, axis=1) if heads > 1 else mixed[0])
        for at, attended in enumerate(results):
            modulated = (attended * gain + shift).astype(BF16)
            mod_ref[jnp.bitwise_xor(me, masks[first + at])] = modulated
    sides = [
        mm_nt(mod_ref[:, rows, :].reshape(count * half, width), proj_ref[...])
        for rows in (slice(0, half), slice(half, part_rows))
    ]
    latent = jnp.concatenate(sides, axis=1).astype(BF16)
    lat_ref[...] = latent.reshape(count, half, 2 * CH)


def attend(sizes, masks, place, received, kept, scales, shifts, proj):
    count, width, heads = sizes.count, sizes.width, sizes.heads
    lat_rows = count * sizes.tok_rows
    query_rows = count * sizes.part_rows
    early = kept[0].shape[0] if kept else 0
    return pl.pallas_call(
        functools.partial(attend_kernel, sizes, masks, early),
        out_shape=(
            jax.ShapeDtypeStruct((count, sizes.part_rows, width), BF16),
            jax.ShapeDtypeStruct((count, sizes.part_rows // 2, 2 * CH), BF16),
        ),
        in_specs=[SMEM_SPEC] + [VMEM_SPEC] * (count + len(kept) + 3),
        out_specs=(VMEM_SPEC, VMEM_SPEC),
        scratch_shapes=piece_scratch(sizes, count),
        compiler_params=limits(16),
        cost_estimate=pl.CostEstimate(
            flops=4 * query_rows * lat_rows * width,
            bytes_accessed=2 * (query_rows * 2 + lat_rows * 2) * width,
            transcendentals=query_rows * lat_rows * heads,
        ),
    )(place, *received, *kept, scales, shifts, proj)


def total_kernel(copies, count, *refs):
    out_ref = refs[-1]
    if count == 1:
        parts = [refs[0][i].astype(F32) for i in range(refs[0].shape[0])]
    else:
        parts = [ref[...].astype(F32) for ref in refs[:count]]
    while len(parts) > 1:
        parts = [parts[i] + parts[i + 1] for i in range(0, len(parts), 2)]
    for copy in range(copies):
        out_ref[copy] = parts[0].astype(BF16)


def total_copies(arrays, copies, others=()):
    return pl.pallas_call(
        functools.partial(total_kernel, copies, len(arrays)),
        out_shape=jax.ShapeDtypeStruct((copies,) + arrays[0].shape[-2:], BF16),
        in_specs=[VMEM_SPEC] * len(arrays) + [ANY_SPEC] * len(others),
        out_specs=VMEM_SPEC,
        compiler_params=limits(),
    )(*arrays, *others)


def lane_mean(x, count):
    return jnp.sum(x, axis=-1, keepdims=True) * (1.0 / count)


def head_kernel(grid_rows, fused, embed_masks, out_factor, place_ref, lat_ref, *refs):
    embed_refs, refs = refs[: len(embed_masks)], refs[len(embed_masks) :]
    pos_ref, pre_ref, post_ref, prompt_ref, cot_ref, mod_ref, *refs = refs
    reward_ref, grad_ref, weight_ref, lat_scr, grad_scr, block_scr, back_scr = refs
    patch_rows = grid_rows // 4
    patch_cols = GW // 4
    patches = patch_rows * patch_cols
    lat_scr[...] = lat_ref[...].astype(F32)

    data = place_ref[1]
    shares = [
        (jnp.bitwise_xor(data, mask), ref, slot)
        for ref, masks in zip(embed_refs, embed_masks)
        for slot, mask in enumerate(masks)
    ]
    share_rows = embed_refs[0].shape[1]
    for hi in range(2):
        wide = []
        for tx in range(4):
            rows = [
                lat_scr[pl.ds((2 * pr + hi) * GW + tx, patch_cols, stride=4), :]
                for pr in range(patch_rows)
            ]
            wide.append(jnp.concatenate(rows, axis=0))
        for side in range(2):
            lanes = slice(side * CH, (side + 1) * CH)
            line = jnp.concatenate([x[:, lanes] for x in wide], axis=1).astype(BF16)
            first = (2 * hi + side) * 4 * CH
            if share_rows >= 4 * CH:
                at = first % share_rows
                block_scr[first // share_rows, :, pl.ds(at, 4 * CH)] = line
            else:
                for at in range(0, 4 * CH, share_rows):
                    block_scr[(first + at) // share_rows] = line[:, at : at + share_rows]
    embedded = pos_ref[...].astype(F32)
    for number, ref, slot in shares:
        embedded = embedded + mm(block_scr[number], ref[slot])
    pre = pre_ref[...].reshape(1, VW)
    post = post_ref[...].reshape(1, VW)
    prompt = prompt_ref[...]
    center = embedded - lane_mean(embedded, VW)
    rstd = lax.rsqrt(lane_mean(center * center, VW) + EPS)
    unit = center * rstd
    pooled = jnp.sum(unit, axis=0, keepdims=True) * (1.0 / patches) * pre
    pooled_center = pooled - lane_mean(pooled, VW)
    pooled_rstd = lax.rsqrt(lane_mean(pooled_center * pooled_center, VW) + EPS)
    pooled_unit = pooled_center * pooled_rstd
    final = pooled_unit * post
    dot = jnp.sum(final * prompt, axis=-1, keepdims=True)
    final_sq = jnp.sum(final * final, axis=-1, keepdims=True)
    prompt_sq = jnp.sum(prompt * prompt, axis=-1, keepdims=True)
    final_len = jnp.sqrt(final_sq)
    prompt_len = jnp.sqrt(prompt_sq)
    cosine = dot / (final_len * prompt_len)
    reward_ref[...] = jnp.broadcast_to(100.0 * cosine, reward_ref.shape)
    cot = cot_ref[:, :1]
    final_grad = (100.0 * cot) * (prompt / (final_len * prompt_len) - final * (cosine / final_sq))
    unit_grad = final_grad * post
    pooled_grad = pooled_rstd * (
        unit_grad
        - lane_mean(unit_grad, VW)
        - pooled_unit * lane_mean(unit_grad * pooled_unit, VW)
    )
    flow = pooled_grad * pre * (1.0 / patches)
    embed_grad = rstd * (flow - lane_mean(flow, VW) - unit * lane_mean(flow * unit, VW))
    high = embed_grad.astype(BF16)
    low = (embed_grad - high.astype(F32)).astype(BF16)
    stacked = jnp.concatenate([high, low], axis=0)
    for number, ref, slot in shares:
        both = mm_nt(stacked, ref[slot])
        back_scr[number] = both[:patches] + both[patches:]
    back = jnp.concatenate([back_scr[i] for i in range(16 * CH // share_rows)], axis=1)
    for hi in range(2):
        for tx in range(4):
            first = (4 * (2 * hi) + tx) * CH
            second = (4 * (2 * hi + 1) + tx) * CH
            piece = jnp.concatenate(
                [back[:, first : first + CH], back[:, second : second + CH]], axis=1
            )
            for pr in range(patch_rows):
                grad_scr[pl.ds((2 * pr + hi) * GW + tx, patch_cols, stride=4), :] = piece[
                    pr * patch_cols : (pr + 1) * patch_cols
                ]
    grad = grad_scr[...].astype(BF16)
    grad_ref[...] = grad
    if fused:
        store_readout_grad(grad, mod_ref, out_factor, weight_ref)
    else:
        weight_ref[...] = jnp.zeros_like(weight_ref)


def store_readout_grad(grad, mod_ref, out_factor, out_ref):
    turned = grad.astype(F32).T.astype(BF16)
    count, rows, width = mod_ref.shape
    half = rows // 2
    first = mod_ref[:, :half, :].reshape(count * half, width)
    second = mod_ref[:, half:, :].reshape(count * half, width)
    total = mm(turned[:CH], first) + mm(turned[CH:], second)
    out_ref[...] = (total * out_factor).astype(BF16)


def reward_head(
    place, latent, embed, pos, pre, post, prompt, cot, modulated, grid_rows, fused, out_factor
):
    patches = grid_rows * GW // 16
    rows = grid_rows * GW // 2
    width = modulated.shape[2]
    embed_arrays, embed_masks = [x for x, _ in embed], [masks for _, masks in embed]
    share_rows = embed_arrays[0].shape[1]
    return pl.pallas_call(
        functools.partial(head_kernel, grid_rows, fused, embed_masks, out_factor),
        out_shape=(
            jax.ShapeDtypeStruct((1, 128), F32),
            jax.ShapeDtypeStruct((rows, 2 * CH), BF16),
            jax.ShapeDtypeStruct((CH, width), BF16),
        ),
        in_specs=[SMEM_SPEC, VMEM_SPEC]
        + [VMEM_SPEC] * len(embed_arrays)
        + [VMEM_SPEC] * 6,
        out_specs=(VMEM_SPEC, VMEM_SPEC, VMEM_SPEC),
        scratch_shapes=[
            pltpu.VMEM((rows, 2 * CH), F32),
            pltpu.VMEM((rows, 2 * CH), F32),
            pltpu.VMEM((16 * CH // share_rows, patches, share_rows), BF16),
            pltpu.VMEM((16 * CH // share_rows, patches, share_rows), F32),
        ],
        compiler_params=limits(16),
        cost_estimate=pl.CostEstimate(
            flops=6 * patches * 16 * CH * VW,
            bytes_accessed=2 * 16 * CH * VW + 2 * patches * VW,
            transcendentals=0,
        ),
    )(place, latent, *embed_arrays, pos, pre, post, prompt, cot, modulated)


def spread_kernel(count, half, heads, grad_ref, scale_ref, proj_ref, out_ref):
    gain = 1.0 + scale_ref[...]
    proj = proj_ref[...]
    zero = jnp.zeros_like(proj)
    sides = (jnp.concatenate([proj, zero], axis=0), jnp.concatenate([zero, proj], axis=0))
    for src in range(count):
        grad = grad_ref[pl.ds(src * half, half), :]
        for side in range(2):
            rows = (mm(grad, sides[side]) * gain).astype(BF16)
            for head in range(heads):
                out_ref[0, head, pl.ds((2 * src + side) * half, half), :] = rows[
                    :, head * HD : (head + 1) * HD
                ]


def spread(grad, scales, proj, count, half, heads):
    return pl.pallas_call(
        functools.partial(spread_kernel, count, half, heads),
        out_shape=jax.ShapeDtypeStruct((1, heads, 2 * count * half, HD), BF16),
        in_specs=[VMEM_SPEC] * 3,
        out_specs=VMEM_SPEC,
        compiler_params=limits(),
        cost_estimate=pl.CostEstimate(
            flops=8 * count * half * CH * heads * HD,
            bytes_accessed=4 * count * half * heads * HD,
            transcendentals=0,
        ),
    )(grad, scales, proj)


def weight_kernel(out_factor, grad_ref, *refs):
    store_readout_grad(grad_ref[...], refs[0], out_factor, refs[1])


def weight_call(grad, modulated, out_factor):
    return pl.pallas_call(
        functools.partial(weight_kernel, out_factor),
        out_shape=jax.ShapeDtypeStruct((CH, modulated.shape[2]), BF16),
        in_specs=[VMEM_SPEC] * 2,
        out_specs=VMEM_SPEC,
        compiler_params=limits(),
    )(grad, modulated)


def finish_kernel(in_ref, out_ref):
    count, _, width = in_ref.shape
    for group in range(count):
        out_ref[:, pl.ds(group * width, width)] = in_ref[group].astype(F32)


def finish(blocks):
    return pl.pallas_call(
        finish_kernel,
        out_shape=jax.ShapeDtypeStruct((CH, HEADS * HD), F32),
        in_specs=[VMEM_SPEC],
        out_specs=VMEM_SPEC,
        compiler_params=limits(),
    )(blocks)


def swap(x, axis, mask):
    count = lax.axis_size(axis)
    return lax.ppermute(x, axis, [(i, i ^ mask) for i in range(count)])


def all_to_all(x, groups=None):
    return lax.all_to_all(
        x, "seq", split_axis=0, concat_axis=0, tiled=True, axis_index_groups=groups
    )


def swap_both(x, seq_mask, data_mask):
    seq_count, data_count = lax.axis_size("seq"), lax.axis_size("dp")
    pairs = [
        (i * data_count + j, (i ^ seq_mask) * data_count + (j ^ data_mask))
        for i in range(seq_count)
        for j in range(data_count)
    ]
    return lax.ppermute(x, ("seq", "dp"), pairs)


def on_device(
    queries,
    keys,
    values,
    shifts,
    scales,
    proj_out,
    patch_embed,
    pos_embed,
    pre_gain,
    post_gain,
    prompt,
    cotangent,
):
    seq_count = lax.axis_size("seq")
    data_count = lax.axis_size("dp")
    tok_rows = queries.shape[1]
    sizes = Sizes(seq_count, data_count, tok_rows, patch_embed)
    query_parts, head_count, part_rows = sizes.query_parts, sizes.heads, sizes.part_rows
    group_count = HEADS // head_count
    seq_index = lax.axis_index("seq")
    head_group = seq_index // query_parts
    query_part = seq_index % query_parts
    half = part_rows // 2
    lat_rows = seq_count * tok_rows
    grid_rows = lat_rows // GW
    canonical = part_rows == 2 * GW
    place = jnp.stack([seq_index, lax.axis_index("dp"), head_group]).astype(jnp.int32)
    proj_turned = proj_out.T
    out_factor = 1.0 / math.sqrt(data_count * lat_rows)

    masks = sizes.pieces()
    packed = pack(
        sizes, in_hbm(queries), in_hbm(keys), in_hbm(values), in_hbm(patch_embed)
    )
    received = [swap(x, "seq", mask) if mask else x for mask, x in zip(masks, packed)]
    bits = [1 << b for b in reversed(range(data_count.bit_length() - 1))]
    shared = sizes.share < patch_embed.shape[0]
    scale, shift, proj, pos, pre, post, words, cot = fetch(
        sizes, place, cotangent, [scales, shifts, proj_turned, pos_embed, pre_gain, post_gain, prompt]
    )

    kept, order = [], list(range(seq_count))
    if seq_count == 8:
        late = [slot for slot, mask in enumerate(masks) if mask in (6, 7)]
        order = [slot for slot in order if slot not in late]
        kept = attend_early(sizes, [received[slot] for slot in order], scale)
        order = order + late
    if sizes.riding:
        ride = [slot for slot, mask in enumerate(masks) if sizes.rides(mask)]
        two = collect(sizes, [received[slot] for slot in ride])
        held = join(two, swap(two, "seq", 2), kept)
        ride_masks = [masks[slot] for slot in ride]
        ride_masks = ride_masks + [mask ^ 2 for mask in ride_masks]
        pairs = [
            (held, swap(held, "seq", 1)),
            (swap(held, "dp", bits[0]), swap_both(held, 1, bits[0])),
        ]

    modulated, latent_part = attend(
        sizes, [masks[slot] for slot in order], place, [received[slot] for slot in order], kept,
        scale, shift, proj,
    )

    if not sizes.riding:
        mine = patch_embed
        if shared:
            mine = lax.dynamic_slice_in_dim(
                patch_embed, lax.axis_index("dp") * sizes.share, sizes.share, 0
            )
        mine = lax.all_gather(mine, "seq", axis=1, tiled=True).reshape(-1, VW)
        embed = [(mine[None], [0])]
        if shared:
            embed = embed + [(swap(mine[None], "dp", bits[0]), [bits[0]])]

    groups = None
    if query_parts > 1:
        groups = [[g * query_parts + r for g in range(group_count)] for r in range(query_parts)]
    per_share = seq_count // group_count
    parts = all_to_all(latent_part.reshape(group_count, per_share * half, 2 * CH), groups)
    summed = total_copies([parts], seq_count)
    if sizes.riding:
        embed = [(arrange(sizes, ride_masks, place, pairs, summed), [0, bits[0]])]
    for bit in bits[1:] if shared else []:
        embed = embed + [(swap(x, "dp", bit), [m ^ bit for m in some]) for x, some in embed]
    latent = all_to_all(summed)
    if canonical:
        latent = latent.reshape(lat_rows // 2, 2 * CH)
    else:
        latent = latent.reshape(group_count, query_parts, per_share, half, 2, CH)
        latent = latent.transpose(0, 2, 1, 4, 3, 5).reshape(grid_rows // 2, 2, GW, CH)
        latent = latent.transpose(0, 2, 1, 3).reshape(lat_rows // 2, 2 * CH)

    reward, grad, weight = reward_head(
        place, latent, embed, pos, pre, post, words,
        cot, modulated, grid_rows, canonical, out_factor,
    )
    if not canonical:
        tokens = grad.reshape(grid_rows // 2, GW, 2, CH).transpose(0, 2, 1, 3)
        tokens = tokens.reshape(seq_count, query_parts, 2, half, CH)
        tokens = lax.dynamic_index_in_dim(tokens, query_part, 1, keepdims=False)
        grad = tokens.transpose(0, 2, 1, 3).reshape(seq_count * half, 2 * CH)
        weight = weight_call(grad, modulated, out_factor)

    parts = [weight] + [swap(weight, "dp", mask) for mask in range(1, data_count)]
    attn_grad = spread(grad, scale, proj, seq_count, half, head_count)
    if query_parts > 1:
        total = total_copies(parts, 1)[0]
        parts = [total] + [swap(total, "seq", mask) for mask in range(1, query_parts)]
    blocks = all_to_all(total_copies(parts, group_count, [attn_grad]), groups)
    return (reward[0, :1], attn_grad, finish(blocks).T)


def solution(mesh):
    return jax.shard_map(
        on_device,
        mesh=mesh,
        in_specs=(
            P("dp", "seq", None),
            P("dp", "seq", None),
            P("dp", "seq", None),
            P("dp", None),
            P("dp", None),
            P(),
            P(None, "seq", None),
            P(),
            P(),
            P(),
            P("dp", None),
            P("dp"),
        ),
        out_specs=(P("dp"), P("dp", "seq", None, None), P()),
        check_vma=False,
    )
```

```python
import functools
import math

import jax
import jax.numpy as jnp
from jax import lax
from jax.experimental import pallas as pl
from jax.experimental.pallas import tpu as pltpu
from jax.sharding import PartitionSpec as P

HEADS = 16
HD = 128
CH = 64
GW = 64
VW = 1280
EPS = 1e-05
BF16 = jnp.bfloat16
F32 = jnp.float32


def mm(a, b):
    return jnp.dot(a, b, preferred_element_type=F32)


def mm_nt(a, b):
    return lax.dot_general(a, b, (((1,), (1,)), ((), ())), preferred_element_type=F32)


def mm_tn(a, b):
    return lax.dot_general(a, b, (((0,), (0,)), ((), ())), preferred_element_type=F32)


SMEM_SPEC = pl.BlockSpec(memory_space=pltpu.SMEM)
VMEM_SPEC = pl.BlockSpec(memory_space=pltpu.VMEM)
HBM_SPEC = pl.BlockSpec(memory_space=pltpu.HBM)
ANY_SPEC = pl.BlockSpec(memory_space=pl.ANY)


def in_hbm(x):
    return pltpu.with_memory_space_constraint(x, pltpu.HBM)


def limits(mib=4):
    return pltpu.CompilerParams(vmem_limit_bytes=mib * 1024 * 1024)


class Sizes:
    def __init__(self, seq_count, data_count, tok_rows, patch_embed):
        self.count = seq_count
        self.query_parts = max(1, seq_count // HEADS)
        self.heads = max(1, HEADS // seq_count)
        self.width = self.heads * HD
        self.tok_rows = tok_rows
        self.part_rows = tok_rows // self.query_parts
        positions, self.local, _ = patch_embed.shape
        self.share = positions // data_count if positions % data_count == 0 else positions
        self.rows = self.part_rows + 2 * tok_rows
        self.share_rows = self.share * self.local
        self.chunks = VW // HD
        self.riding = self.local % 8 == 0 and self.share_rows % 16 == 0 and seq_count == 8
        self.riding = self.riding and 1 < data_count <= positions
        self.ride_rows = self.chunks * self.share_rows if self.riding else 0

    def pieces(self):
        return list(range(1, self.count)) + [0]

    def rides(self, mask):
        return self.riding and mask in (0, 4)

    def piece_shape(self, mask):
        return (self.rows + (self.ride_rows // self.heads if self.rides(mask) else 0), self.width)

    def ride_slices(self):
        deep = self.ride_rows // self.heads
        return [
            (pl.ds(self.rows, deep), pl.ds(at * HD, HD), pl.ds(at * deep, deep))
            for at in range(self.heads)
        ]


def pack_kernel(sizes, q_ref, k_ref, v_ref, embed_ref, *refs):
    pieces = sizes.pieces()
    out_refs = refs[: len(pieces)]
    q_scr, k_scr, v_scr, embed_scr, share_scr, in_sems, out_sems = refs[len(pieces) :]
    me = lax.axis_index("seq")
    tok_rows, part_rows, width = sizes.tok_rows, sizes.part_rows, sizes.width
    share = pl.ds(lax.axis_index("dp") * sizes.share, sizes.share)
    loads = [
        pltpu.make_async_copy(embed_ref.at[share], embed_scr, in_sems.at[3]),
        pltpu.make_async_copy(q_ref.at[0], q_scr, in_sems.at[0]),
        pltpu.make_async_copy(k_ref.at[0], k_scr, in_sems.at[1]),
        pltpu.make_async_copy(v_ref.at[0], v_scr, in_sems.at[2]),
    ]
    for load in loads:
        load.start()
    sent = [[], [], [], []]
    for slot, (mask, out) in enumerate(zip(pieces, out_refs)):
        dest = jnp.bitwise_xor(me, mask)
        group, part = dest // sizes.query_parts, dest % sizes.query_parts
        cols = pl.ds(pl.multiple_of(group * width, HD), width)
        first = pl.ds(pl.multiple_of(part * part_rows, part_rows), part_rows)
        for kind, source, rows in (
            (0, q_scr.at[first, cols], pl.ds(0, part_rows)),
            (1, k_scr.at[:, cols], pl.ds(part_rows, tok_rows)),
            (2, v_scr.at[:, cols], pl.ds(part_rows + tok_rows, tok_rows)),
        ):
            sent[kind].append(pltpu.make_async_copy(source, out.at[rows], out_sems.at[kind, slot]))
        if sizes.rides(mask):
            for at, (rows, place, from_rows) in enumerate(sizes.ride_slices()):
                sent[3].append(
                    pltpu.make_async_copy(
                        share_scr.at[from_rows], out.at[rows, place], out_sems.at[3 + at, slot]
                    )
                )
    loads[0].wait()
    if sizes.riding:
        for chunk in range(sizes.chunks):
            cols = embed_scr[:, :, pl.ds(chunk * HD, HD)].astype(F32)
            share_scr[pl.ds(chunk * sizes.share_rows, sizes.share_rows), :] = cols.reshape(
                sizes.share_rows, HD
            ).astype(BF16)
    for store in sent[3]:
        store.start()
    for kind in range(3):
        loads[kind + 1].wait()
        for store in sent[kind]:
            store.start()
    for stores in sent:
        for store in stores:
            store.wait()


def pack(sizes, queries, keys, values, patch_embed):
    tok_rows, full = queries.shape[1:]
    pieces = sizes.pieces()
    return pl.pallas_call(
        functools.partial(pack_kernel, sizes),
        out_shape=[jax.ShapeDtypeStruct(sizes.piece_shape(mask), BF16) for mask in pieces],
        in_specs=[HBM_SPEC] * 4,
        out_specs=[HBM_SPEC] * len(pieces),
        scratch_shapes=[pltpu.VMEM((tok_rows, full), BF16)] * 3
        + [
            pltpu.VMEM((sizes.share,) + patch_embed.shape[1:], BF16),
            pltpu.VMEM((max(16, sizes.ride_rows), HD), BF16),
            pltpu.SemaphoreType.DMA((4,)),
            pltpu.SemaphoreType.DMA((3 + sizes.heads, len(pieces))),
        ],
        compiler_params=limits(),
        cost_estimate=pl.CostEstimate(
            flops=0, bytes_accessed=12 * tok_rows * full, transcendentals=0
        ),
    )(queries, keys, values, patch_embed)


def collect_kernel(sizes, *refs):
    *in_refs, out_ref, sems = refs
    copies = []
    for slot, ref in enumerate(in_refs):
        for at, (rows, cols, to_rows) in enumerate(sizes.ride_slices()):
            copies.append(
                pltpu.make_async_copy(
                    ref.at[rows, cols], out_ref.at[slot, to_rows], sems.at[at, slot]
                )
            )
    for copy in copies:
        copy.start()
    for copy in copies:
        copy.wait()


def collect(sizes, arrays):
    return pl.pallas_call(
        functools.partial(collect_kernel, sizes),
        out_shape=jax.ShapeDtypeStruct((len(arrays), sizes.ride_rows, HD), BF16),
        in_specs=[ANY_SPEC] * len(arrays),
        out_specs=VMEM_SPEC,
        scratch_shapes=[pltpu.SemaphoreType.DMA((sizes.heads, len(arrays)))],
        compiler_params=limits(),
    )(*arrays)


def join_kernel(first_ref, second_ref, *refs):
    out_ref = refs[-1]
    count = first_ref.shape[0]
    out_ref[:count] = first_ref[...]
    out_ref[count:] = second_ref[...]


def join(first, second, others):
    return pl.pallas_call(
        join_kernel,
        out_shape=jax.ShapeDtypeStruct((2 * first.shape[0],) + first.shape[1:], BF16),
        in_specs=[VMEM_SPEC] * 2 + [ANY_SPEC] * len(others),
        out_specs=VMEM_SPEC,
        compiler_params=limits(),
    )(first, second, *others)


def arrange_kernel(sizes, masks, place_ref, *refs):
    *pair_refs, out_ref = refs[:-2] + refs[-1:]
    me = place_ref[0]
    odd = me % 2 == 1
    local = sizes.local
    for quarter in range(len(pair_refs) // 2):
        held_ref, got_ref = pair_refs[2 * quarter], pair_refs[2 * quarter + 1]
        for slot, mask in enumerate(masks):
            pair = jnp.bitwise_xor(me, mask) // 2
            for chunk in range(sizes.chunks):
                rows = pl.ds(chunk * sizes.share_rows, sizes.share_rows)
                held = held_ref[slot, rows, :].astype(F32)
                got = got_ref[slot, rows, :].astype(F32)
                first = jnp.where(odd, got, held)
                second = jnp.where(odd, held, got)
                for at in range(sizes.share):
                    part = slice(at * local, (at + 1) * local)
                    both = jnp.concatenate([first[part], second[part]], axis=0).astype(BF16)
                    start = pl.multiple_of(at * sizes.count * local + pair * 2 * local, 2 * local)
                    out_ref[quarter, pl.ds(start, 2 * local), pl.ds(chunk * HD, HD)] = both


def arrange(sizes, masks, place, pairs, wait):
    rows = sizes.share * sizes.count * sizes.local
    flat = [x for pair in pairs for x in pair]
    return pl.pallas_call(
        functools.partial(arrange_kernel, sizes, masks),
        out_shape=jax.ShapeDtypeStruct((len(pairs), rows, VW), BF16),
        in_specs=[SMEM_SPEC] + [VMEM_SPEC] * (len(flat) + 1),
        out_specs=VMEM_SPEC,
        compiler_params=limits(),
    )(place, *flat, wait)


def fetch_kernel(sizes, place_ref, cot_ref, *refs):
    *refs, row_ref, sems = refs
    count = len(refs) // 2
    row_ref[...] = jnp.full(row_ref.shape, cot_ref[0], F32)
    mine = pl.ds(pl.multiple_of(place_ref[2] * sizes.width, HD), sizes.width)
    copies = []
    for slot in range(count):
        source = refs[slot].at[:, mine] if slot < 3 else refs[slot]
        copies.append(pltpu.make_async_copy(source, refs[count + slot], sems.at[slot]))
        copies[-1].start()
    for copy in copies:
        copy.wait()


def fetch(sizes, place, cotangent, arrays):
    shapes = [x.shape if slot >= 3 else (x.shape[0], sizes.width) for slot, x in enumerate(arrays)]
    return pl.pallas_call(
        functools.partial(fetch_kernel, sizes),
        out_shape=[jax.ShapeDtypeStruct(shape, x.dtype) for shape, x in zip(shapes, arrays)]
        + [jax.ShapeDtypeStruct((1, 128), F32)],
        in_specs=[SMEM_SPEC] * 2 + [HBM_SPEC] * len(arrays),
        out_specs=[VMEM_SPEC] * (len(arrays) + 1),
        scratch_shapes=[pltpu.SemaphoreType.DMA((len(arrays),))],
        compiler_params=limits(),
        cost_estimate=pl.CostEstimate(flops=1, bytes_accessed=1, transcendentals=0),
    )(place, cotangent, *[in_hbm(x) for x in arrays])


FACTOR = HD ** (-0.5) * math.log2(math.e)


def load_pieces(sizes, in_refs, key_scr, value_scr):
    tok_rows, part_rows = sizes.tok_rows, sizes.part_rows
    for src, ref in enumerate(in_refs):
        rows = pl.ds(src * tok_rows, tok_rows)
        key_scr[rows, :] = ref[pl.ds(part_rows, tok_rows), :]
        for head in range(sizes.heads):
            value_scr[rows, pl.ds(2 * head * HD, HD)] = ref[
                pl.ds(part_rows + tok_rows, tok_rows), pl.ds(head * HD, HD)
            ]
    ones = jnp.ones((len(in_refs) * tok_rows, HD), BF16)
    for head in range(sizes.heads):
        value_scr[:, pl.ds((2 * head + 1) * HD, HD)] = ones


def soft_part(query, key_scr, value_scr, rows, head, before):
    logits = mm_nt(query, key_scr[rows, pl.ds(head * HD, HD)])
    top = jnp.max(logits, axis=-1, keepdims=True)
    if before:
        top = jnp.maximum(top, before[2])
    weights = jnp.exp2((logits - top) * FACTOR).astype(BF16)
    both = mm(weights, value_scr[rows, pl.ds(2 * head * HD, 2 * HD)])
    mixed, total = both[:, :HD], both[:, HD:]
    if before:
        shrink = jnp.exp2((before[2] - top) * FACTOR)
        mixed, total = mixed + before[0] * shrink, total + before[1] * shrink
    return mixed, total, top


def piece_scratch(sizes, count):
    lat_rows = count * sizes.tok_rows
    return [
        pltpu.VMEM((lat_rows, sizes.width), BF16),
        pltpu.VMEM((lat_rows, 2 * sizes.width), BF16),
    ]


def early_kernel(sizes, count, *refs):
    in_refs, refs = refs[:count], refs[count + 1 :]
    sum_ref, stat_ref, key_scr, value_scr = refs
    load_pieces(sizes, in_refs, key_scr, value_scr)
    left = lax.broadcasted_iota(jnp.int32, (sizes.part_rows, HD), 1) < HD // 2
    rows = pl.ds(0, count * sizes.tok_rows)
    for src in range(count):
        results = [
            soft_part(
                in_refs[src][pl.ds(0, sizes.part_rows), pl.ds(head * HD, HD)],
                key_scr, value_scr, rows, head, None,
            )
            for head in range(sizes.heads)
        ]
        for head, (mixed, total, top) in enumerate(results):
            sum_ref[src, head] = mixed
            stat_ref[src, head] = jnp.where(left, top, total)


def attend_early(sizes, received, wait):
    count = len(received)
    shape = jax.ShapeDtypeStruct((count, sizes.heads, sizes.part_rows, HD), F32)
    return pl.pallas_call(
        functools.partial(early_kernel, sizes, count),
        out_shape=(shape, shape),
        in_specs=[VMEM_SPEC] * (count + 1),
        out_specs=(VMEM_SPEC, VMEM_SPEC),
        scratch_shapes=piece_scratch(sizes, count),
        compiler_params=limits(12),
        cost_estimate=pl.CostEstimate(flops=1, bytes_accessed=1, transcendentals=0),
    )(*received, wait)


def attend_kernel(sizes, masks, early, place_ref, *refs):
    count, heads, width = sizes.count, sizes.heads, sizes.width
    tok_rows, part_rows = sizes.tok_rows, sizes.part_rows
    in_refs, refs = refs[:count], refs[count:]
    kept_refs, refs = refs[: 2 if early else 0], refs[2 if early else 0 :]
    scale_ref, shift_ref, proj_ref, mod_ref, lat_ref, *refs = refs
    key_scr, value_scr = refs
    half = part_rows // 2
    me = place_ref[0]
    gain = 1.0 + scale_ref[...]
    shift = shift_ref[...]
    load_pieces(sizes, in_refs, key_scr, value_scr)
    together = 2
    for first in range(0, count, together):
        results = []
        for src in range(first, first + together):
            mixed = []
            for head in range(heads):
                before = None
                rows = pl.ds(0, count * tok_rows)
                if src < early:
                    rows = pl.ds(early * tok_rows, (count - early) * tok_rows)
                    stat = kept_refs[1][src, head]
                    before = (kept_refs[0][src, head], stat[:, HD - 1 :], stat[:, :1])
                query = in_refs[src][pl.ds(0, part_rows), pl.ds(head * HD, HD)]
                value, total, _ = soft_part(query, key_scr, value_scr, rows, head, before)
                mixed.append(value / total)
            results.append(jnp.concatenate(mixed, axis=1) if heads > 1 else mixed[0])
        for at, attended in enumerate(results):
            modulated = (attended * gain + shift).astype(BF16)
            mod_ref[jnp.bitwise_xor(me, masks[first + at])] = modulated
    sides = [
        mm_nt(mod_ref[:, rows, :].reshape(count * half, width), proj_ref[...])
        for rows in (slice(0, half), slice(half, part_rows))
    ]
    latent = jnp.concatenate(sides, axis=1).astype(BF16)
    lat_ref[...] = latent.reshape(count, half, 2 * CH)


def attend(sizes, masks, place, received, kept, scales, shifts, proj):
    count, width, heads = sizes.count, sizes.width, sizes.heads
    lat_rows = count * sizes.tok_rows
    query_rows = count * sizes.part_rows
    early = kept[0].shape[0] if kept else 0
    return pl.pallas_call(
        functools.partial(attend_kernel, sizes, masks, early),
        out_shape=(
            jax.ShapeDtypeStruct((count, sizes.part_rows, width), BF16),
            jax.ShapeDtypeStruct((count, sizes.part_rows // 2, 2 * CH), BF16),
        ),
        in_specs=[SMEM_SPEC] + [VMEM_SPEC] * (count + len(kept) + 3),
        out_specs=(VMEM_SPEC, VMEM_SPEC),
        scratch_shapes=piece_scratch(sizes, count),
        compiler_params=limits(16),
        cost_estimate=pl.CostEstimate(
            flops=4 * query_rows * lat_rows * width,
            bytes_accessed=2 * (query_rows * 2 + lat_rows * 2) * width,
            transcendentals=query_rows * lat_rows * heads,
        ),
    )(place, *received, *kept, scales, shifts, proj)


def total_kernel(copies, count, *refs):
    out_ref = refs[-1]
    if count == 1:
        parts = [refs[0][i].astype(F32) for i in range(refs[0].shape[0])]
    else:
        parts = [ref[...].astype(F32) for ref in refs[:count]]
    while len(parts) > 1:
        parts = [parts[i] + parts[i + 1] for i in range(0, len(parts), 2)]
    for copy in range(copies):
        out_ref[copy] = parts[0].astype(BF16)


def total_copies(arrays, copies, others=()):
    return pl.pallas_call(
        functools.partial(total_kernel, copies, len(arrays)),
        out_shape=jax.ShapeDtypeStruct((copies,) + arrays[0].shape[-2:], BF16),
        in_specs=[VMEM_SPEC] * (len(arrays) + len(others)),
        out_specs=VMEM_SPEC,
        compiler_params=limits(),
    )(*arrays, *others)


def lane_mean(x, count):
    return jnp.sum(x, axis=-1, keepdims=True) * (1.0 / count)


def head_kernel(grid_rows, fused, embed_masks, out_factor, place_ref, lat_ref, *refs):
    embed_refs, refs = refs[: len(embed_masks)], refs[len(embed_masks) :]
    pos_ref, pre_ref, post_ref, prompt_ref, cot_ref, mod_ref, *refs = refs
    reward_ref, grad_ref, weight_ref, lat_scr, grad_scr, block_scr, back_scr = refs
    patch_rows = grid_rows // 4
    patch_cols = GW // 4
    patches = patch_rows * patch_cols
    lat_scr[...] = lat_ref[...].astype(F32)

    data = place_ref[1]
    shares = [
        (jnp.bitwise_xor(data, mask), ref, slot)
        for ref, masks in zip(embed_refs, embed_masks)
        for slot, mask in enumerate(masks)
    ]
    share_rows = embed_refs[0].shape[1]
    for hi in range(2):
        wide = []
        for tx in range(4):
            rows = [
                lat_scr[pl.ds((2 * pr + hi) * GW + tx, patch_cols, stride=4), :]
                for pr in range(patch_rows)
            ]
            wide.append(jnp.concatenate(rows, axis=0))
        for side in range(2):
            lanes = slice(side * CH, (side + 1) * CH)
            line = jnp.concatenate([x[:, lanes] for x in wide], axis=1).astype(BF16)
            first = (2 * hi + side) * 4 * CH
            if share_rows >= 4 * CH:
                at = first % share_rows
                block_scr[first // share_rows, :, pl.ds(at, 4 * CH)] = line
            else:
                for at in range(0, 4 * CH, share_rows):
                    block_scr[(first + at) // share_rows] = line[:, at : at + share_rows]
    embedded = pos_ref[...].astype(F32)
    for number, ref, slot in shares:
        embedded = embedded + mm(block_scr[number], ref[slot])
    pre = pre_ref[...].reshape(1, VW)
    post = post_ref[...].reshape(1, VW)
    prompt = prompt_ref[...]
    center = embedded - lane_mean(embedded, VW)
    rstd = lax.rsqrt(lane_mean(center * center, VW) + EPS)
    unit = center * rstd
    pooled = jnp.sum(unit, axis=0, keepdims=True) * (1.0 / patches) * pre
    pooled_center = pooled - lane_mean(pooled, VW)
    pooled_rstd = lax.rsqrt(lane_mean(pooled_center * pooled_center, VW) + EPS)
    pooled_unit = pooled_center * pooled_rstd
    final = pooled_unit * post
    dot = jnp.sum(final * prompt, axis=-1, keepdims=True)
    final_sq = jnp.sum(final * final, axis=-1, keepdims=True)
    prompt_sq = jnp.sum(prompt * prompt, axis=-1, keepdims=True)
    final_len = jnp.sqrt(final_sq)
    prompt_len = jnp.sqrt(prompt_sq)
    cosine = dot / (final_len * prompt_len)
    reward_ref[...] = jnp.broadcast_to(100.0 * cosine, reward_ref.shape)
    cot = cot_ref[:, :1]
    final_grad = (100.0 * cot) * (prompt / (final_len * prompt_len) - final * (cosine / final_sq))
    unit_grad = final_grad * post
    pooled_grad = pooled_rstd * (
        unit_grad
        - lane_mean(unit_grad, VW)
        - pooled_unit * lane_mean(unit_grad * pooled_unit, VW)
    )
    flow = pooled_grad * pre * (1.0 / patches)
    embed_grad = rstd * (flow - lane_mean(flow, VW) - unit * lane_mean(flow * unit, VW))
    high = embed_grad.astype(BF16)
    low = (embed_grad - high.astype(F32)).astype(BF16)
    stacked = jnp.concatenate([high, low], axis=0)
    for number, ref, slot in shares:
        both = mm_nt(stacked, ref[slot])
        back_scr[number] = both[:patches] + both[patches:]
    back = jnp.concatenate([back_scr[i] for i in range(16 * CH // share_rows)], axis=1)
    for hi in range(2):
        for tx in range(4):
            first = (4 * (2 * hi) + tx) * CH
            second = (4 * (2 * hi + 1) + tx) * CH
            piece = jnp.concatenate(
                [back[:, first : first + CH], back[:, second : second + CH]], axis=1
            )
            for pr in range(patch_rows):
                grad_scr[pl.ds((2 * pr + hi) * GW + tx, patch_cols, stride=4), :] = piece[
                    pr * patch_cols : (pr + 1) * patch_cols
                ]
    grad = grad_scr[...].astype(BF16)
    grad_ref[...] = grad
    if fused:
        store_readout_grad(grad, mod_ref, out_factor, weight_ref)
    else:
        weight_ref[...] = jnp.zeros_like(weight_ref)


def store_readout_grad(grad, mod_ref, out_factor, out_ref):
    turned = grad.astype(F32).T.astype(BF16)
    count, rows, width = mod_ref.shape
    half = rows // 2
    first = mod_ref[:, :half, :].reshape(count * half, width)
    second = mod_ref[:, half:, :].reshape(count * half, width)
    total = mm(turned[:CH], first) + mm(turned[CH:], second)
    out_ref[...] = (total * out_factor).astype(BF16)


def reward_head(
    place, latent, embed, pos, pre, post, prompt, cot, modulated, grid_rows, fused, out_factor
):
    patches = grid_rows * GW // 16
    rows = grid_rows * GW // 2
    width = modulated.shape[2]
    embed_arrays, embed_masks = [x for x, _ in embed], [masks for _, masks in embed]
    share_rows = embed_arrays[0].shape[1]
    return pl.pallas_call(
        functools.partial(head_kernel, grid_rows, fused, embed_masks, out_factor),
        out_shape=(
            jax.ShapeDtypeStruct((1, 128), F32),
            jax.ShapeDtypeStruct((rows, 2 * CH), BF16),
            jax.ShapeDtypeStruct((CH, width), BF16),
        ),
        in_specs=[SMEM_SPEC, VMEM_SPEC]
        + [VMEM_SPEC] * len(embed_arrays)
        + [VMEM_SPEC] * 6,
        out_specs=(VMEM_SPEC, VMEM_SPEC, VMEM_SPEC),
        scratch_shapes=[
            pltpu.VMEM((rows, 2 * CH), F32),
            pltpu.VMEM((rows, 2 * CH), F32),
            pltpu.VMEM((16 * CH // share_rows, patches, share_rows), BF16),
            pltpu.VMEM((16 * CH // share_rows, patches, share_rows), F32),
        ],
        compiler_params=limits(16),
        cost_estimate=pl.CostEstimate(
            flops=6 * patches * 16 * CH * VW,
            bytes_accessed=2 * 16 * CH * VW + 2 * patches * VW,
            transcendentals=0,
        ),
    )(place, latent, *embed_arrays, pos, pre, post, prompt, cot, modulated)


def spread_kernel(count, half, heads, grad_ref, scale_ref, proj_ref, out_ref, token_ref):
    token_ref[...] = jnp.zeros_like(token_ref)
    gain = 1.0 + scale_ref[...]
    proj = proj_ref[...]
    zero = jnp.zeros_like(proj)
    sides = (jnp.concatenate([proj, zero], axis=0), jnp.concatenate([zero, proj], axis=0))
    for src in range(count):
        grad = grad_ref[pl.ds(src * half, half), :]
        for side in range(2):
            rows = (mm(grad, sides[side]) * gain).astype(BF16)
            for head in range(heads):
                out_ref[0, head, pl.ds((2 * src + side) * half, half), :] = rows[
                    :, head * HD : (head + 1) * HD
                ]


def spread(grad, scales, proj, count, half, heads):
    return pl.pallas_call(
        functools.partial(spread_kernel, count, half, heads),
        out_shape=(
            jax.ShapeDtypeStruct((1, heads, 2 * count * half, HD), BF16),
            jax.ShapeDtypeStruct((8, 128), F32),
        ),
        in_specs=[VMEM_SPEC] * 3,
        out_specs=(VMEM_SPEC, VMEM_SPEC),
        compiler_params=limits(),
        cost_estimate=pl.CostEstimate(
            flops=8 * count * half * CH * heads * HD,
            bytes_accessed=4 * count * half * heads * HD,
            transcendentals=0,
        ),
    )(grad, scales, proj)


def weight_kernel(out_factor, grad_ref, *refs):
    store_readout_grad(grad_ref[...], refs[0], out_factor, refs[1])


def weight_call(grad, modulated, out_factor):
    return pl.pallas_call(
        functools.partial(weight_kernel, out_factor),
        out_shape=jax.ShapeDtypeStruct((CH, modulated.shape[2]), BF16),
        in_specs=[VMEM_SPEC] * 2,
        out_specs=VMEM_SPEC,
        compiler_params=limits(),
    )(grad, modulated)


def finish_kernel(in_ref, out_ref):
    count, _, width = in_ref.shape
    for group in range(count):
        out_ref[:, pl.ds(group * width, width)] = in_ref[group].astype(F32)


def finish(blocks):
    return pl.pallas_call(
        finish_kernel,
        out_shape=jax.ShapeDtypeStruct((CH, HEADS * HD), F32),
        in_specs=[VMEM_SPEC],
        out_specs=VMEM_SPEC,
        compiler_params=limits(),
    )(blocks)


def swap(x, axis, mask):
    count = lax.axis_size(axis)
    return lax.ppermute(x, axis, [(i, i ^ mask) for i in range(count)])


def all_to_all(x, groups=None):
    return lax.all_to_all(
        x, "seq", split_axis=0, concat_axis=0, tiled=True, axis_index_groups=groups
    )


def swap_both(x, seq_mask, data_mask):
    seq_count, data_count = lax.axis_size("seq"), lax.axis_size("dp")
    pairs = [
        (i * data_count + j, (i ^ seq_mask) * data_count + (j ^ data_mask))
        for i in range(seq_count)
        for j in range(data_count)
    ]
    return lax.ppermute(x, ("seq", "dp"), pairs)


def on_device(
    queries,
    keys,
    values,
    shifts,
    scales,
    proj_out,
    patch_embed,
    pos_embed,
    pre_gain,
    post_gain,
    prompt,
    cotangent,
):
    seq_count = lax.axis_size("seq")
    data_count = lax.axis_size("dp")
    tok_rows = queries.shape[1]
    sizes = Sizes(seq_count, data_count, tok_rows, patch_embed)
    query_parts, head_count, part_rows = sizes.query_parts, sizes.heads, sizes.part_rows
    group_count = HEADS // head_count
    seq_index = lax.axis_index("seq")
    head_group = seq_index // query_parts
    query_part = seq_index % query_parts
    half = part_rows // 2
    lat_rows = seq_count * tok_rows
    grid_rows = lat_rows // GW
    canonical = part_rows == 2 * GW
    place = jnp.stack([seq_index, lax.axis_index("dp"), head_group]).astype(jnp.int32)
    proj_turned = proj_out.T
    out_factor = 1.0 / math.sqrt(data_count * lat_rows)

    masks = sizes.pieces()
    packed = pack(
        sizes, in_hbm(queries), in_hbm(keys), in_hbm(values), in_hbm(patch_embed)
    )
    received = [swap(x, "seq", mask) if mask else x for mask, x in zip(masks, packed)]
    bits = [1 << b for b in reversed(range(data_count.bit_length() - 1))]
    shared = sizes.share < patch_embed.shape[0]
    scale, shift, proj, pos, pre, post, words, cot = fetch(
        sizes, place, cotangent, [scales, shifts, proj_turned, pos_embed, pre_gain, post_gain, prompt]
    )

    kept, order = [], list(range(seq_count))
    if seq_count == 8:
        late = [slot for slot, mask in enumerate(masks) if mask in (6, 7)]
        order = [slot for slot in order if slot not in late]
        kept = attend_early(sizes, [received[slot] for slot in order], scale)
        order = order + late
    if sizes.riding:
        ride = [slot for slot, mask in enumerate(masks) if sizes.rides(mask)]
        two = collect(sizes, [received[slot] for slot in ride])
        held = join(two, swap(two, "seq", 2), kept)
        ride_masks = [masks[slot] for slot in ride]
        ride_masks = ride_masks + [mask ^ 2 for mask in ride_masks]
        pairs = [
            (held, swap(held, "seq", 1)),
            (swap(held, "dp", bits[0]), swap_both(held, 1, bits[0])),
        ]

    modulated, latent_part = attend(
        sizes, [masks[slot] for slot in order], place, [received[slot] for slot in order], kept,
        scale, shift, proj,
    )

    if not sizes.riding:
        mine = patch_embed
        if shared:
            mine = lax.dynamic_slice_in_dim(
                patch_embed, lax.axis_index("dp") * sizes.share, sizes.share, 0
            )
        mine = lax.all_gather(mine, "seq", axis=1, tiled=True).reshape(-1, VW)
        embed = [(mine[None], [0])]
        if shared:
            embed = embed + [(swap(mine[None], "dp", bits[0]), [bits[0]])]

    groups = None
    if query_parts > 1:
        groups = [[g * query_parts + r for g in range(group_count)] for r in range(query_parts)]
    per_share = seq_count // group_count
    parts = all_to_all(latent_part.reshape(group_count, per_share * half, 2 * CH), groups)
    summed = total_copies([parts], seq_count)
    if sizes.riding:
        embed = [(arrange(sizes, ride_masks, place, pairs, summed), [0, bits[0]])]
    for bit in bits[1:] if shared else []:
        embed = embed + [(swap(x, "dp", bit), [m ^ bit for m in some]) for x, some in embed]
    latent = all_to_all(summed)
    if canonical:
        latent = latent.reshape(lat_rows // 2, 2 * CH)
    else:
        latent = latent.reshape(group_count, query_parts, per_share, half, 2, CH)
        latent = latent.transpose(0, 2, 1, 4, 3, 5).reshape(grid_rows // 2, 2, GW, CH)
        latent = latent.transpose(0, 2, 1, 3).reshape(lat_rows // 2, 2 * CH)

    reward, grad, weight = reward_head(
        place, latent, embed, pos, pre, post, words,
        cot, modulated, grid_rows, canonical, out_factor,
    )
    if not canonical:
        tokens = grad.reshape(grid_rows // 2, GW, 2, CH).transpose(0, 2, 1, 3)
        tokens = tokens.reshape(seq_count, query_parts, 2, half, CH)
        tokens = lax.dynamic_index_in_dim(tokens, query_part, 1, keepdims=False)
        grad = tokens.transpose(0, 2, 1, 3).reshape(seq_count * half, 2 * CH)
        weight = weight_call(grad, modulated, out_factor)

    parts = [weight] + [swap(weight, "dp", mask) for mask in range(1, data_count)]
    attn_grad, token = spread(grad, scale, proj, seq_count, half, head_count)
    if query_parts > 1:
        total = total_copies(parts, 1)[0]
        parts = [total] + [swap(total, "seq", mask) for mask in range(1, query_parts)]
    blocks = all_to_all(total_copies(parts, group_count, [token]), groups)
    return (reward[0, :1], attn_grad, finish(blocks).T)


def solution(mesh):
    return jax.shard_map(
        on_device,
        mesh=mesh,
        in_specs=(
            P("dp", "seq", None),
            P("dp", "seq", None),
            P("dp", "seq", None),
            P("dp", None),
            P("dp", None),
            P(),
            P(None, "seq", None),
            P(),
            P(),
            P(),
            P("dp", None),
            P("dp"),
        ),
        out_specs=(P("dp"), P("dp", "seq", None, None), P()),
        check_vma=False,
    )
```

```python
import functools
import math

import jax
import jax.numpy as jnp
from jax import lax
from jax.experimental import pallas as pl
from jax.experimental.pallas import tpu as pltpu
from jax.sharding import PartitionSpec as P

HEADS = 16
HD = 128
CH = 64
GW = 64
VW = 1280
EPS = 1e-05
BF16 = jnp.bfloat16
F32 = jnp.float32


def mm(a, b):
    return jnp.dot(a, b, preferred_element_type=F32)


def mm_nt(a, b):
    return lax.dot_general(a, b, (((1,), (1,)), ((), ())), preferred_element_type=F32)


def mm_tn(a, b):
    return lax.dot_general(a, b, (((0,), (0,)), ((), ())), preferred_element_type=F32)


SMEM_SPEC = pl.BlockSpec(memory_space=pltpu.SMEM)
VMEM_SPEC = pl.BlockSpec(memory_space=pltpu.VMEM)
HBM_SPEC = pl.BlockSpec(memory_space=pltpu.HBM)
ANY_SPEC = pl.BlockSpec(memory_space=pl.ANY)


def in_hbm(x):
    return pltpu.with_memory_space_constraint(x, pltpu.HBM)


def limits(mib=4):
    return pltpu.CompilerParams(vmem_limit_bytes=mib * 1024 * 1024)


class Sizes:
    def __init__(self, seq_count, data_count, tok_rows, patch_embed):
        self.count = seq_count
        self.query_parts = max(1, seq_count // HEADS)
        self.heads = max(1, HEADS // seq_count)
        self.width = self.heads * HD
        self.tok_rows = tok_rows
        self.part_rows = tok_rows // self.query_parts
        positions, self.local, _ = patch_embed.shape
        self.share = positions // data_count if positions % data_count == 0 else positions
        self.rows = self.part_rows + 2 * tok_rows
        self.share_rows = self.share * self.local
        self.chunks = VW // HD
        self.riding = self.local % 8 == 0 and self.share_rows % 16 == 0 and seq_count == 8
        self.riding = self.riding and 1 < data_count <= positions
        self.ride_rows = self.chunks * self.share_rows if self.riding else 0

    def order(self):
        return [2, 3, 4, 5, 0, 1, 6, 7] if self.count == 8 else list(range(self.count))

    def pieces(self):
        return list(range(1, self.count)) + [0]

    def rides(self, mask):
        return self.riding and mask in (0, 4)

    def piece_shape(self, mask):
        return (self.rows + (self.ride_rows // self.heads if self.rides(mask) else 0), self.width)

    def ride_slices(self):
        deep = self.ride_rows // self.heads
        return [
            (pl.ds(self.rows, deep), pl.ds(at * HD, HD), pl.ds(at * deep, deep))
            for at in range(self.heads)
        ]


def pack_kernel(sizes, q_ref, k_ref, v_ref, embed_ref, *refs):
    pieces = sizes.pieces()
    out_refs = refs[: len(pieces)]
    q_scr, k_scr, v_scr, embed_scr, share_scr, in_sems, out_sems = refs[len(pieces) :]
    me = lax.axis_index("seq")
    tok_rows, part_rows, width = sizes.tok_rows, sizes.part_rows, sizes.width
    share = pl.ds(lax.axis_index("dp") * sizes.share, sizes.share)
    loads = [
        pltpu.make_async_copy(embed_ref.at[share], embed_scr, in_sems.at[3]),
        pltpu.make_async_copy(q_ref.at[0], q_scr, in_sems.at[0]),
        pltpu.make_async_copy(k_ref.at[0], k_scr, in_sems.at[1]),
        pltpu.make_async_copy(v_ref.at[0], v_scr, in_sems.at[2]),
    ]
    for load in loads:
        load.start()
    sent = [[], [], [], []]
    for slot, (mask, out) in enumerate(zip(pieces, out_refs)):
        dest = jnp.bitwise_xor(me, mask)
        group, part = dest // sizes.query_parts, dest % sizes.query_parts
        cols = pl.ds(pl.multiple_of(group * width, HD), width)
        first = pl.ds(pl.multiple_of(part * part_rows, part_rows), part_rows)
        for kind, source, rows in (
            (0, q_scr.at[first, cols], pl.ds(0, part_rows)),
            (1, k_scr.at[:, cols], pl.ds(part_rows, tok_rows)),
            (2, v_scr.at[:, cols], pl.ds(part_rows + tok_rows, tok_rows)),
        ):
            sent[kind].append(pltpu.make_async_copy(source, out.at[rows], out_sems.at[kind, slot]))
        if sizes.rides(mask):
            for at, (rows, place, from_rows) in enumerate(sizes.ride_slices()):
                sent[3].append(
                    pltpu.make_async_copy(
                        share_scr.at[from_rows], out.at[rows, place], out_sems.at[3 + at, slot]
                    )
                )
    loads[0].wait()
    if sizes.riding:
        for chunk in range(sizes.chunks):
            cols = embed_scr[:, :, pl.ds(chunk * HD, HD)].astype(F32)
            share_scr[pl.ds(chunk * sizes.share_rows, sizes.share_rows), :] = cols.reshape(
                sizes.share_rows, HD
            ).astype(BF16)
    for store in sent[3]:
        store.start()
    for kind in range(3):
        loads[kind + 1].wait()
        for store in sent[kind]:
            store.start()
    for stores in sent:
        for store in stores:
            store.wait()


def pack(sizes, queries, keys, values, patch_embed):
    tok_rows, full = queries.shape[1:]
    pieces = sizes.pieces()
    return pl.pallas_call(
        functools.partial(pack_kernel, sizes),
        out_shape=[jax.ShapeDtypeStruct(sizes.piece_shape(mask), BF16) for mask in pieces],
        in_specs=[HBM_SPEC] * 4,
        out_specs=[HBM_SPEC] * len(pieces),
        scratch_shapes=[pltpu.VMEM((tok_rows, full), BF16)] * 3
        + [
            pltpu.VMEM((sizes.share,) + patch_embed.shape[1:], BF16),
            pltpu.VMEM((max(16, sizes.ride_rows), HD), BF16),
            pltpu.SemaphoreType.DMA((4,)),
            pltpu.SemaphoreType.DMA((3 + sizes.heads, len(pieces))),
        ],
        compiler_params=limits(),
        cost_estimate=pl.CostEstimate(
            flops=0, bytes_accessed=12 * tok_rows * full, transcendentals=0
        ),
    )(queries, keys, values, patch_embed)


def collect_kernel(sizes, *refs):
    *in_refs, out_ref, sems = refs
    copies = []
    for slot, ref in enumerate(in_refs):
        for at, (rows, cols, to_rows) in enumerate(sizes.ride_slices()):
            copies.append(
                pltpu.make_async_copy(
                    ref.at[rows, cols], out_ref.at[slot, to_rows], sems.at[at, slot]
                )
            )
    for copy in copies:
        copy.start()
    for copy in copies:
        copy.wait()


def collect(sizes, arrays):
    return pl.pallas_call(
        functools.partial(collect_kernel, sizes),
        out_shape=jax.ShapeDtypeStruct((len(arrays), sizes.ride_rows, HD), BF16),
        in_specs=[ANY_SPEC] * len(arrays),
        out_specs=VMEM_SPEC,
        scratch_shapes=[pltpu.SemaphoreType.DMA((sizes.heads, len(arrays)))],
        compiler_params=limits(),
    )(*arrays)


def join_kernel(first_ref, second_ref, *refs):
    out_ref = refs[-1]
    count = first_ref.shape[0]
    out_ref[:count] = first_ref[...]
    out_ref[count:] = second_ref[...]


def join(first, second, others):
    return pl.pallas_call(
        join_kernel,
        out_shape=jax.ShapeDtypeStruct((2 * first.shape[0],) + first.shape[1:], BF16),
        in_specs=[VMEM_SPEC] * 2 + [ANY_SPEC] * len(others),
        out_specs=VMEM_SPEC,
        compiler_params=limits(),
    )(first, second, *others)


def arrange_kernel(sizes, masks, place_ref, *refs):
    *pair_refs, out_ref = refs[:-2] + refs[-1:]
    me = place_ref[0]
    odd = me % 2 == 1
    local = sizes.local
    for quarter in range(len(pair_refs) // 2):
        held_ref, got_ref = pair_refs[2 * quarter], pair_refs[2 * quarter + 1]
        for slot, mask in enumerate(masks):
            pair = jnp.bitwise_xor(me, mask) // 2
            for chunk in range(sizes.chunks):
                rows = pl.ds(chunk * sizes.share_rows, sizes.share_rows)
                held = held_ref[slot, rows, :].astype(F32)
                got = got_ref[slot, rows, :].astype(F32)
                first = jnp.where(odd, got, held)
                second = jnp.where(odd, held, got)
                for at in range(sizes.share):
                    part = slice(at * local, (at + 1) * local)
                    both = jnp.concatenate([first[part], second[part]], axis=0).astype(BF16)
                    start = pl.multiple_of(at * sizes.count * local + pair * 2 * local, 2 * local)
                    out_ref[quarter, pl.ds(start, 2 * local), pl.ds(chunk * HD, HD)] = both


def arrange(sizes, masks, place, pairs, wait):
    rows = sizes.share * sizes.count * sizes.local
    flat = [x for pair in pairs for x in pair]
    return pl.pallas_call(
        functools.partial(arrange_kernel, sizes, masks),
        out_shape=jax.ShapeDtypeStruct((len(pairs), rows, VW), BF16),
        in_specs=[SMEM_SPEC] + [VMEM_SPEC] * (len(flat) + 1),
        out_specs=VMEM_SPEC,
        compiler_params=limits(),
    )(place, *flat, wait)


def fetch_kernel(sizes, place_ref, cot_ref, *refs):
    *refs, row_ref, sems = refs
    count = len(refs) // 2
    row_ref[...] = jnp.full(row_ref.shape, cot_ref[0], F32)
    mine = pl.ds(pl.multiple_of(place_ref[2] * sizes.width, HD), sizes.width)
    copies = []
    for slot in range(count):
        source = refs[slot].at[:, mine] if slot < 3 else refs[slot]
        copies.append(pltpu.make_async_copy(source, refs[count + slot], sems.at[slot]))
        copies[-1].start()
    for copy in copies:
        copy.wait()


def fetch(sizes, place, cotangent, arrays):
    shapes = [x.shape if slot >= 3 else (x.shape[0], sizes.width) for slot, x in enumerate(arrays)]
    return pl.pallas_call(
        functools.partial(fetch_kernel, sizes),
        out_shape=[jax.ShapeDtypeStruct(shape, x.dtype) for shape, x in zip(shapes, arrays)]
        + [jax.ShapeDtypeStruct((1, 128), F32)],
        in_specs=[SMEM_SPEC] * 2 + [HBM_SPEC] * len(arrays),
        out_specs=[VMEM_SPEC] * (len(arrays) + 1),
        scratch_shapes=[pltpu.SemaphoreType.DMA((len(arrays),))],
        compiler_params=limits(),
        cost_estimate=pl.CostEstimate(flops=1, bytes_accessed=1, transcendentals=0),
    )(place, cotangent, *[in_hbm(x) for x in arrays])


FACTOR = HD ** (-0.5) * math.log2(math.e)


def load_pieces(sizes, in_refs, key_scr, value_scr):
    tok_rows, part_rows = sizes.tok_rows, sizes.part_rows
    for src, ref in enumerate(in_refs):
        rows = pl.ds(src * tok_rows, tok_rows)
        key_scr[rows, :] = ref[pl.ds(part_rows, tok_rows), :]
        for head in range(sizes.heads):
            value_scr[rows, pl.ds(2 * head * HD, HD)] = ref[
                pl.ds(part_rows + tok_rows, tok_rows), pl.ds(head * HD, HD)
            ]
    ones = jnp.ones((len(in_refs) * tok_rows, HD), BF16)
    for head in range(sizes.heads):
        value_scr[:, pl.ds((2 * head + 1) * HD, HD)] = ones


def soft_part(query, key_scr, value_scr, rows, head, before):
    logits = mm_nt(query, key_scr[rows, pl.ds(head * HD, HD)])
    top = jnp.max(logits, axis=-1, keepdims=True)
    if before:
        top = jnp.maximum(top, before[2])
    weights = jnp.exp2((logits - top) * FACTOR).astype(BF16)
    both = mm(weights, value_scr[rows, pl.ds(2 * head * HD, 2 * HD)])
    mixed, total = both[:, :HD], both[:, HD:]
    if before:
        shrink = jnp.exp2((before[2] - top) * FACTOR)
        mixed, total = mixed + before[0] * shrink, total + before[1] * shrink
    return mixed, total, top


def piece_scratch(sizes, count):
    lat_rows = count * sizes.tok_rows
    return [
        pltpu.VMEM((lat_rows, sizes.width), BF16),
        pltpu.VMEM((lat_rows, 2 * sizes.width), BF16),
    ]


def early_kernel(sizes, count, *refs):
    in_refs, refs = refs[:count], refs[count + 1 :]
    sum_ref, stat_ref, key_scr, value_scr = refs
    load_pieces(sizes, in_refs, key_scr, value_scr)
    left = lax.broadcasted_iota(jnp.int32, (sizes.part_rows, HD), 1) < HD // 2
    rows = pl.ds(0, count * sizes.tok_rows)
    for src in range(count):
        results = [
            soft_part(
                in_refs[src][pl.ds(0, sizes.part_rows), pl.ds(head * HD, HD)],
                key_scr, value_scr, rows, head, None,
            )
            for head in range(sizes.heads)
        ]
        for head, (mixed, total, top) in enumerate(results):
            sum_ref[src, head] = mixed
            stat_ref[src, head] = jnp.where(left, top, total)


def attend_early(sizes, received, wait):
    count = len(received)
    shape = jax.ShapeDtypeStruct((count, sizes.heads, sizes.part_rows, HD), F32)
    return pl.pallas_call(
        functools.partial(early_kernel, sizes, count),
        out_shape=(shape, shape),
        in_specs=[VMEM_SPEC] * (count + 1),
        out_specs=(VMEM_SPEC, VMEM_SPEC),
        scratch_shapes=piece_scratch(sizes, count),
        compiler_params=limits(12),
        cost_estimate=pl.CostEstimate(flops=1, bytes_accessed=1, transcendentals=0),
    )(*received, wait)


def attend_kernel(sizes, masks, early, place_ref, *refs):
    count, heads, width = sizes.count, sizes.heads, sizes.width
    tok_rows, part_rows = sizes.tok_rows, sizes.part_rows
    in_refs, refs = refs[:count], refs[count:]
    kept_refs, refs = refs[: 2 if early else 0], refs[2 if early else 0 :]
    scale_ref, shift_ref, proj_ref, mod_ref, lat_ref, *refs = refs
    key_scr, value_scr = refs
    half = part_rows // 2
    me = place_ref[0]
    gain = 1.0 + scale_ref[...]
    shift = shift_ref[...]
    load_pieces(sizes, in_refs, key_scr, value_scr)
    together = 2
    for first in range(0, count, together):
        results = []
        for src in range(first, first + together):
            mixed = []
            for head in range(heads):
                before = None
                rows = pl.ds(0, count * tok_rows)
                if src < early:
                    rows = pl.ds(early * tok_rows, (count - early) * tok_rows)
                    stat = kept_refs[1][src, head]
                    before = (kept_refs[0][src, head], stat[:, HD - 1 :], stat[:, :1])
                query = in_refs[src][pl.ds(0, part_rows), pl.ds(head * HD, HD)]
                value, total, _ = soft_part(query, key_scr, value_scr, rows, head, before)
                mixed.append(value / total)
            results.append(jnp.concatenate(mixed, axis=1) if heads > 1 else mixed[0])
        for at, attended in enumerate(results):
            modulated = (attended * gain + shift).astype(BF16)
            mod_ref[jnp.bitwise_xor(me, masks[first + at])] = modulated
    sides = [
        mm_nt(mod_ref[:, rows, :].reshape(count * half, width), proj_ref[...])
        for rows in (slice(0, half), slice(half, part_rows))
    ]
    latent = jnp.concatenate(sides, axis=1).astype(BF16)
    for spot, place in enumerate(sizes.order()):
        lat_ref[spot] = latent[place * half : (place + 1) * half]


def attend(sizes, masks, place, received, kept, scales, shifts, proj):
    count, width, heads = sizes.count, sizes.width, sizes.heads
    lat_rows = count * sizes.tok_rows
    query_rows = count * sizes.part_rows
    early = kept[0].shape[0] if kept else 0
    return pl.pallas_call(
        functools.partial(attend_kernel, sizes, masks, early),
        out_shape=(
            jax.ShapeDtypeStruct((count, sizes.part_rows, width), BF16),
            jax.ShapeDtypeStruct((count, sizes.part_rows // 2, 2 * CH), BF16),
        ),
        in_specs=[SMEM_SPEC] + [VMEM_SPEC] * (count + len(kept) + 3),
        out_specs=(VMEM_SPEC, VMEM_SPEC),
        scratch_shapes=piece_scratch(sizes, count),
        compiler_params=limits(16),
        cost_estimate=pl.CostEstimate(
            flops=4 * query_rows * lat_rows * width,
            bytes_accessed=2 * (query_rows * 2 + lat_rows * 2) * width,
            transcendentals=query_rows * lat_rows * heads,
        ),
    )(place, *received, *kept, scales, shifts, proj)


def total_kernel(copies, count, *refs):
    out_ref = refs[-1]
    if count == 1:
        parts = [refs[0][i].astype(F32) for i in range(refs[0].shape[0])]
    else:
        parts = [ref[...].astype(F32) for ref in refs[:count]]
    while len(parts) > 1:
        parts = [parts[i] + parts[i + 1] for i in range(0, len(parts), 2)]
    for copy in range(copies):
        out_ref[copy] = parts[0].astype(BF16)


def total_copies(arrays, copies, others=()):
    return pl.pallas_call(
        functools.partial(total_kernel, copies, len(arrays)),
        out_shape=jax.ShapeDtypeStruct((copies,) + arrays[0].shape[-2:], BF16),
        in_specs=[VMEM_SPEC] * (len(arrays) + len(others)),
        out_specs=VMEM_SPEC,
        compiler_params=limits(),
    )(*arrays, *others)


def lane_mean(x, count):
    return jnp.sum(x, axis=-1, keepdims=True) * (1.0 / count)


def head_kernel(grid_rows, fused, order, embed_masks, out_factor, place_ref, lat_ref, *refs):
    embed_refs, refs = refs[: len(embed_masks)], refs[len(embed_masks) :]
    pos_ref, pre_ref, post_ref, prompt_ref, cot_ref, mod_ref, *refs = refs
    reward_ref, grad_ref, weight_ref, lat_scr, grad_scr, block_scr, back_scr = refs
    patch_rows = grid_rows // 4
    patch_cols = GW // 4
    patches = patch_rows * patch_cols
    for spot, place in enumerate(order):
        lat_scr[pl.ds(place * GW, GW), :] = lat_ref[pl.ds(spot * GW, GW), :].astype(F32)

    data = place_ref[1]
    shares = [
        (jnp.bitwise_xor(data, mask), ref, slot)
        for ref, masks in zip(embed_refs, embed_masks)
        for slot, mask in enumerate(masks)
    ]
    share_rows = embed_refs[0].shape[1]
    for hi in range(2):
        wide = []
        for tx in range(4):
            rows = [
                lat_scr[pl.ds((2 * pr + hi) * GW + tx, patch_cols, stride=4), :]
                for pr in range(patch_rows)
            ]
            wide.append(jnp.concatenate(rows, axis=0))
        for side in range(2):
            lanes = slice(side * CH, (side + 1) * CH)
            line = jnp.concatenate([x[:, lanes] for x in wide], axis=1).astype(BF16)
            first = (2 * hi + side) * 4 * CH
            if share_rows >= 4 * CH:
                at = first % share_rows
                block_scr[first // share_rows, :, pl.ds(at, 4 * CH)] = line
            else:
                for at in range(0, 4 * CH, share_rows):
                    block_scr[(first + at) // share_rows] = line[:, at : at + share_rows]
    embedded = pos_ref[...].astype(F32)
    for number, ref, slot in shares:
        embedded = embedded + mm(block_scr[number], ref[slot])
    pre = pre_ref[...].reshape(1, VW)
    post = post_ref[...].reshape(1, VW)
    prompt = prompt_ref[...]
    center = embedded - lane_mean(embedded, VW)
    rstd = lax.rsqrt(lane_mean(center * center, VW) + EPS)
    unit = center * rstd
    pooled = jnp.sum(unit, axis=0, keepdims=True) * (1.0 / patches) * pre
    pooled_center = pooled - lane_mean(pooled, VW)
    pooled_rstd = lax.rsqrt(lane_mean(pooled_center * pooled_center, VW) + EPS)
    pooled_unit = pooled_center * pooled_rstd
    final = pooled_unit * post
    dot = jnp.sum(final * prompt, axis=-1, keepdims=True)
    final_sq = jnp.sum(final * final, axis=-1, keepdims=True)
    prompt_sq = jnp.sum(prompt * prompt, axis=-1, keepdims=True)
    final_len = jnp.sqrt(final_sq)
    prompt_len = jnp.sqrt(prompt_sq)
    cosine = dot / (final_len * prompt_len)
    reward_ref[...] = jnp.broadcast_to(100.0 * cosine, reward_ref.shape)
    cot = cot_ref[:, :1]
    final_grad = (100.0 * cot) * (prompt / (final_len * prompt_len) - final * (cosine / final_sq))
    unit_grad = final_grad * post
    pooled_grad = pooled_rstd * (
        unit_grad
        - lane_mean(unit_grad, VW)
        - pooled_unit * lane_mean(unit_grad * pooled_unit, VW)
    )
    flow = pooled_grad * pre * (1.0 / patches)
    embed_grad = rstd * (flow - lane_mean(flow, VW) - unit * lane_mean(flow * unit, VW))
    high = embed_grad.astype(BF16)
    low = (embed_grad - high.astype(F32)).astype(BF16)
    stacked = jnp.concatenate([high, low], axis=0)
    for number, ref, slot in shares:
        both = mm_nt(stacked, ref[slot])
        back_scr[number] = both[:patches] + both[patches:]
    back = jnp.concatenate([back_scr[i] for i in range(16 * CH // share_rows)], axis=1)
    for hi in range(2):
        for tx in range(4):
            first = (4 * (2 * hi) + tx) * CH
            second = (4 * (2 * hi + 1) + tx) * CH
            piece = jnp.concatenate(
                [back[:, first : first + CH], back[:, second : second + CH]], axis=1
            )
            for pr in range(patch_rows):
                grad_scr[pl.ds((2 * pr + hi) * GW + tx, patch_cols, stride=4), :] = piece[
                    pr * patch_cols : (pr + 1) * patch_cols
                ]
    grad = grad_scr[...].astype(BF16)
    grad_ref[...] = grad
    if fused:
        store_readout_grad(grad, mod_ref, out_factor, weight_ref)
    else:
        weight_ref[...] = jnp.zeros_like(weight_ref)


def store_readout_grad(grad, mod_ref, out_factor, out_ref):
    turned = grad.astype(F32).T.astype(BF16)
    count, rows, width = mod_ref.shape
    half = rows // 2
    first = mod_ref[:, :half, :].reshape(count * half, width)
    second = mod_ref[:, half:, :].reshape(count * half, width)
    total = mm(turned[:CH], first) + mm(turned[CH:], second)
    out_ref[...] = (total * out_factor).astype(BF16)


def reward_head(
    place, order, latent, embed, pos, pre, post, prompt, cot, modulated, grid_rows, fused, out_factor
):
    patches = grid_rows * GW // 16
    rows = grid_rows * GW // 2
    width = modulated.shape[2]
    embed_arrays, embed_masks = [x for x, _ in embed], [masks for _, masks in embed]
    share_rows = embed_arrays[0].shape[1]
    return pl.pallas_call(
        functools.partial(head_kernel, grid_rows, fused, order, embed_masks, out_factor),
        out_shape=(
            jax.ShapeDtypeStruct((1, 128), F32),
            jax.ShapeDtypeStruct((rows, 2 * CH), BF16),
            jax.ShapeDtypeStruct((CH, width), BF16),
        ),
        in_specs=[SMEM_SPEC, VMEM_SPEC]
        + [VMEM_SPEC] * len(embed_arrays)
        + [VMEM_SPEC] * 6,
        out_specs=(VMEM_SPEC, VMEM_SPEC, VMEM_SPEC),
        scratch_shapes=[
            pltpu.VMEM((rows, 2 * CH), F32),
            pltpu.VMEM((rows, 2 * CH), F32),
            pltpu.VMEM((16 * CH // share_rows, patches, share_rows), BF16),
            pltpu.VMEM((16 * CH // share_rows, patches, share_rows), F32),
        ],
        compiler_params=limits(16),
        cost_estimate=pl.CostEstimate(
            flops=6 * patches * 16 * CH * VW,
            bytes_accessed=2 * 16 * CH * VW + 2 * patches * VW,
            transcendentals=0,
        ),
    )(place, latent, *embed_arrays, pos, pre, post, prompt, cot, modulated)


def spread_kernel(count, half, heads, grad_ref, scale_ref, proj_ref, out_ref, token_ref):
    token_ref[...] = jnp.zeros_like(token_ref)
    gain = 1.0 + scale_ref[...]
    proj = proj_ref[...]
    zero = jnp.zeros_like(proj)
    sides = (jnp.concatenate([proj, zero], axis=0), jnp.concatenate([zero, proj], axis=0))
    for src in range(count):
        grad = grad_ref[pl.ds(src * half, half), :]
        for side in range(2):
            rows = (mm(grad, sides[side]) * gain).astype(BF16)
            for head in range(heads):
                out_ref[0, head, pl.ds((2 * src + side) * half, half), :] = rows[
                    :, head * HD : (head + 1) * HD
                ]


def spread(grad, scales, proj, count, half, heads):
    return pl.pallas_call(
        functools.partial(spread_kernel, count, half, heads),
        out_shape=(
            jax.ShapeDtypeStruct((1, heads, 2 * count * half, HD), BF16),
            jax.ShapeDtypeStruct((8, 128), F32),
        ),
        in_specs=[VMEM_SPEC] * 3,
        out_specs=(VMEM_SPEC, VMEM_SPEC),
        compiler_params=limits(),
        cost_estimate=pl.CostEstimate(
            flops=8 * count * half * CH * heads * HD,
            bytes_accessed=4 * count * half * heads * HD,
            transcendentals=0,
        ),
    )(grad, scales, proj)


def weight_kernel(out_factor, grad_ref, *refs):
    store_readout_grad(grad_ref[...], refs[0], out_factor, refs[1])


def weight_call(grad, modulated, out_factor):
    return pl.pallas_call(
        functools.partial(weight_kernel, out_factor),
        out_shape=jax.ShapeDtypeStruct((CH, modulated.shape[2]), BF16),
        in_specs=[VMEM_SPEC] * 2,
        out_specs=VMEM_SPEC,
        compiler_params=limits(),
    )(grad, modulated)


def finish_kernel(order, in_ref, out_ref):
    width = in_ref.shape[2]
    for spot, group in enumerate(order):
        out_ref[:, pl.ds(group * width, width)] = in_ref[spot].astype(F32)


def finish(blocks, order):
    return pl.pallas_call(
        functools.partial(finish_kernel, order),
        out_shape=jax.ShapeDtypeStruct((CH, HEADS * HD), F32),
        in_specs=[VMEM_SPEC],
        out_specs=VMEM_SPEC,
        compiler_params=limits(),
    )(blocks)


def swap(x, axis, mask):
    count = lax.axis_size(axis)
    return lax.ppermute(x, axis, [(i, i ^ mask) for i in range(count)])


def all_to_all(x, groups=None):
    return lax.all_to_all(
        x, "seq", split_axis=0, concat_axis=0, tiled=True, axis_index_groups=groups
    )


def swap_both(x, seq_mask, data_mask):
    seq_count, data_count = lax.axis_size("seq"), lax.axis_size("dp")
    pairs = [
        (i * data_count + j, (i ^ seq_mask) * data_count + (j ^ data_mask))
        for i in range(seq_count)
        for j in range(data_count)
    ]
    return lax.ppermute(x, ("seq", "dp"), pairs)


def on_device(
    queries,
    keys,
    values,
    shifts,
    scales,
    proj_out,
    patch_embed,
    pos_embed,
    pre_gain,
    post_gain,
    prompt,
    cotangent,
):
    seq_count = lax.axis_size("seq")
    data_count = lax.axis_size("dp")
    tok_rows = queries.shape[1]
    sizes = Sizes(seq_count, data_count, tok_rows, patch_embed)
    query_parts, head_count, part_rows = sizes.query_parts, sizes.heads, sizes.part_rows
    group_count = HEADS // head_count
    seq_index = lax.axis_index("seq")
    head_group = seq_index // query_parts
    query_part = seq_index % query_parts
    half = part_rows // 2
    lat_rows = seq_count * tok_rows
    grid_rows = lat_rows // GW
    canonical = part_rows == 2 * GW
    place = jnp.stack([seq_index, lax.axis_index("dp"), head_group]).astype(jnp.int32)
    proj_turned = proj_out.T
    out_factor = 1.0 / math.sqrt(data_count * lat_rows)

    masks = sizes.pieces()
    packed = pack(
        sizes, in_hbm(queries), in_hbm(keys), in_hbm(values), in_hbm(patch_embed)
    )
    received = [swap(x, "seq", mask) if mask else x for mask, x in zip(masks, packed)]
    bits = [1 << b for b in reversed(range(data_count.bit_length() - 1))]
    shared = sizes.share < patch_embed.shape[0]
    scale, shift, proj, pos, pre, post, words, cot = fetch(
        sizes, place, cotangent, [scales, shifts, proj_turned, pos_embed, pre_gain, post_gain, prompt]
    )

    kept, order = [], list(range(seq_count))
    if seq_count == 8:
        late = [slot for slot, mask in enumerate(masks) if mask in (6, 7)]
        order = [slot for slot in order if slot not in late]
        kept = attend_early(sizes, [received[slot] for slot in order], scale)
        order = order + late
    if sizes.riding:
        ride = [slot for slot, mask in enumerate(masks) if sizes.rides(mask)]
        two = collect(sizes, [received[slot] for slot in ride])
        held = join(two, swap(two, "seq", 2), kept)
        ride_masks = [masks[slot] for slot in ride]
        ride_masks = ride_masks + [mask ^ 2 for mask in ride_masks]
        pairs = [
            (held, swap(held, "seq", 1)),
            (swap(held, "dp", bits[0]), swap_both(held, 1, bits[0])),
        ]

    modulated, latent_part = attend(
        sizes, [masks[slot] for slot in order], place, [received[slot] for slot in order], kept,
        scale, shift, proj,
    )

    if not sizes.riding:
        mine = patch_embed
        if shared:
            mine = lax.dynamic_slice_in_dim(
                patch_embed, lax.axis_index("dp") * sizes.share, sizes.share, 0
            )
        mine = lax.all_gather(mine, "seq", axis=1, tiled=True).reshape(-1, VW)
        embed = [(mine[None], [0])]
        if shared:
            embed = embed + [(swap(mine[None], "dp", bits[0]), [bits[0]])]

    groups, order = [sizes.order()], sizes.order()
    if query_parts > 1:
        order = list(range(group_count))
        groups = [[g * query_parts + r for g in range(group_count)] for r in range(query_parts)]
    per_share = seq_count // group_count
    parts = all_to_all(latent_part.reshape(group_count, per_share * half, 2 * CH), groups)
    summed = total_copies([parts], seq_count)
    if sizes.riding:
        embed = [(arrange(sizes, ride_masks, place, pairs, summed), [0, bits[0]])]
    for bit in bits[1:] if shared else []:
        embed = embed + [(swap(x, "dp", bit), [m ^ bit for m in some]) for x, some in embed]
    latent = all_to_all(summed, [sizes.order()])
    if canonical:
        latent = latent.reshape(lat_rows // 2, 2 * CH)
    else:
        latent = latent.reshape(group_count, query_parts, per_share, half, 2, CH)
        latent = latent.transpose(0, 2, 1, 4, 3, 5).reshape(grid_rows // 2, 2, GW, CH)
        latent = latent.transpose(0, 2, 1, 3).reshape(lat_rows // 2, 2 * CH)

    reward, grad, weight = reward_head(
        place, sizes.order() if canonical else list(range(grid_rows // 2)),
        latent, embed, pos, pre, post, words,
        cot, modulated, grid_rows, canonical, out_factor,
    )
    if not canonical:
        tokens = grad.reshape(grid_rows // 2, GW, 2, CH).transpose(0, 2, 1, 3)
        tokens = tokens.reshape(seq_count, query_parts, 2, half, CH)
        tokens = lax.dynamic_index_in_dim(tokens, query_part, 1, keepdims=False)
        grad = tokens.transpose(0, 2, 1, 3).reshape(seq_count * half, 2 * CH)
        weight = weight_call(grad, modulated, out_factor)

    parts = [weight] + [swap(weight, "dp", mask) for mask in range(1, data_count)]
    attn_grad, token = spread(grad, scale, proj, seq_count, half, head_count)
    if query_parts > 1:
        total = total_copies(parts, 1)[0]
        parts = [total] + [swap(total, "seq", mask) for mask in range(1, query_parts)]
    blocks = all_to_all(total_copies(parts, group_count, [token]), groups)
    return (reward[0, :1], attn_grad, finish(blocks, order).T)


def solution(mesh):
    return jax.shard_map(
        on_device,
        mesh=mesh,
        in_specs=(
            P("dp", "seq", None),
            P("dp", "seq", None),
            P("dp", "seq", None),
            P("dp", None),
            P("dp", None),
            P(),
            P(None, "seq", None),
            P(),
            P(),
            P(),
            P("dp", None),
            P("dp"),
        ),
        out_specs=(P("dp"), P("dp", "seq", None, None), P()),
        check_vma=False,
    )
```

```python
import functools
import math

import jax
import jax.numpy as jnp
from jax import lax
from jax.experimental import pallas as pl
from jax.experimental.pallas import tpu as pltpu
from jax.sharding import PartitionSpec as P

HEADS = 16
HD = 128
CH = 64
GW = 64
VW = 1280
EPS = 1e-05
BF16 = jnp.bfloat16
F32 = jnp.float32


def mm(a, b):
    return jnp.dot(a, b, preferred_element_type=F32)


def mm_nt(a, b):
    return lax.dot_general(a, b, (((1,), (1,)), ((), ())), preferred_element_type=F32)


def mm_tn(a, b):
    return lax.dot_general(a, b, (((0,), (0,)), ((), ())), preferred_element_type=F32)


SMEM_SPEC = pl.BlockSpec(memory_space=pltpu.SMEM)
VMEM_SPEC = pl.BlockSpec(memory_space=pltpu.VMEM)
HBM_SPEC = pl.BlockSpec(memory_space=pltpu.HBM)
ANY_SPEC = pl.BlockSpec(memory_space=pl.ANY)


def in_hbm(x):
    return pltpu.with_memory_space_constraint(x, pltpu.HBM)


def limits(mib=4):
    return pltpu.CompilerParams(vmem_limit_bytes=mib * 1024 * 1024)


class Sizes:
    def __init__(self, seq_count, data_count, tok_rows, patch_embed):
        self.count = seq_count
        self.query_parts = max(1, seq_count // HEADS)
        self.heads = max(1, HEADS // seq_count)
        self.width = self.heads * HD
        self.tok_rows = tok_rows
        self.part_rows = tok_rows // self.query_parts
        positions, self.local, _ = patch_embed.shape
        self.share = positions // data_count if positions % data_count == 0 else positions
        self.rows = self.part_rows + 2 * tok_rows
        self.share_rows = self.share * self.local
        self.chunks = VW // HD
        self.riding = self.local % 8 == 0 and self.share_rows % 16 == 0 and seq_count == 8
        self.riding = self.riding and 1 < data_count <= positions
        self.ride_rows = self.chunks * self.share_rows if self.riding else 0

    def order(self):
        return [4, 5, 2, 3, 6, 7, 0, 1] if self.count == 8 else list(range(self.count))

    def pieces(self):
        return list(range(1, self.count)) + [0]

    def rides(self, mask):
        return self.riding and mask in (0, 4)

    def piece_shape(self, mask):
        return (self.rows + (self.ride_rows // self.heads if self.rides(mask) else 0), self.width)

    def ride_slices(self):
        deep = self.ride_rows // self.heads
        return [
            (pl.ds(self.rows, deep), pl.ds(at * HD, HD), pl.ds(at * deep, deep))
            for at in range(self.heads)
        ]


def pack_kernel(sizes, q_ref, k_ref, v_ref, embed_ref, *refs):
    masks = sizes.pieces()
    out_refs = refs[: len(masks)]
    embed_scr, share_scr, embed_sem, sems = refs[len(masks) :]
    me = lax.axis_index("seq")
    tok_rows, part_rows, width = sizes.tok_rows, sizes.part_rows, sizes.width
    share = pl.ds(lax.axis_index("dp") * sizes.share, sizes.share)
    load = pltpu.make_async_copy(embed_ref.at[share], embed_scr, embed_sem.at[0])
    load.start()
    copies = []
    for slot, (mask, out) in enumerate(zip(masks, out_refs)):
        dest = jnp.bitwise_xor(me, mask)
        group, part = dest // sizes.query_parts, dest % sizes.query_parts
        cols = pl.ds(pl.multiple_of(group * width, HD), width)
        first = pl.ds(pl.multiple_of(part * part_rows, part_rows), part_rows)
        for kind, source, rows in (
            (0, q_ref.at[0, first, cols], pl.ds(0, part_rows)),
            (1, k_ref.at[0, :, cols], pl.ds(part_rows, tok_rows)),
            (2, v_ref.at[0, :, cols], pl.ds(part_rows + tok_rows, tok_rows)),
        ):
            copies.append(pltpu.make_async_copy(source, out.at[rows], sems.at[kind, slot]))
    for copy in copies:
        copy.start()
    load.wait()
    if sizes.riding:
        for chunk in range(sizes.chunks):
            cols = embed_scr[:, :, pl.ds(chunk * HD, HD)].astype(F32)
            share_scr[pl.ds(chunk * sizes.share_rows, sizes.share_rows), :] = cols.reshape(
                sizes.share_rows, HD
            ).astype(BF16)
        for mask, out in zip(masks, out_refs):
            if sizes.rides(mask):
                for rows, place, from_rows in sizes.ride_slices():
                    out[rows, place] = share_scr[from_rows, :]
    for copy in copies:
        copy.wait()


def pack(sizes, queries, keys, values, patch_embed):
    tok_rows, full = queries.shape[1:]
    masks = sizes.pieces()
    return pl.pallas_call(
        functools.partial(pack_kernel, sizes),
        out_shape=[jax.ShapeDtypeStruct(sizes.piece_shape(mask), BF16) for mask in masks],
        in_specs=[HBM_SPEC] * 4,
        out_specs=[VMEM_SPEC] * len(masks),
        scratch_shapes=[
            pltpu.VMEM((sizes.share,) + patch_embed.shape[1:], BF16),
            pltpu.VMEM((max(16, sizes.ride_rows), HD), BF16),
            pltpu.SemaphoreType.DMA((1,)),
            pltpu.SemaphoreType.DMA((3, len(masks))),
        ],
        compiler_params=limits(8),
        cost_estimate=pl.CostEstimate(
            flops=0, bytes_accessed=12 * tok_rows * full, transcendentals=0
        ),
    )(queries, keys, values, patch_embed)


def collect_kernel(sizes, *refs):
    *in_refs, out_ref, sems = refs
    copies = []
    for slot, ref in enumerate(in_refs):
        for at, (rows, cols, to_rows) in enumerate(sizes.ride_slices()):
            copies.append(
                pltpu.make_async_copy(
                    ref.at[rows, cols], out_ref.at[slot, to_rows], sems.at[at, slot]
                )
            )
    for copy in copies:
        copy.start()
    for copy in copies:
        copy.wait()


def collect(sizes, arrays):
    return pl.pallas_call(
        functools.partial(collect_kernel, sizes),
        out_shape=jax.ShapeDtypeStruct((len(arrays), sizes.ride_rows, HD), BF16),
        in_specs=[ANY_SPEC] * len(arrays),
        out_specs=VMEM_SPEC,
        scratch_shapes=[pltpu.SemaphoreType.DMA((sizes.heads, len(arrays)))],
        compiler_params=limits(),
    )(*arrays)


def join_kernel(first_ref, second_ref, *refs):
    out_ref = refs[-1]
    count = first_ref.shape[0]
    out_ref[:count] = first_ref[...]
    out_ref[count:] = second_ref[...]


def join(first, second, others):
    return pl.pallas_call(
        join_kernel,
        out_shape=jax.ShapeDtypeStruct((2 * first.shape[0],) + first.shape[1:], BF16),
        in_specs=[VMEM_SPEC] * 2 + [ANY_SPEC] * len(others),
        out_specs=VMEM_SPEC,
        compiler_params=limits(),
    )(first, second, *others)


def arrange_kernel(sizes, masks, place_ref, *refs):
    *pair_refs, out_ref = refs[:-2] + refs[-1:]
    me = place_ref[0]
    odd = me % 2 == 1
    local = sizes.local
    for quarter in range(len(pair_refs) // 2):
        held_ref, got_ref = pair_refs[2 * quarter], pair_refs[2 * quarter + 1]
        for slot, mask in enumerate(masks):
            pair = jnp.bitwise_xor(me, mask) // 2
            for chunk in range(sizes.chunks):
                rows = pl.ds(chunk * sizes.share_rows, sizes.share_rows)
                held = held_ref[slot, rows, :].astype(F32)
                got = got_ref[slot, rows, :].astype(F32)
                first = jnp.where(odd, got, held)
                second = jnp.where(odd, held, got)
                for at in range(sizes.share):
                    part = slice(at * local, (at + 1) * local)
                    both = jnp.concatenate([first[part], second[part]], axis=0).astype(BF16)
                    start = pl.multiple_of(at * sizes.count * local + pair * 2 * local, 2 * local)
                    out_ref[quarter, pl.ds(start, 2 * local), pl.ds(chunk * HD, HD)] = both


def arrange(sizes, masks, place, pairs, wait):
    rows = sizes.share * sizes.count * sizes.local
    flat = [x for pair in pairs for x in pair]
    return pl.pallas_call(
        functools.partial(arrange_kernel, sizes, masks),
        out_shape=jax.ShapeDtypeStruct((len(pairs), rows, VW), BF16),
        in_specs=[SMEM_SPEC] + [VMEM_SPEC] * (len(flat) + 1),
        out_specs=VMEM_SPEC,
        compiler_params=limits(),
    )(place, *flat, wait)


def fetch_kernel(sizes, place_ref, cot_ref, *refs):
    *refs, row_ref, sems = refs
    count = len(refs) // 2
    row_ref[...] = jnp.full(row_ref.shape, cot_ref[0], F32)
    mine = pl.ds(pl.multiple_of(place_ref[2] * sizes.width, HD), sizes.width)
    copies = []
    for slot in range(count):
        source = refs[slot].at[:, mine] if slot < 3 else refs[slot]
        copies.append(pltpu.make_async_copy(source, refs[count + slot], sems.at[slot]))
        copies[-1].start()
    for copy in copies:
        copy.wait()


def fetch(sizes, place, cotangent, arrays):
    shapes = [x.shape if slot >= 3 else (x.shape[0], sizes.width) for slot, x in enumerate(arrays)]
    return pl.pallas_call(
        functools.partial(fetch_kernel, sizes),
        out_shape=[jax.ShapeDtypeStruct(shape, x.dtype) for shape, x in zip(shapes, arrays)]
        + [jax.ShapeDtypeStruct((1, 128), F32)],
        in_specs=[SMEM_SPEC] * 2 + [HBM_SPEC] * len(arrays),
        out_specs=[VMEM_SPEC] * (len(arrays) + 1),
        scratch_shapes=[pltpu.SemaphoreType.DMA((len(arrays),))],
        compiler_params=limits(),
        cost_estimate=pl.CostEstimate(flops=1, bytes_accessed=1, transcendentals=0),
    )(place, cotangent, *[in_hbm(x) for x in arrays])


FACTOR = HD ** (-0.5) * math.log2(math.e)


def load_pieces(sizes, in_refs, key_scr, value_scr):
    tok_rows, part_rows = sizes.tok_rows, sizes.part_rows
    for src, ref in enumerate(in_refs):
        rows = pl.ds(src * tok_rows, tok_rows)
        key_scr[rows, :] = ref[pl.ds(part_rows, tok_rows), :]
        for head in range(sizes.heads):
            value_scr[rows, pl.ds(2 * head * HD, HD)] = ref[
                pl.ds(part_rows + tok_rows, tok_rows), pl.ds(head * HD, HD)
            ]
    ones = jnp.ones((len(in_refs) * tok_rows, HD), BF16)
    for head in range(sizes.heads):
        value_scr[:, pl.ds((2 * head + 1) * HD, HD)] = ones


def soft_part(query, key_scr, value_scr, rows, head, before):
    logits = mm_nt(query, key_scr[rows, pl.ds(head * HD, HD)])
    top = jnp.max(logits, axis=-1, keepdims=True)
    if before:
        top = jnp.maximum(top, before[2])
    weights = jnp.exp2((logits - top) * FACTOR).astype(BF16)
    both = mm(weights, value_scr[rows, pl.ds(2 * head * HD, 2 * HD)])
    mixed, total = both[:, :HD], both[:, HD:]
    if before:
        shrink = jnp.exp2((before[2] - top) * FACTOR)
        mixed, total = mixed + before[0] * shrink, total + before[1] * shrink
    return mixed, total, top


def piece_scratch(sizes, count):
    lat_rows = count * sizes.tok_rows
    return [
        pltpu.VMEM((lat_rows, sizes.width), BF16),
        pltpu.VMEM((lat_rows, 2 * sizes.width), BF16),
    ]


def early_kernel(sizes, count, *refs):
    in_refs, refs = refs[:count], refs[count + 1 :]
    sum_ref, stat_ref, key_scr, value_scr = refs
    load_pieces(sizes, in_refs, key_scr, value_scr)
    left = lax.broadcasted_iota(jnp.int32, (sizes.part_rows, HD), 1) < HD // 2
    rows = pl.ds(0, count * sizes.tok_rows)
    for src in range(count):
        results = [
            soft_part(
                in_refs[src][pl.ds(0, sizes.part_rows), pl.ds(head * HD, HD)],
                key_scr, value_scr, rows, head, None,
            )
            for head in range(sizes.heads)
        ]
        for head, (mixed, total, top) in enumerate(results):
            sum_ref[src, head] = mixed
            stat_ref[src, head] = jnp.where(left, top, total)


def attend_early(sizes, received, wait):
    count = len(received)
    shape = jax.ShapeDtypeStruct((count, sizes.heads, sizes.part_rows, HD), F32)
    return pl.pallas_call(
        functools.partial(early_kernel, sizes, count),
        out_shape=(shape, shape),
        in_specs=[VMEM_SPEC] * (count + 1),
        out_specs=(VMEM_SPEC, VMEM_SPEC),
        scratch_shapes=piece_scratch(sizes, count),
        compiler_params=limits(12),
        cost_estimate=pl.CostEstimate(flops=1, bytes_accessed=1, transcendentals=0),
    )(*received, wait)


def attend_kernel(sizes, masks, early, place_ref, *refs):
    count, heads, width = sizes.count, sizes.heads, sizes.width
    tok_rows, part_rows = sizes.tok_rows, sizes.part_rows
    in_refs, refs = refs[:count], refs[count:]
    kept_refs, refs = refs[: 2 if early else 0], refs[2 if early else 0 :]
    scale_ref, shift_ref, proj_ref, mod_ref, lat_ref, *refs = refs
    key_scr, value_scr = refs
    half = part_rows // 2
    me = place_ref[0]
    gain = 1.0 + scale_ref[...]
    shift = shift_ref[...]
    load_pieces(sizes, in_refs, key_scr, value_scr)
    together = 2
    for first in range(0, count, together):
        results = []
        for src in range(first, first + together):
            mixed = []
            for head in range(heads):
                before = None
                rows = pl.ds(0, count * tok_rows)
                if src < early:
                    rows = pl.ds(early * tok_rows, (count - early) * tok_rows)
                    stat = kept_refs[1][src, head]
                    before = (kept_refs[0][src, head], stat[:, HD - 1 :], stat[:, :1])
                query = in_refs[src][pl.ds(0, part_rows), pl.ds(head * HD, HD)]
                value, total, _ = soft_part(query, key_scr, value_scr, rows, head, before)
                mixed.append(value / total)
            results.append(jnp.concatenate(mixed, axis=1) if heads > 1 else mixed[0])
        for at, attended in enumerate(results):
            modulated = (attended * gain + shift).astype(BF16)
            mod_ref[jnp.bitwise_xor(me, masks[first + at])] = modulated
    sides = [
        mm_nt(mod_ref[:, rows, :].reshape(count * half, width), proj_ref[...])
        for rows in (slice(0, half), slice(half, part_rows))
    ]
    latent = jnp.concatenate(sides, axis=1).astype(BF16)
    for spot, place in enumerate(sizes.order()):
        lat_ref[spot] = latent[place * half : (place + 1) * half]


def attend(sizes, masks, place, received, kept, scales, shifts, proj):
    count, width, heads = sizes.count, sizes.width, sizes.heads
    lat_rows = count * sizes.tok_rows
    query_rows = count * sizes.part_rows
    early = kept[0].shape[0] if kept else 0
    return pl.pallas_call(
        functools.partial(attend_kernel, sizes, masks, early),
        out_shape=(
            jax.ShapeDtypeStruct((count, sizes.part_rows, width), BF16),
            jax.ShapeDtypeStruct((count, sizes.part_rows // 2, 2 * CH), BF16),
        ),
        in_specs=[SMEM_SPEC] + [VMEM_SPEC] * (count + len(kept) + 3),
        out_specs=(VMEM_SPEC, VMEM_SPEC),
        scratch_shapes=piece_scratch(sizes, count),
        compiler_params=limits(16),
        cost_estimate=pl.CostEstimate(
            flops=4 * query_rows * lat_rows * width,
            bytes_accessed=2 * (query_rows * 2 + lat_rows * 2) * width,
            transcendentals=query_rows * lat_rows * heads,
        ),
    )(place, *received, *kept, scales, shifts, proj)


def total_kernel(copies, count, *refs):
    out_ref = refs[-1]
    if count == 1:
        parts = [refs[0][i].astype(F32) for i in range(refs[0].shape[0])]
    else:
        parts = [ref[...].astype(F32) for ref in refs[:count]]
    while len(parts) > 1:
        parts = [parts[i] + parts[i + 1] for i in range(0, len(parts), 2)]
    for copy in range(copies):
        out_ref[copy] = parts[0].astype(BF16)


def total_copies(arrays, copies, others=()):
    return pl.pallas_call(
        functools.partial(total_kernel, copies, len(arrays)),
        out_shape=jax.ShapeDtypeStruct((copies,) + arrays[0].shape[-2:], BF16),
        in_specs=[VMEM_SPEC] * (len(arrays) + len(others)),
        out_specs=VMEM_SPEC,
        compiler_params=limits(),
    )(*arrays, *others)


def lane_mean(x, count):
    return jnp.sum(x, axis=-1, keepdims=True) * (1.0 / count)


def head_kernel(grid_rows, fused, order, embed_masks, out_factor, place_ref, lat_ref, *refs):
    embed_refs, refs = refs[: len(embed_masks)], refs[len(embed_masks) :]
    pos_ref, pre_ref, post_ref, prompt_ref, cot_ref, mod_ref, *refs = refs
    reward_ref, grad_ref, weight_ref, lat_scr, grad_scr, block_scr, back_scr = refs
    patch_rows = grid_rows // 4
    patch_cols = GW // 4
    patches = patch_rows * patch_cols
    for spot, place in enumerate(order):
        lat_scr[pl.ds(place * GW, GW), :] = lat_ref[pl.ds(spot * GW, GW), :].astype(F32)

    data = place_ref[1]
    shares = [
        (jnp.bitwise_xor(data, mask), ref, slot)
        for ref, masks in zip(embed_refs, embed_masks)
        for slot, mask in enumerate(masks)
    ]
    share_rows = embed_refs[0].shape[1]
    for hi in range(2):
        wide = []
        for tx in range(4):
            rows = [
                lat_scr[pl.ds((2 * pr + hi) * GW + tx, patch_cols, stride=4), :]
                for pr in range(patch_rows)
            ]
            wide.append(jnp.concatenate(rows, axis=0))
        for side in range(2):
            lanes = slice(side * CH, (side + 1) * CH)
            line = jnp.concatenate([x[:, lanes] for x in wide], axis=1).astype(BF16)
            first = (2 * hi + side) * 4 * CH
            if share_rows >= 4 * CH:
                at = first % share_rows
                block_scr[first // share_rows, :, pl.ds(at, 4 * CH)] = line
            else:
                for at in range(0, 4 * CH, share_rows):
                    block_scr[(first + at) // share_rows] = line[:, at : at + share_rows]
    embedded = pos_ref[...].astype(F32)
    for number, ref, slot in shares:
        embedded = embedded + mm(block_scr[number], ref[slot])
    pre = pre_ref[...].reshape(1, VW)
    post = post_ref[...].reshape(1, VW)
    prompt = prompt_ref[...]
    center = embedded - lane_mean(embedded, VW)
    rstd = lax.rsqrt(lane_mean(center * center, VW) + EPS)
    unit = center * rstd
    pooled = jnp.sum(unit, axis=0, keepdims=True) * (1.0 / patches) * pre
    pooled_center = pooled - lane_mean(pooled, VW)
    pooled_rstd = lax.rsqrt(lane_mean(pooled_center * pooled_center, VW) + EPS)
    pooled_unit = pooled_center * pooled_rstd
    final = pooled_unit * post
    dot = jnp.sum(final * prompt, axis=-1, keepdims=True)
    final_sq = jnp.sum(final * final, axis=-1, keepdims=True)
    prompt_sq = jnp.sum(prompt * prompt, axis=-1, keepdims=True)
    final_len = jnp.sqrt(final_sq)
    prompt_len = jnp.sqrt(prompt_sq)
    cosine = dot / (final_len * prompt_len)
    reward_ref[...] = jnp.broadcast_to(100.0 * cosine, reward_ref.shape)
    cot = cot_ref[:, :1]
    final_grad = (100.0 * cot) * (prompt / (final_len * prompt_len) - final * (cosine / final_sq))
    unit_grad = final_grad * post
    pooled_grad = pooled_rstd * (
        unit_grad
        - lane_mean(unit_grad, VW)
        - pooled_unit * lane_mean(unit_grad * pooled_unit, VW)
    )
    flow = pooled_grad * pre * (1.0 / patches)
    embed_grad = rstd * (flow - lane_mean(flow, VW) - unit * lane_mean(flow * unit, VW))
    high = embed_grad.astype(BF16)
    low = (embed_grad - high.astype(F32)).astype(BF16)
    stacked = jnp.concatenate([high, low], axis=0)
    for number, ref, slot in shares:
        both = mm_nt(stacked, ref[slot])
        back_scr[number] = both[:patches] + both[patches:]
    back = jnp.concatenate([back_scr[i] for i in range(16 * CH // share_rows)], axis=1)
    for hi in range(2):
        for tx in range(4):
            first = (4 * (2 * hi) + tx) * CH
            second = (4 * (2 * hi + 1) + tx) * CH
            piece = jnp.concatenate(
                [back[:, first : first + CH], back[:, second : second + CH]], axis=1
            )
            for pr in range(patch_rows):
                grad_scr[pl.ds((2 * pr + hi) * GW + tx, patch_cols, stride=4), :] = piece[
                    pr * patch_cols : (pr + 1) * patch_cols
                ]
    grad = grad_scr[...].astype(BF16)
    grad_ref[...] = grad
    if fused:
        store_readout_grad(grad, mod_ref, out_factor, weight_ref)
    else:
        weight_ref[...] = jnp.zeros_like(weight_ref)


def store_readout_grad(grad, mod_ref, out_factor, out_ref):
    turned = grad.astype(F32).T.astype(BF16)
    count, rows, width = mod_ref.shape
    half = rows // 2
    first = mod_ref[:, :half, :].reshape(count * half, width)
    second = mod_ref[:, half:, :].reshape(count * half, width)
    total = mm(turned[:CH], first) + mm(turned[CH:], second)
    out_ref[...] = (total * out_factor).astype(BF16)


def reward_head(
    place, order, latent, embed, pos, pre, post, prompt, cot, modulated, grid_rows, fused, out_factor
):
    patches = grid_rows * GW // 16
    rows = grid_rows * GW // 2
    width = modulated.shape[2]
    embed_arrays, embed_masks = [x for x, _ in embed], [masks for _, masks in embed]
    share_rows = embed_arrays[0].shape[1]
    return pl.pallas_call(
        functools.partial(head_kernel, grid_rows, fused, order, embed_masks, out_factor),
        out_shape=(
            jax.ShapeDtypeStruct((1, 128), F32),
            jax.ShapeDtypeStruct((rows, 2 * CH), BF16),
            jax.ShapeDtypeStruct((CH, width), BF16),
        ),
        in_specs=[SMEM_SPEC, VMEM_SPEC]
        + [VMEM_SPEC] * len(embed_arrays)
        + [VMEM_SPEC] * 6,
        out_specs=(VMEM_SPEC, VMEM_SPEC, VMEM_SPEC),
        scratch_shapes=[
            pltpu.VMEM((rows, 2 * CH), F32),
            pltpu.VMEM((rows, 2 * CH), F32),
            pltpu.VMEM((16 * CH // share_rows, patches, share_rows), BF16),
            pltpu.VMEM((16 * CH // share_rows, patches, share_rows), F32),
        ],
        compiler_params=limits(16),
        cost_estimate=pl.CostEstimate(
            flops=6 * patches * 16 * CH * VW,
            bytes_accessed=2 * 16 * CH * VW + 2 * patches * VW,
            transcendentals=0,
        ),
    )(place, latent, *embed_arrays, pos, pre, post, prompt, cot, modulated)


def spread_kernel(count, half, heads, grad_ref, scale_ref, proj_ref, out_ref, token_ref):
    token_ref[...] = jnp.zeros_like(token_ref)
    gain = 1.0 + scale_ref[...]
    proj = proj_ref[...]
    zero = jnp.zeros_like(proj)
    sides = (jnp.concatenate([proj, zero], axis=0), jnp.concatenate([zero, proj], axis=0))
    for src in range(count):
        grad = grad_ref[pl.ds(src * half, half), :]
        for side in range(2):
            rows = (mm(grad, sides[side]) * gain).astype(BF16)
            for head in range(heads):
                out_ref[0, head, pl.ds((2 * src + side) * half, half), :] = rows[
                    :, head * HD : (head + 1) * HD
                ]


def spread(grad, scales, proj, count, half, heads):
    return pl.pallas_call(
        functools.partial(spread_kernel, count, half, heads),
        out_shape=(
            jax.ShapeDtypeStruct((1, heads, 2 * count * half, HD), BF16),
            jax.ShapeDtypeStruct((8, 128), F32),
        ),
        in_specs=[VMEM_SPEC] * 3,
        out_specs=(VMEM_SPEC, VMEM_SPEC),
        compiler_params=limits(),
        cost_estimate=pl.CostEstimate(
            flops=8 * count * half * CH * heads * HD,
            bytes_accessed=4 * count * half * heads * HD,
            transcendentals=0,
        ),
    )(grad, scales, proj)


def weight_kernel(out_factor, grad_ref, *refs):
    store_readout_grad(grad_ref[...], refs[0], out_factor, refs[1])


def weight_call(grad, modulated, out_factor):
    return pl.pallas_call(
        functools.partial(weight_kernel, out_factor),
        out_shape=jax.ShapeDtypeStruct((CH, modulated.shape[2]), BF16),
        in_specs=[VMEM_SPEC] * 2,
        out_specs=VMEM_SPEC,
        compiler_params=limits(),
    )(grad, modulated)


def finish_kernel(order, in_ref, out_ref):
    width = in_ref.shape[2]
    for spot, group in enumerate(order):
        out_ref[:, pl.ds(group * width, width)] = in_ref[spot].astype(F32)


def finish(blocks, order):
    return pl.pallas_call(
        functools.partial(finish_kernel, order),
        out_shape=jax.ShapeDtypeStruct((CH, HEADS * HD), F32),
        in_specs=[VMEM_SPEC],
        out_specs=VMEM_SPEC,
        compiler_params=limits(),
    )(blocks)


def swap(x, axis, mask):
    count = lax.axis_size(axis)
    return lax.ppermute(x, axis, [(i, i ^ mask) for i in range(count)])


def all_to_all(x, groups=None):
    return lax.all_to_all(
        x, "seq", split_axis=0, concat_axis=0, tiled=True, axis_index_groups=groups
    )


def swap_both(x, seq_mask, data_mask):
    seq_count, data_count = lax.axis_size("seq"), lax.axis_size("dp")
    pairs = [
        (i * data_count + j, (i ^ seq_mask) * data_count + (j ^ data_mask))
        for i in range(seq_count)
        for j in range(data_count)
    ]
    return lax.ppermute(x, ("seq", "dp"), pairs)


def on_device(
    queries,
    keys,
    values,
    shifts,
    scales,
    proj_out,
    patch_embed,
    pos_embed,
    pre_gain,
    post_gain,
    prompt,
    cotangent,
):
    seq_count = lax.axis_size("seq")
    data_count = lax.axis_size("dp")
    tok_rows = queries.shape[1]
    sizes = Sizes(seq_count, data_count, tok_rows, patch_embed)
    query_parts, head_count, part_rows = sizes.query_parts, sizes.heads, sizes.part_rows
    group_count = HEADS // head_count
    seq_index = lax.axis_index("seq")
    head_group = seq_index // query_parts
    query_part = seq_index % query_parts
    half = part_rows // 2
    lat_rows = seq_count * tok_rows
    grid_rows = lat_rows // GW
    canonical = part_rows == 2 * GW
    place = jnp.stack([seq_index, lax.axis_index("dp"), head_group]).astype(jnp.int32)
    proj_turned = proj_out.T
    out_factor = 1.0 / math.sqrt(data_count * lat_rows)

    masks = sizes.pieces()
    packed = pack(
        sizes, in_hbm(queries), in_hbm(keys), in_hbm(values), in_hbm(patch_embed)
    )
    received = [swap(x, "seq", mask) if mask else x for mask, x in zip(masks, packed)]
    bits = [1 << b for b in reversed(range(data_count.bit_length() - 1))]
    shared = sizes.share < patch_embed.shape[0]
    scale, shift, proj, pos, pre, post, words, cot = fetch(
        sizes, place, cotangent, [scales, shifts, proj_turned, pos_embed, pre_gain, post_gain, prompt]
    )

    kept, order = [], list(range(seq_count))
    if seq_count == 8:
        late = [slot for slot, mask in enumerate(masks) if mask in (6, 7)]
        order = [slot for slot in order if slot not in late]
        kept = attend_early(sizes, [received[slot] for slot in order], scale)
        order = order + late
    if sizes.riding:
        ride = [slot for slot, mask in enumerate(masks) if sizes.rides(mask)]
        two = collect(sizes, [received[slot] for slot in ride])
        held = join(two, swap(two, "seq", 2), kept)
        ride_masks = [masks[slot] for slot in ride]
        ride_masks = ride_masks + [mask ^ 2 for mask in ride_masks]
        pairs = [
            (held, swap(held, "seq", 1)),
            (swap(held, "dp", bits[0]), swap_both(held, 1, bits[0])),
        ]

    modulated, latent_part = attend(
        sizes, [masks[slot] for slot in order], place, [received[slot] for slot in order], kept,
        scale, shift, proj,
    )

    if not sizes.riding:
        mine = patch_embed
        if shared:
            mine = lax.dynamic_slice_in_dim(
                patch_embed, lax.axis_index("dp") * sizes.share, sizes.share, 0
            )
        mine = lax.all_gather(mine, "seq", axis=1, tiled=True).reshape(-1, VW)
        embed = [(mine[None], [0])]
        if shared:
            embed = embed + [(swap(mine[None], "dp", bits[0]), [bits[0]])]

    groups, order = [sizes.order()], sizes.order()
    if query_parts > 1:
        order = list(range(group_count))
        groups = [[g * query_parts + r for g in range(group_count)] for r in range(query_parts)]
    per_share = seq_count // group_count
    parts = all_to_all(latent_part.reshape(group_count, per_share * half, 2 * CH), groups)
    summed = total_copies([parts], seq_count)
    if sizes.riding:
        embed = [(arrange(sizes, ride_masks, place, pairs, summed), [0, bits[0]])]
    for bit in bits[1:] if shared else []:
        embed = embed + [(swap(x, "dp", bit), [m ^ bit for m in some]) for x, some in embed]
    latent = all_to_all(summed, [sizes.order()])
    if canonical:
        latent = latent.reshape(lat_rows // 2, 2 * CH)
    else:
        latent = latent.reshape(group_count, query_parts, per_share, half, 2, CH)
        latent = latent.transpose(0, 2, 1, 4, 3, 5).reshape(grid_rows // 2, 2, GW, CH)
        latent = latent.transpose(0, 2, 1, 3).reshape(lat_rows // 2, 2 * CH)

    reward, grad, weight = reward_head(
        place, sizes.order() if canonical else list(range(grid_rows // 2)),
        latent, embed, pos, pre, post, words,
        cot, modulated, grid_rows, canonical, out_factor,
    )
    if not canonical:
        tokens = grad.reshape(grid_rows // 2, GW, 2, CH).transpose(0, 2, 1, 3)
        tokens = tokens.reshape(seq_count, query_parts, 2, half, CH)
        tokens = lax.dynamic_index_in_dim(tokens, query_part, 1, keepdims=False)
        grad = tokens.transpose(0, 2, 1, 3).reshape(seq_count * half, 2 * CH)
        weight = weight_call(grad, modulated, out_factor)

    parts = [weight] + [swap(weight, "dp", mask) for mask in range(1, data_count)]
    attn_grad, token = spread(grad, scale, proj, seq_count, half, head_count)
    if query_parts > 1:
        total = total_copies(parts, 1)[0]
        parts = [total] + [swap(total, "seq", mask) for mask in range(1, query_parts)]
    blocks = all_to_all(total_copies(parts, group_count, [token]), groups)
    return (reward[0, :1], attn_grad, finish(blocks, order).T)


def solution(mesh):
    return jax.shard_map(
        on_device,
        mesh=mesh,
        in_specs=(
            P("dp", "seq", None),
            P("dp", "seq", None),
            P("dp", "seq", None),
            P("dp", None),
            P("dp", None),
            P(),
            P(None, "seq", None),
            P(),
            P(),
            P(),
            P("dp", None),
            P("dp"),
        ),
        out_specs=(P("dp"), P("dp", "seq", None, None), P()),
        check_vma=False,
    )
```

```python
import functools
import math

import jax
import jax.numpy as jnp
from jax import lax
from jax.experimental import pallas as pl
from jax.experimental.pallas import tpu as pltpu
from jax.sharding import PartitionSpec as P

HEADS = 16
HD = 128
CH = 64
GW = 64
VW = 1280
EPS = 1e-05
BF16 = jnp.bfloat16
F32 = jnp.float32


def mm(a, b):
    return jnp.dot(a, b, preferred_element_type=F32)


def mm_nt(a, b):
    return lax.dot_general(a, b, (((1,), (1,)), ((), ())), preferred_element_type=F32)


def mm_tn(a, b):
    return lax.dot_general(a, b, (((0,), (0,)), ((), ())), preferred_element_type=F32)


SMEM_SPEC = pl.BlockSpec(memory_space=pltpu.SMEM)
VMEM_SPEC = pl.BlockSpec(memory_space=pltpu.VMEM)
HBM_SPEC = pl.BlockSpec(memory_space=pltpu.HBM)
ANY_SPEC = pl.BlockSpec(memory_space=pl.ANY)


def in_hbm(x):
    return pltpu.with_memory_space_constraint(x, pltpu.HBM)


def limits(mib=4):
    return pltpu.CompilerParams(vmem_limit_bytes=mib * 1024 * 1024)


class Sizes:
    def __init__(self, seq_count, data_count, tok_rows, patch_embed):
        self.count = seq_count
        self.query_parts = max(1, seq_count // HEADS)
        self.heads = max(1, HEADS // seq_count)
        self.width = self.heads * HD
        self.tok_rows = tok_rows
        self.part_rows = tok_rows // self.query_parts
        positions, self.local, _ = patch_embed.shape
        self.share = positions // data_count if positions % data_count == 0 else positions
        self.rows = self.part_rows + 2 * tok_rows
        self.share_rows = self.share * self.local
        self.chunks = VW // HD
        self.riding = self.local % 8 == 0 and self.share_rows % 16 == 0 and seq_count == 8
        self.riding = self.riding and 1 < data_count <= positions
        self.ride_rows = self.chunks * self.share_rows if self.riding else 0

    def order(self):
        return [4, 5, 2, 3, 6, 7, 0, 1] if self.count == 8 else list(range(self.count))

    def pieces(self):
        return list(range(1, self.count)) + [0]

    def rides(self, mask):
        return self.riding and mask in (0, 4)

    def piece_shape(self, mask):
        return (self.rows + (self.ride_rows // self.heads if self.rides(mask) else 0), self.width)

    def ride_slices(self):
        deep = self.ride_rows // self.heads
        return [
            (pl.ds(self.rows, deep), pl.ds(at * HD, HD), pl.ds(at * deep, deep))
            for at in range(self.heads)
        ]


def pack_kernel(sizes, q_ref, k_ref, v_ref, embed_ref, *refs):
    masks = sizes.pieces()
    out_refs = refs[: len(masks)]
    embed_scr, share_scr, embed_sem, sems = refs[len(masks) :]
    me = lax.axis_index("seq")
    tok_rows, part_rows, width = sizes.tok_rows, sizes.part_rows, sizes.width
    share = pl.ds(lax.axis_index("dp") * sizes.share, sizes.share)
    load = pltpu.make_async_copy(embed_ref.at[share], embed_scr, embed_sem.at[0])
    load.start()
    copies = []
    for slot, (mask, out) in enumerate(zip(masks, out_refs)):
        dest = jnp.bitwise_xor(me, mask)
        group, part = dest // sizes.query_parts, dest % sizes.query_parts
        cols = pl.ds(pl.multiple_of(group * width, HD), width)
        first = pl.ds(pl.multiple_of(part * part_rows, part_rows), part_rows)
        for kind, source, rows in (
            (0, q_ref.at[0, first, cols], pl.ds(0, part_rows)),
            (1, k_ref.at[0, :, cols], pl.ds(part_rows, tok_rows)),
            (2, v_ref.at[0, :, cols], pl.ds(part_rows + tok_rows, tok_rows)),
        ):
            copies.append(pltpu.make_async_copy(source, out.at[rows], sems.at[kind, slot]))
    for copy in copies:
        copy.start()
    load.wait()
    if sizes.riding:
        for chunk in range(sizes.chunks):
            cols = embed_scr[:, :, pl.ds(chunk * HD, HD)].astype(F32)
            share_scr[pl.ds(chunk * sizes.share_rows, sizes.share_rows), :] = cols.reshape(
                sizes.share_rows, HD
            ).astype(BF16)
        for mask, out in zip(masks, out_refs):
            if sizes.rides(mask):
                for rows, place, from_rows in sizes.ride_slices():
                    out[rows, place] = share_scr[from_rows, :]
    for copy in copies:
        copy.wait()


def pack(sizes, queries, keys, values, patch_embed):
    tok_rows, full = queries.shape[1:]
    masks = sizes.pieces()
    return pl.pallas_call(
        functools.partial(pack_kernel, sizes),
        out_shape=[jax.ShapeDtypeStruct(sizes.piece_shape(mask), BF16) for mask in masks],
        in_specs=[HBM_SPEC] * 4,
        out_specs=[VMEM_SPEC] * len(masks),
        scratch_shapes=[
            pltpu.VMEM((sizes.share,) + patch_embed.shape[1:], BF16),
            pltpu.VMEM((max(16, sizes.ride_rows), HD), BF16),
            pltpu.SemaphoreType.DMA((1,)),
            pltpu.SemaphoreType.DMA((3, len(masks))),
        ],
        compiler_params=limits(8),
        cost_estimate=pl.CostEstimate(
            flops=0, bytes_accessed=12 * tok_rows * full, transcendentals=0
        ),
    )(queries, keys, values, patch_embed)


def collect_kernel(sizes, *refs):
    *in_refs, out_ref, sems = refs
    copies = []
    for slot, ref in enumerate(in_refs):
        for at, (rows, cols, to_rows) in enumerate(sizes.ride_slices()):
            copies.append(
                pltpu.make_async_copy(
                    ref.at[rows, cols], out_ref.at[slot, to_rows], sems.at[at, slot]
                )
            )
    for copy in copies:
        copy.start()
    for copy in copies:
        copy.wait()


def collect(sizes, arrays):
    return pl.pallas_call(
        functools.partial(collect_kernel, sizes),
        out_shape=jax.ShapeDtypeStruct((len(arrays), sizes.ride_rows, HD), BF16),
        in_specs=[ANY_SPEC] * len(arrays),
        out_specs=VMEM_SPEC,
        scratch_shapes=[pltpu.SemaphoreType.DMA((sizes.heads, len(arrays)))],
        compiler_params=limits(),
    )(*arrays)


def join_kernel(first_ref, second_ref, *refs):
    out_ref = refs[-1]
    count = first_ref.shape[0]
    out_ref[:count] = first_ref[...]
    out_ref[count:] = second_ref[...]


def join(first, second, others):
    return pl.pallas_call(
        join_kernel,
        out_shape=jax.ShapeDtypeStruct((2 * first.shape[0],) + first.shape[1:], BF16),
        in_specs=[VMEM_SPEC] * 2 + [ANY_SPEC] * len(others),
        out_specs=VMEM_SPEC,
        compiler_params=limits(),
    )(first, second, *others)


def arrange_kernel(sizes, masks, place_ref, *refs):
    *pair_refs, out_ref = refs[:-2] + refs[-1:]
    me = place_ref[0]
    odd = me % 2 == 1
    local = sizes.local
    for quarter in range(len(pair_refs) // 2):
        held_ref, got_ref = pair_refs[2 * quarter], pair_refs[2 * quarter + 1]
        for slot, mask in enumerate(masks):
            pair = jnp.bitwise_xor(me, mask) // 2
            for chunk in range(sizes.chunks):
                rows = pl.ds(chunk * sizes.share_rows, sizes.share_rows)
                held = held_ref[slot, rows, :].astype(F32)
                got = got_ref[slot, rows, :].astype(F32)
                first = jnp.where(odd, got, held)
                second = jnp.where(odd, held, got)
                for at in range(sizes.share):
                    part = slice(at * local, (at + 1) * local)
                    both = jnp.concatenate([first[part], second[part]], axis=0).astype(BF16)
                    start = pl.multiple_of(at * sizes.count * local + pair * 2 * local, 2 * local)
                    out_ref[quarter, pl.ds(start, 2 * local), pl.ds(chunk * HD, HD)] = both


def arrange(sizes, masks, place, pairs, wait):
    rows = sizes.share * sizes.count * sizes.local
    flat = [x for pair in pairs for x in pair]
    return pl.pallas_call(
        functools.partial(arrange_kernel, sizes, masks),
        out_shape=jax.ShapeDtypeStruct((len(pairs), rows, VW), BF16),
        in_specs=[SMEM_SPEC] + [VMEM_SPEC] * (len(flat) + 1),
        out_specs=VMEM_SPEC,
        compiler_params=limits(),
    )(place, *flat, wait)


def fetch_kernel(sizes, place_ref, cot_ref, *refs):
    *refs, row_ref, sems = refs
    count = len(refs) // 2
    row_ref[...] = jnp.full(row_ref.shape, cot_ref[0], F32)
    mine = pl.ds(pl.multiple_of(place_ref[2] * sizes.width, HD), sizes.width)
    copies = []
    for slot in range(count):
        source = refs[slot].at[:, mine] if slot < 3 else refs[slot]
        copies.append(pltpu.make_async_copy(source, refs[count + slot], sems.at[slot]))
        copies[-1].start()
    for copy in copies:
        copy.wait()


def fetch(sizes, place, cotangent, arrays):
    shapes = [x.shape if slot >= 3 else (x.shape[0], sizes.width) for slot, x in enumerate(arrays)]
    return pl.pallas_call(
        functools.partial(fetch_kernel, sizes),
        out_shape=[jax.ShapeDtypeStruct(shape, x.dtype) for shape, x in zip(shapes, arrays)]
        + [jax.ShapeDtypeStruct((1, 128), F32)],
        in_specs=[SMEM_SPEC] * 2 + [HBM_SPEC] * len(arrays),
        out_specs=[VMEM_SPEC] * (len(arrays) + 1),
        scratch_shapes=[pltpu.SemaphoreType.DMA((len(arrays),))],
        compiler_params=limits(),
        cost_estimate=pl.CostEstimate(flops=1, bytes_accessed=1, transcendentals=0),
    )(place, cotangent, *[in_hbm(x) for x in arrays])


FACTOR = HD ** (-0.5) * math.log2(math.e)


def load_pieces(sizes, in_refs, key_scr, value_scr):
    tok_rows, part_rows = sizes.tok_rows, sizes.part_rows
    for src, ref in enumerate(in_refs):
        rows = pl.ds(src * tok_rows, tok_rows)
        key_scr[rows, :] = ref[pl.ds(part_rows, tok_rows), :]
        for head in range(sizes.heads):
            value_scr[rows, pl.ds(2 * head * HD, HD)] = ref[
                pl.ds(part_rows + tok_rows, tok_rows), pl.ds(head * HD, HD)
            ]
    ones = jnp.ones((len(in_refs) * tok_rows, HD), BF16)
    for head in range(sizes.heads):
        value_scr[:, pl.ds((2 * head + 1) * HD, HD)] = ones


def soft_part(query, key_scr, value_scr, rows, head, before):
    logits = mm_nt(query, key_scr[rows, pl.ds(head * HD, HD)])
    top = jnp.max(logits, axis=-1, keepdims=True)
    if before:
        top = jnp.maximum(top, before[2])
    weights = jnp.exp2((logits - top) * FACTOR).astype(BF16)
    both = mm(weights, value_scr[rows, pl.ds(2 * head * HD, 2 * HD)])
    mixed, total = both[:, :HD], both[:, HD:]
    if before:
        shrink = jnp.exp2((before[2] - top) * FACTOR)
        mixed, total = mixed + before[0] * shrink, total + before[1] * shrink
    return mixed, total, top


def piece_scratch(sizes, count):
    lat_rows = count * sizes.tok_rows
    return [
        pltpu.VMEM((lat_rows, sizes.width), BF16),
        pltpu.VMEM((lat_rows, 2 * sizes.width), BF16),
    ]


def early_kernel(sizes, count, *refs):
    in_refs, refs = refs[:count], refs[count + 1 :]
    sum_ref, stat_ref, key_scr, value_scr = refs
    load_pieces(sizes, in_refs, key_scr, value_scr)
    left = lax.broadcasted_iota(jnp.int32, (sizes.part_rows, HD), 1) < HD // 2
    rows = pl.ds(0, count * sizes.tok_rows)
    for src in range(count):
        results = [
            soft_part(
                in_refs[src][pl.ds(0, sizes.part_rows), pl.ds(head * HD, HD)],
                key_scr, value_scr, rows, head, None,
            )
            for head in range(sizes.heads)
        ]
        for head, (mixed, total, top) in enumerate(results):
            sum_ref[src, head] = mixed
            stat_ref[src, head] = jnp.where(left, top, total)


def attend_early(sizes, received, wait):
    count = len(received)
    shape = jax.ShapeDtypeStruct((count, sizes.heads, sizes.part_rows, HD), F32)
    return pl.pallas_call(
        functools.partial(early_kernel, sizes, count),
        out_shape=(shape, shape),
        in_specs=[VMEM_SPEC] * (count + 1),
        out_specs=(VMEM_SPEC, VMEM_SPEC),
        scratch_shapes=piece_scratch(sizes, count),
        compiler_params=limits(12),
        cost_estimate=pl.CostEstimate(flops=1, bytes_accessed=1, transcendentals=0),
    )(*received, wait)


def attend_kernel(sizes, masks, early, place_ref, *refs):
    count, heads, width = sizes.count, sizes.heads, sizes.width
    tok_rows, part_rows = sizes.tok_rows, sizes.part_rows
    in_refs, refs = refs[:count], refs[count:]
    kept_refs, refs = refs[: 2 if early else 0], refs[2 if early else 0 :]
    scale_ref, shift_ref, proj_ref, mod_ref, lat_ref, *refs = refs
    key_scr, value_scr = refs
    half = part_rows // 2
    me = place_ref[0]
    gain = 1.0 + scale_ref[...]
    shift = shift_ref[...]
    load_pieces(sizes, in_refs, key_scr, value_scr)
    together = 2
    for first in range(0, count, together):
        results = []
        for src in range(first, first + together):
            mixed = []
            for head in range(heads):
                before = None
                rows = pl.ds(0, count * tok_rows)
                if src < early:
                    rows = pl.ds(early * tok_rows, (count - early) * tok_rows)
                    stat = kept_refs[1][src, head]
                    before = (kept_refs[0][src, head], stat[:, HD - 1 :], stat[:, :1])
                query = in_refs[src][pl.ds(0, part_rows), pl.ds(head * HD, HD)]
                value, total, _ = soft_part(query, key_scr, value_scr, rows, head, before)
                mixed.append(value / total)
            results.append(jnp.concatenate(mixed, axis=1) if heads > 1 else mixed[0])
        for at, attended in enumerate(results):
            modulated = (attended * gain + shift).astype(BF16)
            mod_ref[jnp.bitwise_xor(me, masks[first + at])] = modulated
    sides = [
        mm_nt(mod_ref[:, rows, :].reshape(count * half, width), proj_ref[...])
        for rows in (slice(0, half), slice(half, part_rows))
    ]
    latent = jnp.concatenate(sides, axis=1).astype(BF16)
    for spot, place in enumerate(sizes.order()):
        lat_ref[spot] = latent[place * half : (place + 1) * half]


def attend(sizes, masks, place, received, kept, scales, shifts, proj):
    count, width, heads = sizes.count, sizes.width, sizes.heads
    lat_rows = count * sizes.tok_rows
    query_rows = count * sizes.part_rows
    early = kept[0].shape[0] if kept else 0
    return pl.pallas_call(
        functools.partial(attend_kernel, sizes, masks, early),
        out_shape=(
            jax.ShapeDtypeStruct((count, sizes.part_rows, width), BF16),
            jax.ShapeDtypeStruct((count, sizes.part_rows // 2, 2 * CH), BF16),
        ),
        in_specs=[SMEM_SPEC] + [VMEM_SPEC] * (count + len(kept) + 3),
        out_specs=(VMEM_SPEC, VMEM_SPEC),
        scratch_shapes=piece_scratch(sizes, count),
        compiler_params=limits(16),
        cost_estimate=pl.CostEstimate(
            flops=4 * query_rows * lat_rows * width,
            bytes_accessed=2 * (query_rows * 2 + lat_rows * 2) * width,
            transcendentals=query_rows * lat_rows * heads,
        ),
    )(place, *received, *kept, scales, shifts, proj)


def total_kernel(copies, count, *refs):
    out_ref = refs[-1]
    if len(refs[0].shape) == 3:
        parts = [refs[0][i].astype(F32) for i in range(refs[0].shape[0])]
    else:
        parts = [ref[...].astype(F32) for ref in refs[:count]]
    while len(parts) > 1:
        parts = [parts[i] + parts[i + 1] for i in range(0, len(parts), 2)]
    for copy in range(copies):
        out_ref[copy] = parts[0].astype(BF16)


def total_copies(arrays, copies, others=()):
    return pl.pallas_call(
        functools.partial(total_kernel, copies, len(arrays)),
        out_shape=jax.ShapeDtypeStruct((copies,) + arrays[0].shape[-2:], BF16),
        in_specs=[VMEM_SPEC] * (len(arrays) + len(others)),
        out_specs=VMEM_SPEC,
        compiler_params=limits(),
    )(*arrays, *others)


def lane_mean(x, count):
    return jnp.sum(x, axis=-1, keepdims=True) * (1.0 / count)


def head_kernel(grid_rows, fused, order, embed_masks, out_factor, place_ref, lat_ref, *refs):
    embed_refs, refs = refs[: len(embed_masks)], refs[len(embed_masks) :]
    pos_ref, pre_ref, post_ref, prompt_ref, cot_ref, mod_ref, *refs = refs
    reward_ref, grad_ref, weight_ref, lat_scr, grad_scr, block_scr, back_scr = refs
    patch_rows = grid_rows // 4
    patch_cols = GW // 4
    patches = patch_rows * patch_cols
    for spot, place in enumerate(order):
        lat_scr[pl.ds(place * GW, GW), :] = lat_ref[pl.ds(spot * GW, GW), :].astype(F32)

    data = place_ref[1]
    shares = [
        (jnp.bitwise_xor(data, mask), ref, slot)
        for ref, masks in zip(embed_refs, embed_masks)
        for slot, mask in enumerate(masks)
    ]
    share_rows = embed_refs[0].shape[1]
    for hi in range(2):
        wide = []
        for tx in range(4):
            rows = [
                lat_scr[pl.ds((2 * pr + hi) * GW + tx, patch_cols, stride=4), :]
                for pr in range(patch_rows)
            ]
            wide.append(jnp.concatenate(rows, axis=0))
        for side in range(2):
            lanes = slice(side * CH, (side + 1) * CH)
            line = jnp.concatenate([x[:, lanes] for x in wide], axis=1).astype(BF16)
            first = (2 * hi + side) * 4 * CH
            if share_rows >= 4 * CH:
                at = first % share_rows
                block_scr[first // share_rows, :, pl.ds(at, 4 * CH)] = line
            else:
                for at in range(0, 4 * CH, share_rows):
                    block_scr[(first + at) // share_rows] = line[:, at : at + share_rows]
    embedded = pos_ref[...].astype(F32)
    for number, ref, slot in shares:
        embedded = embedded + mm(block_scr[number], ref[slot])
    pre = pre_ref[...].reshape(1, VW)
    post = post_ref[...].reshape(1, VW)
    prompt = prompt_ref[...]
    center = embedded - lane_mean(embedded, VW)
    rstd = lax.rsqrt(lane_mean(center * center, VW) + EPS)
    unit = center * rstd
    pooled = jnp.sum(unit, axis=0, keepdims=True) * (1.0 / patches) * pre
    pooled_center = pooled - lane_mean(pooled, VW)
    pooled_rstd = lax.rsqrt(lane_mean(pooled_center * pooled_center, VW) + EPS)
    pooled_unit = pooled_center * pooled_rstd
    final = pooled_unit * post
    dot = jnp.sum(final * prompt, axis=-1, keepdims=True)
    final_sq = jnp.sum(final * final, axis=-1, keepdims=True)
    prompt_sq = jnp.sum(prompt * prompt, axis=-1, keepdims=True)
    final_len = jnp.sqrt(final_sq)
    prompt_len = jnp.sqrt(prompt_sq)
    cosine = dot / (final_len * prompt_len)
    reward_ref[...] = jnp.broadcast_to(100.0 * cosine, reward_ref.shape)
    cot = cot_ref[:, :1]
    final_grad = (100.0 * cot) * (prompt / (final_len * prompt_len) - final * (cosine / final_sq))
    unit_grad = final_grad * post
    pooled_grad = pooled_rstd * (
        unit_grad
        - lane_mean(unit_grad, VW)
        - pooled_unit * lane_mean(unit_grad * pooled_unit, VW)
    )
    flow = pooled_grad * pre * (1.0 / patches)
    embed_grad = rstd * (flow - lane_mean(flow, VW) - unit * lane_mean(flow * unit, VW))
    high = embed_grad.astype(BF16)
    low = (embed_grad - high.astype(F32)).astype(BF16)
    stacked = jnp.concatenate([high, low], axis=0)
    for number, ref, slot in shares:
        both = mm_nt(stacked, ref[slot])
        back_scr[number] = both[:patches] + both[patches:]
    back = jnp.concatenate([back_scr[i] for i in range(16 * CH // share_rows)], axis=1)
    for hi in range(2):
        for tx in range(4):
            first = (4 * (2 * hi) + tx) * CH
            second = (4 * (2 * hi + 1) + tx) * CH
            piece = jnp.concatenate(
                [back[:, first : first + CH], back[:, second : second + CH]], axis=1
            )
            for pr in range(patch_rows):
                grad_scr[pl.ds((2 * pr + hi) * GW + tx, patch_cols, stride=4), :] = piece[
                    pr * patch_cols : (pr + 1) * patch_cols
                ]
    grad = grad_scr[...].astype(BF16)
    grad_ref[...] = grad
    if fused:
        store_readout_grad(grad, mod_ref, out_factor, weight_ref)
    else:
        weight_ref[...] = jnp.zeros_like(weight_ref)


def store_readout_grad(grad, mod_ref, out_factor, out_ref):
    turned = grad.astype(F32).T.astype(BF16)
    count, rows, width = mod_ref.shape
    half = rows // 2
    first = mod_ref[:, :half, :].reshape(count * half, width)
    second = mod_ref[:, half:, :].reshape(count * half, width)
    total = mm(turned[:CH], first) + mm(turned[CH:], second)
    out_ref[...] = (total * out_factor).astype(BF16)


def reward_head(
    place, order, latent, embed, pos, pre, post, prompt, cot, modulated, grid_rows, fused, out_factor
):
    patches = grid_rows * GW // 16
    rows = grid_rows * GW // 2
    width = modulated.shape[2]
    embed_arrays, embed_masks = [x for x, _ in embed], [masks for _, masks in embed]
    share_rows = embed_arrays[0].shape[1]
    return pl.pallas_call(
        functools.partial(head_kernel, grid_rows, fused, order, embed_masks, out_factor),
        out_shape=(
            jax.ShapeDtypeStruct((1, 128), F32),
            jax.ShapeDtypeStruct((rows, 2 * CH), BF16),
            jax.ShapeDtypeStruct((CH, width), BF16),
        ),
        in_specs=[SMEM_SPEC, VMEM_SPEC]
        + [VMEM_SPEC] * len(embed_arrays)
        + [VMEM_SPEC] * 6,
        out_specs=(VMEM_SPEC, VMEM_SPEC, VMEM_SPEC),
        scratch_shapes=[
            pltpu.VMEM((rows, 2 * CH), F32),
            pltpu.VMEM((rows, 2 * CH), F32),
            pltpu.VMEM((16 * CH // share_rows, patches, share_rows), BF16),
            pltpu.VMEM((16 * CH // share_rows, patches, share_rows), F32),
        ],
        compiler_params=limits(16),
        cost_estimate=pl.CostEstimate(
            flops=6 * patches * 16 * CH * VW,
            bytes_accessed=2 * 16 * CH * VW + 2 * patches * VW,
            transcendentals=0,
        ),
    )(place, latent, *embed_arrays, pos, pre, post, prompt, cot, modulated)


def spread_kernel(count, half, heads, grad_ref, scale_ref, proj_ref, out_ref, token_ref):
    token_ref[...] = jnp.zeros_like(token_ref)
    gain = 1.0 + scale_ref[...]
    proj = proj_ref[...]
    zero = jnp.zeros_like(proj)
    sides = (jnp.concatenate([proj, zero], axis=0), jnp.concatenate([zero, proj], axis=0))
    for src in range(count):
        grad = grad_ref[pl.ds(src * half, half), :]
        for side in range(2):
            rows = (mm(grad, sides[side]) * gain).astype(BF16)
            for head in range(heads):
                out_ref[0, head, pl.ds((2 * src + side) * half, half), :] = rows[
                    :, head * HD : (head + 1) * HD
                ]


def spread(grad, scales, proj, count, half, heads):
    return pl.pallas_call(
        functools.partial(spread_kernel, count, half, heads),
        out_shape=(
            jax.ShapeDtypeStruct((1, heads, 2 * count * half, HD), BF16),
            jax.ShapeDtypeStruct((8, 128), F32),
        ),
        in_specs=[VMEM_SPEC] * 3,
        out_specs=(VMEM_SPEC, VMEM_SPEC),
        compiler_params=limits(),
        cost_estimate=pl.CostEstimate(
            flops=8 * count * half * CH * heads * HD,
            bytes_accessed=4 * count * half * heads * HD,
            transcendentals=0,
        ),
    )(grad, scales, proj)


def weight_kernel(out_factor, grad_ref, *refs):
    store_readout_grad(grad_ref[...], refs[0], out_factor, refs[1])


def weight_call(grad, modulated, out_factor):
    return pl.pallas_call(
        functools.partial(weight_kernel, out_factor),
        out_shape=jax.ShapeDtypeStruct((CH, modulated.shape[2]), BF16),
        in_specs=[VMEM_SPEC] * 2,
        out_specs=VMEM_SPEC,
        compiler_params=limits(),
    )(grad, modulated)


def finish_kernel(order, in_ref, out_ref):
    width = in_ref.shape[2]
    for spot, group in enumerate(order):
        out_ref[:, pl.ds(group * width, width)] = in_ref[spot].astype(F32)


def finish(blocks, order):
    return pl.pallas_call(
        functools.partial(finish_kernel, order),
        out_shape=jax.ShapeDtypeStruct((CH, HEADS * HD), F32),
        in_specs=[VMEM_SPEC],
        out_specs=VMEM_SPEC,
        compiler_params=limits(),
    )(blocks)


def swap(x, axis, mask):
    count = lax.axis_size(axis)
    return lax.ppermute(x, axis, [(i, i ^ mask) for i in range(count)])


def all_to_all(x, groups=None):
    return lax.all_to_all(
        x, "seq", split_axis=0, concat_axis=0, tiled=True, axis_index_groups=groups
    )


def swap_both(x, seq_mask, data_mask):
    seq_count, data_count = lax.axis_size("seq"), lax.axis_size("dp")
    pairs = [
        (i * data_count + j, (i ^ seq_mask) * data_count + (j ^ data_mask))
        for i in range(seq_count)
        for j in range(data_count)
    ]
    return lax.ppermute(x, ("seq", "dp"), pairs)


def on_device(
    queries,
    keys,
    values,
    shifts,
    scales,
    proj_out,
    patch_embed,
    pos_embed,
    pre_gain,
    post_gain,
    prompt,
    cotangent,
):
    seq_count = lax.axis_size("seq")
    data_count = lax.axis_size("dp")
    tok_rows = queries.shape[1]
    sizes = Sizes(seq_count, data_count, tok_rows, patch_embed)
    query_parts, head_count, part_rows = sizes.query_parts, sizes.heads, sizes.part_rows
    group_count = HEADS // head_count
    seq_index = lax.axis_index("seq")
    head_group = seq_index // query_parts
    query_part = seq_index % query_parts
    half = part_rows // 2
    lat_rows = seq_count * tok_rows
    grid_rows = lat_rows // GW
    canonical = part_rows == 2 * GW
    place = jnp.stack([seq_index, lax.axis_index("dp"), head_group]).astype(jnp.int32)
    proj_turned = proj_out.T
    out_factor = 1.0 / math.sqrt(data_count * lat_rows)

    masks = sizes.pieces()
    packed = pack(
        sizes, in_hbm(queries), in_hbm(keys), in_hbm(values), in_hbm(patch_embed)
    )
    received = [swap(x, "seq", mask) if mask else x for mask, x in zip(masks, packed)]
    bits = [1 << b for b in reversed(range(data_count.bit_length() - 1))]
    shared = sizes.share < patch_embed.shape[0]
    scale, shift, proj, pos, pre, post, words, cot = fetch(
        sizes, place, cotangent, [scales, shifts, proj_turned, pos_embed, pre_gain, post_gain, prompt]
    )

    kept, order = [], list(range(seq_count))
    if seq_count == 8:
        late = [slot for slot, mask in enumerate(masks) if mask in (5, 6, 7)]
        order = [slot for slot in order if slot not in late]
        kept = attend_early(sizes, [received[slot] for slot in order], scale)
        order = order + late
    if sizes.riding:
        ride = [slot for slot, mask in enumerate(masks) if sizes.rides(mask)]
        two = collect(sizes, [received[slot] for slot in ride])
        held = join(two, swap(two, "seq", 2), kept)
        ride_masks = [masks[slot] for slot in ride]
        ride_masks = ride_masks + [mask ^ 2 for mask in ride_masks]
        pairs = [
            (held, swap(held, "seq", 1)),
            (swap(held, "dp", bits[0]), swap_both(held, 1, bits[0])),
        ]

    modulated, latent_part = attend(
        sizes, [masks[slot] for slot in order], place, [received[slot] for slot in order], kept,
        scale, shift, proj,
    )

    if not sizes.riding:
        mine = patch_embed
        if shared:
            mine = lax.dynamic_slice_in_dim(
                patch_embed, lax.axis_index("dp") * sizes.share, sizes.share, 0
            )
        mine = lax.all_gather(mine, "seq", axis=1, tiled=True).reshape(-1, VW)
        embed = [(mine[None], [0])]
        if shared:
            embed = embed + [(swap(mine[None], "dp", bits[0]), [bits[0]])]

    groups, order = [sizes.order()], sizes.order()
    if query_parts > 1:
        order = list(range(group_count))
        groups = [[g * query_parts + r for g in range(group_count)] for r in range(query_parts)]
    per_share = seq_count // group_count
    parts = all_to_all(latent_part.reshape(group_count, per_share * half, 2 * CH), groups)
    summed = total_copies([parts], seq_count)
    if sizes.riding:
        embed = [(arrange(sizes, ride_masks, place, pairs, summed), [0, bits[0]])]
    for bit in bits[1:] if shared else []:
        embed = embed + [(swap(x, "dp", bit), [m ^ bit for m in some]) for x, some in embed]
    latent = all_to_all(summed, [sizes.order()])
    if canonical:
        latent = latent.reshape(lat_rows // 2, 2 * CH)
    else:
        latent = latent.reshape(group_count, query_parts, per_share, half, 2, CH)
        latent = latent.transpose(0, 2, 1, 4, 3, 5).reshape(grid_rows // 2, 2, GW, CH)
        latent = latent.transpose(0, 2, 1, 3).reshape(lat_rows // 2, 2 * CH)

    reward, grad, weight = reward_head(
        place, sizes.order() if canonical else list(range(grid_rows // 2)),
        latent, embed, pos, pre, post, words,
        cot, modulated, grid_rows, canonical, out_factor,
    )
    if not canonical:
        tokens = grad.reshape(grid_rows // 2, GW, 2, CH).transpose(0, 2, 1, 3)
        tokens = tokens.reshape(seq_count, query_parts, 2, half, CH)
        tokens = lax.dynamic_index_in_dim(tokens, query_part, 1, keepdims=False)
        grad = tokens.transpose(0, 2, 1, 3).reshape(seq_count * half, 2 * CH)
        weight = weight_call(grad, modulated, out_factor)

    parts = [weight] + [swap(weight, "dp", mask) for mask in range(1, data_count)]
    attn_grad, token = spread(grad, scale, proj, seq_count, half, head_count)
    if query_parts > 1:
        total = total_copies(parts, 1)[0]
        parts = [total] + [swap(total, "seq", mask) for mask in range(1, query_parts)]
    blocks = all_to_all(total_copies(parts, group_count, [token]), groups)
    return (reward[0, :1], attn_grad, finish(blocks, order).T)


def solution(mesh):
    return jax.shard_map(
        on_device,
        mesh=mesh,
        in_specs=(
            P("dp", "seq", None),
            P("dp", "seq", None),
            P("dp", "seq", None),
            P("dp", None),
            P("dp", None),
            P(),
            P(None, "seq", None),
            P(),
            P(),
            P(),
            P("dp", None),
            P("dp"),
        ),
        out_specs=(P("dp"), P("dp", "seq", None, None), P()),
        check_vma=False,
    )
```

```python
import functools
import math

import jax
import jax.numpy as jnp
from jax import lax
from jax.experimental import pallas as pl
from jax.experimental.pallas import tpu as pltpu
from jax.sharding import PartitionSpec as P

HEADS = 16
HD = 128
CH = 64
GW = 64
VW = 1280
EPS = 1e-05
BF16 = jnp.bfloat16
F32 = jnp.float32


def mm(a, b):
    return jnp.dot(a, b, preferred_element_type=F32)


def mm_nt(a, b):
    return lax.dot_general(a, b, (((1,), (1,)), ((), ())), preferred_element_type=F32)


def mm_tn(a, b):
    return lax.dot_general(a, b, (((0,), (0,)), ((), ())), preferred_element_type=F32)


SMEM_SPEC = pl.BlockSpec(memory_space=pltpu.SMEM)
VMEM_SPEC = pl.BlockSpec(memory_space=pltpu.VMEM)
HBM_SPEC = pl.BlockSpec(memory_space=pltpu.HBM)
ANY_SPEC = pl.BlockSpec(memory_space=pl.ANY)


def in_hbm(x):
    return pltpu.with_memory_space_constraint(x, pltpu.HBM)


def limits(mib=4):
    return pltpu.CompilerParams(vmem_limit_bytes=mib * 1024 * 1024)


class Sizes:
    def __init__(self, seq_count, data_count, tok_rows, patch_embed):
        self.count = seq_count
        self.query_parts = max(1, seq_count // HEADS)
        self.heads = max(1, HEADS // seq_count)
        self.width = self.heads * HD
        self.tok_rows = tok_rows
        self.part_rows = tok_rows // self.query_parts
        positions, self.local, _ = patch_embed.shape
        self.share = positions // data_count if positions % data_count == 0 else positions
        self.rows = self.part_rows + 2 * tok_rows
        self.share_rows = self.share * self.local
        self.chunks = VW // HD
        self.riding = self.local % 8 == 0 and self.share_rows % 16 == 0 and seq_count == 8
        self.riding = self.riding and 1 < data_count <= positions
        self.ride_rows = self.chunks * self.share_rows if self.riding else 0

    def order(self):
        return [4, 5, 2, 3, 6, 7, 0, 1] if self.count == 8 else list(range(self.count))

    def pieces(self):
        return list(range(1, self.count)) + [0]

    def rides(self, mask):
        return self.riding and mask in (0, 4)

    def piece_shape(self, mask):
        return (self.rows + (self.ride_rows // self.heads if self.rides(mask) else 0), self.width)

    def ride_slices(self):
        deep = self.ride_rows // self.heads
        return [
            (pl.ds(self.rows, deep), pl.ds(at * HD, HD), pl.ds(at * deep, deep))
            for at in range(self.heads)
        ]


def pack_kernel(sizes, q_ref, k_ref, v_ref, embed_ref, *refs):
    masks = sizes.pieces()
    out_refs = refs[: len(masks)]
    embed_scr, share_scr, embed_sem, sems = refs[len(masks) :]
    me = lax.axis_index("seq")
    tok_rows, part_rows, width = sizes.tok_rows, sizes.part_rows, sizes.width
    share = pl.ds(lax.axis_index("dp") * sizes.share, sizes.share)
    load = pltpu.make_async_copy(embed_ref.at[share], embed_scr, embed_sem.at[0])
    load.start()
    copies = []
    for slot, (mask, out) in enumerate(zip(masks, out_refs)):
        dest = jnp.bitwise_xor(me, mask)
        group, part = dest // sizes.query_parts, dest % sizes.query_parts
        cols = pl.ds(pl.multiple_of(group * width, HD), width)
        first = pl.ds(pl.multiple_of(part * part_rows, part_rows), part_rows)
        for kind, source, rows in (
            (0, q_ref.at[0, first, cols], pl.ds(0, part_rows)),
            (1, k_ref.at[0, :, cols], pl.ds(part_rows, tok_rows)),
            (2, v_ref.at[0, :, cols], pl.ds(part_rows + tok_rows, tok_rows)),
        ):
            copies.append(pltpu.make_async_copy(source, out.at[rows], sems.at[kind, slot]))
    for copy in copies:
        copy.start()
    load.wait()
    if sizes.riding:
        for chunk in range(sizes.chunks):
            cols = embed_scr[:, :, pl.ds(chunk * HD, HD)].astype(F32)
            share_scr[pl.ds(chunk * sizes.share_rows, sizes.share_rows), :] = cols.reshape(
                sizes.share_rows, HD
            ).astype(BF16)
        for mask, out in zip(masks, out_refs):
            if sizes.rides(mask):
                for rows, place, from_rows in sizes.ride_slices():
                    out[rows, place] = share_scr[from_rows, :]
    for copy in copies:
        copy.wait()


def pack(sizes, queries, keys, values, patch_embed):
    tok_rows, full = queries.shape[1:]
    masks = sizes.pieces()
    return pl.pallas_call(
        functools.partial(pack_kernel, sizes),
        out_shape=[jax.ShapeDtypeStruct(sizes.piece_shape(mask), BF16) for mask in masks],
        in_specs=[HBM_SPEC] * 4,
        out_specs=[VMEM_SPEC] * len(masks),
        scratch_shapes=[
            pltpu.VMEM((sizes.share,) + patch_embed.shape[1:], BF16),
            pltpu.VMEM((max(16, sizes.ride_rows), HD), BF16),
            pltpu.SemaphoreType.DMA((1,)),
            pltpu.SemaphoreType.DMA((3, len(masks))),
        ],
        compiler_params=limits(8),
        cost_estimate=pl.CostEstimate(
            flops=0, bytes_accessed=12 * tok_rows * full, transcendentals=0
        ),
    )(queries, keys, values, patch_embed)


def collect_kernel(sizes, *refs):
    *in_refs, out_ref, sems = refs
    copies = []
    for slot, ref in enumerate(in_refs):
        for at, (rows, cols, to_rows) in enumerate(sizes.ride_slices()):
            copies.append(
                pltpu.make_async_copy(
                    ref.at[rows, cols], out_ref.at[slot, to_rows], sems.at[at, slot]
                )
            )
    for copy in copies:
        copy.start()
    for copy in copies:
        copy.wait()


def collect(sizes, arrays):
    return pl.pallas_call(
        functools.partial(collect_kernel, sizes),
        out_shape=jax.ShapeDtypeStruct((len(arrays), sizes.ride_rows, HD), BF16),
        in_specs=[ANY_SPEC] * len(arrays),
        out_specs=VMEM_SPEC,
        scratch_shapes=[pltpu.SemaphoreType.DMA((sizes.heads, len(arrays)))],
        compiler_params=limits(),
    )(*arrays)


def join_kernel(first_ref, second_ref, *refs):
    out_ref = refs[-1]
    count = first_ref.shape[0]
    out_ref[:count] = first_ref[...]
    out_ref[count:] = second_ref[...]


def join(first, second, others):
    return pl.pallas_call(
        join_kernel,
        out_shape=jax.ShapeDtypeStruct((2 * first.shape[0],) + first.shape[1:], BF16),
        in_specs=[VMEM_SPEC] * 2 + [ANY_SPEC] * len(others),
        out_specs=VMEM_SPEC,
        compiler_params=limits(),
    )(first, second, *others)


def arrange_kernel(sizes, masks, place_ref, *refs):
    *pair_refs, out_ref = refs[:-2] + refs[-1:]
    me = place_ref[0]
    odd = me % 2 == 1
    local = sizes.local
    for quarter in range(len(pair_refs) // 2):
        held_ref, got_ref = pair_refs[2 * quarter], pair_refs[2 * quarter + 1]
        for slot, mask in enumerate(masks):
            pair = jnp.bitwise_xor(me, mask) // 2
            for chunk in range(sizes.chunks):
                rows = pl.ds(chunk * sizes.share_rows, sizes.share_rows)
                held = held_ref[slot, rows, :].astype(F32)
                got = got_ref[slot, rows, :].astype(F32)
                first = jnp.where(odd, got, held)
                second = jnp.where(odd, held, got)
                for at in range(sizes.share):
                    part = slice(at * local, (at + 1) * local)
                    both = jnp.concatenate([first[part], second[part]], axis=0).astype(BF16)
                    start = pl.multiple_of(at * sizes.count * local + pair * 2 * local, 2 * local)
                    out_ref[quarter, pl.ds(start, 2 * local), pl.ds(chunk * HD, HD)] = both


def arrange(sizes, masks, place, pairs, wait):
    rows = sizes.share * sizes.count * sizes.local
    flat = [x for pair in pairs for x in pair]
    return pl.pallas_call(
        functools.partial(arrange_kernel, sizes, masks),
        out_shape=jax.ShapeDtypeStruct((len(pairs), rows, VW), BF16),
        in_specs=[SMEM_SPEC] + [VMEM_SPEC] * (len(flat) + 1),
        out_specs=VMEM_SPEC,
        compiler_params=limits(),
    )(place, *flat, wait)


def fetch_kernel(sizes, place_ref, cot_ref, *refs):
    *refs, row_ref, sems = refs
    count = len(refs) // 2
    row_ref[...] = jnp.full(row_ref.shape, cot_ref[0], F32)
    mine = pl.ds(pl.multiple_of(place_ref[2] * sizes.width, HD), sizes.width)
    copies = []
    for slot in range(count):
        source = refs[slot].at[:, mine] if slot < 3 else refs[slot]
        copies.append(pltpu.make_async_copy(source, refs[count + slot], sems.at[slot]))
        copies[-1].start()
    for copy in copies:
        copy.wait()


def fetch(sizes, place, cotangent, arrays):
    shapes = [x.shape if slot >= 3 else (x.shape[0], sizes.width) for slot, x in enumerate(arrays)]
    return pl.pallas_call(
        functools.partial(fetch_kernel, sizes),
        out_shape=[jax.ShapeDtypeStruct(shape, x.dtype) for shape, x in zip(shapes, arrays)]
        + [jax.ShapeDtypeStruct((1, 128), F32)],
        in_specs=[SMEM_SPEC] * 2 + [HBM_SPEC] * len(arrays),
        out_specs=[VMEM_SPEC] * (len(arrays) + 1),
        scratch_shapes=[pltpu.SemaphoreType.DMA((len(arrays),))],
        compiler_params=limits(),
        cost_estimate=pl.CostEstimate(flops=1, bytes_accessed=1, transcendentals=0),
    )(place, cotangent, *[in_hbm(x) for x in arrays])


FACTOR = HD ** (-0.5) * math.log2(math.e)


def load_pieces(sizes, in_refs, key_scr, value_scr):
    tok_rows, part_rows = sizes.tok_rows, sizes.part_rows
    for src, ref in enumerate(in_refs):
        rows = pl.ds(src * tok_rows, tok_rows)
        key_scr[rows, :] = ref[pl.ds(part_rows, tok_rows), :]
        for head in range(sizes.heads):
            value_scr[rows, pl.ds(2 * head * HD, HD)] = ref[
                pl.ds(part_rows + tok_rows, tok_rows), pl.ds(head * HD, HD)
            ]
    ones = jnp.ones((len(in_refs) * tok_rows, HD), BF16)
    for head in range(sizes.heads):
        value_scr[:, pl.ds((2 * head + 1) * HD, HD)] = ones


def soft_part(query, key_scr, value_scr, rows, head, before):
    logits = mm_nt(query, key_scr[rows, pl.ds(head * HD, HD)])
    top = jnp.max(logits, axis=-1, keepdims=True)
    if before:
        top = jnp.maximum(top, before[2])
    weights = jnp.exp2((logits - top) * FACTOR).astype(BF16)
    both = mm(weights, value_scr[rows, pl.ds(2 * head * HD, 2 * HD)])
    mixed, total = both[:, :HD], both[:, HD:]
    if before:
        shrink = jnp.exp2((before[2] - top) * FACTOR)
        mixed, total = mixed + before[0] * shrink, total + before[1] * shrink
    return mixed, total, top


def piece_scratch(sizes, count):
    lat_rows = count * sizes.tok_rows
    return [
        pltpu.VMEM((lat_rows, sizes.width), BF16),
        pltpu.VMEM((lat_rows, 2 * sizes.width), BF16),
    ]


def early_kernel(sizes, count, *refs):
    in_refs, refs = refs[:count], refs[count + 1 :]
    sum_ref, stat_ref, key_scr, value_scr = refs
    load_pieces(sizes, in_refs, key_scr, value_scr)
    left = lax.broadcasted_iota(jnp.int32, (sizes.part_rows, HD), 1) < HD // 2
    rows = pl.ds(0, count * sizes.tok_rows)
    for src in range(count):
        results = [
            soft_part(
                in_refs[src][pl.ds(0, sizes.part_rows), pl.ds(head * HD, HD)],
                key_scr, value_scr, rows, head, None,
            )
            for head in range(sizes.heads)
        ]
        for head, (mixed, total, top) in enumerate(results):
            sum_ref[src, head] = mixed
            stat_ref[src, head] = jnp.where(left, top, total)


def attend_early(sizes, received, wait):
    count = len(received)
    shape = jax.ShapeDtypeStruct((count, sizes.heads, sizes.part_rows, HD), F32)
    return pl.pallas_call(
        functools.partial(early_kernel, sizes, count),
        out_shape=(shape, shape),
        in_specs=[VMEM_SPEC] * (count + 1),
        out_specs=(VMEM_SPEC, VMEM_SPEC),
        scratch_shapes=piece_scratch(sizes, count),
        compiler_params=limits(12),
        cost_estimate=pl.CostEstimate(flops=1, bytes_accessed=1, transcendentals=0),
    )(*received, wait)


def attend_kernel(sizes, masks, early, place_ref, *refs):
    count, heads, width = sizes.count, sizes.heads, sizes.width
    tok_rows, part_rows = sizes.tok_rows, sizes.part_rows
    in_refs, refs = refs[:count], refs[count:]
    kept_refs, refs = refs[: 2 if early else 0], refs[2 if early else 0 :]
    scale_ref, shift_ref, proj_ref, mod_ref, lat_ref, *refs = refs
    key_scr, value_scr = refs
    half = part_rows // 2
    me = place_ref[0]
    gain = 1.0 + scale_ref[...]
    shift = shift_ref[...]
    load_pieces(sizes, in_refs, key_scr, value_scr)
    together = 2
    for first in range(0, count, together):
        results = []
        for src in range(first, first + together):
            mixed = []
            for head in range(heads):
                before = None
                rows = pl.ds(0, count * tok_rows)
                if src < early:
                    rows = pl.ds(early * tok_rows, (count - early) * tok_rows)
                    stat = kept_refs[1][src, head]
                    before = (kept_refs[0][src, head], stat[:, HD - 1 :], stat[:, :1])
                query = in_refs[src][pl.ds(0, part_rows), pl.ds(head * HD, HD)]
                value, total, _ = soft_part(query, key_scr, value_scr, rows, head, before)
                mixed.append(value / total)
            results.append(jnp.concatenate(mixed, axis=1) if heads > 1 else mixed[0])
        for at, attended in enumerate(results):
            modulated = (attended * gain + shift).astype(BF16)
            mod_ref[jnp.bitwise_xor(me, masks[first + at])] = modulated
    sides = [
        mm_nt(mod_ref[:, rows, :].reshape(count * half, width), proj_ref[...])
        for rows in (slice(0, half), slice(half, part_rows))
    ]
    latent = jnp.concatenate(sides, axis=1).astype(BF16)
    for spot, place in enumerate(sizes.order()):
        lat_ref[spot] = latent[place * half : (place + 1) * half]


def attend(sizes, masks, place, received, kept, scales, shifts, proj):
    count, width, heads = sizes.count, sizes.width, sizes.heads
    lat_rows = count * sizes.tok_rows
    query_rows = count * sizes.part_rows
    early = kept[0].shape[0] if kept else 0
    return pl.pallas_call(
        functools.partial(attend_kernel, sizes, masks, early),
        out_shape=(
            jax.ShapeDtypeStruct((count, sizes.part_rows, width), BF16),
            jax.ShapeDtypeStruct((count, sizes.part_rows // 2, 2 * CH), BF16),
        ),
        in_specs=[SMEM_SPEC] + [VMEM_SPEC] * (count + len(kept) + 3),
        out_specs=(VMEM_SPEC, VMEM_SPEC),
        scratch_shapes=piece_scratch(sizes, count),
        compiler_params=limits(16),
        cost_estimate=pl.CostEstimate(
            flops=4 * query_rows * lat_rows * width,
            bytes_accessed=2 * (query_rows * 2 + lat_rows * 2) * width,
            transcendentals=query_rows * lat_rows * heads,
        ),
    )(place, *received, *kept, scales, shifts, proj)


def total_kernel(copies, count, *refs):
    out_ref = refs[-1]
    if len(refs[0].shape) == 3:
        parts = [refs[0][i].astype(F32) for i in range(refs[0].shape[0])]
    else:
        parts = [ref[...].astype(F32) for ref in refs[:count]]
    while len(parts) > 1:
        parts = [parts[i] + parts[i + 1] for i in range(0, len(parts), 2)]
    for copy in range(copies):
        out_ref[copy] = parts[0].astype(BF16)


def total_copies(arrays, copies, others=()):
    return pl.pallas_call(
        functools.partial(total_kernel, copies, len(arrays)),
        out_shape=jax.ShapeDtypeStruct((copies,) + arrays[0].shape[-2:], BF16),
        in_specs=[VMEM_SPEC] * (len(arrays) + len(others)),
        out_specs=VMEM_SPEC,
        compiler_params=limits(),
    )(*arrays, *others)


def lane_mean(x, count):
    return jnp.sum(x, axis=-1, keepdims=True) * (1.0 / count)


def head_kernel(grid_rows, fused, order, embed_masks, out_factor, place_ref, lat_ref, *refs):
    embed_refs, refs = refs[: len(embed_masks)], refs[len(embed_masks) :]
    pos_ref, pre_ref, post_ref, prompt_ref, cot_ref, mod_ref, *refs = refs
    reward_ref, grad_ref, weight_ref, lat_scr, grad_scr, block_scr, back_scr = refs
    patch_rows = grid_rows // 4
    patch_cols = GW // 4
    patches = patch_rows * patch_cols
    for spot, place in enumerate(order):
        lat_scr[pl.ds(place * GW, GW), :] = lat_ref[pl.ds(spot * GW, GW), :].astype(F32)

    data = place_ref[1]
    shares = [
        (jnp.bitwise_xor(data, mask), ref, slot)
        for ref, masks in zip(embed_refs, embed_masks)
        for slot, mask in enumerate(masks)
    ]
    share_rows = embed_refs[0].shape[1]
    for hi in range(2):
        wide = []
        for tx in range(4):
            rows = [
                lat_scr[pl.ds((2 * pr + hi) * GW + tx, patch_cols, stride=4), :]
                for pr in range(patch_rows)
            ]
            wide.append(jnp.concatenate(rows, axis=0))
        for side in range(2):
            lanes = slice(side * CH, (side + 1) * CH)
            line = jnp.concatenate([x[:, lanes] for x in wide], axis=1).astype(BF16)
            first = (2 * hi + side) * 4 * CH
            if share_rows >= 4 * CH:
                at = first % share_rows
                block_scr[first // share_rows, :, pl.ds(at, 4 * CH)] = line
            else:
                for at in range(0, 4 * CH, share_rows):
                    block_scr[(first + at) // share_rows] = line[:, at : at + share_rows]
    embedded = pos_ref[...].astype(F32)
    for number, ref, slot in shares:
        embedded = embedded + mm(block_scr[number], ref[slot])
    pre = pre_ref[...].reshape(1, VW)
    post = post_ref[...].reshape(1, VW)
    prompt = prompt_ref[...]
    center = embedded - lane_mean(embedded, VW)
    rstd = lax.rsqrt(lane_mean(center * center, VW) + EPS)
    unit = center * rstd
    pooled = jnp.sum(unit, axis=0, keepdims=True) * (1.0 / patches) * pre
    pooled_center = pooled - lane_mean(pooled, VW)
    pooled_rstd = lax.rsqrt(lane_mean(pooled_center * pooled_center, VW) + EPS)
    pooled_unit = pooled_center * pooled_rstd
    final = pooled_unit * post
    dot = jnp.sum(final * prompt, axis=-1, keepdims=True)
    final_sq = jnp.sum(final * final, axis=-1, keepdims=True)
    prompt_sq = jnp.sum(prompt * prompt, axis=-1, keepdims=True)
    final_len = jnp.sqrt(final_sq)
    prompt_len = jnp.sqrt(prompt_sq)
    cosine = dot / (final_len * prompt_len)
    reward_ref[...] = jnp.broadcast_to(100.0 * cosine, reward_ref.shape)
    cot = cot_ref[:, :1]
    final_grad = (100.0 * cot) * (prompt / (final_len * prompt_len) - final * (cosine / final_sq))
    unit_grad = final_grad * post
    pooled_grad = pooled_rstd * (
        unit_grad
        - lane_mean(unit_grad, VW)
        - pooled_unit * lane_mean(unit_grad * pooled_unit, VW)
    )
    flow = pooled_grad * pre * (1.0 / patches)
    embed_grad = rstd * (flow - lane_mean(flow, VW) - unit * lane_mean(flow * unit, VW))
    high = embed_grad.astype(BF16)
    low = (embed_grad - high.astype(F32)).astype(BF16)
    stacked = jnp.concatenate([high, low], axis=0)
    for number, ref, slot in shares:
        both = mm_nt(stacked, ref[slot])
        back_scr[number] = both[:patches] + both[patches:]
    back = jnp.concatenate([back_scr[i] for i in range(16 * CH // share_rows)], axis=1)
    for hi in range(2):
        for tx in range(4):
            first = (4 * (2 * hi) + tx) * CH
            second = (4 * (2 * hi + 1) + tx) * CH
            piece = jnp.concatenate(
                [back[:, first : first + CH], back[:, second : second + CH]], axis=1
            )
            for pr in range(patch_rows):
                grad_scr[pl.ds((2 * pr + hi) * GW + tx, patch_cols, stride=4), :] = piece[
                    pr * patch_cols : (pr + 1) * patch_cols
                ]
    grad = grad_scr[...].astype(BF16)
    grad_ref[...] = grad
    if fused:
        store_readout_grad(grad, mod_ref, out_factor, weight_ref)
    else:
        weight_ref[...] = jnp.zeros_like(weight_ref)


def store_readout_grad(grad, mod_ref, out_factor, out_ref):
    turned = grad.astype(F32).T.astype(BF16)
    count, rows, width = mod_ref.shape
    half = rows // 2
    first = mod_ref[:, :half, :].reshape(count * half, width)
    second = mod_ref[:, half:, :].reshape(count * half, width)
    total = mm(turned[:CH], first) + mm(turned[CH:], second)
    out_ref[...] = (total * out_factor).astype(BF16)


def reward_head(
    place, order, latent, embed, pos, pre, post, prompt, cot, modulated, grid_rows, fused, out_factor
):
    patches = grid_rows * GW // 16
    rows = grid_rows * GW // 2
    width = modulated.shape[2]
    embed_arrays, embed_masks = [x for x, _ in embed], [masks for _, masks in embed]
    share_rows = embed_arrays[0].shape[1]
    return pl.pallas_call(
        functools.partial(head_kernel, grid_rows, fused, order, embed_masks, out_factor),
        out_shape=(
            jax.ShapeDtypeStruct((1, 128), F32),
            jax.ShapeDtypeStruct((rows, 2 * CH), BF16),
            jax.ShapeDtypeStruct((CH, width), BF16),
        ),
        in_specs=[SMEM_SPEC, VMEM_SPEC]
        + [VMEM_SPEC] * len(embed_arrays)
        + [VMEM_SPEC] * 6,
        out_specs=(VMEM_SPEC, VMEM_SPEC, VMEM_SPEC),
        scratch_shapes=[
            pltpu.VMEM((rows, 2 * CH), F32),
            pltpu.VMEM((rows, 2 * CH), F32),
            pltpu.VMEM((16 * CH // share_rows, patches, share_rows), BF16),
            pltpu.VMEM((16 * CH // share_rows, patches, share_rows), F32),
        ],
        compiler_params=limits(16),
        cost_estimate=pl.CostEstimate(
            flops=6 * patches * 16 * CH * VW,
            bytes_accessed=2 * 16 * CH * VW + 2 * patches * VW,
            transcendentals=0,
        ),
    )(place, latent, *embed_arrays, pos, pre, post, prompt, cot, modulated)


def spread_kernel(count, half, heads, grad_ref, scale_ref, proj_ref, out_ref, token_ref):
    token_ref[...] = jnp.zeros_like(token_ref)
    gain = 1.0 + scale_ref[...]
    proj = proj_ref[...]
    zero = jnp.zeros_like(proj)
    sides = (jnp.concatenate([proj, zero], axis=0), jnp.concatenate([zero, proj], axis=0))
    for src in range(count):
        grad = grad_ref[pl.ds(src * half, half), :]
        for side in range(2):
            rows = (mm(grad, sides[side]) * gain).astype(BF16)
            for head in range(heads):
                out_ref[0, head, pl.ds((2 * src + side) * half, half), :] = rows[
                    :, head * HD : (head + 1) * HD
                ]


def spread(grad, scales, proj, count, half, heads):
    return pl.pallas_call(
        functools.partial(spread_kernel, count, half, heads),
        out_shape=(
            jax.ShapeDtypeStruct((1, heads, 2 * count * half, HD), BF16),
            jax.ShapeDtypeStruct((8, 128), F32),
        ),
        in_specs=[VMEM_SPEC] * 3,
        out_specs=(VMEM_SPEC, VMEM_SPEC),
        compiler_params=limits(),
        cost_estimate=pl.CostEstimate(
            flops=8 * count * half * CH * heads * HD,
            bytes_accessed=4 * count * half * heads * HD,
            transcendentals=0,
        ),
    )(grad, scales, proj)


def weight_kernel(out_factor, grad_ref, *refs):
    store_readout_grad(grad_ref[...], refs[0], out_factor, refs[1])


def weight_call(grad, modulated, out_factor):
    return pl.pallas_call(
        functools.partial(weight_kernel, out_factor),
        out_shape=jax.ShapeDtypeStruct((CH, modulated.shape[2]), BF16),
        in_specs=[VMEM_SPEC] * 2,
        out_specs=VMEM_SPEC,
        compiler_params=limits(),
    )(grad, modulated)


def finish_kernel(order, in_ref, out_ref):
    width = in_ref.shape[2]
    for spot, group in enumerate(order):
        out_ref[:, pl.ds(group * width, width)] = in_ref[spot].astype(F32)


def finish(blocks, order):
    return pl.pallas_call(
        functools.partial(finish_kernel, order),
        out_shape=jax.ShapeDtypeStruct((CH, HEADS * HD), F32),
        in_specs=[VMEM_SPEC],
        out_specs=VMEM_SPEC,
        compiler_params=limits(),
    )(blocks)


def swap(x, axis, mask):
    count = lax.axis_size(axis)
    return lax.ppermute(x, axis, [(i, i ^ mask) for i in range(count)])


def all_to_all(x, groups=None):
    return lax.all_to_all(
        x, "seq", split_axis=0, concat_axis=0, tiled=True, axis_index_groups=groups
    )


def swap_both(x, seq_mask, data_mask):
    seq_count, data_count = lax.axis_size("seq"), lax.axis_size("dp")
    pairs = [
        (i * data_count + j, (i ^ seq_mask) * data_count + (j ^ data_mask))
        for i in range(seq_count)
        for j in range(data_count)
    ]
    return lax.ppermute(x, ("seq", "dp"), pairs)


def on_device(
    queries,
    keys,
    values,
    shifts,
    scales,
    proj_out,
    patch_embed,
    pos_embed,
    pre_gain,
    post_gain,
    prompt,
    cotangent,
):
    seq_count = lax.axis_size("seq")
    data_count = lax.axis_size("dp")
    tok_rows = queries.shape[1]
    sizes = Sizes(seq_count, data_count, tok_rows, patch_embed)
    query_parts, head_count, part_rows = sizes.query_parts, sizes.heads, sizes.part_rows
    group_count = HEADS // head_count
    seq_index = lax.axis_index("seq")
    head_group = seq_index // query_parts
    query_part = seq_index % query_parts
    half = part_rows // 2
    lat_rows = seq_count * tok_rows
    grid_rows = lat_rows // GW
    canonical = part_rows == 2 * GW
    place = jnp.stack([seq_index, lax.axis_index("dp"), head_group]).astype(jnp.int32)
    proj_turned = proj_out.T
    out_factor = 1.0 / math.sqrt(data_count * lat_rows)

    masks = sizes.pieces()
    packed = pack(
        sizes, in_hbm(queries), in_hbm(keys), in_hbm(values), in_hbm(patch_embed)
    )
    received = [swap(x, "seq", mask) if mask else x for mask, x in zip(masks, packed)]
    bits = [1 << b for b in reversed(range(data_count.bit_length() - 1))]
    shared = sizes.share < patch_embed.shape[0]
    scale, shift, proj, pos, pre, post, words, cot = fetch(
        sizes, place, cotangent, [scales, shifts, proj_turned, pos_embed, pre_gain, post_gain, prompt]
    )

    kept, order = [], list(range(seq_count))
    if seq_count == 8:
        late = [slot for slot, mask in enumerate(masks) if mask in (6, 7)]
        order = [slot for slot in order if slot not in late]
        kept = attend_early(sizes, [received[slot] for slot in order], scale)
        order = order + late
    if sizes.riding:
        ride = [slot for slot, mask in enumerate(masks) if sizes.rides(mask)]
        two = collect(sizes, [received[slot] for slot in ride])
        held = join(two, swap(two, "seq", 2), kept)
        ride_masks = [masks[slot] for slot in ride]
        ride_masks = ride_masks + [mask ^ 2 for mask in ride_masks]
        pairs = [
            (held, swap(held, "seq", 1)),
            (swap(held, "dp", bits[0]), swap_both(held, 1, bits[0])),
        ]

    modulated, latent_part = attend(
        sizes, [masks[slot] for slot in order], place, [received[slot] for slot in order], kept,
        scale, shift, proj,
    )

    if not sizes.riding:
        mine = patch_embed
        if shared:
            mine = lax.dynamic_slice_in_dim(
                patch_embed, lax.axis_index("dp") * sizes.share, sizes.share, 0
            )
        mine = lax.all_gather(mine, "seq", axis=1, tiled=True).reshape(-1, VW)
        embed = [(mine[None], [0])]
        if shared:
            embed = embed + [(swap(mine[None], "dp", bits[0]), [bits[0]])]

    groups, order = [sizes.order()], sizes.order()
    if query_parts > 1:
        order = list(range(group_count))
        groups = [[g * query_parts + r for g in range(group_count)] for r in range(query_parts)]
    per_share = seq_count // group_count
    parts = all_to_all(latent_part.reshape(group_count, per_share * half, 2 * CH), groups)
    summed = total_copies([parts], seq_count)
    if sizes.riding:
        embed = [(arrange(sizes, ride_masks, place, pairs, summed), [0, bits[0]])]
    for bit in bits[1:] if shared else []:
        embed = embed + [(swap(x, "dp", bit), [m ^ bit for m in some]) for x, some in embed]
    latent = all_to_all(summed, [sizes.order()])
    if canonical:
        latent = latent.reshape(lat_rows // 2, 2 * CH)
    else:
        latent = latent.reshape(group_count, query_parts, per_share, half, 2, CH)
        latent = latent.transpose(0, 2, 1, 4, 3, 5).reshape(grid_rows // 2, 2, GW, CH)
        latent = latent.transpose(0, 2, 1, 3).reshape(lat_rows // 2, 2 * CH)

    reward, grad, weight = reward_head(
        place, sizes.order() if canonical else list(range(grid_rows // 2)),
        latent, embed, pos, pre, post, words,
        cot, modulated, grid_rows, canonical, out_factor,
    )
    if not canonical:
        tokens = grad.reshape(grid_rows // 2, GW, 2, CH).transpose(0, 2, 1, 3)
        tokens = tokens.reshape(seq_count, query_parts, 2, half, CH)
        tokens = lax.dynamic_index_in_dim(tokens, query_part, 1, keepdims=False)
        grad = tokens.transpose(0, 2, 1, 3).reshape(seq_count * half, 2 * CH)
        weight = weight_call(grad, modulated, out_factor)

    parts = [weight] + [swap(weight, "dp", mask) for mask in range(1, data_count)]
    attn_grad, token = spread(grad, scale, proj, seq_count, half, head_count)
    if query_parts > 1:
        total = total_copies(parts, 1)[0]
        parts = [total] + [swap(total, "seq", mask) for mask in range(1, query_parts)]
    blocks = all_to_all(total_copies(parts, group_count, [token]), groups)
    return (reward[0, :1], attn_grad, finish(blocks, order).T)


def solution(mesh):
    return jax.shard_map(
        on_device,
        mesh=mesh,
        in_specs=(
            P("dp", "seq", None),
            P("dp", "seq", None),
            P("dp", "seq", None),
            P("dp", None),
            P("dp", None),
            P(),
            P(None, "seq", None),
            P(),
            P(),
            P(),
            P("dp", None),
            P("dp"),
        ),
        out_specs=(P("dp"), P("dp", "seq", None, None), P()),
        check_vma=False,
    )
```

```python
import functools
import math

import jax
import jax.numpy as jnp
from jax import lax
from jax.experimental import pallas as pl
from jax.experimental.pallas import tpu as pltpu
from jax.sharding import PartitionSpec as P

HEADS = 16
HD = 128
CH = 64
GW = 64
VW = 1280
EPS = 1e-05
BF16 = jnp.bfloat16
F32 = jnp.float32


def mm(a, b):
    return jnp.dot(a, b, preferred_element_type=F32)


def mm_nt(a, b):
    return lax.dot_general(a, b, (((1,), (1,)), ((), ())), preferred_element_type=F32)


def mm_tn(a, b):
    return lax.dot_general(a, b, (((0,), (0,)), ((), ())), preferred_element_type=F32)


SMEM_SPEC = pl.BlockSpec(memory_space=pltpu.SMEM)
VMEM_SPEC = pl.BlockSpec(memory_space=pltpu.VMEM)
HBM_SPEC = pl.BlockSpec(memory_space=pltpu.HBM)
ANY_SPEC = pl.BlockSpec(memory_space=pl.ANY)


def in_hbm(x):
    return pltpu.with_memory_space_constraint(x, pltpu.HBM)


def limits(mib=4):
    return pltpu.CompilerParams(vmem_limit_bytes=mib * 1024 * 1024)


class Sizes:
    def __init__(self, seq_count, data_count, tok_rows, patch_embed):
        self.count = seq_count
        self.query_parts = max(1, seq_count // HEADS)
        self.heads = max(1, HEADS // seq_count)
        self.width = self.heads * HD
        self.tok_rows = tok_rows
        self.part_rows = tok_rows // self.query_parts
        positions, self.local, _ = patch_embed.shape
        self.share = positions // data_count if positions % data_count == 0 else positions
        self.rows = self.part_rows + 2 * tok_rows
        self.share_rows = self.share * self.local
        self.chunks = VW // HD
        self.riding = self.local % 8 == 0 and self.share_rows % 16 == 0 and seq_count == 8
        self.riding = self.riding and 1 < data_count <= positions
        self.ride_rows = self.chunks * self.share_rows if self.riding else 0

    def order(self):
        return [4, 5, 2, 3, 6, 7, 0, 1] if self.count == 8 else list(range(self.count))

    def pieces(self):
        return list(range(1, self.count)) + [0]

    def rides(self, mask):
        return self.riding and mask in (0, 4)

    def piece_shape(self, mask):
        return (self.rows + (self.ride_rows // self.heads if self.rides(mask) else 0), self.width)

    def ride_slices(self):
        deep = self.ride_rows // self.heads
        return [
            (pl.ds(self.rows, deep), pl.ds(at * HD, HD), pl.ds(at * deep, deep))
            for at in range(self.heads)
        ]


def pack_kernel(sizes, q_ref, k_ref, v_ref, embed_ref, *refs):
    masks = sizes.pieces()
    out_refs = refs[: len(masks)]
    embed_scr, share_scr, embed_sem, sems = refs[len(masks) :]
    me = lax.axis_index("seq")
    tok_rows, part_rows, width = sizes.tok_rows, sizes.part_rows, sizes.width
    share = pl.ds(lax.axis_index("dp") * sizes.share, sizes.share)
    load = pltpu.make_async_copy(embed_ref.at[share], embed_scr, embed_sem.at[0])
    load.start()
    copies = []
    for slot, (mask, out) in enumerate(zip(masks, out_refs)):
        dest = jnp.bitwise_xor(me, mask)
        group, part = dest // sizes.query_parts, dest % sizes.query_parts
        cols = pl.ds(pl.multiple_of(group * width, HD), width)
        first = pl.ds(pl.multiple_of(part * part_rows, part_rows), part_rows)
        for kind, source, rows in (
            (0, q_ref.at[0, first, cols], pl.ds(0, part_rows)),
            (1, k_ref.at[0, :, cols], pl.ds(part_rows, tok_rows)),
            (2, v_ref.at[0, :, cols], pl.ds(part_rows + tok_rows, tok_rows)),
        ):
            copies.append(pltpu.make_async_copy(source, out.at[rows], sems.at[kind, slot]))
    for copy in copies:
        copy.start()
    load.wait()
    if sizes.riding:
        for chunk in range(sizes.chunks):
            cols = embed_scr[:, :, pl.ds(chunk * HD, HD)].astype(F32)
            share_scr[pl.ds(chunk * sizes.share_rows, sizes.share_rows), :] = cols.reshape(
                sizes.share_rows, HD
            ).astype(BF16)
        for mask, out in zip(masks, out_refs):
            if sizes.rides(mask):
                for rows, place, from_rows in sizes.ride_slices():
                    out[rows, place] = share_scr[from_rows, :]
    for copy in copies:
        copy.wait()


def pack(sizes, queries, keys, values, patch_embed):
    tok_rows, full = queries.shape[1:]
    masks = sizes.pieces()
    return pl.pallas_call(
        functools.partial(pack_kernel, sizes),
        out_shape=[jax.ShapeDtypeStruct(sizes.piece_shape(mask), BF16) for mask in masks],
        in_specs=[HBM_SPEC] * 4,
        out_specs=[VMEM_SPEC] * len(masks),
        scratch_shapes=[
            pltpu.VMEM((sizes.share,) + patch_embed.shape[1:], BF16),
            pltpu.VMEM((max(16, sizes.ride_rows), HD), BF16),
            pltpu.SemaphoreType.DMA((1,)),
            pltpu.SemaphoreType.DMA((3, len(masks))),
        ],
        compiler_params=limits(8),
        cost_estimate=pl.CostEstimate(
            flops=0, bytes_accessed=12 * tok_rows * full, transcendentals=0
        ),
    )(queries, keys, values, patch_embed)


def collect_kernel(sizes, *refs):
    *in_refs, out_ref, sems = refs
    copies = []
    for slot, ref in enumerate(in_refs):
        for at, (rows, cols, to_rows) in enumerate(sizes.ride_slices()):
            copies.append(
                pltpu.make_async_copy(
                    ref.at[rows, cols], out_ref.at[slot, to_rows], sems.at[at, slot]
                )
            )
    for copy in copies:
        copy.start()
    for copy in copies:
        copy.wait()


def collect(sizes, arrays):
    return pl.pallas_call(
        functools.partial(collect_kernel, sizes),
        out_shape=jax.ShapeDtypeStruct((len(arrays), sizes.ride_rows, HD), BF16),
        in_specs=[ANY_SPEC] * len(arrays),
        out_specs=VMEM_SPEC,
        scratch_shapes=[pltpu.SemaphoreType.DMA((sizes.heads, len(arrays)))],
        compiler_params=limits(),
    )(*arrays)


def join_kernel(first_ref, second_ref, *refs):
    out_ref = refs[-1]
    count = first_ref.shape[0]
    out_ref[:count] = first_ref[...]
    out_ref[count:] = second_ref[...]


def join(first, second, others):
    return pl.pallas_call(
        join_kernel,
        out_shape=jax.ShapeDtypeStruct((2 * first.shape[0],) + first.shape[1:], BF16),
        in_specs=[VMEM_SPEC] * 2 + [ANY_SPEC] * len(others),
        out_specs=VMEM_SPEC,
        compiler_params=limits(),
    )(first, second, *others)


def arrange_kernel(sizes, masks, place_ref, *refs):
    *pair_refs, out_ref = refs[:-2] + refs[-1:]
    me = place_ref[0]
    odd = me % 2 == 1
    local = sizes.local
    for quarter in range(len(pair_refs) // 2):
        held_ref, got_ref = pair_refs[2 * quarter], pair_refs[2 * quarter + 1]
        for slot, mask in enumerate(masks):
            pair = jnp.bitwise_xor(me, mask) // 2
            for chunk in range(sizes.chunks):
                rows = pl.ds(chunk * sizes.share_rows, sizes.share_rows)
                held = held_ref[slot, rows, :].astype(F32)
                got = got_ref[slot, rows, :].astype(F32)
                first = jnp.where(odd, got, held)
                second = jnp.where(odd, held, got)
                for at in range(sizes.share):
                    part = slice(at * local, (at + 1) * local)
                    both = jnp.concatenate([first[part], second[part]], axis=0).astype(BF16)
                    start = pl.multiple_of(at * sizes.count * local + pair * 2 * local, 2 * local)
                    out_ref[quarter, pl.ds(start, 2 * local), pl.ds(chunk * HD, HD)] = both


def arrange(sizes, masks, place, pairs, wait):
    rows = sizes.share * sizes.count * sizes.local
    flat = [x for pair in pairs for x in pair]
    return pl.pallas_call(
        functools.partial(arrange_kernel, sizes, masks),
        out_shape=jax.ShapeDtypeStruct((len(pairs), rows, VW), BF16),
        in_specs=[SMEM_SPEC] + [VMEM_SPEC] * (len(flat) + 1),
        out_specs=VMEM_SPEC,
        compiler_params=limits(),
    )(place, *flat, wait)


def fetch_kernel(sizes, place_ref, cot_ref, *refs):
    *refs, row_ref, sems = refs
    count = len(refs) // 2
    row_ref[...] = jnp.full(row_ref.shape, cot_ref[0], F32)
    mine = pl.ds(pl.multiple_of(place_ref[2] * sizes.width, HD), sizes.width)
    copies = []
    for slot in range(count):
        source = refs[slot].at[:, mine] if slot < 3 else refs[slot]
        copies.append(pltpu.make_async_copy(source, refs[count + slot], sems.at[slot]))
        copies[-1].start()
    for copy in copies:
        copy.wait()


def fetch(sizes, place, cotangent, arrays):
    shapes = [x.shape if slot >= 3 else (x.shape[0], sizes.width) for slot, x in enumerate(arrays)]
    return pl.pallas_call(
        functools.partial(fetch_kernel, sizes),
        out_shape=[jax.ShapeDtypeStruct(shape, x.dtype) for shape, x in zip(shapes, arrays)]
        + [jax.ShapeDtypeStruct((1, 128), F32)],
        in_specs=[SMEM_SPEC] * 2 + [HBM_SPEC] * len(arrays),
        out_specs=[VMEM_SPEC] * (len(arrays) + 1),
        scratch_shapes=[pltpu.SemaphoreType.DMA((len(arrays),))],
        compiler_params=limits(),
        cost_estimate=pl.CostEstimate(flops=1, bytes_accessed=1, transcendentals=0),
    )(place, cotangent, *[in_hbm(x) for x in arrays])


FACTOR = HD ** (-0.5) * math.log2(math.e)


def load_pieces(sizes, in_refs, key_scr, value_scr):
    tok_rows, part_rows = sizes.tok_rows, sizes.part_rows
    for src, ref in enumerate(in_refs):
        rows = pl.ds(src * tok_rows, tok_rows)
        key_scr[rows, :] = ref[pl.ds(part_rows, tok_rows), :]
        for head in range(sizes.heads):
            value_scr[rows, pl.ds(2 * head * HD, HD)] = ref[
                pl.ds(part_rows + tok_rows, tok_rows), pl.ds(head * HD, HD)
            ]
    ones = jnp.ones((len(in_refs) * tok_rows, HD), BF16)
    for head in range(sizes.heads):
        value_scr[:, pl.ds((2 * head + 1) * HD, HD)] = ones


def soft_part(query, key_scr, value_scr, rows, head, before):
    logits = mm_nt(query, key_scr[rows, pl.ds(head * HD, HD)])
    top = jnp.max(logits, axis=-1, keepdims=True)
    if before:
        top = jnp.maximum(top, before[2])
    weights = jnp.exp2((logits - top) * FACTOR).astype(BF16)
    both = mm(weights, value_scr[rows, pl.ds(2 * head * HD, 2 * HD)])
    mixed, total = both[:, :HD], both[:, HD:]
    if before:
        shrink = jnp.exp2((before[2] - top) * FACTOR)
        mixed, total = mixed + before[0] * shrink, total + before[1] * shrink
    return mixed, total, top


def piece_scratch(sizes, count):
    lat_rows = count * sizes.tok_rows
    return [
        pltpu.VMEM((lat_rows, sizes.width), BF16),
        pltpu.VMEM((lat_rows, 2 * sizes.width), BF16),
    ]


def early_kernel(sizes, count, *refs):
    in_refs, refs = refs[:count], refs[count + 1 :]
    sum_ref, stat_ref, key_scr, value_scr = refs
    load_pieces(sizes, in_refs, key_scr, value_scr)
    left = lax.broadcasted_iota(jnp.int32, (sizes.part_rows, HD), 1) < HD // 2
    rows = pl.ds(0, count * sizes.tok_rows)
    for src in range(count):
        results = [
            soft_part(
                in_refs[src][pl.ds(0, sizes.part_rows), pl.ds(head * HD, HD)],
                key_scr, value_scr, rows, head, None,
            )
            for head in range(sizes.heads)
        ]
        for head, (mixed, total, top) in enumerate(results):
            sum_ref[src, head] = mixed
            stat_ref[src, head] = jnp.where(left, top, total)


def attend_early(sizes, received, wait):
    count = len(received)
    shape = jax.ShapeDtypeStruct((count, sizes.heads, sizes.part_rows, HD), F32)
    return pl.pallas_call(
        functools.partial(early_kernel, sizes, count),
        out_shape=(shape, shape),
        in_specs=[VMEM_SPEC] * (count + 1),
        out_specs=(VMEM_SPEC, VMEM_SPEC),
        scratch_shapes=piece_scratch(sizes, count),
        compiler_params=limits(12),
        cost_estimate=pl.CostEstimate(flops=1, bytes_accessed=1, transcendentals=0),
    )(*received, wait)


def attend_kernel(sizes, masks, early, place_ref, *refs):
    count, heads, width = sizes.count, sizes.heads, sizes.width
    tok_rows, part_rows = sizes.tok_rows, sizes.part_rows
    in_refs, refs = refs[:count], refs[count:]
    kept_refs, refs = refs[: 2 if early else 0], refs[2 if early else 0 :]
    scale_ref, shift_ref, proj_ref, mod_ref, lat_ref, *refs = refs
    key_scr, value_scr = refs
    half = part_rows // 2
    me = place_ref[0]
    gain = 1.0 + scale_ref[...]
    shift = shift_ref[...]
    load_pieces(sizes, in_refs, key_scr, value_scr)
    groups = [range(early), range(early, count)] if early else [[src] for src in range(count)]
    for group in groups:
        mixed = []
        for head in range(heads):
            before = None
            rows = pl.ds(0, count * tok_rows)
            if group[0] < early:
                rows = pl.ds(early * tok_rows, (count - early) * tok_rows)
                sums = kept_refs[0][:, head].reshape(early * part_rows, HD)
                stat = kept_refs[1][:, head].reshape(early * part_rows, HD)
                before = (sums, stat[:, HD - 1 :], stat[:, :1])
            cols = pl.ds(head * HD, HD)
            query = jnp.concatenate([in_refs[src][pl.ds(0, part_rows), cols] for src in group], axis=0)
            value, total, _ = soft_part(query, key_scr, value_scr, rows, head, before)
            mixed.append(value / total)
        attended = jnp.concatenate(mixed, axis=1) if heads > 1 else mixed[0]
        modulated = (attended * gain + shift).astype(BF16)
        for at, src in enumerate(group):
            mod_ref[jnp.bitwise_xor(me, masks[src])] = modulated[at * part_rows : (at + 1) * part_rows]
    sides = [
        mm_nt(mod_ref[:, rows, :].reshape(count * half, width), proj_ref[...])
        for rows in (slice(0, half), slice(half, part_rows))
    ]
    latent = jnp.concatenate(sides, axis=1).astype(BF16)
    for spot, place in enumerate(sizes.order()):
        lat_ref[spot] = latent[place * half : (place + 1) * half]


def attend(sizes, masks, place, received, kept, scales, shifts, proj):
    count, width, heads = sizes.count, sizes.width, sizes.heads
    lat_rows = count * sizes.tok_rows
    query_rows = count * sizes.part_rows
    early = kept[0].shape[0] if kept else 0
    return pl.pallas_call(
        functools.partial(attend_kernel, sizes, masks, early),
        out_shape=(
            jax.ShapeDtypeStruct((count, sizes.part_rows, width), BF16),
            jax.ShapeDtypeStruct((count, sizes.part_rows // 2, 2 * CH), BF16),
        ),
        in_specs=[SMEM_SPEC] + [VMEM_SPEC] * (count + len(kept) + 3),
        out_specs=(VMEM_SPEC, VMEM_SPEC),
        scratch_shapes=piece_scratch(sizes, count),
        compiler_params=limits(16),
        cost_estimate=pl.CostEstimate(
            flops=4 * query_rows * lat_rows * width,
            bytes_accessed=2 * (query_rows * 2 + lat_rows * 2) * width,
            transcendentals=query_rows * lat_rows * heads,
        ),
    )(place, *received, *kept, scales, shifts, proj)


def total_kernel(copies, count, *refs):
    out_ref = refs[-1]
    if len(refs[0].shape) == 3:
        parts = [refs[0][i].astype(F32) for i in range(refs[0].shape[0])]
    else:
        parts = [ref[...].astype(F32) for ref in refs[:count]]
    while len(parts) > 1:
        parts = [parts[i] + parts[i + 1] for i in range(0, len(parts), 2)]
    for copy in range(copies):
        out_ref[copy] = parts[0].astype(BF16)


def total_copies(arrays, copies, others=()):
    return pl.pallas_call(
        functools.partial(total_kernel, copies, len(arrays)),
        out_shape=jax.ShapeDtypeStruct((copies,) + arrays[0].shape[-2:], BF16),
        in_specs=[VMEM_SPEC] * (len(arrays) + len(others)),
        out_specs=VMEM_SPEC,
        compiler_params=limits(),
    )(*arrays, *others)


def lane_mean(x, count):
    return jnp.sum(x, axis=-1, keepdims=True) * (1.0 / count)


def head_kernel(grid_rows, fused, order, embed_masks, out_factor, place_ref, lat_ref, *refs):
    embed_refs, refs = refs[: len(embed_masks)], refs[len(embed_masks) :]
    pos_ref, pre_ref, post_ref, prompt_ref, cot_ref, mod_ref, *refs = refs
    reward_ref, grad_ref, weight_ref, lat_scr, grad_scr, block_scr, back_scr = refs
    patch_rows = grid_rows // 4
    patch_cols = GW // 4
    patches = patch_rows * patch_cols
    for spot, place in enumerate(order):
        lat_scr[pl.ds(place * GW, GW), :] = lat_ref[pl.ds(spot * GW, GW), :].astype(F32)

    data = place_ref[1]
    shares = [
        (jnp.bitwise_xor(data, mask), ref, slot)
        for ref, masks in zip(embed_refs, embed_masks)
        for slot, mask in enumerate(masks)
    ]
    share_rows = embed_refs[0].shape[1]
    for hi in range(2):
        wide = []
        for tx in range(4):
            rows = [
                lat_scr[pl.ds((2 * pr + hi) * GW + tx, patch_cols, stride=4), :]
                for pr in range(patch_rows)
            ]
            wide.append(jnp.concatenate(rows, axis=0))
        for side in range(2):
            lanes = slice(side * CH, (side + 1) * CH)
            line = jnp.concatenate([x[:, lanes] for x in wide], axis=1).astype(BF16)
            first = (2 * hi + side) * 4 * CH
            if share_rows >= 4 * CH:
                at = first % share_rows
                block_scr[first // share_rows, :, pl.ds(at, 4 * CH)] = line
            else:
                for at in range(0, 4 * CH, share_rows):
                    block_scr[(first + at) // share_rows] = line[:, at : at + share_rows]
    embedded = pos_ref[...].astype(F32)
    for number, ref, slot in shares:
        embedded = embedded + mm(block_scr[number], ref[slot])
    pre = pre_ref[...].reshape(1, VW)
    post = post_ref[...].reshape(1, VW)
    prompt = prompt_ref[...]
    center = embedded - lane_mean(embedded, VW)
    rstd = lax.rsqrt(lane_mean(center * center, VW) + EPS)
    unit = center * rstd
    pooled = jnp.sum(unit, axis=0, keepdims=True) * (1.0 / patches) * pre
    pooled_center = pooled - lane_mean(pooled, VW)
    pooled_rstd = lax.rsqrt(lane_mean(pooled_center * pooled_center, VW) + EPS)
    pooled_unit = pooled_center * pooled_rstd
    final = pooled_unit * post
    dot = jnp.sum(final * prompt, axis=-1, keepdims=True)
    final_sq = jnp.sum(final * final, axis=-1, keepdims=True)
    prompt_sq = jnp.sum(prompt * prompt, axis=-1, keepdims=True)
    final_len = jnp.sqrt(final_sq)
    prompt_len = jnp.sqrt(prompt_sq)
    cosine = dot / (final_len * prompt_len)
    reward_ref[...] = jnp.broadcast_to(100.0 * cosine, reward_ref.shape)
    cot = cot_ref[:, :1]
    final_grad = (100.0 * cot) * (prompt / (final_len * prompt_len) - final * (cosine / final_sq))
    unit_grad = final_grad * post
    pooled_grad = pooled_rstd * (
        unit_grad
        - lane_mean(unit_grad, VW)
        - pooled_unit * lane_mean(unit_grad * pooled_unit, VW)
    )
    flow = pooled_grad * pre * (1.0 / patches)
    embed_grad = rstd * (flow - lane_mean(flow, VW) - unit * lane_mean(flow * unit, VW))
    high = embed_grad.astype(BF16)
    low = (embed_grad - high.astype(F32)).astype(BF16)
    stacked = jnp.concatenate([high, low], axis=0)
    for number, ref, slot in shares:
        both = mm_nt(stacked, ref[slot])
        back_scr[number] = both[:patches] + both[patches:]
    back = jnp.concatenate([back_scr[i] for i in range(16 * CH // share_rows)], axis=1)
    for hi in range(2):
        for tx in range(4):
            first = (4 * (2 * hi) + tx) * CH
            second = (4 * (2 * hi + 1) + tx) * CH
            piece = jnp.concatenate(
                [back[:, first : first + CH], back[:, second : second + CH]], axis=1
            )
            for pr in range(patch_rows):
                grad_scr[pl.ds((2 * pr + hi) * GW + tx, patch_cols, stride=4), :] = piece[
                    pr * patch_cols : (pr + 1) * patch_cols
                ]
    grad = grad_scr[...].astype(BF16)
    grad_ref[...] = grad
    if fused:
        store_readout_grad(grad, mod_ref, out_factor, weight_ref)
    else:
        weight_ref[...] = jnp.zeros_like(weight_ref)


def store_readout_grad(grad, mod_ref, out_factor, out_ref):
    turned = grad.astype(F32).T.astype(BF16)
    count, rows, width = mod_ref.shape
    half = rows // 2
    first = mod_ref[:, :half, :].reshape(count * half, width)
    second = mod_ref[:, half:, :].reshape(count * half, width)
    total = mm(turned[:CH], first) + mm(turned[CH:], second)
    out_ref[...] = (total * out_factor).astype(BF16)


def reward_head(
    place, order, latent, embed, pos, pre, post, prompt, cot, modulated, grid_rows, fused, out_factor
):
    patches = grid_rows * GW // 16
    rows = grid_rows * GW // 2
    width = modulated.shape[2]
    embed_arrays, embed_masks = [x for x, _ in embed], [masks for _, masks in embed]
    share_rows = embed_arrays[0].shape[1]
    return pl.pallas_call(
        functools.partial(head_kernel, grid_rows, fused, order, embed_masks, out_factor),
        out_shape=(
            jax.ShapeDtypeStruct((1, 128), F32),
            jax.ShapeDtypeStruct((rows, 2 * CH), BF16),
            jax.ShapeDtypeStruct((CH, width), BF16),
        ),
        in_specs=[SMEM_SPEC, VMEM_SPEC]
        + [VMEM_SPEC] * len(embed_arrays)
        + [VMEM_SPEC] * 6,
        out_specs=(VMEM_SPEC, VMEM_SPEC, VMEM_SPEC),
        scratch_shapes=[
            pltpu.VMEM((rows, 2 * CH), F32),
            pltpu.VMEM((rows, 2 * CH), F32),
            pltpu.VMEM((16 * CH // share_rows, patches, share_rows), BF16),
            pltpu.VMEM((16 * CH // share_rows, patches, share_rows), F32),
        ],
        compiler_params=limits(16),
        cost_estimate=pl.CostEstimate(
            flops=6 * patches * 16 * CH * VW,
            bytes_accessed=2 * 16 * CH * VW + 2 * patches * VW,
            transcendentals=0,
        ),
    )(place, latent, *embed_arrays, pos, pre, post, prompt, cot, modulated)


def spread_kernel(count, half, heads, grad_ref, scale_ref, proj_ref, out_ref, token_ref):
    token_ref[...] = jnp.zeros_like(token_ref)
    gain = 1.0 + scale_ref[...]
    proj = proj_ref[...]
    zero = jnp.zeros_like(proj)
    sides = (jnp.concatenate([proj, zero], axis=0), jnp.concatenate([zero, proj], axis=0))
    for src in range(count):
        grad = grad_ref[pl.ds(src * half, half), :]
        for side in range(2):
            rows = (mm(grad, sides[side]) * gain).astype(BF16)
            for head in range(heads):
                out_ref[0, head, pl.ds((2 * src + side) * half, half), :] = rows[
                    :, head * HD : (head + 1) * HD
                ]


def spread(grad, scales, proj, count, half, heads):
    return pl.pallas_call(
        functools.partial(spread_kernel, count, half, heads),
        out_shape=(
            jax.ShapeDtypeStruct((1, heads, 2 * count * half, HD), BF16),
            jax.ShapeDtypeStruct((8, 128), F32),
        ),
        in_specs=[VMEM_SPEC] * 3,
        out_specs=(VMEM_SPEC, VMEM_SPEC),
        compiler_params=limits(),
        cost_estimate=pl.CostEstimate(
            flops=8 * count * half * CH * heads * HD,
            bytes_accessed=4 * count * half * heads * HD,
            transcendentals=0,
        ),
    )(grad, scales, proj)


def weight_kernel(out_factor, grad_ref, *refs):
    store_readout_grad(grad_ref[...], refs[0], out_factor, refs[1])


def weight_call(grad, modulated, out_factor):
    return pl.pallas_call(
        functools.partial(weight_kernel, out_factor),
        out_shape=jax.ShapeDtypeStruct((CH, modulated.shape[2]), BF16),
        in_specs=[VMEM_SPEC] * 2,
        out_specs=VMEM_SPEC,
        compiler_params=limits(),
    )(grad, modulated)


def finish_kernel(order, in_ref, out_ref):
    width = in_ref.shape[2]
    for spot, group in enumerate(order):
        out_ref[:, pl.ds(group * width, width)] = in_ref[spot].astype(F32)


def finish(blocks, order):
    return pl.pallas_call(
        functools.partial(finish_kernel, order),
        out_shape=jax.ShapeDtypeStruct((CH, HEADS * HD), F32),
        in_specs=[VMEM_SPEC],
        out_specs=VMEM_SPEC,
        compiler_params=limits(),
    )(blocks)


def swap(x, axis, mask):
    count = lax.axis_size(axis)
    return lax.ppermute(x, axis, [(i, i ^ mask) for i in range(count)])


def all_to_all(x, groups=None):
    return lax.all_to_all(
        x, "seq", split_axis=0, concat_axis=0, tiled=True, axis_index_groups=groups
    )


def swap_both(x, seq_mask, data_mask):
    seq_count, data_count = lax.axis_size("seq"), lax.axis_size("dp")
    pairs = [
        (i * data_count + j, (i ^ seq_mask) * data_count + (j ^ data_mask))
        for i in range(seq_count)
        for j in range(data_count)
    ]
    return lax.ppermute(x, ("seq", "dp"), pairs)


def on_device(
    queries,
    keys,
    values,
    shifts,
    scales,
    proj_out,
    patch_embed,
    pos_embed,
    pre_gain,
    post_gain,
    prompt,
    cotangent,
):
    seq_count = lax.axis_size("seq")
    data_count = lax.axis_size("dp")
    tok_rows = queries.shape[1]
    sizes = Sizes(seq_count, data_count, tok_rows, patch_embed)
    query_parts, head_count, part_rows = sizes.query_parts, sizes.heads, sizes.part_rows
    group_count = HEADS // head_count
    seq_index = lax.axis_index("seq")
    head_group = seq_index // query_parts
    query_part = seq_index % query_parts
    half = part_rows // 2
    lat_rows = seq_count * tok_rows
    grid_rows = lat_rows // GW
    canonical = part_rows == 2 * GW
    place = jnp.stack([seq_index, lax.axis_index("dp"), head_group]).astype(jnp.int32)
    proj_turned = proj_out.T
    out_factor = 1.0 / math.sqrt(data_count * lat_rows)

    masks = sizes.pieces()
    packed = pack(
        sizes, in_hbm(queries), in_hbm(keys), in_hbm(values), in_hbm(patch_embed)
    )
    received = [swap(x, "seq", mask) if mask else x for mask, x in zip(masks, packed)]
    bits = [1 << b for b in reversed(range(data_count.bit_length() - 1))]
    shared = sizes.share < patch_embed.shape[0]
    scale, shift, proj, pos, pre, post, words, cot = fetch(
        sizes, place, cotangent, [scales, shifts, proj_turned, pos_embed, pre_gain, post_gain, prompt]
    )

    kept, order = [], list(range(seq_count))
    if seq_count == 8:
        late = [slot for slot, mask in enumerate(masks) if mask in (6, 7)]
        order = [slot for slot in order if slot not in late]
        kept = attend_early(sizes, [received[slot] for slot in order], scale)
        order = order + late
    if sizes.riding:
        ride = [slot for slot, mask in enumerate(masks) if sizes.rides(mask)]
        two = collect(sizes, [received[slot] for slot in ride])
        held = join(two, swap(two, "seq", 2), kept)
        ride_masks = [masks[slot] for slot in ride]
        ride_masks = ride_masks + [mask ^ 2 for mask in ride_masks]
        pairs = [
            (held, swap(held, "seq", 1)),
            (swap(held, "dp", bits[0]), swap_both(held, 1, bits[0])),
        ]

    modulated, latent_part = attend(
        sizes, [masks[slot] for slot in order], place, [received[slot] for slot in order], kept,
        scale, shift, proj,
    )

    if not sizes.riding:
        mine = patch_embed
        if shared:
            mine = lax.dynamic_slice_in_dim(
                patch_embed, lax.axis_index("dp") * sizes.share, sizes.share, 0
            )
        mine = lax.all_gather(mine, "seq", axis=1, tiled=True).reshape(-1, VW)
        embed = [(mine[None], [0])]
        if shared:
            embed = embed + [(swap(mine[None], "dp", bits[0]), [bits[0]])]

    groups, order = [sizes.order()], sizes.order()
    if query_parts > 1:
        order = list(range(group_count))
        groups = [[g * query_parts + r for g in range(group_count)] for r in range(query_parts)]
    per_share = seq_count // group_count
    parts = all_to_all(latent_part.reshape(group_count, per_share * half, 2 * CH), groups)
    summed = total_copies([parts], seq_count)
    if sizes.riding:
        embed = [(arrange(sizes, ride_masks, place, pairs, summed), [0, bits[0]])]
    for bit in bits[1:] if shared else []:
        embed = embed + [(swap(x, "dp", bit), [m ^ bit for m in some]) for x, some in embed]
    latent = all_to_all(summed, [sizes.order()])
    if canonical:
        latent = latent.reshape(lat_rows // 2, 2 * CH)
    else:
        latent = latent.reshape(group_count, query_parts, per_share, half, 2, CH)
        latent = latent.transpose(0, 2, 1, 4, 3, 5).reshape(grid_rows // 2, 2, GW, CH)
        latent = latent.transpose(0, 2, 1, 3).reshape(lat_rows // 2, 2 * CH)

    reward, grad, weight = reward_head(
        place, sizes.order() if canonical else list(range(grid_rows // 2)),
        latent, embed, pos, pre, post, words,
        cot, modulated, grid_rows, canonical, out_factor,
    )
    if not canonical:
        tokens = grad.reshape(grid_rows // 2, GW, 2, CH).transpose(0, 2, 1, 3)
        tokens = tokens.reshape(seq_count, query_parts, 2, half, CH)
        tokens = lax.dynamic_index_in_dim(tokens, query_part, 1, keepdims=False)
        grad = tokens.transpose(0, 2, 1, 3).reshape(seq_count * half, 2 * CH)
        weight = weight_call(grad, modulated, out_factor)

    parts = [weight] + [swap(weight, "dp", mask) for mask in range(1, data_count)]
    attn_grad, token = spread(grad, scale, proj, seq_count, half, head_count)
    if query_parts > 1:
        total = total_copies(parts, 1)[0]
        parts = [total] + [swap(total, "seq", mask) for mask in range(1, query_parts)]
    blocks = all_to_all(total_copies(parts, group_count, [token]), groups)
    return (reward[0, :1], attn_grad, finish(blocks, order).T)


def solution(mesh):
    return jax.shard_map(
        on_device,
        mesh=mesh,
        in_specs=(
            P("dp", "seq", None),
            P("dp", "seq", None),
            P("dp", "seq", None),
            P("dp", None),
            P("dp", None),
            P(),
            P(None, "seq", None),
            P(),
            P(),
            P(),
            P("dp", None),
            P("dp"),
        ),
        out_specs=(P("dp"), P("dp", "seq", None, None), P()),
        check_vma=False,
    )
```
